512 devices in a mesh: dp: 64 (over x, z), sub: 8 (over y, core).
Axes of the slice: x: 4, y: 4, z: 16, core: 2. Of those that a mesh axis runs over, the one named last changes fastest.
Arguments:
- points: bfloat16 [65536, 768], P(('dp', 'sub'))
- cand_rows: int32 [3, 2048], P(None, ('dp', 'sub')), may hold values from 0 to 127
- cand_count: int32 [3, 512], P(None, ('dp', 'sub')), may hold values from 0 to 4, as said below
Outputs:
- weights: float32 [3, 65536], P(None, ('dp', 'sub'))
The draws below stay inside these ranges and needn't reach their ends.
Inputs may be any that keep to these rules, and one draw needn't show every extreme that they name: `cand_rows`: local row numbers on the device whose slots they fill; slots at or past the count are ignored. `cand_count`: in every round the devices of each group along sub hold exactly 16 candidates together; in every round some device holds 4.
All inputs are finite; a program needn't handle non-finite values.
Results may differ from the reference program's by a relative error of at most 0.0003.
Values may be sent and summed in bfloat16 or wider, within the bound.
A program may use at most 64 MiB of HBM per device.

```python
import math
import jax
import jax.numpy as jnp
from jax import lax

D = 768
P_DEV = 128
ROUNDS = 3
CAND_DEV = 2
SLOTS = 4
NPTS = 65536
CANDS = 1024
DEVICES = 512


def unit_rows(values):
    return values * lax.rsqrt(jnp.sum(values * values, axis=1, keepdims=True))


def draw_points(key, part):
    key = jax.random.fold_in(key, 11)
    first, second, third, fourth = jax.random.split(key, 4)
    centre_total = max(CANDS // 4, 4)
    member = jax.random.randint(first, (NPTS,), 0, centre_total)
    position = jnp.arange(NPTS, dtype=jnp.float32) / NPTS
    raw = jax.random.normal(second, (centre_total, D), jnp.float32)
    noise = jax.random.normal(third, (NPTS, D), jnp.float32)
    spread = jnp.exp(jax.random.uniform(fourth, (NPTS,), jnp.float32, math.log(0.7), math.log(1.4)))
    sigma = (0.2 + 0.6 * position) * spread
    centres = unit_rows(raw)
    values = centres[member] + noise * (sigma * (1.0 / math.sqrt(D)))[:, None]
    return unit_rows(values).astype(jnp.bfloat16)


def draw_cand_count(key, part):
    key = jax.random.fold_in(key, 23)
    first, second = jax.random.split(key)
    pairs = DEVICES // 2
    shift = jax.random.randint(first, (ROUNDS, pairs), 0, CAND_DEV + 1)
    shift = shift.at[:, 0].set(CAND_DEV)
    sign = 2 * jax.random.randint(second, (ROUNDS, pairs), 0, 2) - 1
    upper = CAND_DEV + shift * sign
    lower = CAND_DEV - shift * sign
    return jnp.stack([upper, lower], axis=2).reshape(ROUNDS, DEVICES).astype(jnp.int32)


def place_ends(result, rng, least, high):
    spot = [jax.random.randint(jax.random.fold_in(rng, axis), (), 0, length) for axis, length in enumerate(result.shape)]
    main_axis = result.shape.index(max(result.shape))
    neighbour = spot[:main_axis] + [(spot[main_axis] + 1) % result.shape[main_axis]] + spot[main_axis + 1:]
    return result.at[tuple(spot)].set(least).at[tuple(neighbour)].set(high)


def setup_inputs(seed: int = 0) -> dict:
    key_list = jax.random.split(jax.random.key(seed), 4)
    points = draw_points(jax.random.fold_in(key_list[3], 71), 0)
    cand_rows = place_ends(jax.random.randint(key_list[1], (ROUNDS, DEVICES * SLOTS), 0, P_DEV), jax.random.fold_in(key_list[1], 1), 0, P_DEV - 1).astype(jnp.int32)
    cand_count = draw_cand_count(jax.random.fold_in(key_list[3], 71), 0)
    return {"points": points, "cand_rows": cand_rows, "cand_count": cand_count}


def reference(points, cand_rows, cand_count):
    blocks = points.reshape(DEVICES, P_DEV, D)
    sq = jnp.sum(jnp.square(points.astype(jnp.float32)), axis=1).reshape(DEVICES, P_DEV)
    nearest = jnp.full((DEVICES, P_DEV), jnp.inf, jnp.float32)
    outputs = []
    for step in range(ROUNDS):
        index = cand_rows[step].reshape(DEVICES, SLOTS)
        chosen = jax.vmap(lambda blk, idx: blk[idx])(blocks, index).reshape(DEVICES * SLOTS, D)
        slot = jnp.arange(SLOTS, dtype=jnp.int32)[None, :]
        live = (slot < cand_count[step][:, None]).reshape(DEVICES * SLOTS)
        cands = chosen.astype(jnp.float32)
        csq = jnp.sum(jnp.square(cands), axis=1)

        def closest(args):
            block, bsq = args
            dots = jnp.dot(block.astype(jnp.float32), cands.T, precision=lax.Precision.HIGHEST)
            dist = jnp.maximum(bsq[:, None] + csq[None, :] - 2.0 * dots, 0.0)
            dist = jnp.where(live[None, :], dist, jnp.inf)
            return jnp.min(dist, axis=1)

        best = lax.map(closest, (blocks, sq))
        nearest = jnp.minimum(nearest, best)
        cost = jnp.sum(nearest)
        outputs.append((float(NPTS) * nearest / cost).reshape(NPTS))
    return jnp.stack(outputs)
```

```python
import jax
import jax.numpy as jnp
from jax import lax
from jax.experimental import pallas as pl
from jax.experimental.pallas import tpu as pltpu
from jax.sharding import PartitionSpec as P

ROUNDS = 3
SLOTS = 4
XS = 4
ZS = 16
YS = 4
SUBS = 8
BLK = 16
PEN = ROUNDS * SLOTS
HALF = ZS // 2
MESH = pl.DeviceIdType.MESH
F32 = jnp.float32
INF = float("inf")


def kernel(
    npts,
    rows_ref,
    cnt_ref,
    points_ref,
    out_ref,
    cand,
    pall,
    mins,
    line,
    near,
    zsum,
    xsum,
    local_sem,
    ring_send,
    x_send,
    opp_send,
    opp_recv,
    ring_recv,
    x_recv,
    pts_send,
    pts_recv,
    line_send,
    line_recv,
    z_send,
    z_recv,
    c_send,
    c_recv,
):
    dp = lax.axis_index("dp")
    sub = lax.axis_index("sub")
    x, z = lax.div(dp, ZS), lax.rem(dp, ZS)
    y, core = lax.div(sub, 2), lax.rem(sub, 2)
    npd, width = points_ref.shape

    def at_x(d):
        return (lax.rem(x + d, XS) * ZS + z, sub)

    def at_z(d):
        return (x * ZS + lax.rem(z + d, ZS), sub)

    def at_y(d):
        return (dp, lax.rem(y + d, YS) * 2 + core)

    other_core = (dp, y * 2 + (1 - core))
    z_right, z_left = at_z(1), at_z(ZS - 1)
    x_right, x_left, x_far = at_x(1), at_x(3), at_x(2)
    y_right, y_left = at_y(1), at_y(3)

    own_points = pltpu.make_async_copy(points_ref, pall.at[sub], local_sem)
    own_points.start()
    barrier = pltpu.get_barrier_semaphore()
    partners = (z_right, z_left, x_right, x_left, x_far, y_right, y_left, other_core)
    for device in partners:
        pl.semaphore_signal(barrier, inc=1, device_id=device, device_id_type=MESH)

    row = lax.broadcasted_iota(jnp.int32, (BLK, npd), 0)
    lane = lax.broadcasted_iota(jnp.int32, (BLK, npd), 1)
    target = jnp.full((BLK, npd), -1, jnp.int32)
    penalty = jnp.zeros((BLK, npd), F32)
    for r in range(ROUNDS):
        for i in range(SLOTS):
            j = r * SLOTS + i
            live = i < cnt_ref[r, 0]
            target = jnp.where(row == j, jnp.where(live, rows_ref[r, i], -1), target)
            penalty = jnp.where(lane == j, jnp.where(live, 0.0, INF), penalty)
    pick = jnp.where(lane == target, 1.0, 0.0).astype(jnp.bfloat16)
    own_points.wait()
    mine = pall[sub]
    block = jnp.dot(pick, mine, preferred_element_type=F32)
    head = jnp.where(row == PEN, penalty, block[:, :npd])
    cand[0, 0, :, :npd] = head.astype(jnp.bfloat16)
    cand[0, 0, :, npd:] = block[:, npd:].astype(jnp.bfloat16)
    eye = lax.broadcasted_iota(jnp.int32, (npd, npd), 0) == lax.broadcasted_iota(jnp.int32, (npd, npd), 1)
    wide = mine.astype(F32)
    sq_col = jnp.sum(wide * wide, axis=1, keepdims=True)
    sq_row = jnp.sum(jnp.where(eye, sq_col, 0.0), axis=0, keepdims=True)
    member = lax.broadcasted_iota(jnp.int32, (SUBS, npd), 0)
    line[sub, 3] = jnp.where(member == sub, sq_row, 0.0)

    pl.semaphore_wait(barrier, len(partners))

    def remote(src, dst, send, recv, device):
        return pltpu.make_async_remote_copy(
            src_ref=src, dst_ref=dst, send_sem=send, recv_sem=recv, device_id=device, device_id_type=MESH
        )

    def ring(chain, side, step):
        there = 2 * step - 1 + side if not isinstance(step, int) or step < HALF else 2 * HALF - 1
        if isinstance(step, int):
            here = 0 if step == 1 else 2 * step - 3 + side
        else:
            here = 2 * step - 3 + side
        return remote(
            cand.at[here, chain],
            cand.at[there, chain],
            ring_send,
            ring_recv.at[chain, side, step],
            (z_right, z_left)[side],
        )

    def ring_wait(chain, side, step):
        place = cand.at[2 * step - 1 + side if not isinstance(step, int) or step < HALF else 2 * HALF - 1, chain]
        pltpu.make_async_copy(place, place, ring_recv.at[chain, side, step]).wait()

    def across(place, count, part):
        src = cand.at[pl.ds(place, count), 0]
        to_right = remote(src, cand.at[pl.ds(place, count), 3], x_send, x_recv.at[part], x_right)
        to_left = remote(src, cand.at[pl.ds(place, count), 2], x_send, x_recv.at[part], x_left)
        return to_right, to_left

    def start_all(copies):
        for copy in copies:
            copy.start()

    def wait_bytes(ref, sem):
        pltpu.make_async_copy(ref, ref, sem).wait()

    ring(0, 0, 1).start()
    ring(0, 1, 1).start()
    opposite = remote(cand.at[0, 0], cand.at[0, 1], opp_send, opp_recv, x_far)
    opposite.start()
    start_all(across(0, 1, 0))
    slot_right, slot_left, slot_far = (lax.rem(y + d, YS) * 2 + core for d in (1, 3, 2))
    top, low = pl.ds(0, npd // 2), pl.ds(npd // 2, npd // 2)
    mine_at = pall.at[sub]
    pts_right = remote(mine_at, mine_at, pts_send.at[0], pts_recv.at[0], y_right)
    pts_left = remote(mine_at, mine_at, pts_send.at[1], pts_recv.at[1], y_left)
    pts_core = remote(mine_at, mine_at, pts_send.at[2], pts_recv.at[2], other_core)
    start_all((pts_right, pts_left, pts_core))

    def step(k, last_a_left=False, first=False):
        ring_wait(0, 0, k)
        ring(0, 0, k + 1).start()
        ring_wait(0, 1, k)
        if not last_a_left:
            ring(0, 1, k + 1).start()
        if first:
            opposite.wait_recv()
        else:
            ring_wait(1, 0, k - 1)
        ring(1, 0, k).start()
        if not first:
            ring_wait(1, 1, k - 1)
        ring(1, 1, k).start()

    def loop_step(k, carry):
        step(k)
        start_all(across(2 * k - 1, 2, 0))
        return carry

    step(1, first=True)
    start_all(across(1, 2, 0))
    lax.fori_loop(2, 5, loop_step, 0)

    pts_right.wait_recv()
    near_left = pall.at[slot_left]
    far_top = remote(near_left.at[top], near_left.at[top], pts_send.at[3], pts_recv.at[3], y_right)
    core_left = remote(near_left, near_left, pts_send.at[4], pts_recv.at[4], other_core)
    start_all((far_top, core_left))
    pts_left.wait_recv()
    near_right = pall.at[slot_right]
    far_low = remote(near_right.at[low], near_right.at[low], pts_send.at[5], pts_recv.at[5], y_left)
    core_right = remote(near_right, near_right, pts_send.at[6], pts_recv.at[6], other_core)
    start_all((far_low, core_right))

    lax.fori_loop(5, 7, loop_step, 0)
    step(7, last_a_left=True)
    start_all(across(13, 2, 1))

    far_top.wait_recv()
    far_low.wait_recv()
    far = pall.at[slot_far]
    core_far = remote(far, far, pts_send.at[7], pts_recv.at[7], other_core)
    core_far.start()

    ring_wait(0, 0, 8)
    start_all(across(15, 1, 1))
    ring_wait(1, 0, 7)
    ring_wait(1, 1, 7)
    ring(1, 1, 8).start()

    def absorb(first_place, last_place):
        places = last_place - first_place
        rows = cand[first_place:last_place].reshape(places * XS, BLK, width)
        half = jnp.zeros((places * XS, BLK, npd), F32)
        for t in range(width // npd):
            piece = rows[:, :, t * npd : (t + 1) * npd].astype(F32)
            half = half + piece * piece
        pen = rows[:, :, :npd].astype(F32)[:, PEN : PEN + 1, :]
        half = 0.5 * half + jnp.where((row == lane)[None], pen, 0.0)
        half = jnp.sum(half, axis=2, keepdims=True)
        flat = rows.reshape(places * XS * BLK, width)

        def pair(j, carry):
            group = pall[pl.ds(2 * j, 2)].reshape(2 * npd, width)
            dots = lax.dot_general(flat, group, (((1,), (1,)), ((), ())), preferred_element_type=F32)
            value = half - dots.reshape(places * XS, BLK, 2 * npd)
            best = jnp.min(value, axis=0)
            mins[j] = best if first_place == 0 else jnp.minimum(mins[j], best)
            return carry

        lax.fori_loop(0, SUBS // 2, pair, 0)

    pts_core.wait_recv()
    core_left.wait_recv()
    core_right.wait_recv()
    core_far.wait_recv()
    wait_bytes(cand.at[pl.ds(0, 13), pl.ds(2, 2)], x_recv.at[0])
    absorb(0, 13)
    ring_wait(1, 1, 8)
    wait_bytes(cand.at[pl.ds(0, 3), pl.ds(2, 2)], x_recv.at[1])
    absorb(13, 16)

    for j in range(SUBS // 2):
        for r in range(ROUNDS):
            low_r = jnp.min(mins[j, r * SLOTS : (r + 1) * SLOTS, :], axis=0, keepdims=True)
            for h in range(2):
                line[sub, r, 2 * j + h : 2 * j + h + 1, :] = low_r[:, h * npd : (h + 1) * npd]

    def to_line(d, carry):
        device = (dp, lax.rem(sub + d, SUBS))
        remote(line.at[sub], line.at[sub], line_send, line_recv, device).start()
        return carry

    lax.fori_loop(1, SUBS, to_line, 0)
    wait_bytes(line.at[pl.ds(0, SUBS - 1)], line_recv)

    lanes = lax.broadcasted_iota(jnp.int32, (1, npd), 1)
    squares = jnp.sum(line[:, 3], axis=0)
    least = None
    total = jnp.zeros((1, npd), F32)
    for r in range(ROUNDS):
        now = jnp.min(line[:, r], axis=0)
        least = now if least is None else jnp.minimum(least, now)
        dist = jnp.maximum(squares + 2.0 * least, 0.0)
        near[r] = dist
        part = jnp.sum(jnp.sum(dist, axis=0, keepdims=True), axis=1, keepdims=True)
        total = jnp.where(lanes == r, part, total)

    zsum[0] = total

    def to_z(d, carry):
        remote(zsum.at[0], zsum.at[ZS - d], z_send, z_recv, at_z(d)).start()
        return carry

    lax.fori_loop(1, ZS, to_z, 0)
    wait_bytes(zsum.at[pl.ds(0, ZS - 1)], z_recv)
    xsum[0] = jnp.sum(zsum[...], axis=0)
    for d, device in ((1, x_right), (2, x_far), (3, x_left)):
        remote(xsum.at[0], xsum.at[XS - d], c_send, c_recv, device).start()
    wait_bytes(xsum.at[pl.ds(0, XS - 1)], c_recv)
    cost = jnp.sum(xsum[...], axis=0)
    for r in range(ROUNDS):
        cost_r = jnp.sum(jnp.where(lanes == r, cost, 0.0), axis=1, keepdims=True)
        out_ref[r : r + 1, :] = npts * near[r, pl.ds(sub, 1), :] / cost_r

    wait_bytes(cand.at[pl.ds(0, 15), pl.ds(0, 2)], ring_send)
    opposite.wait_send()
    wait_bytes(cand.at[pl.ds(0, 16), pl.ds(0, 2)], x_send)
    for copy in (pts_right, pts_left, pts_core, far_top, core_left, far_low, core_right, core_far):
        copy.wait_send()
    wait_bytes(line.at[pl.ds(0, SUBS - 1)], line_send)
    wait_bytes(zsum.at[pl.ds(0, ZS - 1)], z_send)
    wait_bytes(xsum.at[pl.ds(0, XS - 1)], c_send)


def shards(points, cand_rows, cand_count):
    npd, width = points.shape
    npts = float(npd * lax.axis_size(("dp", "sub")))
    dma = pltpu.SemaphoreType.DMA
    return pl.pallas_call(
        lambda *refs: kernel(npts, *refs),
        out_shape=jax.ShapeDtypeStruct((ROUNDS, npd), F32),
        in_specs=[
            pl.BlockSpec(memory_space=pltpu.SMEM),
            pl.BlockSpec(memory_space=pltpu.SMEM),
            pl.BlockSpec(memory_space=pl.ANY),
        ],
        out_specs=pl.BlockSpec(memory_space=pltpu.VMEM),
        scratch_shapes=[
            pltpu.VMEM((ZS, XS, BLK, width), jnp.bfloat16),
            pltpu.VMEM((SUBS, npd, width), jnp.bfloat16),
            pltpu.VMEM((SUBS // 2, BLK, 2 * npd), F32),
            pltpu.VMEM((SUBS, 4, SUBS, npd), F32),
            pltpu.VMEM((ROUNDS, SUBS, npd), F32),
            pltpu.VMEM((ZS, 1, npd), F32),
            pltpu.VMEM((XS, 1, npd), F32),
            dma,
            dma,
            dma,
            dma,
            dma,
            dma((2, 2, HALF + 1)),
            dma((2,)),
            dma((8,)),
            dma((8,)),
            dma,
            dma,
            dma,
            dma,
            dma,
            dma,
        ],
        compiler_params=pltpu.CompilerParams(
            collective_id=0, has_side_effects=True, vmem_limit_bytes=40 * 1024 * 1024
        ),
        cost_estimate=pl.CostEstimate(
            flops=2 * 1024 * 1024 * width, bytes_accessed=npd * width * 2, transcendentals=0
        ),
    )(cand_rows, cand_count, points)


def solution(mesh):
    in_specs = (P(("dp", "sub"), None), P(None, ("dp", "sub")), P(None, ("dp", "sub")))
    out_specs = P(None, ("dp", "sub"))
    return jax.shard_map(shards, mesh=mesh, in_specs=in_specs, out_specs=out_specs, check_vma=False)
```

```python
import jax
import jax.numpy as jnp
from jax import lax
from jax.experimental import pallas as pl
from jax.experimental.pallas import tpu as pltpu
from jax.sharding import PartitionSpec as P

ROUNDS = 3
SLOTS = 4
XS = 4
ZS = 16
YS = 4
SUBS = 8
BLK = 16
PEN = ROUNDS * SLOTS
MESH = pl.DeviceIdType.MESH
F32 = jnp.float32
INF = float("inf")


def kernel(
    npts,
    rows_ref,
    cnt_ref,
    points_ref,
    out_ref,
    cand,
    pall,
    mins,
    line,
    near,
    zsum,
    xsum,
    local_sem,
    hi_send,
    lo_send,
    x_send,
    hi_recv,
    lo_recv,
    x_recv,
    pts_send,
    pts_recv,
    line_send,
    line_recv,
    z_send,
    z_recv,
    c_send,
    c_recv,
):
    dp = lax.axis_index("dp")
    sub = lax.axis_index("sub")
    x, z = lax.div(dp, ZS), lax.rem(dp, ZS)
    y, core = lax.div(sub, 2), lax.rem(sub, 2)
    npd, width = points_ref.shape

    def at_x(d):
        return (lax.rem(x + d, XS) * ZS + z, sub)

    def at_z(d):
        return (x * ZS + lax.rem(z + d, ZS), sub)

    def at_y(d):
        return (dp, lax.rem(y + d, YS) * 2 + core)

    other_core = (dp, y * 2 + (1 - core))
    z_right, z_left, z_right2, z_left2 = at_z(1), at_z(ZS - 1), at_z(2), at_z(ZS - 2)
    x_to = {d: at_x(d) for d in (1, 2, 3)}
    y_right, y_left = at_y(1), at_y(3)

    own_points = pltpu.make_async_copy(points_ref, pall.at[sub], local_sem)
    own_points.start()
    barrier = pltpu.get_barrier_semaphore()
    near_z = (z_right, z_left, z_right2, z_left2, at_z(4), at_z(8), at_z(12))
    partners = near_z + (x_to[1], x_to[2], x_to[3], y_right, y_left, other_core)
    for device in partners:
        pl.semaphore_signal(barrier, inc=1, device_id=device, device_id_type=MESH)

    row = lax.broadcasted_iota(jnp.int32, (BLK, npd), 0)
    lane = lax.broadcasted_iota(jnp.int32, (BLK, npd), 1)
    target = jnp.full((BLK, npd), -1, jnp.int32)
    penalty = jnp.zeros((BLK, npd), F32)
    for r in range(ROUNDS):
        for i in range(SLOTS):
            j = r * SLOTS + i
            live = i < cnt_ref[0, r]
            target = jnp.where(row == j, jnp.where(live, rows_ref[r, i], -1), target)
            penalty = jnp.where(lane == j, jnp.where(live, 0.0, INF), penalty)
    pick = jnp.where(lane == target, 1.0, 0.0).astype(jnp.bfloat16)
    own_points.wait()
    mine = pall[sub]
    block = jnp.dot(pick, mine, preferred_element_type=F32)
    head = jnp.where(row == PEN, penalty, block[:, :npd])
    cand[0, 0, 0, :, :npd] = head.astype(jnp.bfloat16)
    cand[0, 0, 0, :, npd:] = block[:, npd:].astype(jnp.bfloat16)
    eye = lax.broadcasted_iota(jnp.int32, (npd, npd), 0) == lax.broadcasted_iota(jnp.int32, (npd, npd), 1)
    wide = mine.astype(F32)
    sq_col = jnp.sum(wide * wide, axis=1, keepdims=True)
    sq_row = jnp.sum(jnp.where(eye, sq_col, 0.0), axis=0, keepdims=True)
    member = lax.broadcasted_iota(jnp.int32, (SUBS, npd), 0)
    line[sub, 3] = jnp.where(member == sub, sq_row, 0.0)

    pl.semaphore_wait(barrier, len(partners))

    def remote(src, dst, send, recv, device):
        return pltpu.make_async_remote_copy(
            src_ref=src, dst_ref=dst, send_sem=send, recv_sem=recv, device_id=device, device_id_type=MESH
        )

    def to_col(block_lo, block_hi):
        for d in (1, 3, 2):
            src = cand.at[block_lo, block_hi, 0]
            remote(src, cand.at[block_lo, block_hi, d], x_send, x_recv.at[block_lo], x_to[d]).start()

    def hop(block_hi, lo, place, device):
        return remote(cand.at[0, block_hi, 0], cand.at[lo, place, 0], lo_send, lo_recv.at[lo, place], device)

    def jump(d):
        return remote(cand.at[0, 0, 0], cand.at[0, d, 0], hi_send, hi_recv.at[d], at_z(4 * d))

    def wait_bytes(ref, sem):
        pltpu.make_async_copy(ref, ref, sem).wait()

    def lo_arrived(lo, place):
        wait_bytes(cand.at[lo, place, 0], lo_recv.at[lo, place])
        to_col(lo, place)

    jumps = {d: jump(d) for d in (1, 3, 2)}
    for d in (1, 3, 2):
        jumps[d].start()
    hop(0, 1, 0, z_right).start()
    hop(0, 3, 0, z_left).start()
    hop(0, 2, 0, z_right2).start()
    hop(0, 2, 2, z_left2).start()
    to_col(0, 0)

    slot_right, slot_left, slot_far = (lax.rem(y + d, YS) * 2 + core for d in (1, 3, 2))
    top, low = pl.ds(0, npd // 2), pl.ds(npd // 2, npd // 2)
    mine_at = pall.at[sub]
    pts_right = remote(mine_at, mine_at, pts_send.at[0], pts_recv.at[0], y_right)
    pts_left = remote(mine_at, mine_at, pts_send.at[1], pts_recv.at[1], y_left)
    pts_core = remote(mine_at, mine_at, pts_send.at[2], pts_recv.at[2], other_core)
    pts_right.start()
    pts_left.start()
    pts_core.start()

    jumps[1].wait_recv()
    hop(1, 1, 1, z_right).start()
    hop(1, 3, 1, z_left).start()
    hop(1, 2, 1, z_right2).start()
    jumps[3].wait_recv()
    hop(3, 1, 3, z_right).start()
    hop(3, 3, 3, z_left).start()
    hop(3, 2, 3, z_left2).start()
    jumps[2].wait_recv()
    hop(2, 1, 2, z_right).start()
    hop(2, 3, 2, z_left).start()
    for d in (1, 3, 2):
        to_col(0, d)
    for lo, place in ((1, 0), (3, 0), (2, 0), (2, 2), (1, 1), (3, 3), (3, 1), (1, 3), (2, 1), (2, 3), (1, 2), (3, 2)):
        lo_arrived(lo, place)

    pts_right.wait_recv()
    near_left = pall.at[slot_left]
    far_top = remote(near_left.at[top], near_left.at[top], pts_send.at[3], pts_recv.at[3], y_right)
    core_left = remote(near_left, near_left, pts_send.at[4], pts_recv.at[4], other_core)
    far_top.start()
    core_left.start()
    pts_left.wait_recv()
    near_right = pall.at[slot_right]
    far_low = remote(near_right.at[low], near_right.at[low], pts_send.at[5], pts_recv.at[5], y_left)
    core_right = remote(near_right, near_right, pts_send.at[6], pts_recv.at[6], other_core)
    far_low.start()
    core_right.start()
    far_top.wait_recv()
    far_low.wait_recv()
    far = pall.at[slot_far]
    core_far = remote(far, far, pts_send.at[7], pts_recv.at[7], other_core)
    core_far.start()

    def absorb(lo):
        rows = cand[lo].reshape(ZS, BLK, width)
        half = jnp.zeros((ZS, BLK, npd), F32)
        for t in range(width // npd):
            piece = rows[:, :, t * npd : (t + 1) * npd].astype(F32)
            half = half + piece * piece
        pen = rows[:, :, :npd].astype(F32)[:, PEN : PEN + 1, :]
        half = 0.5 * half + jnp.where((row == lane)[None], pen, 0.0)
        half = jnp.sum(half, axis=2, keepdims=True)
        flat = rows.reshape(ZS * BLK, width)

        def pair(j, carry):
            group = pall[pl.ds(2 * j, 2)].reshape(2 * npd, width)
            dots = lax.dot_general(flat, group, (((1,), (1,)), ((), ())), preferred_element_type=F32)
            value = half - dots.reshape(ZS, BLK, 2 * npd)
            best = jnp.min(value, axis=0)
            mins[j] = best if lo == 0 else jnp.minimum(mins[j], best)
            return carry

        lax.fori_loop(0, SUBS // 2, pair, 0)

    pts_core.wait_recv()
    core_left.wait_recv()
    core_right.wait_recv()
    core_far.wait_recv()
    for lo in (0, 1, 3, 2):
        wait_bytes(cand.at[lo, :, pl.ds(1, 3)], x_recv.at[lo])
        absorb(lo)

    for j in range(SUBS // 2):
        for r in range(ROUNDS):
            low_r = jnp.min(mins[j, r * SLOTS : (r + 1) * SLOTS, :], axis=0, keepdims=True)
            for h in range(2):
                line[sub, r, 2 * j + h : 2 * j + h + 1, :] = low_r[:, h * npd : (h + 1) * npd]

    def to_line(d, carry):
        device = (dp, lax.rem(sub + d, SUBS))
        remote(line.at[sub], line.at[sub], line_send, line_recv, device).start()
        return carry

    lax.fori_loop(1, SUBS, to_line, 0)
    wait_bytes(line.at[pl.ds(0, SUBS - 1)], line_recv)

    lanes = lax.broadcasted_iota(jnp.int32, (1, npd), 1)
    squares = jnp.sum(line[:, 3], axis=0)
    least = None
    total = jnp.zeros((1, npd), F32)
    for r in range(ROUNDS):
        now = jnp.min(line[:, r], axis=0)
        least = now if least is None else jnp.minimum(least, now)
        dist = jnp.maximum(squares + 2.0 * least, 0.0)
        near[r] = dist
        part = jnp.sum(jnp.sum(dist, axis=0, keepdims=True), axis=1, keepdims=True)
        total = jnp.where(lanes == r, part, total)

    zsum[0] = total

    def to_z(d, carry):
        remote(zsum.at[0], zsum.at[ZS - d], z_send, z_recv, at_z(d)).start()
        return carry

    lax.fori_loop(1, ZS, to_z, 0)
    wait_bytes(zsum.at[pl.ds(0, ZS - 1)], z_recv)
    xsum[0] = jnp.sum(zsum[...], axis=0)
    for d in (1, 3, 2):
        remote(xsum.at[0], xsum.at[XS - d], c_send, c_recv, x_to[d]).start()
    wait_bytes(xsum.at[pl.ds(0, XS - 1)], c_recv)
    cost = jnp.sum(xsum[...], axis=0)
    for r in range(ROUNDS):
        cost_r = jnp.sum(jnp.where(lanes == r, cost, 0.0), axis=1, keepdims=True)
        out_ref[r : r + 1, :] = npts * near[r, pl.ds(sub, 1), :] / cost_r

    wait_bytes(cand.at[0, 0, pl.ds(0, 3)], hi_send)
    wait_bytes(cand.at[pl.ds(0, 3), :, 0], lo_send)
    wait_bytes(cand.at[:, :, pl.ds(0, 3)], x_send)
    for copy in (pts_right, pts_left, pts_core, far_top, core_left, far_low, core_right, core_far):
        copy.wait_send()
    wait_bytes(line.at[pl.ds(0, SUBS - 1)], line_send)
    wait_bytes(zsum.at[pl.ds(0, ZS - 1)], z_send)
    wait_bytes(xsum.at[pl.ds(0, XS - 1)], c_send)


def shards(points, cand_rows, cand_count):
    npd, width = points.shape
    npts = float(npd * lax.axis_size(("dp", "sub")))
    dma = pltpu.SemaphoreType.DMA
    return pl.pallas_call(
        lambda *refs: kernel(npts, *refs),
        out_shape=jax.ShapeDtypeStruct((ROUNDS, npd), F32),
        in_specs=[
            pl.BlockSpec(memory_space=pltpu.SMEM),
            pl.BlockSpec(memory_space=pltpu.SMEM),
            pl.BlockSpec(memory_space=pl.ANY),
        ],
        out_specs=pl.BlockSpec(memory_space=pltpu.VMEM),
        scratch_shapes=[
            pltpu.VMEM((4, 4, XS, BLK, width), jnp.bfloat16),
            pltpu.VMEM((SUBS, npd, width), jnp.bfloat16),
            pltpu.VMEM((SUBS // 2, BLK, 2 * npd), F32),
            pltpu.VMEM((SUBS, 4, SUBS, npd), F32),
            pltpu.VMEM((ROUNDS, SUBS, npd), F32),
            pltpu.VMEM((ZS, 1, npd), F32),
            pltpu.VMEM((XS, 1, npd), F32),
            dma,
            dma,
            dma,
            dma,
            dma((4,)),
            dma((4, 4)),
            dma((4,)),
            dma((8,)),
            dma((8,)),
            dma,
            dma,
            dma,
            dma,
            dma,
            dma,
        ],
        compiler_params=pltpu.CompilerParams(
            collective_id=0, has_side_effects=True, vmem_limit_bytes=60 * 1024 * 1024
        ),
        cost_estimate=pl.CostEstimate(
            flops=2 * 1024 * 1024 * width, bytes_accessed=npd * width * 2, transcendentals=0
        ),
    )(cand_rows, cand_count.reshape(1, ROUNDS), points)


def solution(mesh):
    in_specs = (P(("dp", "sub"), None), P(None, ("dp", "sub")), P(None, ("dp", "sub")))
    out_specs = P(None, ("dp", "sub"))
    return jax.shard_map(shards, mesh=mesh, in_specs=in_specs, out_specs=out_specs, check_vma=False)
```

```python
import jax
import jax.numpy as jnp
from jax import lax
from jax.experimental import pallas as pl
from jax.experimental.pallas import tpu as pltpu
from jax.sharding import PartitionSpec as P

ROUNDS = 3
SLOTS = 4
XS = 4
ZS = 16
YS = 4
SUBS = 8
RAW = 16
BLK = 8
SHARE = 2
MESH = pl.DeviceIdType.MESH
F32 = jnp.float32
INF = float("inf")


def kernel(
    npts,
    rows_ref,
    cnt_ref,
    points_ref,
    out_ref,
    raw,
    slots,
    cand,
    pall,
    mins,
    squares,
    line,
    near,
    zsum,
    xsum,
    local_sem,
    slots_send,
    slots_recv,
    hi_send,
    lo_send,
    x_send,
    hi_recv,
    lo_recv,
    x_recv,
    pts_send,
    pts_recv,
    line_send,
    line_recv,
    z_send,
    z_recv,
    c_send,
    c_recv,
):
    dp = lax.axis_index("dp")
    sub = lax.axis_index("sub")
    x, z = lax.div(dp, ZS), lax.rem(dp, ZS)
    y, core = lax.div(sub, 2), lax.rem(sub, 2)
    npd, width = points_ref.shape

    def at_x(d):
        return (lax.rem(x + d, XS) * ZS + z, sub)

    def at_z(d):
        return (x * ZS + lax.rem(z + d, ZS), sub)

    def at_y(d):
        return (dp, lax.rem(y + d, YS) * 2 + core)

    other_core = (dp, y * 2 + (1 - core))
    z_right, z_left, z_right2, z_left2 = at_z(1), at_z(ZS - 1), at_z(2), at_z(ZS - 2)
    x_to = {d: at_x(d) for d in (1, 2, 3)}
    y_right, y_left = at_y(1), at_y(3)

    own_points = pltpu.make_async_copy(points_ref, raw, local_sem)
    own_points.start()
    barrier = pltpu.get_barrier_semaphore()
    near_z = (z_right, z_left, z_right2, z_left2, at_z(4), at_z(8), at_z(12))
    members = [(dp, lax.rem(sub + d, SUBS)) for d in range(1, SUBS)]
    partners = near_z + (x_to[1], x_to[2], x_to[3], *members)
    for device in partners:
        pl.semaphore_signal(barrier, inc=1, device_id=device, device_id_type=MESH)

    row = lax.broadcasted_iota(jnp.int32, (RAW, npd), 0)
    lane = lax.broadcasted_iota(jnp.int32, (RAW, npd), 1)
    target = jnp.full((RAW, npd), -1, jnp.int32)
    counts = jnp.zeros((RAW, npd), F32)
    for r in range(ROUNDS):
        counts = jnp.where(row == ROUNDS * SLOTS + r, cnt_ref[0, r].astype(F32), counts)
        for i in range(SLOTS):
            target = jnp.where(row == r * SLOTS + i, rows_ref[r, i], target)
    pick = jnp.where(lane == target, 1.0, 0.0).astype(jnp.bfloat16)
    here = lax.broadcasted_iota(jnp.int32, (npd, npd), 0)
    there = lax.broadcasted_iota(jnp.int32, (npd, npd), 1)
    same_round = lax.rem(here, RAW) == ROUNDS * SLOTS + lax.div(lax.rem(there, RAW), SLOTS)
    before = jnp.where(same_round & (lax.div(here, RAW) < lax.div(there, RAW)), 1.0, 0.0)
    itself = jnp.where(same_round & (lax.div(here, RAW) == lax.div(there, RAW)), 1.0, 0.0)
    slot = lax.rem(lane, RAW)
    slot_round = jnp.where(slot < ROUNDS * SLOTS, lax.div(slot, SLOTS), -1)
    slot_index = lax.rem(slot, SLOTS).astype(F32)
    wanted = (SHARE * sub + lax.rem(row, SHARE)).astype(F32)
    wanted_round = slot_round == lax.div(row, SHARE)
    own_points.wait()
    mine = raw[...]
    block = jnp.dot(pick, mine, preferred_element_type=F32)
    slots[sub, :, :npd] = (block[:, :npd] + counts).astype(jnp.bfloat16)
    slots[sub, :, npd:] = block[:, npd:].astype(jnp.bfloat16)
    pall[sub] = mine.T

    pl.semaphore_wait(barrier, len(partners))

    def remote(src, dst, send, recv, device):
        return pltpu.make_async_remote_copy(
            src_ref=src, dst_ref=dst, send_sem=send, recv_sem=recv, device_id=device, device_id_type=MESH
        )

    def to_col(block_lo, block_hi):
        for d in (1, 3, 2):
            src = cand.at[block_lo, block_hi, 0]
            remote(src, cand.at[block_lo, block_hi, d], x_send, x_recv.at[block_lo], x_to[d]).start()

    def hop(block_hi, lo, place, device):
        return remote(cand.at[0, block_hi, 0], cand.at[lo, place, 0], lo_send, lo_recv.at[lo, place], device)

    def jump(d):
        return remote(cand.at[0, 0, 0], cand.at[0, d, 0], hi_send, hi_recv.at[d], at_z(4 * d))

    def wait_bytes(ref, sem):
        pltpu.make_async_copy(ref, ref, sem).wait()

    def lo_arrived(lo, place):
        wait_bytes(cand.at[lo, place, 0], lo_recv.at[lo, place])
        to_col(lo, place)

    for device in members:
        remote(slots.at[sub], slots.at[sub], slots_send, slots_recv, device).start()
    slot_right, slot_left, slot_far = (lax.rem(y + d, YS) * 2 + core for d in (1, 3, 2))
    top, low = pl.ds(0, width // 2), pl.ds(width // 2, width // 2)
    mine_at = pall.at[sub]
    pts_right = remote(mine_at, mine_at, pts_send.at[0], pts_recv.at[0], y_right)
    pts_left = remote(mine_at, mine_at, pts_send.at[1], pts_recv.at[1], y_left)
    pts_core = remote(mine_at, mine_at, pts_send.at[2], pts_recv.at[2], other_core)
    pts_right.start()
    pts_left.start()
    pts_core.start()

    wait_bytes(slots.at[pl.ds(0, SUBS - 1)], slots_recv)
    flat = slots[...].reshape(SUBS * RAW, width)
    known = flat[:, :npd].astype(F32)
    offset = jnp.sum(known * before, axis=0, keepdims=True)
    count = jnp.sum(known * itself, axis=0, keepdims=True)
    choice = wanted_round & (slot_index < count) & (offset + slot_index == wanted)
    share = jnp.dot(jnp.where(choice, 1.0, 0.0).astype(jnp.bfloat16), flat, preferred_element_type=F32)
    cand[0, 0, 0] = share[:BLK].astype(jnp.bfloat16)

    jumps = {d: jump(d) for d in (1, 3, 2)}
    for d in (1, 3, 2):
        jumps[d].start()
    hop(0, 1, 0, z_right).start()
    hop(0, 3, 0, z_left).start()
    hop(0, 2, 0, z_right2).start()
    hop(0, 2, 2, z_left2).start()
    to_col(0, 0)

    jumps[1].wait_recv()
    hop(1, 1, 1, z_right).start()
    hop(1, 3, 1, z_left).start()
    hop(1, 2, 1, z_right2).start()
    jumps[3].wait_recv()
    hop(3, 1, 3, z_right).start()
    hop(3, 3, 3, z_left).start()
    hop(3, 2, 3, z_left2).start()
    jumps[2].wait_recv()
    hop(2, 1, 2, z_right).start()
    hop(2, 3, 2, z_left).start()
    for d in (1, 3, 2):
        to_col(0, d)
    for lo, place in ((1, 0), (3, 0), (2, 0), (2, 2), (1, 1), (3, 3), (3, 1), (1, 3), (2, 1), (2, 3), (1, 2), (3, 2)):
        lo_arrived(lo, place)

    pts_right.wait_recv()
    near_left = pall.at[slot_left]
    far_top = remote(near_left.at[top], near_left.at[top], pts_send.at[3], pts_recv.at[3], y_right)
    core_left = remote(near_left, near_left, pts_send.at[4], pts_recv.at[4], other_core)
    far_top.start()
    core_left.start()
    pts_left.wait_recv()
    near_right = pall.at[slot_right]
    far_low = remote(near_right.at[low], near_right.at[low], pts_send.at[5], pts_recv.at[5], y_left)
    core_right = remote(near_right, near_right, pts_send.at[6], pts_recv.at[6], other_core)
    far_low.start()
    core_right.start()
    far_top.wait_recv()
    far_low.wait_recv()
    far = pall.at[slot_far]
    core_far = remote(far, far, pts_send.at[7], pts_recv.at[7], other_core)
    core_far.start()

    def absorb(lo):
        rows = cand[lo].reshape(ZS, BLK, width)
        half = jnp.zeros((ZS, BLK, npd), F32)
        for t in range(width // npd):
            piece = rows[:, :, t * npd : (t + 1) * npd].astype(F32)
            half = half + piece * piece
        half = 0.5 * jnp.sum(half, axis=2, keepdims=True)
        flat = rows.reshape(ZS * BLK, width)

        def pair(j, carry):
            group = jnp.concatenate([pall[2 * j], pall[2 * j + 1]], axis=1)
            dots = jnp.dot(flat, group, preferred_element_type=F32)
            value = half - dots.reshape(ZS, BLK, 2 * npd)
            best = jnp.min(value, axis=0)
            mins[j] = best if lo == 0 else jnp.minimum(mins[j], best)
            return carry

        lax.fori_loop(0, SUBS // 2, pair, 0)

    pts_core.wait_recv()
    core_left.wait_recv()
    core_right.wait_recv()
    core_far.wait_recv()
    for b in range(SUBS):
        wide = pall[b].astype(F32)
        squares[b : b + 1, :] = jnp.sum(wide * wide, axis=0, keepdims=True)
    for lo in (0, 1, 3, 2):
        wait_bytes(cand.at[lo, :, pl.ds(1, 3)], x_recv.at[lo])
        absorb(lo)

    for j in range(SUBS // 2):
        for r in range(ROUNDS):
            low_r = jnp.min(mins[j, r * SHARE : (r + 1) * SHARE, :], axis=0, keepdims=True)
            for h in range(2):
                line[sub, r, 2 * j + h : 2 * j + h + 1, :] = low_r[:, h * npd : (h + 1) * npd]

    for device in members:
        remote(line.at[sub], line.at[sub], line_send, line_recv, device).start()
    wait_bytes(line.at[pl.ds(0, SUBS - 1)], line_recv)

    lanes = lax.broadcasted_iota(jnp.int32, (1, npd), 1)
    least = None
    total = jnp.zeros((1, npd), F32)
    for r in range(ROUNDS):
        now = jnp.min(line[:, r], axis=0)
        least = now if least is None else jnp.minimum(least, now)
        dist = jnp.maximum(squares[...] + 2.0 * least, 0.0)
        near[r] = dist
        part = jnp.sum(jnp.sum(dist, axis=0, keepdims=True), axis=1, keepdims=True)
        total = jnp.where(lanes == r, part, total)

    zsum[0] = total

    def to_z(d, carry):
        remote(zsum.at[0], zsum.at[ZS - d], z_send, z_recv, at_z(d)).start()
        return carry

    lax.fori_loop(1, ZS, to_z, 0)
    wait_bytes(zsum.at[pl.ds(0, ZS - 1)], z_recv)
    xsum[0] = jnp.sum(zsum[...], axis=0)
    for d in (1, 3, 2):
        remote(xsum.at[0], xsum.at[XS - d], c_send, c_recv, x_to[d]).start()
    wait_bytes(xsum.at[pl.ds(0, XS - 1)], c_recv)
    cost = jnp.sum(xsum[...], axis=0)
    for r in range(ROUNDS):
        cost_r = jnp.sum(jnp.where(lanes == r, cost, 0.0), axis=1, keepdims=True)
        out_ref[r : r + 1, :] = npts * near[r, pl.ds(sub, 1), :] / cost_r

    wait_bytes(slots.at[pl.ds(0, SUBS - 1)], slots_send)
    wait_bytes(cand.at[0, 0, pl.ds(0, 3)], hi_send)
    wait_bytes(cand.at[pl.ds(0, 3), :, 0], lo_send)
    wait_bytes(cand.at[:, :, pl.ds(0, 3)], x_send)
    for copy in (pts_right, pts_left, pts_core, far_top, core_left, far_low, core_right, core_far):
        copy.wait_send()
    wait_bytes(line.at[pl.ds(0, SUBS - 1)], line_send)
    wait_bytes(zsum.at[pl.ds(0, ZS - 1)], z_send)
    wait_bytes(xsum.at[pl.ds(0, XS - 1)], c_send)


def shards(points, cand_rows, cand_count):
    npd, width = points.shape
    npts = float(npd * lax.axis_size(("dp", "sub")))
    dma = pltpu.SemaphoreType.DMA
    return pl.pallas_call(
        lambda *refs: kernel(npts, *refs),
        out_shape=jax.ShapeDtypeStruct((ROUNDS, npd), F32),
        in_specs=[
            pl.BlockSpec(memory_space=pltpu.SMEM),
            pl.BlockSpec(memory_space=pltpu.SMEM),
            pl.BlockSpec(memory_space=pltpu.HBM),
        ],
        out_specs=pl.BlockSpec(memory_space=pltpu.VMEM),
        scratch_shapes=[
            pltpu.VMEM((npd, width), jnp.bfloat16),
            pltpu.VMEM((SUBS, RAW, width), jnp.bfloat16),
            pltpu.VMEM((4, 4, XS, BLK, width), jnp.bfloat16),
            pltpu.VMEM((SUBS, width, npd), jnp.bfloat16),
            pltpu.VMEM((SUBS // 2, BLK, 2 * npd), F32),
            pltpu.VMEM((SUBS, npd), F32),
            pltpu.VMEM((SUBS, ROUNDS, SUBS, npd), F32),
            pltpu.VMEM((ROUNDS, SUBS, npd), F32),
            pltpu.VMEM((ZS, 1, npd), F32),
            pltpu.VMEM((XS, 1, npd), F32),
            dma,
            dma,
            dma,
            dma,
            dma,
            dma,
            dma((4,)),
            dma((4, 4)),
            dma((4,)),
            dma((8,)),
            dma((8,)),
            dma,
            dma,
            dma,
            dma,
            dma,
            dma,
        ],
        compiler_params=pltpu.CompilerParams(
            collective_id=0, has_side_effects=True, vmem_limit_bytes=32 * 1024 * 1024
        ),
        cost_estimate=pl.CostEstimate(
            flops=2 * 1024 * 1024 * width, bytes_accessed=npd * width * 2, transcendentals=0
        ),
    )(cand_rows, cand_count.reshape(1, ROUNDS), points)


def solution(mesh):
    in_specs = (P(("dp", "sub"), None), P(None, ("dp", "sub")), P(None, ("dp", "sub")))
    out_specs = P(None, ("dp", "sub"))
    return jax.shard_map(shards, mesh=mesh, in_specs=in_specs, out_specs=out_specs, check_vma=False)
```

```python
import jax
import jax.numpy as jnp
from jax import lax
from jax.experimental import pallas as pl
from jax.experimental.pallas import tpu as pltpu
from jax.sharding import PartitionSpec as P

ROUNDS = 3
SLOTS = 4
XS = 4
ZS = 16
YS = 4
SUBS = 8
RAW = 16
BLK = 8
SHARE = 2
MESH = pl.DeviceIdType.MESH
F32 = jnp.float32
INF = float("inf")


def kernel(
    npts,
    rows_ref,
    cnt_ref,
    points_ref,
    out_ref,
    raw,
    slots,
    cand,
    pall,
    mins,
    squares,
    line,
    near,
    zsum,
    xsum,
    local_sem,
    slots_send,
    slots_recv,
    hi_send,
    lo_send,
    x_send,
    hi_recv,
    lo_recv,
    x_recv,
    pts_send,
    pts_recv,
    line_send,
    line_recv,
    z_send,
    z_recv,
    c_send,
    c_recv,
):
    dp = lax.axis_index("dp")
    sub = lax.axis_index("sub")
    x, z = lax.div(dp, ZS), lax.rem(dp, ZS)
    y, core = lax.div(sub, 2), lax.rem(sub, 2)
    npd, width = points_ref.shape

    def at_x(d):
        return (lax.rem(x + d, XS) * ZS + z, sub)

    def at_z(d):
        return (x * ZS + lax.rem(z + d, ZS), sub)

    def at_y(d):
        return (dp, lax.rem(y + d, YS) * 2 + core)

    other_core = (dp, y * 2 + (1 - core))
    z_right, z_left, z_right2, z_left2 = at_z(1), at_z(ZS - 1), at_z(2), at_z(ZS - 2)
    z_jump = {d: at_z(4 * d) for d in (1, 2, 3)}
    x_to = {d: at_x(d) for d in (1, 2, 3)}
    y_right, y_left = at_y(1), at_y(3)

    own_points = pltpu.make_async_copy(points_ref, raw, local_sem)
    own_points.start()
    barrier = pltpu.get_barrier_semaphore()
    near_z = (z_right, z_left, z_right2, z_left2, z_jump[1], z_jump[2], z_jump[3])
    members = [(dp, lax.rem(sub + d, SUBS)) for d in range(1, SUBS)]
    partners = near_z + (x_to[1], x_to[2], x_to[3], *members)
    for device in partners:
        pl.semaphore_signal(barrier, inc=1, device_id=device, device_id_type=MESH)

    row = lax.broadcasted_iota(jnp.int32, (RAW, npd), 0)
    lane = lax.broadcasted_iota(jnp.int32, (RAW, npd), 1)
    target = jnp.full((RAW, npd), -1, jnp.int32)
    counts = jnp.zeros((RAW, npd), F32)
    for r in range(ROUNDS):
        counts = jnp.where(row == ROUNDS * SLOTS + r, cnt_ref[0, r].astype(F32), counts)
        for i in range(SLOTS):
            target = jnp.where(row == r * SLOTS + i, rows_ref[r, i], target)
    pick = jnp.where(lane == target, 1.0, 0.0).astype(jnp.bfloat16)
    here = lax.broadcasted_iota(jnp.int32, (npd, npd), 0)
    there = lax.broadcasted_iota(jnp.int32, (npd, npd), 1)
    same_round = lax.rem(here, RAW) == ROUNDS * SLOTS + lax.div(lax.rem(there, RAW), SLOTS)
    before = jnp.where(same_round & (lax.div(here, RAW) < lax.div(there, RAW)), 1.0, 0.0)
    itself = jnp.where(same_round & (lax.div(here, RAW) == lax.div(there, RAW)), 1.0, 0.0)
    slot = lax.rem(lane, RAW)
    slot_round = jnp.where(slot < ROUNDS * SLOTS, lax.div(slot, SLOTS), -1)
    slot_index = lax.rem(slot, SLOTS).astype(F32)
    wanted = (SHARE * sub + lax.rem(row, SHARE)).astype(F32)
    wanted_round = slot_round == lax.div(row, SHARE)
    own_points.wait()
    mine = raw[...]
    block = jnp.dot(pick, mine, preferred_element_type=F32)
    slots[sub, :, :npd] = (block[:, :npd] + counts).astype(jnp.bfloat16)
    slots[sub, :, npd:] = block[:, npd:].astype(jnp.bfloat16)
    pall[sub] = mine.T

    pl.semaphore_wait(barrier, len(partners))

    def remote(src, dst, send, recv, device):
        return pltpu.make_async_remote_copy(
            src_ref=src, dst_ref=dst, send_sem=send, recv_sem=recv, device_id=device, device_id_type=MESH
        )

    def to_cols(lo, places):
        for d in (1, 3, 2):
            remote(cand.at[0, lo, places], cand.at[d, lo, places], x_send, x_recv.at[lo], x_to[d]).start()

    def hop(lo, hi, count, place, part, device):
        src, dst = cand.at[0, 0, pl.ds(hi, count)], cand.at[0, lo, pl.ds(place, count)]
        return remote(src, dst, lo_send, lo_recv.at[lo, part], device)

    def jump(hi, device):
        return remote(cand.at[0, 0, 0], cand.at[0, 0, hi], hi_send, hi_recv.at[hi], device)

    def wait_bytes(ref, sem):
        pltpu.make_async_copy(ref, ref, sem).wait()

    for device in members:
        remote(slots.at[sub], slots.at[sub], slots_send, slots_recv, device).start()
    slot_right, slot_left, slot_far = (lax.rem(y + d, YS) * 2 + core for d in (1, 3, 2))
    top, low = pl.ds(0, width // 2), pl.ds(width // 2, width // 2)
    mine_at = pall.at[sub]
    pts_right = remote(mine_at, mine_at, pts_send.at[0], pts_recv.at[0], y_right)
    pts_left = remote(mine_at, mine_at, pts_send.at[1], pts_recv.at[1], y_left)
    pts_core = remote(mine_at, mine_at, pts_send.at[2], pts_recv.at[2], other_core)
    pts_right.start()
    pts_left.start()
    pts_core.start()

    wait_bytes(slots.at[pl.ds(0, SUBS - 1)], slots_recv)
    flat = slots[...].reshape(SUBS * RAW, width)
    known = flat[:, :npd].astype(F32)
    offset = jnp.sum(known * before, axis=0, keepdims=True)
    count = jnp.sum(known * itself, axis=0, keepdims=True)
    choice = wanted_round & (slot_index < count) & (offset + slot_index == wanted)
    share = jnp.dot(jnp.where(choice, 1.0, 0.0).astype(jnp.bfloat16), flat, preferred_element_type=F32)
    cand[0, 0, 0] = share[:BLK].astype(jnp.bfloat16)

    jumps = [jump(1, z_jump[1]), jump(2, z_jump[3]), jump(3, z_jump[2])]
    for copy in jumps:
        copy.start()
    hop(1, 0, 1, 0, 0, z_right).start()
    hop(2, 0, 1, 0, 0, z_left).start()
    hop(3, 0, 1, 0, 0, z_right2).start()
    hop(3, 0, 1, 3, 3, z_left2).start()
    to_cols(0, pl.ds(0, 1))

    jumps[0].wait_recv()
    jumps[1].wait_recv()
    hop(1, 1, 2, 1, 1, z_right).start()
    hop(2, 1, 2, 1, 1, z_left).start()
    hop(3, 1, 1, 1, 1, z_right2).start()
    hop(3, 2, 1, 2, 2, z_left2).start()
    jumps[2].wait_recv()
    hop(1, 3, 1, 3, 2, z_right).start()
    hop(2, 3, 1, 3, 2, z_left).start()
    to_cols(0, pl.ds(1, 3))

    pts_right.wait_recv()
    near_left = pall.at[slot_left]
    far_top = remote(near_left.at[top], near_left.at[top], pts_send.at[3], pts_recv.at[3], y_right)
    core_left = remote(near_left, near_left, pts_send.at[4], pts_recv.at[4], other_core)
    far_top.start()
    core_left.start()
    pts_left.wait_recv()
    near_right = pall.at[slot_right]
    far_low = remote(near_right.at[low], near_right.at[low], pts_send.at[5], pts_recv.at[5], y_left)
    core_right = remote(near_right, near_right, pts_send.at[6], pts_recv.at[6], other_core)
    far_low.start()
    core_right.start()
    for lo in (1, 2):
        for part, place, count in ((0, 0, 1), (1, 1, 2), (2, 3, 1)):
            wait_bytes(cand.at[0, lo, pl.ds(place, count)], lo_recv.at[lo, part])
        to_cols(lo, pl.ds(0, 4))
    for part in range(4):
        wait_bytes(cand.at[0, 3, part], lo_recv.at[3, part])
    to_cols(3, pl.ds(0, 4))

    far_top.wait_recv()
    far_low.wait_recv()
    far = pall.at[slot_far]
    core_far = remote(far, far, pts_send.at[7], pts_recv.at[7], other_core)
    core_far.start()

    def absorb(lo, carry):
        wait_bytes(cand.at[pl.ds(1, 3), lo], x_recv.at[lo])
        rows = cand[:, lo].reshape(ZS, BLK, width)
        half = jnp.zeros((ZS, BLK, npd), F32)
        for t in range(width // npd):
            piece = rows[:, :, t * npd : (t + 1) * npd].astype(F32)
            half = half + piece * piece
        half = 0.5 * jnp.sum(half, axis=2, keepdims=True)
        flat = rows.reshape(ZS * BLK, width)

        def pair(j, carry):
            group = jnp.concatenate([pall[2 * j], pall[2 * j + 1]], axis=1)
            dots = jnp.dot(flat, group, preferred_element_type=F32)
            value = half - dots.reshape(ZS, BLK, 2 * npd)
            mins[j] = jnp.minimum(mins[j], jnp.min(value, axis=0))
            return carry

        return lax.fori_loop(0, SUBS // 2, pair, carry)

    pts_core.wait_recv()
    core_left.wait_recv()
    core_right.wait_recv()
    core_far.wait_recv()
    for b in range(SUBS):
        wide = pall[b].astype(F32)
        squares[b : b + 1, :] = jnp.sum(wide * wide, axis=0, keepdims=True)
    mins[...] = jnp.full(mins.shape, jnp.inf, F32)
    lax.fori_loop(0, 4, absorb, 0)

    for j in range(SUBS // 2):
        for r in range(ROUNDS):
            low_r = jnp.min(mins[j, r * SHARE : (r + 1) * SHARE, :], axis=0, keepdims=True)
            for h in range(2):
                line[sub, r, 2 * j + h : 2 * j + h + 1, :] = low_r[:, h * npd : (h + 1) * npd]

    for device in members:
        remote(line.at[sub], line.at[sub], line_send, line_recv, device).start()
    wait_bytes(line.at[pl.ds(0, SUBS - 1)], line_recv)

    lanes = lax.broadcasted_iota(jnp.int32, (1, npd), 1)
    least = None
    total = jnp.zeros((1, npd), F32)
    for r in range(ROUNDS):
        now = jnp.min(line[:, r], axis=0)
        least = now if least is None else jnp.minimum(least, now)
        dist = jnp.maximum(squares[...] + 2.0 * least, 0.0)
        near[r] = dist
        part = jnp.sum(jnp.sum(dist, axis=0, keepdims=True), axis=1, keepdims=True)
        total = jnp.where(lanes == r, part, total)

    zsum[0] = total

    def to_z(d, carry):
        remote(zsum.at[0], zsum.at[ZS - d], z_send, z_recv, at_z(d)).start()
        return carry

    lax.fori_loop(1, ZS, to_z, 0)
    wait_bytes(zsum.at[pl.ds(0, ZS - 1)], z_recv)
    xsum[0] = jnp.sum(zsum[...], axis=0)
    for d in (1, 3, 2):
        remote(xsum.at[0], xsum.at[XS - d], c_send, c_recv, x_to[d]).start()
    wait_bytes(xsum.at[pl.ds(0, XS - 1)], c_recv)
    cost = jnp.sum(xsum[...], axis=0)
    for r in range(ROUNDS):
        cost_r = jnp.sum(jnp.where(lanes == r, cost, 0.0), axis=1, keepdims=True)
        out_ref[r : r + 1, :] = npts * near[r, pl.ds(sub, 1), :] / cost_r

    wait_bytes(slots.at[pl.ds(0, SUBS - 1)], slots_send)
    wait_bytes(cand.at[0, 0, pl.ds(0, 3)], hi_send)
    wait_bytes(cand.at[0, pl.ds(0, 3)], lo_send)
    wait_bytes(cand.at[pl.ds(0, 3)], x_send)
    for copy in (pts_right, pts_left, pts_core, far_top, core_left, far_low, core_right, core_far):
        copy.wait_send()
    wait_bytes(line.at[pl.ds(0, SUBS - 1)], line_send)
    wait_bytes(zsum.at[pl.ds(0, ZS - 1)], z_send)
    wait_bytes(xsum.at[pl.ds(0, XS - 1)], c_send)


def shards(points, cand_rows, cand_count):
    npd, width = points.shape
    npts = float(npd * lax.axis_size(("dp", "sub")))
    dma = pltpu.SemaphoreType.DMA
    return pl.pallas_call(
        lambda *refs: kernel(npts, *refs),
        out_shape=jax.ShapeDtypeStruct((ROUNDS, npd), F32),
        in_specs=[
            pl.BlockSpec(memory_space=pltpu.SMEM),
            pl.BlockSpec(memory_space=pltpu.SMEM),
            pl.BlockSpec(memory_space=pl.ANY),
        ],
        out_specs=pl.BlockSpec(memory_space=pltpu.VMEM),
        scratch_shapes=[
            pltpu.VMEM((npd, width), jnp.bfloat16),
            pltpu.VMEM((SUBS, RAW, width), jnp.bfloat16),
            pltpu.VMEM((4, 4, XS, BLK, width), jnp.bfloat16),
            pltpu.VMEM((SUBS, width, npd), jnp.bfloat16),
            pltpu.VMEM((SUBS // 2, BLK, 2 * npd), F32),
            pltpu.VMEM((SUBS, npd), F32),
            pltpu.VMEM((SUBS, ROUNDS, SUBS, npd), F32),
            pltpu.VMEM((ROUNDS, SUBS, npd), F32),
            pltpu.VMEM((ZS, 1, npd), F32),
            pltpu.VMEM((XS, 1, npd), F32),
            dma,
            dma,
            dma,
            dma,
            dma,
            dma,
            dma((4,)),
            dma((4, 4)),
            dma((4,)),
            dma((8,)),
            dma((8,)),
            dma,
            dma,
            dma,
            dma,
            dma,
            dma,
        ],
        compiler_params=pltpu.CompilerParams(
            collective_id=0, has_side_effects=True, vmem_limit_bytes=60 * 1024 * 1024
        ),
        cost_estimate=pl.CostEstimate(
            flops=2 * 1024 * 1024 * width, bytes_accessed=npd * width * 2, transcendentals=0
        ),
    )(cand_rows, cand_count.reshape(1, ROUNDS), points)


def solution(mesh):
    in_specs = (P(("dp", "sub"), None), P(None, ("dp", "sub")), P(None, ("dp", "sub")))
    out_specs = P(None, ("dp", "sub"))
    return jax.shard_map(shards, mesh=mesh, in_specs=in_specs, out_specs=out_specs, check_vma=False)
```

```python
import jax
import jax.numpy as jnp
from jax import lax
from jax.experimental import pallas as pl
from jax.experimental.pallas import tpu as pltpu
from jax.sharding import PartitionSpec as P

ROUNDS = 3
SLOTS = 4
XS = 4
ZS = 16
YS = 4
SUBS = 8
RAW = 16
BLK = 8
SHARE = 2
MESH = pl.DeviceIdType.MESH
F32 = jnp.float32
INF = float("inf")


def kernel(
    npts,
    rows_ref,
    cnt_ref,
    points_ref,
    out_ref,
    raw,
    slots,
    cand,
    pall,
    mins,
    squares,
    line,
    near,
    zsum,
    xsum,
    local_sem,
    slots_send,
    slots_recv,
    z_block_send,
    x_send,
    z_block_recv,
    x_recv,
    pts_send,
    pts_recv,
    line_send,
    line_recv,
    z_send,
    z_recv,
    c_send,
    c_recv,
):
    dp = lax.axis_index("dp")
    sub = lax.axis_index("sub")
    x, z = lax.div(dp, ZS), lax.rem(dp, ZS)
    y, core = lax.div(sub, 2), lax.rem(sub, 2)
    npd, width = points_ref.shape

    def at_x(d):
        return (lax.rem(x + d, XS) * ZS + z, sub)

    def at_z(d):
        return (x * ZS + lax.rem(z + d, ZS), sub)

    def at_y(d):
        return (dp, lax.rem(y + d, YS) * 2 + core)

    other_core = (dp, y * 2 + (1 - core))
    z_to = {d: at_z(d % ZS) for d in (1, -1, 2, -2, 3, -3, 4, -4)}
    x_to = {d: at_x(d) for d in (1, 2, 3)}
    y_right, y_left = at_y(1), at_y(3)

    own_points = pltpu.make_async_copy(points_ref, raw, local_sem)
    own_points.start()
    barrier = pltpu.get_barrier_semaphore()
    members = [(dp, lax.rem(sub + d, SUBS)) for d in range(1, SUBS)]
    partners = [*z_to.values(), *x_to.values(), *members]
    for device in partners:
        pl.semaphore_signal(barrier, inc=1, device_id=device, device_id_type=MESH)

    row = lax.broadcasted_iota(jnp.int32, (RAW, npd), 0)
    lane = lax.broadcasted_iota(jnp.int32, (RAW, npd), 1)
    target = jnp.full((RAW, npd), -1, jnp.int32)
    counts = jnp.zeros((RAW, npd), F32)
    for r in range(ROUNDS):
        counts = jnp.where(row == ROUNDS * SLOTS + r, cnt_ref[0, r].astype(F32), counts)
        for i in range(SLOTS):
            target = jnp.where(row == r * SLOTS + i, rows_ref[r, i], target)
    pick = jnp.where(lane == target, 1.0, 0.0).astype(jnp.bfloat16)
    here = lax.broadcasted_iota(jnp.int32, (npd, npd), 0)
    there = lax.broadcasted_iota(jnp.int32, (npd, npd), 1)
    same_round = lax.rem(here, RAW) == ROUNDS * SLOTS + lax.div(lax.rem(there, RAW), SLOTS)
    before = jnp.where(same_round & (lax.div(here, RAW) < lax.div(there, RAW)), 1.0, 0.0)
    itself = jnp.where(same_round & (lax.div(here, RAW) == lax.div(there, RAW)), 1.0, 0.0)
    slot = lax.rem(lane, RAW)
    slot_round = jnp.where(slot < ROUNDS * SLOTS, lax.div(slot, SLOTS), -1)
    slot_index = lax.rem(slot, SLOTS).astype(F32)
    wanted = (SHARE * sub + lax.rem(row, SHARE)).astype(F32)
    wanted_round = slot_round == lax.div(row, SHARE)
    own_points.wait()
    mine = raw[...]
    block = jnp.dot(pick, mine, preferred_element_type=F32)
    slots[sub, :, :npd] = (block[:, :npd] + counts).astype(jnp.bfloat16)
    slots[sub, :, npd:] = block[:, npd:].astype(jnp.bfloat16)
    pall[sub] = mine.T

    pl.semaphore_wait(barrier, len(partners))

    def remote(src, dst, send, recv, device):
        return pltpu.make_async_remote_copy(
            src_ref=src, dst_ref=dst, send_sem=send, recv_sem=recv, device_id=device, device_id_type=MESH
        )

    def to_cols(place, count, group):
        for d in (1, 3, 2):
            src, dst = cand.at[0, pl.ds(place, count)], cand.at[d, pl.ds(place, count)]
            remote(src, dst, x_send, x_recv.at[group], x_to[d]).start()

    def along_z(src, place, d, lanes=None):
        if lanes is None:
            src, dst = cand.at[0, src], cand.at[0, place]
        else:
            part = pl.ds(lanes * (width // 2), width // 2)
            src, dst = cand.at[0, src, :, part], cand.at[0, place, :, part]
        remote(src, dst, z_block_send, z_block_recv.at[place + (lanes or 0)], z_to[d]).start()

    def z_arrived(*places):
        for place in places:
            wait_bytes(cand.at[0, place], z_block_recv.at[place])

    def wait_bytes(ref, sem):
        pltpu.make_async_copy(ref, ref, sem).wait()

    for device in members:
        remote(slots.at[sub], slots.at[sub], slots_send, slots_recv, device).start()
    slot_right, slot_left, slot_far = (lax.rem(y + d, YS) * 2 + core for d in (1, 3, 2))
    top, low = pl.ds(0, width // 2), pl.ds(width // 2, width // 2)
    mine_at = pall.at[sub]
    pts_right = remote(mine_at, mine_at, pts_send.at[0], pts_recv.at[0], y_right)
    pts_left = remote(mine_at, mine_at, pts_send.at[1], pts_recv.at[1], y_left)
    pts_core = remote(mine_at, mine_at, pts_send.at[2], pts_recv.at[2], other_core)
    pts_right.start()
    pts_left.start()
    pts_core.start()

    wait_bytes(slots.at[pl.ds(0, SUBS - 1)], slots_recv)
    flat = slots[...].reshape(SUBS * RAW, width)
    known = flat[:, :npd].astype(F32)
    offset = jnp.sum(known * before, axis=0, keepdims=True)
    count = jnp.sum(known * itself, axis=0, keepdims=True)
    choice = wanted_round & (slot_index < count) & (offset + slot_index == wanted)
    share = jnp.dot(jnp.where(choice, 1.0, 0.0).astype(jnp.bfloat16), flat, preferred_element_type=F32)
    cand[0, 12] = share[:BLK].astype(jnp.bfloat16)

    for place, d in ((13, 4), (14, -4), (0, 2), (2, -2), (4, 1), (8, -1)):
        along_z(12, place, d)
    to_cols(12, 1, 3)

    z_arrived(13)
    along_z(13, 15, 4, 0)
    for place, d in ((7, 3), (1, 2), (5, 1), (9, -1)):
        along_z(13, place, d)
    z_arrived(14)
    along_z(14, 15, -4, 1)
    for place, d in ((11, -3), (3, -2), (10, -1), (6, 1)):
        along_z(14, place, d)
    to_cols(13, 2, 3)

    pts_right.wait_recv()
    near_left = pall.at[slot_left]
    far_top = remote(near_left.at[top], near_left.at[top], pts_send.at[3], pts_recv.at[3], y_right)
    core_left = remote(near_left, near_left, pts_send.at[4], pts_recv.at[4], other_core)
    far_top.start()
    core_left.start()
    pts_left.wait_recv()
    near_right = pall.at[slot_right]
    far_low = remote(near_right.at[low], near_right.at[low], pts_send.at[5], pts_recv.at[5], y_left)
    core_right = remote(near_right, near_right, pts_send.at[6], pts_recv.at[6], other_core)
    far_low.start()
    core_right.start()
    for group in range(3):
        z_arrived(*range(4 * group, 4 * group + 4))
        to_cols(4 * group, 4, group)
    half_block = cand.at[0, 15, :, pl.ds(0, width // 2)]
    wait_bytes(half_block, z_block_recv.at[15])
    wait_bytes(half_block, z_block_recv.at[16])
    to_cols(15, 1, 3)

    far_top.wait_recv()
    far_low.wait_recv()
    far = pall.at[slot_far]
    core_far = remote(far, far, pts_send.at[7], pts_recv.at[7], other_core)
    core_far.start()

    def absorb(group, carry):
        wait_bytes(cand.at[pl.ds(1, 3), pl.ds(0, 4)], x_recv.at[group])
        rows = cand[:, pl.ds(4 * group, 4)].reshape(ZS, BLK, width)
        half = jnp.zeros((ZS, BLK, npd), F32)
        for t in range(width // npd):
            piece = rows[:, :, t * npd : (t + 1) * npd].astype(F32)
            half = half + piece * piece
        half = 0.5 * jnp.sum(half, axis=2, keepdims=True)
        flat = rows.reshape(ZS * BLK, width)

        def pair(j, carry):
            group = jnp.concatenate([pall[2 * j], pall[2 * j + 1]], axis=1)
            dots = jnp.dot(flat, group, preferred_element_type=F32)
            value = half - dots.reshape(ZS, BLK, 2 * npd)
            mins[j] = jnp.minimum(mins[j], jnp.min(value, axis=0))
            return carry

        return lax.fori_loop(0, SUBS // 2, pair, carry)

    pts_core.wait_recv()
    core_left.wait_recv()
    core_right.wait_recv()
    core_far.wait_recv()
    for b in range(SUBS):
        wide = pall[b].astype(F32)
        squares[b : b + 1, :] = jnp.sum(wide * wide, axis=0, keepdims=True)
    mins[...] = jnp.full(mins.shape, jnp.inf, F32)
    lax.fori_loop(0, 4, absorb, 0)

    for j in range(SUBS // 2):
        for r in range(ROUNDS):
            low_r = jnp.min(mins[j, r * SHARE : (r + 1) * SHARE, :], axis=0, keepdims=True)
            for h in range(2):
                line[sub, r, 2 * j + h : 2 * j + h + 1, :] = low_r[:, h * npd : (h + 1) * npd]

    for device in members:
        remote(line.at[sub], line.at[sub], line_send, line_recv, device).start()
    wait_bytes(line.at[pl.ds(0, SUBS - 1)], line_recv)

    lanes = lax.broadcasted_iota(jnp.int32, (1, npd), 1)
    least = None
    total = jnp.zeros((1, npd), F32)
    for r in range(ROUNDS):
        now = jnp.min(line[:, r], axis=0)
        least = now if least is None else jnp.minimum(least, now)
        dist = jnp.maximum(squares[...] + 2.0 * least, 0.0)
        near[r] = dist
        part = jnp.sum(jnp.sum(dist, axis=0, keepdims=True), axis=1, keepdims=True)
        total = jnp.where(lanes == r, part, total)

    zsum[0] = total

    def to_z(d, carry):
        remote(zsum.at[0], zsum.at[ZS - d], z_send, z_recv, at_z(d)).start()
        return carry

    lax.fori_loop(1, ZS, to_z, 0)
    wait_bytes(zsum.at[pl.ds(0, ZS - 1)], z_recv)
    xsum[0] = jnp.sum(zsum[...], axis=0)
    for d in (1, 3, 2):
        remote(xsum.at[0], xsum.at[XS - d], c_send, c_recv, x_to[d]).start()
    wait_bytes(xsum.at[pl.ds(0, XS - 1)], c_recv)
    cost = jnp.sum(xsum[...], axis=0)
    for r in range(ROUNDS):
        cost_r = jnp.sum(jnp.where(lanes == r, cost, 0.0), axis=1, keepdims=True)
        out_ref[r : r + 1, :] = npts * near[r, pl.ds(sub, 1), :] / cost_r

    wait_bytes(slots.at[pl.ds(0, SUBS - 1)], slots_send)
    wait_bytes(cand.at[0, pl.ds(0, 15)], z_block_send)
    wait_bytes(cand.at[pl.ds(0, 3)], x_send)
    for copy in (pts_right, pts_left, pts_core, far_top, core_left, far_low, core_right, core_far):
        copy.wait_send()
    wait_bytes(line.at[pl.ds(0, SUBS - 1)], line_send)
    wait_bytes(zsum.at[pl.ds(0, ZS - 1)], z_send)
    wait_bytes(xsum.at[pl.ds(0, XS - 1)], c_send)


def shards(points, cand_rows, cand_count):
    npd, width = points.shape
    npts = float(npd * lax.axis_size(("dp", "sub")))
    dma = pltpu.SemaphoreType.DMA
    return pl.pallas_call(
        lambda *refs: kernel(npts, *refs),
        out_shape=jax.ShapeDtypeStruct((ROUNDS, npd), F32),
        in_specs=[
            pl.BlockSpec(memory_space=pltpu.SMEM),
            pl.BlockSpec(memory_space=pltpu.SMEM),
            pl.BlockSpec(memory_space=pl.ANY),
        ],
        out_specs=pl.BlockSpec(memory_space=pltpu.VMEM),
        scratch_shapes=[
            pltpu.VMEM((npd, width), jnp.bfloat16),
            pltpu.VMEM((SUBS, RAW, width), jnp.bfloat16),
            pltpu.VMEM((XS, ZS, BLK, width), jnp.bfloat16),
            pltpu.VMEM((SUBS, width, npd), jnp.bfloat16),
            pltpu.VMEM((SUBS // 2, BLK, 2 * npd), F32),
            pltpu.VMEM((SUBS, npd), F32),
            pltpu.VMEM((SUBS, ROUNDS, SUBS, npd), F32),
            pltpu.VMEM((ROUNDS, SUBS, npd), F32),
            pltpu.VMEM((ZS, 1, npd), F32),
            pltpu.VMEM((XS, 1, npd), F32),
            dma,
            dma,
            dma,
            dma,
            dma,
            dma((17,)),
            dma((4,)),
            dma((8,)),
            dma((8,)),
            dma,
            dma,
            dma,
            dma,
            dma,
            dma,
        ],
        compiler_params=pltpu.CompilerParams(
            collective_id=0, has_side_effects=True, vmem_limit_bytes=60 * 1024 * 1024
        ),
        cost_estimate=pl.CostEstimate(
            flops=2 * 1024 * 1024 * width, bytes_accessed=npd * width * 2, transcendentals=0
        ),
    )(cand_rows, cand_count.reshape(1, ROUNDS), points)


def solution(mesh):
    in_specs = (P(("dp", "sub"), None), P(None, ("dp", "sub")), P(None, ("dp", "sub")))
    out_specs = P(None, ("dp", "sub"))
    return jax.shard_map(shards, mesh=mesh, in_specs=in_specs, out_specs=out_specs, check_vma=False)
```

```python
import jax
import jax.numpy as jnp
from jax import lax
from jax.experimental import pallas as pl
from jax.experimental.pallas import tpu as pltpu
from jax.sharding import PartitionSpec as P

ROUNDS = 3
SLOTS = 4
XS = 4
ZS = 16
YS = 4
SUBS = 8
RAW = 16
BLK = 8
SHARE = 2
MESH = pl.DeviceIdType.MESH
F32 = jnp.float32
INF = float("inf")


def kernel(
    npts,
    rows_ref,
    cnt_ref,
    points_ref,
    out_ref,
    raw,
    slots,
    cand,
    pall,
    mins,
    squares,
    line,
    near,
    zsum,
    xsum,
    local_sem,
    slots_send,
    slots_recv,
    z_block_send,
    x_send,
    z_block_recv,
    x_recv,
    far_send,
    far_z_send,
    far_recv,
    far_z_recv,
    pts_send,
    pts_recv,
    line_send,
    line_recv,
    z_send,
    z_recv,
    c_send,
    c_recv,
):
    dp = lax.axis_index("dp")
    sub = lax.axis_index("sub")
    x, z = lax.div(dp, ZS), lax.rem(dp, ZS)
    y, core = lax.div(sub, 2), lax.rem(sub, 2)
    npd, width = points_ref.shape

    def at_x(d):
        return (lax.rem(x + d, XS) * ZS + z, sub)

    def at_z(d):
        return (x * ZS + lax.rem(z + d, ZS), sub)

    def at_y(d):
        return (dp, lax.rem(y + d, YS) * 2 + core)

    other_core = (dp, y * 2 + (1 - core))
    z_to = {d: at_z(d % ZS) for d in (1, -1, 2, -2, 3, -3, 4, -4)}
    x_to = {d: at_x(d) for d in (1, 2, 3)}
    y_right, y_left = at_y(1), at_y(3)

    own_points = pltpu.make_async_copy(points_ref, raw, local_sem)
    own_points.start()
    barrier = pltpu.get_barrier_semaphore()
    members = [(dp, lax.rem(sub + d, SUBS)) for d in range(1, SUBS)]
    partners = [*z_to.values(), *x_to.values(), *members]
    for device in partners:
        pl.semaphore_signal(barrier, inc=1, device_id=device, device_id_type=MESH)

    row = lax.broadcasted_iota(jnp.int32, (RAW, npd), 0)
    lane = lax.broadcasted_iota(jnp.int32, (RAW, npd), 1)
    target = jnp.full((RAW, npd), -1, jnp.int32)
    counts = jnp.zeros((RAW, npd), F32)
    for r in range(ROUNDS):
        counts = jnp.where(row == ROUNDS * SLOTS + r, cnt_ref[0, r].astype(F32), counts)
        for i in range(SLOTS):
            target = jnp.where(row == r * SLOTS + i, rows_ref[r, i], target)
    pick = jnp.where(lane == target, 1.0, 0.0).astype(jnp.bfloat16)
    here = lax.broadcasted_iota(jnp.int32, (npd, npd), 0)
    there = lax.broadcasted_iota(jnp.int32, (npd, npd), 1)
    same_round = lax.rem(here, RAW) == ROUNDS * SLOTS + lax.div(lax.rem(there, RAW), SLOTS)
    before = jnp.where(same_round & (lax.div(here, RAW) < lax.div(there, RAW)), 1.0, 0.0)
    itself = jnp.where(same_round & (lax.div(here, RAW) == lax.div(there, RAW)), 1.0, 0.0)
    slot = lax.rem(lane, RAW)
    slot_round = jnp.where(slot < ROUNDS * SLOTS, lax.div(slot, SLOTS), -1)
    slot_index = lax.rem(slot, SLOTS).astype(F32)
    wanted = (SHARE * sub + lax.rem(row, SHARE)).astype(F32)
    wanted_round = slot_round == lax.div(row, SHARE)
    own_points.wait()
    mine = raw[...]
    block = jnp.dot(pick, mine, preferred_element_type=F32)
    slots[sub, :, :npd] = (block[:, :npd] + counts).astype(jnp.bfloat16)
    slots[sub, :, npd:] = block[:, npd:].astype(jnp.bfloat16)

    pl.semaphore_wait(barrier, len(partners))

    def remote(src, dst, send, recv, device):
        return pltpu.make_async_remote_copy(
            src_ref=src, dst_ref=dst, send_sem=send, recv_sem=recv, device_id=device, device_id_type=MESH
        )

    def to_sides(place, count, group):
        for d, column in ((1, 2), (3, 3)):
            src, dst = cand.at[0, pl.ds(place, count)], cand.at[column, pl.ds(place, count)]
            remote(src, dst, x_send, x_recv.at[group], x_to[d]).start()

    def to_far(place):
        remote(cand.at[0, place], cand.at[1, place], far_send, far_recv.at[place - 12], x_to[2]).start()

    def far_along_z(src, place, count, group, d, lanes=None):
        src, dst = cand.at[1, pl.ds(src, count)], cand.at[1, pl.ds(place, count)]
        if lanes is not None:
            part = pl.ds(lanes * (width // 2), width // 2)
            src, dst = src.at[:, :, part], dst.at[:, :, part]
        remote(src, dst, far_z_send, far_z_recv.at[group], z_to[d]).start()

    def along_z(src, place, d, lanes=None):
        if lanes is None:
            src, dst = cand.at[0, src], cand.at[0, place]
        else:
            part = pl.ds(lanes * (width // 2), width // 2)
            src, dst = cand.at[0, src, :, part], cand.at[0, place, :, part]
        remote(src, dst, z_block_send, z_block_recv.at[place + (lanes or 0)], z_to[d]).start()

    def z_arrived(*places):
        for place in places:
            wait_bytes(cand.at[0, place], z_block_recv.at[place])

    def wait_bytes(ref, sem):
        pltpu.make_async_copy(ref, ref, sem).wait()

    for device in members:
        remote(slots.at[sub], slots.at[sub], slots_send, slots_recv, device).start()
    pall[sub] = mine.T
    slot_right, slot_left, slot_far = (lax.rem(y + d, YS) * 2 + core for d in (1, 3, 2))
    top, low = pl.ds(0, width // 2), pl.ds(width // 2, width // 2)
    mine_at = pall.at[sub]
    pts_right = remote(mine_at, mine_at, pts_send.at[0], pts_recv.at[0], y_right)
    pts_left = remote(mine_at, mine_at, pts_send.at[1], pts_recv.at[1], y_left)
    pts_core = remote(mine_at, mine_at, pts_send.at[2], pts_recv.at[2], other_core)
    pts_right.start()
    pts_left.start()
    pts_core.start()

    wait_bytes(slots.at[pl.ds(0, SUBS - 1)], slots_recv)
    flat = slots[...].reshape(SUBS * RAW, width)
    known = flat[:, :npd].astype(F32)
    offset = jnp.sum(known * before, axis=0, keepdims=True)
    count = jnp.sum(known * itself, axis=0, keepdims=True)
    choice = wanted_round & (slot_index < count) & (offset + slot_index == wanted)
    share = jnp.dot(jnp.where(choice, 1.0, 0.0).astype(jnp.bfloat16), flat, preferred_element_type=F32)
    cand[0, 13] = share[:BLK].astype(jnp.bfloat16)

    along_z(13, 12, 4)
    along_z(13, 14, -4)
    to_far(13)
    for place, d in ((1, 2), (2, -2), (5, 1), (9, -1)):
        along_z(13, place, d)
    to_sides(13, 1, 3)

    z_arrived(12)
    to_far(12)
    along_z(12, 15, 4, 0)
    for place, d in ((7, 3), (0, 2), (4, 1), (8, -1)):
        along_z(12, place, d)
    z_arrived(14)
    to_far(14)
    along_z(14, 15, -4, 1)
    for place, d in ((11, -3), (3, -2), (10, -1), (6, 1)):
        along_z(14, place, d)
    to_sides(12, 1, 3)
    to_sides(14, 1, 3)

    for place in (12, 13, 14):
        wait_bytes(cand.at[1, place], far_recv.at[place - 12])
    far_along_z(12, 15, 1, 3, 4, 0)
    far_along_z(14, 15, 1, 3, -4, 1)
    far_along_z(12, 7, 1, 1, 3)
    far_along_z(14, 11, 1, 2, -3)
    far_along_z(12, 0, 2, 0, 2)
    far_along_z(13, 2, 2, 0, -2)
    far_along_z(12, 4, 3, 1, 1)
    far_along_z(12, 8, 3, 2, -1)

    pts_right.wait_recv()
    near_left = pall.at[slot_left]
    far_top = remote(near_left.at[top], near_left.at[top], pts_send.at[3], pts_recv.at[3], y_right)
    core_left = remote(near_left, near_left, pts_send.at[4], pts_recv.at[4], other_core)
    far_top.start()
    core_left.start()
    pts_left.wait_recv()
    near_right = pall.at[slot_right]
    far_low = remote(near_right.at[low], near_right.at[low], pts_send.at[5], pts_recv.at[5], y_left)
    core_right = remote(near_right, near_right, pts_send.at[6], pts_recv.at[6], other_core)
    far_low.start()
    core_right.start()
    for group in range(3):
        z_arrived(*range(4 * group, 4 * group + 4))
        to_sides(4 * group, 4, group)
    half_block = cand.at[0, 15, :, pl.ds(0, width // 2)]
    wait_bytes(half_block, z_block_recv.at[15])
    wait_bytes(half_block, z_block_recv.at[16])
    to_sides(15, 1, 3)

    far_top.wait_recv()
    far_low.wait_recv()
    far = pall.at[slot_far]
    core_far = remote(far, far, pts_send.at[7], pts_recv.at[7], other_core)
    core_far.start()

    def absorb(group, carry):
        wait_bytes(cand.at[pl.ds(2, 2), pl.ds(0, 4)], x_recv.at[group])

        @pl.when(group < 3)
        def _():
            wait_bytes(cand.at[1, pl.ds(0, 4)], far_z_recv.at[group])

        @pl.when(group == 3)
        def _():
            wait_bytes(cand.at[1, 15], far_z_recv.at[group])

        rows = cand[:, pl.ds(4 * group, 4)].reshape(ZS, BLK, width)
        half = jnp.zeros((ZS, BLK, npd), F32)
        for t in range(width // npd):
            piece = rows[:, :, t * npd : (t + 1) * npd].astype(F32)
            half = half + piece * piece
        half = 0.5 * jnp.sum(half, axis=2, keepdims=True)
        flat = rows.reshape(ZS * BLK, width)

        def pair(j, carry):
            group = jnp.concatenate([pall[2 * j], pall[2 * j + 1]], axis=1)
            dots = jnp.dot(flat, group, preferred_element_type=F32)
            value = half - dots.reshape(ZS, BLK, 2 * npd)
            mins[j] = jnp.minimum(mins[j], jnp.min(value, axis=0))
            return carry

        return lax.fori_loop(0, SUBS // 2, pair, carry)

    pts_core.wait_recv()
    core_left.wait_recv()
    core_right.wait_recv()
    core_far.wait_recv()
    for b in range(SUBS):
        wide = pall[b].astype(F32)
        squares[b : b + 1, :] = jnp.sum(wide * wide, axis=0, keepdims=True)
    mins[...] = jnp.full(mins.shape, jnp.inf, F32)
    lax.fori_loop(0, 4, absorb, 0)

    for j in range(SUBS // 2):
        for r in range(ROUNDS):
            low_r = jnp.min(mins[j, r * SHARE : (r + 1) * SHARE, :], axis=0, keepdims=True)
            for h in range(2):
                line[sub, r, 2 * j + h : 2 * j + h + 1, :] = low_r[:, h * npd : (h + 1) * npd]

    for device in members:
        remote(line.at[sub], line.at[sub], line_send, line_recv, device).start()
    wait_bytes(line.at[pl.ds(0, SUBS - 1)], line_recv)

    lanes = lax.broadcasted_iota(jnp.int32, (1, npd), 1)
    least = None
    total = jnp.zeros((1, npd), F32)
    for r in range(ROUNDS):
        now = jnp.min(line[:, r], axis=0)
        least = now if least is None else jnp.minimum(least, now)
        dist = jnp.maximum(squares[...] + 2.0 * least, 0.0)
        near[r] = dist
        part = jnp.sum(jnp.sum(dist, axis=0, keepdims=True), axis=1, keepdims=True)
        total = jnp.where(lanes == r, part, total)

    zsum[0] = total

    def to_z(d, carry):
        remote(zsum.at[0], zsum.at[ZS - d], z_send, z_recv, at_z(d)).start()
        return carry

    lax.fori_loop(1, ZS, to_z, 0)
    wait_bytes(zsum.at[pl.ds(0, ZS - 1)], z_recv)
    xsum[0] = jnp.sum(zsum[...], axis=0)
    for d in (1, 3, 2):
        remote(xsum.at[0], xsum.at[XS - d], c_send, c_recv, x_to[d]).start()
    wait_bytes(xsum.at[pl.ds(0, XS - 1)], c_recv)
    cost = jnp.sum(xsum[...], axis=0)
    for r in range(ROUNDS):
        cost_r = jnp.sum(jnp.where(lanes == r, cost, 0.0), axis=1, keepdims=True)
        out_ref[r : r + 1, :] = npts * near[r, pl.ds(sub, 1), :] / cost_r

    wait_bytes(slots.at[pl.ds(0, SUBS - 1)], slots_send)
    wait_bytes(cand.at[0, pl.ds(0, 15)], z_block_send)
    wait_bytes(cand.at[pl.ds(0, 2)], x_send)
    wait_bytes(cand.at[0, pl.ds(0, 3)], far_send)
    wait_bytes(cand.at[0, pl.ds(0, 13)], far_z_send)
    for copy in (pts_right, pts_left, pts_core, far_top, core_left, far_low, core_right, core_far):
        copy.wait_send()
    wait_bytes(line.at[pl.ds(0, SUBS - 1)], line_send)
    wait_bytes(zsum.at[pl.ds(0, ZS - 1)], z_send)
    wait_bytes(xsum.at[pl.ds(0, XS - 1)], c_send)


def shards(points, cand_rows, cand_count):
    npd, width = points.shape
    npts = float(npd * lax.axis_size(("dp", "sub")))
    dma = pltpu.SemaphoreType.DMA
    return pl.pallas_call(
        lambda *refs: kernel(npts, *refs),
        out_shape=jax.ShapeDtypeStruct((ROUNDS, npd), F32),
        in_specs=[
            pl.BlockSpec(memory_space=pltpu.SMEM),
            pl.BlockSpec(memory_space=pltpu.SMEM),
            pl.BlockSpec(memory_space=pl.ANY),
        ],
        out_specs=pl.BlockSpec(memory_space=pltpu.VMEM),
        scratch_shapes=[
            pltpu.VMEM((npd, width), jnp.bfloat16),
            pltpu.VMEM((SUBS, RAW, width), jnp.bfloat16),
            pltpu.VMEM((XS, ZS, BLK, width), jnp.bfloat16),
            pltpu.VMEM((SUBS, width, npd), jnp.bfloat16),
            pltpu.VMEM((SUBS // 2, BLK, 2 * npd), F32),
            pltpu.VMEM((SUBS, npd), F32),
            pltpu.VMEM((SUBS, ROUNDS, SUBS, npd), F32),
            pltpu.VMEM((ROUNDS, SUBS, npd), F32),
            pltpu.VMEM((ZS, 1, npd), F32),
            pltpu.VMEM((XS, 1, npd), F32),
            dma,
            dma,
            dma,
            dma,
            dma,
            dma((17,)),
            dma((4,)),
            dma,
            dma,
            dma((3,)),
            dma((4,)),
            dma((8,)),
            dma((8,)),
            dma,
            dma,
            dma,
            dma,
            dma,
            dma,
        ],
        compiler_params=pltpu.CompilerParams(
            collective_id=0, has_side_effects=True, vmem_limit_bytes=60 * 1024 * 1024
        ),
        cost_estimate=pl.CostEstimate(
            flops=2 * 1024 * 1024 * width, bytes_accessed=npd * width * 2, transcendentals=0
        ),
    )(cand_rows, cand_count.reshape(1, ROUNDS), points)


def solution(mesh):
    in_specs = (P(("dp", "sub"), None), P(None, ("dp", "sub")), P(None, ("dp", "sub")))
    out_specs = P(None, ("dp", "sub"))
    return jax.shard_map(shards, mesh=mesh, in_specs=in_specs, out_specs=out_specs, check_vma=False)
```

```python
import jax
import jax.numpy as jnp
from jax import lax
from jax.experimental import pallas as pl
from jax.experimental.pallas import tpu as pltpu
from jax.sharding import PartitionSpec as P

ROUNDS = 3
SLOTS = 4
XS = 4
ZS = 16
YS = 4
SUBS = 8
RAW = 16
BLK = 8
SHARE = 2
MESH = pl.DeviceIdType.MESH
F32 = jnp.float32
INF = float("inf")


def kernel(
    npts,
    rows_ref,
    cnt_ref,
    points_ref,
    out_ref,
    raw,
    slots,
    cand,
    pall,
    mins,
    squares,
    line,
    near,
    zsum,
    xsum,
    local_sem,
    slots_send,
    slots_recv,
    z_block_send,
    x_send,
    z_block_recv,
    x_recv,
    far_send,
    far_z_send,
    far_recv,
    far_z_recv,
    pts_send,
    pts_recv,
    line_send,
    line_recv,
    z_send,
    z_recv,
    c_send,
    c_recv,
):
    dp = lax.axis_index("dp")
    sub = lax.axis_index("sub")
    x, z = lax.div(dp, ZS), lax.rem(dp, ZS)
    y, core = lax.div(sub, 2), lax.rem(sub, 2)
    npd, width = points_ref.shape

    def at_x(d):
        return (lax.rem(x + d, XS) * ZS + z, sub)

    def at_z(d):
        return (x * ZS + lax.rem(z + d, ZS), sub)

    def at_y(d):
        return (dp, lax.rem(y + d, YS) * 2 + core)

    other_core = (dp, y * 2 + (1 - core))
    z_to = {d: at_z(d % ZS) for d in (1, -1, 2, -2, 3, -3, 4, -4)}
    x_to = {d: at_x(d) for d in (1, 2, 3)}
    y_right, y_left = at_y(1), at_y(3)

    own_points = pltpu.make_async_copy(points_ref, raw, local_sem)
    own_points.start()
    barrier = pltpu.get_barrier_semaphore()
    far_first = ((2, 0), (2, 1), (1, 0), (3, 0), (1, 1), (3, 1), (0, 1))
    members = [(dp, lax.rem(y + d, YS) * 2 + (1 - core if other else core)) for d, other in far_first]
    partners = [*z_to.values(), *x_to.values(), *members]
    for device in partners:
        pl.semaphore_signal(barrier, inc=1, device_id=device, device_id_type=MESH)

    row = lax.broadcasted_iota(jnp.int32, (RAW, npd), 0)
    lane = lax.broadcasted_iota(jnp.int32, (RAW, npd), 1)
    target = jnp.full((RAW, npd), -1, jnp.int32)
    counts = jnp.zeros((RAW, npd), F32)
    for r in range(ROUNDS):
        counts = jnp.where(row == ROUNDS * SLOTS + r, cnt_ref[0, r].astype(F32), counts)
        for i in range(SLOTS):
            target = jnp.where(row == r * SLOTS + i, rows_ref[r, i], target)
    pick = jnp.where(lane == target, 1.0, 0.0).astype(jnp.bfloat16)
    here = lax.broadcasted_iota(jnp.int32, (npd, npd), 0)
    there = lax.broadcasted_iota(jnp.int32, (npd, npd), 1)
    same_round = (here & (RAW - 1)) == ROUNDS * SLOTS + ((there & (RAW - 1)) >> 2)
    before = jnp.where(same_round & ((here >> 4) < (there >> 4)), 1.0, 0.0)
    itself = jnp.where(same_round & ((here >> 4) == (there >> 4)), 1.0, 0.0)
    slot = lane & (RAW - 1)
    slot_round = jnp.where(slot < ROUNDS * SLOTS, slot >> 2, -1)
    slot_index = (slot & (SLOTS - 1)).astype(F32)
    wanted = (SHARE * sub + (row & 1)).astype(F32)
    wanted_round = slot_round == (row >> 1)
    own_points.wait()
    mine = raw[...]
    block = jnp.dot(pick, mine, preferred_element_type=F32)
    slots[sub, :, :npd] = (block[:, :npd] + counts).astype(jnp.bfloat16)
    slots[sub, :, npd:] = block[:, npd:].astype(jnp.bfloat16)

    pl.semaphore_wait(barrier, len(partners))

    def remote(src, dst, send, recv, device):
        return pltpu.make_async_remote_copy(
            src_ref=src, dst_ref=dst, send_sem=send, recv_sem=recv, device_id=device, device_id_type=MESH
        )

    def to_sides(place, count, group):
        for d, column in ((1, 2), (3, 3)):
            src, dst = cand.at[0, pl.ds(place, count)], cand.at[column, pl.ds(place, count)]
            remote(src, dst, x_send, x_recv.at[group], x_to[d]).start()

    def to_far(place):
        remote(cand.at[0, place], cand.at[1, place], far_send, far_recv.at[place - 12], x_to[2]).start()

    def far_along_z(src, place, count, group, d, lanes=None):
        src, dst = cand.at[1, pl.ds(src, count)], cand.at[1, pl.ds(place, count)]
        if lanes is not None:
            part = pl.ds(lanes * (width // 2), width // 2)
            src, dst = src.at[:, :, part], dst.at[:, :, part]
        remote(src, dst, far_z_send, far_z_recv.at[group], z_to[d]).start()

    def along_z(src, place, d, lanes=None):
        if lanes is None:
            src, dst = cand.at[0, src], cand.at[0, place]
        else:
            part = pl.ds(lanes * (width // 2), width // 2)
            src, dst = cand.at[0, src, :, part], cand.at[0, place, :, part]
        remote(src, dst, z_block_send, z_block_recv.at[place + (lanes or 0)], z_to[d]).start()

    def z_arrived(*places):
        for place in places:
            wait_bytes(cand.at[0, place], z_block_recv.at[place])

    def wait_bytes(ref, sem):
        pltpu.make_async_copy(ref, ref, sem).wait()

    for device in members:
        remote(slots.at[sub], slots.at[sub], slots_send, slots_recv, device).start()
    pall[sub] = mine.T
    slot_right, slot_left, slot_far = (lax.rem(y + d, YS) * 2 + core for d in (1, 3, 2))
    top, low = pl.ds(0, width // 2), pl.ds(width // 2, width // 2)
    mine_at = pall.at[sub]
    pts_right = remote(mine_at, mine_at, pts_send.at[0], pts_recv.at[0], y_right)
    pts_left = remote(mine_at, mine_at, pts_send.at[1], pts_recv.at[1], y_left)
    pts_core = remote(mine_at, mine_at, pts_send.at[2], pts_recv.at[2], other_core)
    pts_right.start()
    pts_left.start()
    pts_core.start()

    wait_bytes(slots.at[pl.ds(0, SUBS - 1)], slots_recv)
    flat = slots[...].reshape(SUBS * RAW, width)
    known = flat[:, :npd].astype(F32)
    offset = jnp.sum(known * before, axis=0, keepdims=True)
    count = jnp.sum(known * itself, axis=0, keepdims=True)
    choice = wanted_round & (slot_index < count) & (offset + slot_index == wanted)
    share = jnp.dot(jnp.where(choice, 1.0, 0.0).astype(jnp.bfloat16), flat, preferred_element_type=F32)
    cand[0, 13] = share[:BLK].astype(jnp.bfloat16)

    along_z(13, 12, 4)
    along_z(13, 14, -4)
    to_far(13)
    for place, d in ((1, 2), (2, -2), (5, 1), (9, -1)):
        along_z(13, place, d)
    to_sides(13, 1, 3)

    z_arrived(12)
    to_far(12)
    along_z(12, 15, 4, 0)
    for place, d in ((7, 3), (0, 2), (4, 1), (8, -1)):
        along_z(12, place, d)
    z_arrived(14)
    to_far(14)
    along_z(14, 15, -4, 1)
    for place, d in ((11, -3), (3, -2), (10, -1), (6, 1)):
        along_z(14, place, d)
    to_sides(12, 1, 3)
    to_sides(14, 1, 3)

    pts_right.wait_recv()
    near_left = pall.at[slot_left]
    far_top = remote(near_left.at[top], near_left.at[top], pts_send.at[3], pts_recv.at[3], y_right)
    core_left = remote(near_left, near_left, pts_send.at[4], pts_recv.at[4], other_core)
    far_top.start()
    core_left.start()
    pts_left.wait_recv()
    near_right = pall.at[slot_right]
    far_low = remote(near_right.at[low], near_right.at[low], pts_send.at[5], pts_recv.at[5], y_left)
    core_right = remote(near_right, near_right, pts_send.at[6], pts_recv.at[6], other_core)
    far_low.start()
    core_right.start()
    for place in (12, 13, 14):
        wait_bytes(cand.at[1, place], far_recv.at[place - 12])
    far_along_z(12, 15, 1, 3, 4, 0)
    far_along_z(14, 15, 1, 3, -4, 1)
    far_along_z(12, 7, 1, 1, 3)
    far_along_z(14, 11, 1, 2, -3)
    far_along_z(12, 0, 2, 0, 2)
    far_along_z(13, 2, 2, 0, -2)
    far_along_z(12, 4, 3, 1, 1)
    far_along_z(12, 8, 3, 2, -1)

    for group in range(3):
        z_arrived(*range(4 * group, 4 * group + 4))
        to_sides(4 * group, 4, group)
    half_block = cand.at[0, 15, :, pl.ds(0, width // 2)]
    wait_bytes(half_block, z_block_recv.at[15])
    wait_bytes(half_block, z_block_recv.at[16])
    to_sides(15, 1, 3)

    far_top.wait_recv()
    far_low.wait_recv()
    far = pall.at[slot_far]
    core_far = remote(far, far, pts_send.at[7], pts_recv.at[7], other_core)
    core_far.start()

    def absorb(first, count):
        for group in range(first, first + count):
            wait_bytes(cand.at[pl.ds(2, 2), pl.ds(0, 4)], x_recv.at[group])
            wait_bytes(cand.at[1, pl.ds(0, 4 if group < 3 else 1)], far_z_recv.at[group])
        blocks = XS * 4 * count
        rows = cand[:, 4 * first : 4 * (first + count)].reshape(blocks, BLK, width)
        half = jnp.zeros((blocks, BLK, npd), F32)
        for t in range(width // npd):
            piece = rows[:, :, t * npd : (t + 1) * npd].astype(F32)
            half = half + piece * piece
        half = 0.5 * jnp.sum(half, axis=2, keepdims=True)
        flat = rows.reshape(blocks * BLK, width)
        for j in range(SUBS // 2):
            group = jnp.concatenate([pall[2 * j], pall[2 * j + 1]], axis=1)
            dots = jnp.dot(flat, group, preferred_element_type=F32)
            best = jnp.min(half - dots.reshape(blocks, BLK, 2 * npd), axis=0)
            mins[j] = best if first == 0 else jnp.minimum(mins[j], best)

    pts_core.wait_recv()
    core_left.wait_recv()
    core_right.wait_recv()
    core_far.wait_recv()
    absorb(0, 3)
    for b in range(SUBS):
        wide = pall[b].astype(F32)
        squares[b : b + 1, :] = jnp.sum(wide * wide, axis=0, keepdims=True)
    absorb(3, 1)

    for j in range(SUBS // 2):
        for r in range(ROUNDS):
            low_r = jnp.min(mins[j, r * SHARE : (r + 1) * SHARE, :], axis=0, keepdims=True)
            for h in range(2):
                line[sub, r, 2 * j + h : 2 * j + h + 1, :] = low_r[:, h * npd : (h + 1) * npd]

    for device in members:
        remote(line.at[sub], line.at[sub], line_send, line_recv, device).start()
    wait_bytes(line.at[pl.ds(0, SUBS - 1)], line_recv)

    lanes = lax.broadcasted_iota(jnp.int32, (1, npd), 1)
    least = None
    total = jnp.zeros((1, npd), F32)
    for r in range(ROUNDS):
        now = jnp.min(line[:, r], axis=0)
        least = now if least is None else jnp.minimum(least, now)
        dist = jnp.maximum(squares[...] + 2.0 * least, 0.0)
        near[r] = dist
        part = jnp.sum(jnp.sum(dist, axis=0, keepdims=True), axis=1, keepdims=True)
        total = jnp.where(lanes == r, part, total)

    zsum[0] = total

    for d in (8, 7, 9, 6, 10, 5, 11, 4, 12, 3, 13, 2, 14, 1, 15):
        remote(zsum.at[0], zsum.at[ZS - d], z_send, z_recv, at_z(d)).start()
    wait_bytes(zsum.at[pl.ds(0, ZS - 1)], z_recv)
    xsum[0] = jnp.sum(zsum[...], axis=0)
    for d in (1, 3, 2):
        remote(xsum.at[0], xsum.at[XS - d], c_send, c_recv, x_to[d]).start()
    wait_bytes(xsum.at[pl.ds(0, XS - 1)], c_recv)
    cost = jnp.sum(xsum[...], axis=0)
    for r in range(ROUNDS):
        cost_r = jnp.sum(jnp.where(lanes == r, cost, 0.0), axis=1, keepdims=True)
        out_ref[r : r + 1, :] = npts * near[r, pl.ds(sub, 1), :] / cost_r

    wait_bytes(slots.at[pl.ds(0, SUBS - 1)], slots_send)
    wait_bytes(cand.at[0, pl.ds(0, 15)], z_block_send)
    wait_bytes(cand.at[pl.ds(0, 2)], x_send)
    wait_bytes(cand.at[0, pl.ds(0, 3)], far_send)
    wait_bytes(cand.at[0, pl.ds(0, 13)], far_z_send)
    for copy in (pts_right, pts_left, pts_core, far_top, core_left, far_low, core_right, core_far):
        copy.wait_send()
    wait_bytes(line.at[pl.ds(0, SUBS - 1)], line_send)
    wait_bytes(zsum.at[pl.ds(0, ZS - 1)], z_send)
    wait_bytes(xsum.at[pl.ds(0, XS - 1)], c_send)


def shards(points, cand_rows, cand_count):
    npd, width = points.shape
    npts = float(npd * lax.axis_size(("dp", "sub")))
    dma = pltpu.SemaphoreType.DMA
    return pl.pallas_call(
        lambda *refs: kernel(npts, *refs),
        out_shape=jax.ShapeDtypeStruct((ROUNDS, npd), F32),
        in_specs=[
            pl.BlockSpec(memory_space=pltpu.SMEM),
            pl.BlockSpec(memory_space=pltpu.SMEM),
            pl.BlockSpec(memory_space=pl.ANY),
        ],
        out_specs=pl.BlockSpec(memory_space=pltpu.VMEM),
        scratch_shapes=[
            pltpu.VMEM((npd, width), jnp.bfloat16),
            pltpu.VMEM((SUBS, RAW, width), jnp.bfloat16),
            pltpu.VMEM((XS, ZS, BLK, width), jnp.bfloat16),
            pltpu.VMEM((SUBS, width, npd), jnp.bfloat16),
            pltpu.VMEM((SUBS // 2, BLK, 2 * npd), F32),
            pltpu.VMEM((SUBS, npd), F32),
            pltpu.VMEM((SUBS, ROUNDS, SUBS, npd), F32),
            pltpu.VMEM((ROUNDS, SUBS, npd), F32),
            pltpu.VMEM((ZS, 1, npd), F32),
            pltpu.VMEM((XS, 1, npd), F32),
            dma,
            dma,
            dma,
            dma,
            dma,
            dma((17,)),
            dma((4,)),
            dma,
            dma,
            dma((3,)),
            dma((4,)),
            dma((8,)),
            dma((8,)),
            dma,
            dma,
            dma,
            dma,
            dma,
            dma,
        ],
        compiler_params=pltpu.CompilerParams(
            collective_id=0, has_side_effects=True, vmem_limit_bytes=60 * 1024 * 1024
        ),
        cost_estimate=pl.CostEstimate(
            flops=2 * 1024 * 1024 * width, bytes_accessed=npd * width * 2, transcendentals=0
        ),
    )(cand_rows, cand_count.reshape(1, ROUNDS), points)


def solution(mesh):
    in_specs = (P(("dp", "sub"), None), P(None, ("dp", "sub")), P(None, ("dp", "sub")))
    out_specs = P(None, ("dp", "sub"))
    return jax.shard_map(shards, mesh=mesh, in_specs=in_specs, out_specs=out_specs, check_vma=False)
```

```python
import jax
import jax.numpy as jnp
from jax import lax
from jax.experimental import pallas as pl
from jax.experimental.pallas import tpu as pltpu
from jax.sharding import PartitionSpec as P

ROUNDS = 3
SLOTS = 4
XS = 4
ZS = 16
YS = 4
SUBS = 8
RAW = 16
BLK = 8
SHARE = 2
MESH = pl.DeviceIdType.MESH
F32 = jnp.float32
INF = float("inf")


def kernel(
    npts,
    rows_in,
    counts_in,
    points_ref,
    out_ref,
    rows_ref,
    cnt_ref,
    raw,
    slots,
    cand,
    pall,
    mins,
    squares,
    line,
    near,
    zsum,
    xsum,
    local_sem,
    slots_send,
    slots_recv,
    z_block_send,
    x_send,
    z_block_recv,
    x_recv,
    far_send,
    far_z_send,
    far_recv,
    far_z_recv,
    pts_send,
    pts_recv,
    line_send,
    line_recv,
    z_send,
    z_recv,
    c_send,
    c_recv,
):
    dp = lax.axis_index("dp")
    sub = lax.axis_index("sub")
    x, z = lax.div(dp, ZS), lax.rem(dp, ZS)
    y, core = lax.div(sub, 2), lax.rem(sub, 2)
    npd, width = points_ref.shape

    def at_x(d):
        return (lax.rem(x + d, XS) * ZS + z, sub)

    def at_z(d):
        return (x * ZS + lax.rem(z + d, ZS), sub)

    def at_y(d):
        return (dp, lax.rem(y + d, YS) * 2 + core)

    other_core = (dp, y * 2 + (1 - core))
    z_to = {d: at_z(d % ZS) for d in (1, -1, 2, -2, 3, -3, 4, -4)}
    x_to = {d: at_x(d) for d in (1, 2, 3)}
    y_right, y_left = at_y(1), at_y(3)

    own_points = pltpu.make_async_copy(points_ref, raw, local_sem.at[0])
    own_points.start()
    own_rows = pltpu.make_async_copy(rows_in, rows_ref, local_sem.at[1])
    own_rows.start()
    own_counts = pltpu.make_async_copy(counts_in, cnt_ref, local_sem.at[2])
    own_counts.start()
    barrier = pltpu.get_barrier_semaphore()
    far_first = ((2, 0), (2, 1), (1, 0), (3, 0), (1, 1), (3, 1), (0, 1))
    members = [(dp, lax.rem(y + d, YS) * 2 + (1 - core if other else core)) for d, other in far_first]
    partners = [*z_to.values(), *x_to.values(), *members]
    for device in partners:
        pl.semaphore_signal(barrier, inc=1, device_id=device, device_id_type=MESH)

    row = lax.broadcasted_iota(jnp.int32, (RAW, npd), 0)
    lane = lax.broadcasted_iota(jnp.int32, (RAW, npd), 1)
    here = lax.broadcasted_iota(jnp.int32, (npd, npd), 0)
    there = lax.broadcasted_iota(jnp.int32, (npd, npd), 1)
    same_round = (here & (RAW - 1)) == ROUNDS * SLOTS + ((there & (RAW - 1)) >> 2)
    before = jnp.where(same_round & ((here >> 4) < (there >> 4)), 1.0, 0.0)
    itself = jnp.where(same_round & ((here >> 4) == (there >> 4)), 1.0, 0.0)
    slot = lane & (RAW - 1)
    slot_round = jnp.where(slot < ROUNDS * SLOTS, slot >> 2, -1)
    slot_index = (slot & (SLOTS - 1)).astype(F32)
    wanted = (SHARE * sub + (row & 1)).astype(F32)
    wanted_round = slot_round == (row >> 1)
    own_rows.wait()
    own_counts.wait()
    target = jnp.full((RAW, npd), -1, jnp.int32)
    counts = jnp.zeros((RAW, npd), F32)
    for r in range(ROUNDS):
        counts = jnp.where(row == ROUNDS * SLOTS + r, cnt_ref[0, r].astype(F32), counts)
        for i in range(SLOTS):
            target = jnp.where(row == r * SLOTS + i, rows_ref[r, i], target)
    pick = jnp.where(lane == target, 1.0, 0.0).astype(jnp.bfloat16)
    own_points.wait()
    mine = raw[...]
    block = jnp.dot(pick, mine, preferred_element_type=F32)
    slots[sub, :, :npd] = (block[:, :npd] + counts).astype(jnp.bfloat16)
    slots[sub, :, npd:] = block[:, npd:].astype(jnp.bfloat16)

    pl.semaphore_wait(barrier, len(partners))

    def remote(src, dst, send, recv, device):
        return pltpu.make_async_remote_copy(
            src_ref=src, dst_ref=dst, send_sem=send, recv_sem=recv, device_id=device, device_id_type=MESH
        )

    def to_sides(place, count, group):
        for d, column in ((1, 2), (3, 3)):
            src, dst = cand.at[0, pl.ds(place, count)], cand.at[column, pl.ds(place, count)]
            remote(src, dst, x_send, x_recv.at[group], x_to[d]).start()

    def to_far(place):
        remote(cand.at[0, place], cand.at[1, place], far_send, far_recv.at[place - 12], x_to[2]).start()

    def far_along_z(src, place, count, group, d, lanes=None):
        src, dst = cand.at[1, pl.ds(src, count)], cand.at[1, pl.ds(place, count)]
        if lanes is not None:
            part = pl.ds(lanes * (width // 2), width // 2)
            src, dst = src.at[:, :, part], dst.at[:, :, part]
        remote(src, dst, far_z_send, far_z_recv.at[group], z_to[d]).start()

    def along_z(src, place, d, lanes=None):
        if lanes is None:
            src, dst = cand.at[0, src], cand.at[0, place]
        else:
            part = pl.ds(lanes * (width // 2), width // 2)
            src, dst = cand.at[0, src, :, part], cand.at[0, place, :, part]
        remote(src, dst, z_block_send, z_block_recv.at[place + (lanes or 0)], z_to[d]).start()

    def z_arrived(*places):
        for place in places:
            wait_bytes(cand.at[0, place], z_block_recv.at[place])

    def wait_bytes(ref, sem):
        pltpu.make_async_copy(ref, ref, sem).wait()

    for device in members:
        remote(slots.at[sub], slots.at[sub], slots_send, slots_recv, device).start()
    pall[sub] = mine.T
    slot_right, slot_left, slot_far = (lax.rem(y + d, YS) * 2 + core for d in (1, 3, 2))
    top, low = pl.ds(0, width // 2), pl.ds(width // 2, width // 2)
    mine_at = pall.at[sub]
    pts_right = remote(mine_at, mine_at, pts_send.at[0], pts_recv.at[0], y_right)
    pts_left = remote(mine_at, mine_at, pts_send.at[1], pts_recv.at[1], y_left)
    pts_core = remote(mine_at, mine_at, pts_send.at[2], pts_recv.at[2], other_core)
    pts_right.start()
    pts_left.start()
    pts_core.start()

    wait_bytes(slots.at[pl.ds(0, SUBS - 1)], slots_recv)
    flat = slots[...].reshape(SUBS * RAW, width)
    known = flat[:, :npd].astype(F32)
    offset = jnp.sum(known * before, axis=0, keepdims=True)
    count = jnp.sum(known * itself, axis=0, keepdims=True)
    choice = wanted_round & (slot_index < count) & (offset + slot_index == wanted)
    share = jnp.dot(jnp.where(choice, 1.0, 0.0).astype(jnp.bfloat16), flat, preferred_element_type=F32)
    cand[0, 13] = share[:BLK].astype(jnp.bfloat16)

    along_z(13, 12, 4)
    along_z(13, 14, -4)
    to_far(13)
    for place, d in ((1, 2), (2, -2), (5, 1), (9, -1)):
        along_z(13, place, d)
    to_sides(13, 1, 3)

    z_arrived(12)
    to_far(12)
    along_z(12, 15, 4, 0)
    for place, d in ((7, 3), (0, 2), (4, 1), (8, -1)):
        along_z(12, place, d)
    z_arrived(14)
    to_far(14)
    along_z(14, 15, -4, 1)
    for place, d in ((11, -3), (3, -2), (10, -1), (6, 1)):
        along_z(14, place, d)
    to_sides(12, 1, 3)
    to_sides(14, 1, 3)

    pts_right.wait_recv()
    near_left = pall.at[slot_left]
    far_top = remote(near_left.at[top], near_left.at[top], pts_send.at[3], pts_recv.at[3], y_right)
    core_left = remote(near_left, near_left, pts_send.at[4], pts_recv.at[4], other_core)
    far_top.start()
    core_left.start()
    pts_left.wait_recv()
    near_right = pall.at[slot_right]
    far_low = remote(near_right.at[low], near_right.at[low], pts_send.at[5], pts_recv.at[5], y_left)
    core_right = remote(near_right, near_right, pts_send.at[6], pts_recv.at[6], other_core)
    far_low.start()
    core_right.start()
    for place in (12, 13, 14):
        wait_bytes(cand.at[1, place], far_recv.at[place - 12])
    far_along_z(12, 15, 1, 3, 4, 0)
    far_along_z(14, 15, 1, 3, -4, 1)
    far_along_z(12, 7, 1, 1, 3)
    far_along_z(14, 11, 1, 2, -3)
    far_along_z(12, 0, 2, 0, 2)
    far_along_z(13, 2, 2, 0, -2)
    far_along_z(12, 4, 3, 1, 1)
    far_along_z(12, 8, 3, 2, -1)

    for group in range(3):
        z_arrived(*range(4 * group, 4 * group + 4))
        to_sides(4 * group, 4, group)
    half_block = cand.at[0, 15, :, pl.ds(0, width // 2)]
    wait_bytes(half_block, z_block_recv.at[15])
    wait_bytes(half_block, z_block_recv.at[16])
    to_sides(15, 1, 3)

    far_top.wait_recv()
    far_low.wait_recv()
    far = pall.at[slot_far]
    core_far = remote(far, far, pts_send.at[7], pts_recv.at[7], other_core)
    core_far.start()

    def absorb(first, count):
        for group in range(first, first + count):
            wait_bytes(cand.at[pl.ds(2, 2), pl.ds(0, 4)], x_recv.at[group])
            wait_bytes(cand.at[1, pl.ds(0, 4 if group < 3 else 1)], far_z_recv.at[group])
        blocks = XS * 4 * count
        rows = cand[:, 4 * first : 4 * (first + count)].reshape(blocks, BLK, width)
        half = jnp.zeros((blocks, BLK, npd), F32)
        for t in range(width // npd):
            piece = rows[:, :, t * npd : (t + 1) * npd].astype(F32)
            half = half + piece * piece
        half = 0.5 * jnp.sum(half, axis=2, keepdims=True)
        flat = rows.reshape(blocks * BLK, width)
        for j in range(SUBS // 2):
            group = jnp.concatenate([pall[2 * j], pall[2 * j + 1]], axis=1)
            dots = jnp.dot(flat, group, preferred_element_type=F32)
            best = jnp.min(half - dots.reshape(blocks, BLK, 2 * npd), axis=0)
            mins[j] = best if first == 0 else jnp.minimum(mins[j], best)

    pts_core.wait_recv()
    core_left.wait_recv()
    core_right.wait_recv()
    core_far.wait_recv()
    absorb(0, 3)
    for b in range(SUBS):
        wide = pall[b].astype(F32)
        squares[b : b + 1, :] = jnp.sum(wide * wide, axis=0, keepdims=True)
    absorb(3, 1)

    for j in range(SUBS // 2):
        for r in range(ROUNDS):
            low_r = jnp.min(mins[j, r * SHARE : (r + 1) * SHARE, :], axis=0, keepdims=True)
            for h in range(2):
                line[sub, r, 2 * j + h : 2 * j + h + 1, :] = low_r[:, h * npd : (h + 1) * npd]

    for device in members:
        remote(line.at[sub], line.at[sub], line_send, line_recv, device).start()
    wait_bytes(line.at[pl.ds(0, SUBS - 1)], line_recv)

    lanes = lax.broadcasted_iota(jnp.int32, (1, npd), 1)
    least = None
    total = jnp.zeros((1, npd), F32)
    for r in range(ROUNDS):
        now = jnp.min(line[:, r], axis=0)
        least = now if least is None else jnp.minimum(least, now)
        dist = jnp.maximum(squares[...] + 2.0 * least, 0.0)
        near[r] = dist
        part = jnp.sum(jnp.sum(dist, axis=0, keepdims=True), axis=1, keepdims=True)
        total = jnp.where(lanes == r, part, total)

    zsum[0] = total

    for d in (8, 7, 9, 6, 10, 5, 11, 4, 12, 3, 13, 2, 14, 1, 15):
        remote(zsum.at[0], zsum.at[ZS - d], z_send, z_recv, at_z(d)).start()
    wait_bytes(zsum.at[pl.ds(0, ZS - 1)], z_recv)
    xsum[0] = jnp.sum(zsum[...], axis=0)
    for d in (1, 3, 2):
        remote(xsum.at[0], xsum.at[XS - d], c_send, c_recv, x_to[d]).start()
    wait_bytes(xsum.at[pl.ds(0, XS - 1)], c_recv)
    cost = jnp.sum(xsum[...], axis=0)
    for r in range(ROUNDS):
        cost_r = jnp.sum(jnp.where(lanes == r, cost, 0.0), axis=1, keepdims=True)
        out_ref[r : r + 1, :] = npts * near[r, pl.ds(sub, 1), :] / cost_r

    wait_bytes(slots.at[pl.ds(0, SUBS - 1)], slots_send)
    wait_bytes(cand.at[0, pl.ds(0, 15)], z_block_send)
    wait_bytes(cand.at[pl.ds(0, 2)], x_send)
    wait_bytes(cand.at[0, pl.ds(0, 3)], far_send)
    wait_bytes(cand.at[0, pl.ds(0, 13)], far_z_send)
    for copy in (pts_right, pts_left, pts_core, far_top, core_left, far_low, core_right, core_far):
        copy.wait_send()
    wait_bytes(line.at[pl.ds(0, SUBS - 1)], line_send)
    wait_bytes(zsum.at[pl.ds(0, ZS - 1)], z_send)
    wait_bytes(xsum.at[pl.ds(0, XS - 1)], c_send)


def shards(points, cand_rows, cand_count):
    npd, width = points.shape
    npts = float(npd * lax.axis_size(("dp", "sub")))
    dma = pltpu.SemaphoreType.DMA
    operands = (cand_rows, cand_count.reshape(1, ROUNDS), points)
    return pl.pallas_call(
        lambda *refs: kernel(npts, *refs),
        out_shape=jax.ShapeDtypeStruct((ROUNDS, npd), F32),
        in_specs=[
            pl.BlockSpec(memory_space=pl.ANY),
            pl.BlockSpec(memory_space=pl.ANY),
            pl.BlockSpec(memory_space=pl.ANY),
        ],
        out_specs=pl.BlockSpec(memory_space=pltpu.VMEM),
        scratch_shapes=[
            pltpu.SMEM((ROUNDS, SLOTS), jnp.int32),
            pltpu.SMEM((1, ROUNDS), jnp.int32),
            pltpu.VMEM((npd, width), jnp.bfloat16),
            pltpu.VMEM((SUBS, RAW, width), jnp.bfloat16),
            pltpu.VMEM((XS, ZS, BLK, width), jnp.bfloat16),
            pltpu.VMEM((SUBS, width, npd), jnp.bfloat16),
            pltpu.VMEM((SUBS // 2, BLK, 2 * npd), F32),
            pltpu.VMEM((SUBS, npd), F32),
            pltpu.VMEM((SUBS, ROUNDS, SUBS, npd), F32),
            pltpu.VMEM((ROUNDS, SUBS, npd), F32),
            pltpu.VMEM((ZS, 1, npd), F32),
            pltpu.VMEM((XS, 1, npd), F32),
            dma((3,)),
            dma,
            dma,
            dma,
            dma,
            dma((17,)),
            dma((4,)),
            dma,
            dma,
            dma((3,)),
            dma((4,)),
            dma((8,)),
            dma((8,)),
            dma,
            dma,
            dma,
            dma,
            dma,
            dma,
        ],
        compiler_params=pltpu.CompilerParams(
            collective_id=0, has_side_effects=True, vmem_limit_bytes=40 * 1024 * 1024
        ),
        cost_estimate=pl.CostEstimate(
            flops=2 * 1024 * 1024 * width, bytes_accessed=npd * width * 2, transcendentals=0
        ),
    )(*(pltpu.with_memory_space_constraint(value, pltpu.HBM) for value in operands))


def solution(mesh):
    in_specs = (P(("dp", "sub"), None), P(None, ("dp", "sub")), P(None, ("dp", "sub")))
    out_specs = P(None, ("dp", "sub"))
    return jax.shard_map(shards, mesh=mesh, in_specs=in_specs, out_specs=out_specs, check_vma=False)
```

```python
import jax
import jax.numpy as jnp
from jax import lax
from jax.experimental import pallas as pl
from jax.experimental.pallas import tpu as pltpu
from jax.sharding import PartitionSpec as P

ROUNDS = 3
SLOTS = 4
XS = 4
ZS = 16
YS = 4
SUBS = 8
RAW = 16
BLK = 8
SHARE = 2
MESH = pl.DeviceIdType.MESH
F32 = jnp.float32
INF = float("inf")


def kernel(
    npts,
    rows_in,
    counts_in,
    points_ref,
    out_ref,
    rows_ref,
    cnt_ref,
    raw,
    slots,
    cand,
    pall,
    mins,
    squares,
    line,
    near,
    zsum,
    xsum,
    local_sem,
    slots_send,
    slots_recv,
    z_block_send,
    x_send,
    z_block_recv,
    x_recv,
    far_send,
    far_z_send,
    far_recv,
    far_z_recv,
    pts_send,
    pts_recv,
    line_send,
    line_recv,
    z_send,
    z_recv,
    c_send,
    c_recv,
):
    dp = lax.axis_index("dp")
    sub = lax.axis_index("sub")
    x, z = lax.div(dp, ZS), lax.rem(dp, ZS)
    y, core = lax.div(sub, 2), lax.rem(sub, 2)
    npd, width = points_ref.shape

    def at_x(d):
        return (lax.rem(x + d, XS) * ZS + z, sub)

    def at_z(d):
        return (x * ZS + lax.rem(z + d, ZS), sub)

    def at_y(d):
        return (dp, lax.rem(y + d, YS) * 2 + core)

    other_core = (dp, y * 2 + (1 - core))
    z_to = {d: at_z(d % ZS) for d in (1, -1, 2, -2, 3, -3, 4, -4)}
    x_to = {d: at_x(d) for d in (1, 2, 3)}
    y_right, y_left = at_y(1), at_y(3)

    own_points = pltpu.make_async_copy(points_ref, raw, local_sem.at[0])
    own_points.start()
    own_rows = pltpu.make_async_copy(rows_in, rows_ref, local_sem.at[1])
    own_rows.start()
    own_counts = pltpu.make_async_copy(counts_in, cnt_ref, local_sem.at[2])
    own_counts.start()
    barrier = pltpu.get_barrier_semaphore()
    far_first = ((2, 0), (2, 1), (1, 0), (3, 0), (1, 1), (3, 1), (0, 1))
    members = [(dp, lax.rem(y + d, YS) * 2 + (1 - core if other else core)) for d, other in far_first]
    partners = [*z_to.values(), *x_to.values(), *members]
    for device in partners:
        pl.semaphore_signal(barrier, inc=1, device_id=device, device_id_type=MESH)

    row = lax.broadcasted_iota(jnp.int32, (RAW, npd), 0)
    lane = lax.broadcasted_iota(jnp.int32, (RAW, npd), 1)
    here = lax.broadcasted_iota(jnp.int32, (npd, npd), 0)
    there = lax.broadcasted_iota(jnp.int32, (npd, npd), 1)
    same_round = (here & (RAW - 1)) == ROUNDS * SLOTS + ((there & (RAW - 1)) >> 2)
    before = jnp.where(same_round & ((here >> 4) < (there >> 4)), 1.0, 0.0)
    itself = jnp.where(same_round & ((here >> 4) == (there >> 4)), 1.0, 0.0)
    slot = lane & (RAW - 1)
    slot_round = jnp.where(slot < ROUNDS * SLOTS, slot >> 2, -1)
    slot_index = (slot & (SLOTS - 1)).astype(F32)
    wanted = (SHARE * sub + (row & 1)).astype(F32)
    wanted_round = slot_round == (row >> 1)
    own_rows.wait()
    own_counts.wait()
    target = jnp.full((RAW, npd), -1, jnp.int32)
    counts = jnp.zeros((RAW, npd), F32)
    for r in range(ROUNDS):
        counts = jnp.where(row == ROUNDS * SLOTS + r, cnt_ref[0, r].astype(F32), counts)
        for i in range(SLOTS):
            target = jnp.where(row == r * SLOTS + i, rows_ref[r, i], target)
    pick = jnp.where(lane == target, 1.0, 0.0).astype(jnp.bfloat16)
    own_points.wait()
    mine = raw[...]
    block = jnp.dot(pick, mine, preferred_element_type=F32)
    slots[sub, :, :npd] = (block[:, :npd] + counts).astype(jnp.bfloat16)
    slots[sub, :, npd:] = block[:, npd:].astype(jnp.bfloat16)

    pl.semaphore_wait(barrier, len(partners))

    def remote(src, dst, send, recv, device):
        return pltpu.make_async_remote_copy(
            src_ref=src, dst_ref=dst, send_sem=send, recv_sem=recv, device_id=device, device_id_type=MESH
        )

    def to_sides(place, count, group):
        for d, column in ((1, 2), (3, 3)):
            src, dst = cand.at[0, pl.ds(place, count)], cand.at[column, pl.ds(place, count)]
            remote(src, dst, x_send, x_recv.at[group], x_to[d]).start()

    def to_far(place):
        remote(cand.at[0, place], cand.at[1, place], far_send, far_recv.at[place - 12], x_to[2]).start()

    def far_along_z(src, place, count, group, d, lanes=None):
        src, dst = cand.at[1, pl.ds(src, count)], cand.at[1, pl.ds(place, count)]
        if lanes is not None:
            part = pl.ds(lanes * (width // 2), width // 2)
            src, dst = src.at[:, :, part], dst.at[:, :, part]
        remote(src, dst, far_z_send, far_z_recv.at[group], z_to[d]).start()

    def along_z(src, place, d, lanes=None):
        if lanes is None:
            src, dst = cand.at[0, src], cand.at[0, place]
        else:
            part = pl.ds(lanes * (width // 2), width // 2)
            src, dst = cand.at[0, src, :, part], cand.at[0, place, :, part]
        remote(src, dst, z_block_send, z_block_recv.at[place + (lanes or 0)], z_to[d]).start()

    def z_arrived(*places):
        for place in places:
            wait_bytes(cand.at[0, place], z_block_recv.at[place])

    def wait_bytes(ref, sem):
        pltpu.make_async_copy(ref, ref, sem).wait()

    for device in members:
        remote(slots.at[sub], slots.at[sub], slots_send, slots_recv, device).start()
    pall[sub] = mine.T
    wait_bytes(slots.at[pl.ds(0, SUBS - 1)], slots_recv)
    flat = slots[...].reshape(SUBS * RAW, width)
    known = flat[:, :npd].astype(F32)
    offset = jnp.sum(known * before, axis=0, keepdims=True)
    count = jnp.sum(known * itself, axis=0, keepdims=True)
    choice = wanted_round & (slot_index < count) & (offset + slot_index == wanted)
    share = jnp.dot(jnp.where(choice, 1.0, 0.0).astype(jnp.bfloat16), flat, preferred_element_type=F32)
    cand[0, 13] = share[:BLK].astype(jnp.bfloat16)

    along_z(13, 12, 4)
    along_z(13, 14, -4)
    to_far(13)
    for place, d in ((1, 2), (2, -2), (5, 1), (9, -1)):
        along_z(13, place, d)
    to_sides(13, 1, 3)

    slot_right, slot_left, slot_far = (lax.rem(y + d, YS) * 2 + core for d in (1, 3, 2))
    top, low = pl.ds(0, width // 2), pl.ds(width // 2, width // 2)
    mine_at = pall.at[sub]
    pts_right = remote(mine_at, mine_at, pts_send.at[0], pts_recv.at[0], y_right)
    pts_left = remote(mine_at, mine_at, pts_send.at[1], pts_recv.at[1], y_left)
    pts_core = remote(mine_at, mine_at, pts_send.at[2], pts_recv.at[2], other_core)
    pts_right.start()
    pts_left.start()
    pts_core.start()

    z_arrived(12)
    to_far(12)
    along_z(12, 15, 4, 0)
    for place, d in ((7, 3), (0, 2), (4, 1), (8, -1)):
        along_z(12, place, d)
    z_arrived(14)
    to_far(14)
    along_z(14, 15, -4, 1)
    for place, d in ((11, -3), (3, -2), (10, -1), (6, 1)):
        along_z(14, place, d)
    to_sides(12, 1, 3)
    to_sides(14, 1, 3)

    pts_right.wait_recv()
    near_left = pall.at[slot_left]
    far_top = remote(near_left.at[top], near_left.at[top], pts_send.at[3], pts_recv.at[3], y_right)
    core_left = remote(near_left, near_left, pts_send.at[4], pts_recv.at[4], other_core)
    far_top.start()
    core_left.start()
    pts_left.wait_recv()
    near_right = pall.at[slot_right]
    far_low = remote(near_right.at[low], near_right.at[low], pts_send.at[5], pts_recv.at[5], y_left)
    core_right = remote(near_right, near_right, pts_send.at[6], pts_recv.at[6], other_core)
    far_low.start()
    core_right.start()
    for place in (12, 13, 14):
        wait_bytes(cand.at[1, place], far_recv.at[place - 12])
    far_along_z(12, 15, 1, 3, 4, 0)
    far_along_z(14, 15, 1, 3, -4, 1)
    far_along_z(12, 7, 1, 1, 3)
    far_along_z(14, 11, 1, 2, -3)
    far_along_z(12, 0, 2, 0, 2)
    far_along_z(13, 2, 2, 0, -2)
    far_along_z(12, 4, 3, 1, 1)
    far_along_z(12, 8, 3, 2, -1)

    for group in range(3):
        z_arrived(*range(4 * group, 4 * group + 4))
        to_sides(4 * group, 4, group)
    half_block = cand.at[0, 15, :, pl.ds(0, width // 2)]
    wait_bytes(half_block, z_block_recv.at[15])
    wait_bytes(half_block, z_block_recv.at[16])
    to_sides(15, 1, 3)

    far_top.wait_recv()
    far_low.wait_recv()
    far = pall.at[slot_far]
    core_far = remote(far, far, pts_send.at[7], pts_recv.at[7], other_core)
    core_far.start()

    def absorb(first, count):
        for group in range(first, first + count):
            wait_bytes(cand.at[pl.ds(2, 2), pl.ds(0, 4)], x_recv.at[group])
            wait_bytes(cand.at[1, pl.ds(0, 4 if group < 3 else 1)], far_z_recv.at[group])
        blocks = XS * 4 * count
        rows = cand[:, 4 * first : 4 * (first + count)].reshape(blocks, BLK, width)
        half = jnp.zeros((blocks, BLK, npd), F32)
        for t in range(width // npd):
            piece = rows[:, :, t * npd : (t + 1) * npd].astype(F32)
            half = half + piece * piece
        half = 0.5 * jnp.sum(half, axis=2, keepdims=True)
        flat = rows.reshape(blocks * BLK, width)
        for j in range(SUBS // 2):
            group = jnp.concatenate([pall[2 * j], pall[2 * j + 1]], axis=1)
            dots = jnp.dot(flat, group, preferred_element_type=F32)
            best = jnp.min(half - dots.reshape(blocks, BLK, 2 * npd), axis=0)
            mins[j] = best if first == 0 else jnp.minimum(mins[j], best)

    pts_core.wait_recv()
    core_left.wait_recv()
    core_right.wait_recv()
    core_far.wait_recv()
    absorb(0, 3)
    for b in range(SUBS):
        wide = pall[b].astype(F32)
        squares[b : b + 1, :] = jnp.sum(wide * wide, axis=0, keepdims=True)
    absorb(3, 1)

    for j in range(SUBS // 2):
        for r in range(ROUNDS):
            low_r = jnp.min(mins[j, r * SHARE : (r + 1) * SHARE, :], axis=0, keepdims=True)
            for h in range(2):
                line[sub, r, 2 * j + h : 2 * j + h + 1, :] = low_r[:, h * npd : (h + 1) * npd]

    for device in members:
        remote(line.at[sub], line.at[sub], line_send, line_recv, device).start()
    wait_bytes(line.at[pl.ds(0, SUBS - 1)], line_recv)

    lanes = lax.broadcasted_iota(jnp.int32, (1, npd), 1)
    least = None
    total = jnp.zeros((1, npd), F32)
    for r in range(ROUNDS):
        now = jnp.min(line[:, r], axis=0)
        least = now if least is None else jnp.minimum(least, now)
        dist = jnp.maximum(squares[...] + 2.0 * least, 0.0)
        near[r] = dist
        part = jnp.sum(jnp.sum(dist, axis=0, keepdims=True), axis=1, keepdims=True)
        total = jnp.where(lanes == r, part, total)

    zsum[0] = total

    for d in (8, 7, 9, 6, 10, 5, 11, 4, 12, 3, 13, 2, 14, 1, 15):
        remote(zsum.at[0], zsum.at[ZS - d], z_send, z_recv, at_z(d)).start()
    wait_bytes(zsum.at[pl.ds(0, ZS - 1)], z_recv)
    xsum[0] = jnp.sum(zsum[...], axis=0)
    for d in (1, 3, 2):
        remote(xsum.at[0], xsum.at[XS - d], c_send, c_recv, x_to[d]).start()
    wait_bytes(xsum.at[pl.ds(0, XS - 1)], c_recv)
    cost = jnp.sum(xsum[...], axis=0)
    for r in range(ROUNDS):
        cost_r = jnp.sum(jnp.where(lanes == r, cost, 0.0), axis=1, keepdims=True)
        out_ref[r : r + 1, :] = npts * near[r, pl.ds(sub, 1), :] / cost_r

    wait_bytes(slots.at[pl.ds(0, SUBS - 1)], slots_send)
    wait_bytes(cand.at[0, pl.ds(0, 15)], z_block_send)
    wait_bytes(cand.at[pl.ds(0, 2)], x_send)
    wait_bytes(cand.at[0, pl.ds(0, 3)], far_send)
    wait_bytes(cand.at[0, pl.ds(0, 13)], far_z_send)
    for copy in (pts_right, pts_left, pts_core, far_top, core_left, far_low, core_right, core_far):
        copy.wait_send()
    wait_bytes(line.at[pl.ds(0, SUBS - 1)], line_send)
    wait_bytes(zsum.at[pl.ds(0, ZS - 1)], z_send)
    wait_bytes(xsum.at[pl.ds(0, XS - 1)], c_send)


def shards(points, cand_rows, cand_count):
    npd, width = points.shape
    npts = float(npd * lax.axis_size(("dp", "sub")))
    dma = pltpu.SemaphoreType.DMA
    operands = (cand_rows, cand_count.reshape(1, ROUNDS), points)
    return pl.pallas_call(
        lambda *refs: kernel(npts, *refs),
        out_shape=jax.ShapeDtypeStruct((ROUNDS, npd), F32),
        in_specs=[
            pl.BlockSpec(memory_space=pl.ANY),
            pl.BlockSpec(memory_space=pl.ANY),
            pl.BlockSpec(memory_space=pl.ANY),
        ],
        out_specs=pl.BlockSpec(memory_space=pltpu.VMEM),
        scratch_shapes=[
            pltpu.SMEM((ROUNDS, SLOTS), jnp.int32),
            pltpu.SMEM((1, ROUNDS), jnp.int32),
            pltpu.VMEM((npd, width), jnp.bfloat16),
            pltpu.VMEM((SUBS, RAW, width), jnp.bfloat16),
            pltpu.VMEM((XS, ZS, BLK, width), jnp.bfloat16),
            pltpu.VMEM((SUBS, width, npd), jnp.bfloat16),
            pltpu.VMEM((SUBS // 2, BLK, 2 * npd), F32),
            pltpu.VMEM((SUBS, npd), F32),
            pltpu.VMEM((SUBS, ROUNDS, SUBS, npd), F32),
            pltpu.VMEM((ROUNDS, SUBS, npd), F32),
            pltpu.VMEM((ZS, 1, npd), F32),
            pltpu.VMEM((XS, 1, npd), F32),
            dma((3,)),
            dma,
            dma,
            dma,
            dma,
            dma((17,)),
            dma((4,)),
            dma,
            dma,
            dma((3,)),
            dma((4,)),
            dma((8,)),
            dma((8,)),
            dma,
            dma,
            dma,
            dma,
            dma,
            dma,
        ],
        compiler_params=pltpu.CompilerParams(
            collective_id=0, has_side_effects=True, vmem_limit_bytes=40 * 1024 * 1024
        ),
        cost_estimate=pl.CostEstimate(
            flops=2 * 1024 * 1024 * width, bytes_accessed=npd * width * 2, transcendentals=0
        ),
    )(*(pltpu.with_memory_space_constraint(value, pltpu.HBM) for value in operands))


def solution(mesh):
    in_specs = (P(("dp", "sub"), None), P(None, ("dp", "sub")), P(None, ("dp", "sub")))
    out_specs = P(None, ("dp", "sub"))
    return jax.shard_map(shards, mesh=mesh, in_specs=in_specs, out_specs=out_specs, check_vma=False)
```

```python
import jax
import jax.numpy as jnp
from jax import lax
from jax.experimental import pallas as pl
from jax.experimental.pallas import tpu as pltpu
from jax.sharding import PartitionSpec as P

ROUNDS = 3
SLOTS = 4
XS = 4
ZS = 16
YS = 4
SUBS = 8
RAW = 16
BLK = 8
SHARE = 2
MESH = pl.DeviceIdType.MESH
F32 = jnp.float32
INF = float("inf")


def kernel(
    npts,
    rows_in,
    counts_in,
    points_ref,
    out_ref,
    rows_ref,
    cnt_ref,
    raw,
    slots,
    cand,
    pall,
    mins,
    squares,
    line,
    near,
    zsum,
    xsum,
    local_sem,
    slots_send,
    slots_recv,
    z_block_send,
    x_send,
    z_block_recv,
    x_recv,
    far_send,
    far_z_send,
    far_recv,
    far_z_recv,
    pts_send,
    pts_recv,
    line_send,
    line_recv,
    z_send,
    z_recv,
    c_send,
    c_recv,
):
    dp = lax.axis_index("dp")
    sub = lax.axis_index("sub")
    x, z = lax.div(dp, ZS), lax.rem(dp, ZS)
    y, core = lax.div(sub, 2), lax.rem(sub, 2)
    npd, width = points_ref.shape

    def at_x(d):
        return (lax.rem(x + d, XS) * ZS + z, sub)

    def at_z(d):
        return (x * ZS + lax.rem(z + d, ZS), sub)

    def at_y(d):
        return (dp, lax.rem(y + d, YS) * 2 + core)

    other_core = (dp, y * 2 + (1 - core))
    z_to = {d: at_z(d % ZS) for d in (1, -1, 2, -2, 3, -3, 4, -4)}
    x_to = {d: at_x(d) for d in (1, 2, 3)}
    y_right, y_left = at_y(1), at_y(3)

    own_points = pltpu.make_async_copy(points_ref, raw, local_sem.at[0])
    own_points.start()
    own_rows = pltpu.make_async_copy(rows_in, rows_ref, local_sem.at[1])
    own_rows.start()
    own_counts = pltpu.make_async_copy(counts_in, cnt_ref, local_sem.at[2])
    own_counts.start()
    barrier = pltpu.get_barrier_semaphore()
    far_first = ((2, 0), (2, 1), (1, 0), (3, 0), (1, 1), (3, 1), (0, 1))
    members = [(dp, lax.rem(y + d, YS) * 2 + (1 - core if other else core)) for d, other in far_first]
    partners = [*z_to.values(), *x_to.values(), *members]
    for device in partners:
        pl.semaphore_signal(barrier, inc=1, device_id=device, device_id_type=MESH)

    row = lax.broadcasted_iota(jnp.int32, (RAW, npd), 0)
    lane = lax.broadcasted_iota(jnp.int32, (RAW, npd), 1)
    here = lax.broadcasted_iota(jnp.int32, (npd, npd), 0)
    there = lax.broadcasted_iota(jnp.int32, (npd, npd), 1)
    same_round = (here & (RAW - 1)) == ROUNDS * SLOTS + ((there & (RAW - 1)) >> 2)
    before = jnp.where(same_round & ((here >> 4) < (there >> 4)), 1.0, 0.0)
    itself = jnp.where(same_round & ((here >> 4) == (there >> 4)), 1.0, 0.0)
    slot = lane & (RAW - 1)
    slot_round = jnp.where(slot < ROUNDS * SLOTS, slot >> 2, -1)
    slot_index = (slot & (SLOTS - 1)).astype(F32)
    wanted = (SHARE * sub + (row & 1)).astype(F32)
    wanted_round = slot_round == (row >> 1)
    own_rows.wait()
    own_counts.wait()
    target = jnp.full((RAW, npd), -1, jnp.int32)
    counts = jnp.zeros((RAW, npd), F32)
    for r in range(ROUNDS):
        counts = jnp.where(row == ROUNDS * SLOTS + r, cnt_ref[0, r].astype(F32), counts)
        for i in range(SLOTS):
            target = jnp.where(row == r * SLOTS + i, rows_ref[r, i], target)
    pick = jnp.where(lane == target, 1.0, 0.0).astype(jnp.bfloat16)
    own_points.wait()
    mine = raw[...]
    block = jnp.dot(pick, mine, preferred_element_type=F32)
    slots[sub, :, :npd] = (block[:, :npd] + counts).astype(jnp.bfloat16)
    slots[sub, :, npd:] = block[:, npd:].astype(jnp.bfloat16)

    pl.semaphore_wait(barrier, len(partners))

    def remote(src, dst, send, recv, device):
        return pltpu.make_async_remote_copy(
            src_ref=src, dst_ref=dst, send_sem=send, recv_sem=recv, device_id=device, device_id_type=MESH
        )

    def to_sides(place, count, group):
        for d, column in ((1, 1), (3, 2)):
            src, dst = cand.at[0, pl.ds(place, count)], cand.at[column, pl.ds(place, count)]
            remote(src, dst, x_send, x_recv.at[group], x_to[d]).start()

    def to_far(place):
        remote(cand.at[0, place], cand.at[3, place], far_send, far_recv.at[place - 12], x_to[2]).start()

    def far_along_z(src, place, count, group, d, lanes=None):
        src, dst = cand.at[3, pl.ds(src, count)], cand.at[3, pl.ds(place, count)]
        if lanes is not None:
            part = pl.ds(lanes * (width // 2), width // 2)
            src, dst = src.at[:, :, part], dst.at[:, :, part]
        remote(src, dst, far_z_send, far_z_recv.at[group], z_to[d]).start()

    def along_z(src, place, d, lanes=None):
        if lanes is None:
            src, dst = cand.at[0, src], cand.at[0, place]
        else:
            part = pl.ds(lanes * (width // 2), width // 2)
            src, dst = cand.at[0, src, :, part], cand.at[0, place, :, part]
        remote(src, dst, z_block_send, z_block_recv.at[place + (lanes or 0)], z_to[d]).start()

    def z_arrived(*places):
        for place in places:
            wait_bytes(cand.at[0, place], z_block_recv.at[place])

    def wait_bytes(ref, sem):
        pltpu.make_async_copy(ref, ref, sem).wait()

    for device in members:
        remote(slots.at[sub], slots.at[sub], slots_send, slots_recv, device).start()
    pall[sub] = mine.T
    wait_bytes(slots.at[pl.ds(0, SUBS - 1)], slots_recv)
    flat = slots[...].reshape(SUBS * RAW, width)
    known = flat[:, :npd].astype(F32)
    offset = jnp.sum(known * before, axis=0, keepdims=True)
    count = jnp.sum(known * itself, axis=0, keepdims=True)
    choice = wanted_round & (slot_index < count) & (offset + slot_index == wanted)
    share = jnp.dot(jnp.where(choice, 1.0, 0.0).astype(jnp.bfloat16), flat, preferred_element_type=F32)
    cand[0, 13] = share[:BLK].astype(jnp.bfloat16)

    along_z(13, 12, 4)
    along_z(13, 14, -4)
    to_far(13)
    for place, d in ((1, 2), (2, -2), (5, 1), (9, -1)):
        along_z(13, place, d)
    to_sides(13, 1, 3)

    slot_right, slot_left, slot_far = (lax.rem(y + d, YS) * 2 + core for d in (1, 3, 2))
    top, low = pl.ds(0, width // 2), pl.ds(width // 2, width // 2)
    mine_at = pall.at[sub]
    pts_right = remote(mine_at, mine_at, pts_send.at[0], pts_recv.at[0], y_right)
    pts_left = remote(mine_at, mine_at, pts_send.at[1], pts_recv.at[1], y_left)
    pts_core = remote(mine_at, mine_at, pts_send.at[2], pts_recv.at[2], other_core)
    pts_right.start()
    pts_left.start()
    pts_core.start()

    z_arrived(12)
    to_far(12)
    along_z(12, 15, 4, 0)
    for place, d in ((7, 3), (0, 2), (4, 1), (8, -1)):
        along_z(12, place, d)
    z_arrived(14)
    to_far(14)
    along_z(14, 15, -4, 1)
    for place, d in ((11, -3), (3, -2), (10, -1), (6, 1)):
        along_z(14, place, d)
    to_sides(12, 1, 3)
    to_sides(14, 1, 3)

    for place in (12, 13, 14):
        wait_bytes(cand.at[3, place], far_recv.at[place - 12])
    far_along_z(12, 15, 1, 3, 4, 0)
    far_along_z(14, 15, 1, 3, -4, 1)
    far_along_z(12, 7, 1, 1, 3)
    far_along_z(14, 11, 1, 2, -3)
    far_along_z(12, 0, 2, 0, 2)
    far_along_z(13, 2, 2, 0, -2)
    far_along_z(12, 4, 3, 1, 1)
    far_along_z(12, 8, 3, 2, -1)

    pts_right.wait_recv()
    near_left = pall.at[slot_left]
    far_top = remote(near_left.at[top], near_left.at[top], pts_send.at[3], pts_recv.at[3], y_right)
    core_left = remote(near_left, near_left, pts_send.at[4], pts_recv.at[4], other_core)
    far_top.start()
    core_left.start()
    pts_left.wait_recv()
    near_right = pall.at[slot_right]
    far_low = remote(near_right.at[low], near_right.at[low], pts_send.at[5], pts_recv.at[5], y_left)
    core_right = remote(near_right, near_right, pts_send.at[6], pts_recv.at[6], other_core)
    far_low.start()
    core_right.start()

    for group in range(3):
        z_arrived(*range(4 * group, 4 * group + 4))
        to_sides(4 * group, 4, group)
    half_block = cand.at[0, 15, :, pl.ds(0, width // 2)]
    wait_bytes(half_block, z_block_recv.at[15])
    wait_bytes(half_block, z_block_recv.at[16])
    to_sides(15, 1, 3)

    far_top.wait_recv()
    far_low.wait_recv()
    far = pall.at[slot_far]
    core_far = remote(far, far, pts_send.at[7], pts_recv.at[7], other_core)
    core_far.start()

    def absorb(rows):
        blocks = rows.shape[0]
        half = jnp.zeros((blocks, BLK, npd), F32)
        for t in range(width // npd):
            piece = rows[:, :, t * npd : (t + 1) * npd].astype(F32)
            half = half + piece * piece
        half = 0.5 * jnp.sum(half, axis=2, keepdims=True)
        flat = rows.reshape(blocks * BLK, width)
        for j in range(SUBS // 2):
            group = jnp.concatenate([pall[2 * j], pall[2 * j + 1]], axis=1)
            dots = jnp.dot(flat, group, preferred_element_type=F32)
            best = jnp.min(half - dots.reshape(blocks, BLK, 2 * npd), axis=0)
            mins[j] = jnp.minimum(mins[j], best)

    def absorb_group(group, carry):
        wait_bytes(cand.at[pl.ds(1, 2), pl.ds(0, 4)], x_recv.at[group])
        absorb(cand[0:3, pl.ds(4 * group, 4)].reshape(3 * 4, BLK, width))
        return carry

    mins[...] = jnp.full(mins.shape, jnp.inf, F32)
    pts_core.wait_recv()
    core_left.wait_recv()
    core_right.wait_recv()
    core_far.wait_recv()
    for b in range(SUBS):
        wide = pall[b].astype(F32)
        squares[b : b + 1, :] = jnp.sum(wide * wide, axis=0, keepdims=True)
    lax.fori_loop(0, 4, absorb_group, 0)
    for group in range(4):
        wait_bytes(cand.at[3, pl.ds(0, 4 if group < 3 else 1)], far_z_recv.at[group])
    absorb(cand[3])

    for j in range(SUBS // 2):
        for r in range(ROUNDS):
            low_r = jnp.min(mins[j, r * SHARE : (r + 1) * SHARE, :], axis=0, keepdims=True)
            for h in range(2):
                line[sub, r, 2 * j + h : 2 * j + h + 1, :] = low_r[:, h * npd : (h + 1) * npd]

    for device in members:
        remote(line.at[sub], line.at[sub], line_send, line_recv, device).start()
    wait_bytes(line.at[pl.ds(0, SUBS - 1)], line_recv)

    lanes = lax.broadcasted_iota(jnp.int32, (1, npd), 1)
    least = None
    total = jnp.zeros((1, npd), F32)
    for r in range(ROUNDS):
        now = jnp.min(line[:, r], axis=0)
        least = now if least is None else jnp.minimum(least, now)
        dist = jnp.maximum(squares[...] + 2.0 * least, 0.0)
        near[r] = dist
        part = jnp.sum(jnp.sum(dist, axis=0, keepdims=True), axis=1, keepdims=True)
        total = jnp.where(lanes == r, part, total)

    zsum[0] = total

    for d in (8, 7, 9, 6, 10, 5, 11, 4, 12, 3, 13, 2, 14, 1, 15):
        remote(zsum.at[0], zsum.at[ZS - d], z_send, z_recv, at_z(d)).start()
    wait_bytes(zsum.at[pl.ds(0, ZS - 1)], z_recv)
    xsum[0] = jnp.sum(zsum[...], axis=0)
    for d in (1, 3, 2):
        remote(xsum.at[0], xsum.at[XS - d], c_send, c_recv, x_to[d]).start()
    wait_bytes(xsum.at[pl.ds(0, XS - 1)], c_recv)
    cost = jnp.sum(xsum[...], axis=0)
    for r in range(ROUNDS):
        cost_r = jnp.sum(jnp.where(lanes == r, cost, 0.0), axis=1, keepdims=True)
        out_ref[r : r + 1, :] = npts * near[r, pl.ds(sub, 1), :] / cost_r

    wait_bytes(slots.at[pl.ds(0, SUBS - 1)], slots_send)
    wait_bytes(cand.at[0, pl.ds(0, 15)], z_block_send)
    wait_bytes(cand.at[pl.ds(0, 2)], x_send)
    wait_bytes(cand.at[0, pl.ds(0, 3)], far_send)
    wait_bytes(cand.at[0, pl.ds(0, 13)], far_z_send)
    for copy in (pts_right, pts_left, pts_core, far_top, core_left, far_low, core_right, core_far):
        copy.wait_send()
    wait_bytes(line.at[pl.ds(0, SUBS - 1)], line_send)
    wait_bytes(zsum.at[pl.ds(0, ZS - 1)], z_send)
    wait_bytes(xsum.at[pl.ds(0, XS - 1)], c_send)


def shards(points, cand_rows, cand_count):
    npd, width = points.shape
    npts = float(npd * lax.axis_size(("dp", "sub")))
    dma = pltpu.SemaphoreType.DMA
    operands = (cand_rows, cand_count.reshape(1, ROUNDS), points)
    return pl.pallas_call(
        lambda *refs: kernel(npts, *refs),
        out_shape=jax.ShapeDtypeStruct((ROUNDS, npd), F32),
        in_specs=[
            pl.BlockSpec(memory_space=pl.ANY),
            pl.BlockSpec(memory_space=pl.ANY),
            pl.BlockSpec(memory_space=pl.ANY),
        ],
        out_specs=pl.BlockSpec(memory_space=pltpu.VMEM),
        scratch_shapes=[
            pltpu.SMEM((ROUNDS, SLOTS), jnp.int32),
            pltpu.SMEM((1, ROUNDS), jnp.int32),
            pltpu.VMEM((npd, width), jnp.bfloat16),
            pltpu.VMEM((SUBS, RAW, width), jnp.bfloat16),
            pltpu.VMEM((XS, ZS, BLK, width), jnp.bfloat16),
            pltpu.VMEM((SUBS, width, npd), jnp.bfloat16),
            pltpu.VMEM((SUBS // 2, BLK, 2 * npd), F32),
            pltpu.VMEM((SUBS, npd), F32),
            pltpu.VMEM((SUBS, ROUNDS, SUBS, npd), F32),
            pltpu.VMEM((ROUNDS, SUBS, npd), F32),
            pltpu.VMEM((ZS, 1, npd), F32),
            pltpu.VMEM((XS, 1, npd), F32),
            dma((3,)),
            dma,
            dma,
            dma,
            dma,
            dma((17,)),
            dma((4,)),
            dma,
            dma,
            dma((3,)),
            dma((4,)),
            dma((8,)),
            dma((8,)),
            dma,
            dma,
            dma,
            dma,
            dma,
            dma,
        ],
        compiler_params=pltpu.CompilerParams(
            collective_id=0, has_side_effects=True, vmem_limit_bytes=40 * 1024 * 1024
        ),
        cost_estimate=pl.CostEstimate(
            flops=2 * 1024 * 1024 * width, bytes_accessed=npd * width * 2, transcendentals=0
        ),
    )(*(pltpu.with_memory_space_constraint(value, pltpu.HBM) for value in operands))


def solution(mesh):
    in_specs = (P(("dp", "sub"), None), P(None, ("dp", "sub")), P(None, ("dp", "sub")))
    out_specs = P(None, ("dp", "sub"))
    return jax.shard_map(shards, mesh=mesh, in_specs=in_specs, out_specs=out_specs, check_vma=False)
```

```python
import jax
import jax.numpy as jnp
from jax import lax
from jax.experimental import pallas as pl
from jax.experimental.pallas import tpu as pltpu
from jax.sharding import PartitionSpec as P

ROUNDS = 3
SLOTS = 4
XS = 4
ZS = 16
YS = 4
SUBS = 8
RAW = 16
BLK = 8
SHARE = 2
MESH = pl.DeviceIdType.MESH
F32 = jnp.float32
INF = float("inf")


def kernel(
    npts,
    rows_in,
    counts_in,
    points_ref,
    out_ref,
    rows_ref,
    cnt_ref,
    raw,
    slots,
    cand,
    pall,
    mins,
    squares,
    line,
    near,
    zsum,
    xsum,
    local_sem,
    slots_send,
    slots_recv,
    z_block_send,
    x_send,
    z_block_recv,
    x_recv,
    far_send,
    far_z_send,
    far_recv,
    far_z_recv,
    pts_send,
    pts_recv,
    line_send,
    line_recv,
    z_send,
    z_recv,
    c_send,
    c_recv,
):
    dp = lax.axis_index("dp")
    sub = lax.axis_index("sub")
    x, z = lax.div(dp, ZS), lax.rem(dp, ZS)
    y, core = lax.div(sub, 2), lax.rem(sub, 2)
    npd, width = points_ref.shape

    def at_x(d):
        return (lax.rem(x + d, XS) * ZS + z, sub)

    def at_z(d):
        return (x * ZS + lax.rem(z + d, ZS), sub)

    def at_y(d):
        return (dp, lax.rem(y + d, YS) * 2 + core)

    other_core = (dp, y * 2 + (1 - core))
    z_to = {d: at_z(d % ZS) for d in (1, -1, 2, -2, 3, -3, 4, -4)}
    x_to = {d: at_x(d) for d in (1, 2, 3)}
    y_right, y_left = at_y(1), at_y(3)

    own_points = pltpu.make_async_copy(points_ref, raw, local_sem.at[0])
    own_points.start()
    own_rows = pltpu.make_async_copy(rows_in, rows_ref, local_sem.at[1])
    own_rows.start()
    own_counts = pltpu.make_async_copy(counts_in, cnt_ref, local_sem.at[2])
    own_counts.start()
    barrier = pltpu.get_barrier_semaphore()
    far_first = ((2, 0), (2, 1), (1, 0), (3, 0), (1, 1), (3, 1), (0, 1))
    members = [(dp, lax.rem(y + d, YS) * 2 + (1 - core if other else core)) for d, other in far_first]
    partners = [*z_to.values(), *x_to.values(), *members]
    for device in partners:
        pl.semaphore_signal(barrier, inc=1, device_id=device, device_id_type=MESH)

    row = lax.broadcasted_iota(jnp.int32, (RAW, npd), 0)
    lane = lax.broadcasted_iota(jnp.int32, (RAW, npd), 1)
    here = lax.broadcasted_iota(jnp.int32, (npd, npd), 0)
    there = lax.broadcasted_iota(jnp.int32, (npd, npd), 1)
    same_round = (here & (RAW - 1)) == ROUNDS * SLOTS + ((there & (RAW - 1)) >> 2)
    before = jnp.where(same_round & ((here >> 4) < (there >> 4)), 1.0, 0.0)
    itself = jnp.where(same_round & ((here >> 4) == (there >> 4)), 1.0, 0.0)
    slot = lane & (RAW - 1)
    slot_round = jnp.where(slot < ROUNDS * SLOTS, slot >> 2, -1)
    slot_index = (slot & (SLOTS - 1)).astype(F32)
    wanted = (SHARE * sub + (row & 1)).astype(F32)
    wanted_round = slot_round == (row >> 1)
    own_rows.wait()
    own_counts.wait()
    target = jnp.full((RAW, npd), -1, jnp.int32)
    counts = jnp.zeros((RAW, npd), F32)
    for r in range(ROUNDS):
        counts = jnp.where(row == ROUNDS * SLOTS + r, cnt_ref[0, r].astype(F32), counts)
        for i in range(SLOTS):
            target = jnp.where(row == r * SLOTS + i, rows_ref[r, i], target)
    pick = jnp.where(lane == target, 1.0, 0.0).astype(jnp.bfloat16)
    own_points.wait()
    mine = raw[...]
    block = jnp.dot(pick, mine, preferred_element_type=F32)
    slots[sub, :, :npd] = (block[:, :npd] + counts).astype(jnp.bfloat16)
    slots[sub, :, npd:] = block[:, npd:].astype(jnp.bfloat16)

    pl.semaphore_wait(barrier, len(partners))

    def remote(src, dst, send, recv, device):
        return pltpu.make_async_remote_copy(
            src_ref=src, dst_ref=dst, send_sem=send, recv_sem=recv, device_id=device, device_id_type=MESH
        )

    def to_sides(place, count, group):
        for d, column in ((1, 2), (3, 3)):
            src, dst = cand.at[0, pl.ds(place, count)], cand.at[column, pl.ds(place, count)]
            remote(src, dst, x_send, x_recv.at[group], x_to[d]).start()

    def to_far(place):
        remote(cand.at[0, place], cand.at[1, place], far_send, far_recv.at[place - 12], x_to[2]).start()

    def far_along_z(src, place, count, group, d, lanes=None):
        src, dst = cand.at[1, pl.ds(src, count)], cand.at[1, pl.ds(place, count)]
        if lanes is not None:
            part = pl.ds(lanes * (width // 2), width // 2)
            src, dst = src.at[:, :, part], dst.at[:, :, part]
        remote(src, dst, far_z_send, far_z_recv.at[group], z_to[d]).start()

    def along_z(src, place, d, lanes=None):
        if lanes is None:
            src, dst = cand.at[0, src], cand.at[0, place]
        else:
            part = pl.ds(lanes * (width // 2), width // 2)
            src, dst = cand.at[0, src, :, part], cand.at[0, place, :, part]
        remote(src, dst, z_block_send, z_block_recv.at[place + (lanes or 0)], z_to[d]).start()

    def z_arrived(*places):
        for place in places:
            wait_bytes(cand.at[0, place], z_block_recv.at[place])

    def wait_bytes(ref, sem):
        pltpu.make_async_copy(ref, ref, sem).wait()

    for device in members:
        remote(slots.at[sub], slots.at[sub], slots_send, slots_recv, device).start()
    pall[sub] = mine.T
    wait_bytes(slots.at[pl.ds(0, SUBS - 1)], slots_recv)
    flat = slots[...].reshape(SUBS * RAW, width)
    known = flat[:, :npd].astype(F32)
    offset = jnp.sum(known * before, axis=0, keepdims=True)
    count = jnp.sum(known * itself, axis=0, keepdims=True)
    choice = wanted_round & (slot_index < count) & (offset + slot_index == wanted)
    share = jnp.dot(jnp.where(choice, 1.0, 0.0).astype(jnp.bfloat16), flat, preferred_element_type=F32)
    cand[0, 13] = share[:BLK].astype(jnp.bfloat16)

    along_z(13, 12, 4)
    along_z(13, 14, -4)
    to_far(13)
    for place, d in ((1, 2), (2, -2), (5, 1), (9, -1)):
        along_z(13, place, d)
    to_sides(13, 1, 3)

    slot_right, slot_left, slot_far = (lax.rem(y + d, YS) * 2 + core for d in (1, 3, 2))
    top, low = pl.ds(0, width // 2), pl.ds(width // 2, width // 2)
    mine_at = pall.at[sub]
    pts_right = remote(mine_at, mine_at, pts_send.at[0], pts_recv.at[0], y_right)
    pts_left = remote(mine_at, mine_at, pts_send.at[1], pts_recv.at[1], y_left)
    pts_core = remote(mine_at, mine_at, pts_send.at[2], pts_recv.at[2], other_core)
    pts_right.start()
    pts_left.start()
    pts_core.start()

    z_arrived(12)
    to_far(12)
    along_z(12, 15, 4, 0)
    for place, d in ((7, 3), (0, 2), (4, 1), (8, -1)):
        along_z(12, place, d)
    z_arrived(14)
    to_far(14)
    along_z(14, 15, -4, 1)
    for place, d in ((11, -3), (3, -2), (10, -1), (6, 1)):
        along_z(14, place, d)
    to_sides(12, 1, 3)
    to_sides(14, 1, 3)

    pts_right.wait_recv()
    near_left = pall.at[slot_left]
    far_top = remote(near_left.at[top], near_left.at[top], pts_send.at[3], pts_recv.at[3], y_right)
    core_left = remote(near_left, near_left, pts_send.at[4], pts_recv.at[4], other_core)
    far_top.start()
    core_left.start()
    pts_left.wait_recv()
    near_right = pall.at[slot_right]
    far_low = remote(near_right.at[low], near_right.at[low], pts_send.at[5], pts_recv.at[5], y_left)
    core_right = remote(near_right, near_right, pts_send.at[6], pts_recv.at[6], other_core)
    far_low.start()
    core_right.start()
    for place in (12, 13, 14):
        wait_bytes(cand.at[1, place], far_recv.at[place - 12])
    far_along_z(12, 15, 1, 3, 4, 0)
    far_along_z(14, 15, 1, 3, -4, 1)
    far_along_z(12, 7, 1, 1, 3)
    far_along_z(14, 11, 1, 2, -3)
    far_along_z(12, 0, 2, 0, 2)
    far_along_z(13, 2, 2, 0, -2)
    far_along_z(12, 4, 3, 1, 1)
    far_along_z(12, 8, 3, 2, -1)

    for group in range(3):
        z_arrived(*range(4 * group, 4 * group + 4))
        to_sides(4 * group, 4, group)
    half_block = cand.at[0, 15, :, pl.ds(0, width // 2)]
    wait_bytes(half_block, z_block_recv.at[15])
    wait_bytes(half_block, z_block_recv.at[16])
    to_sides(15, 1, 3)

    far_top.wait_recv()
    far_low.wait_recv()
    far = pall.at[slot_far]
    core_far = remote(far, far, pts_send.at[7], pts_recv.at[7], other_core)
    core_far.start()

    def absorb(first, count):
        for group in range(first, first + count):
            wait_bytes(cand.at[pl.ds(2, 2), pl.ds(0, 4)], x_recv.at[group])
            wait_bytes(cand.at[1, pl.ds(0, 4 if group < 3 else 1)], far_z_recv.at[group])
        blocks = XS * 4 * count
        rows = cand[:, 4 * first : 4 * (first + count)].reshape(blocks, BLK, width)
        half = jnp.zeros((blocks, BLK, npd), F32)
        for t in range(width // npd):
            piece = rows[:, :, t * npd : (t + 1) * npd].astype(F32)
            half = half + piece * piece
        half = 0.5 * jnp.sum(half, axis=2, keepdims=True)
        flat = rows.reshape(blocks * BLK, width)
        for j in range(SUBS // 2):
            group = jnp.concatenate([pall[2 * j], pall[2 * j + 1]], axis=1)
            dots = jnp.dot(flat, group, preferred_element_type=F32)
            best = jnp.min(half - dots.reshape(blocks, BLK, 2 * npd), axis=0)
            mins[j] = best if first == 0 else jnp.minimum(mins[j], best)

    pts_core.wait_recv()
    core_left.wait_recv()
    core_right.wait_recv()
    core_far.wait_recv()
    for b in range(SUBS):
        wide = pall[b].astype(F32)
        squares[b : b + 1, :] = jnp.sum(wide * wide, axis=0, keepdims=True)
    absorb(0, 4)

    for j in range(SUBS // 2):
        for r in range(ROUNDS):
            low_r = jnp.min(mins[j, r * SHARE : (r + 1) * SHARE, :], axis=0, keepdims=True)
            for h in range(2):
                line[sub, r, 2 * j + h : 2 * j + h + 1, :] = low_r[:, h * npd : (h + 1) * npd]

    for device in members:
        remote(line.at[sub], line.at[sub], line_send, line_recv, device).start()
    wait_bytes(line.at[pl.ds(0, SUBS - 1)], line_recv)

    lanes = lax.broadcasted_iota(jnp.int32, (1, npd), 1)
    least = None
    total = jnp.zeros((1, npd), F32)
    for r in range(ROUNDS):
        now = jnp.min(line[:, r], axis=0)
        least = now if least is None else jnp.minimum(least, now)
        dist = jnp.maximum(squares[...] + 2.0 * least, 0.0)
        near[r] = dist
        part = jnp.sum(jnp.sum(dist, axis=0, keepdims=True), axis=1, keepdims=True)
        total = jnp.where(lanes == r, part, total)

    zsum[0] = total

    for d in (8, 7, 9, 6, 10, 5, 11, 4, 12, 3, 13, 2, 14, 1, 15):
        remote(zsum.at[0], zsum.at[ZS - d], z_send, z_recv, at_z(d)).start()
    wait_bytes(zsum.at[pl.ds(0, ZS - 1)], z_recv)
    xsum[0] = jnp.sum(zsum[...], axis=0)
    for d in (1, 3, 2):
        remote(xsum.at[0], xsum.at[XS - d], c_send, c_recv, x_to[d]).start()
    wait_bytes(xsum.at[pl.ds(0, XS - 1)], c_recv)
    cost = jnp.sum(xsum[...], axis=0)
    for r in range(ROUNDS):
        cost_r = jnp.sum(jnp.where(lanes == r, cost, 0.0), axis=1, keepdims=True)
        out_ref[r : r + 1, :] = npts * near[r, pl.ds(sub, 1), :] / cost_r

    wait_bytes(slots.at[pl.ds(0, SUBS - 1)], slots_send)
    wait_bytes(cand.at[0, pl.ds(0, 15)], z_block_send)
    wait_bytes(cand.at[pl.ds(0, 2)], x_send)
    wait_bytes(cand.at[0, pl.ds(0, 3)], far_send)
    wait_bytes(cand.at[0, pl.ds(0, 13)], far_z_send)
    for copy in (pts_right, pts_left, pts_core, far_top, core_left, far_low, core_right, core_far):
        copy.wait_send()
    wait_bytes(line.at[pl.ds(0, SUBS - 1)], line_send)
    wait_bytes(zsum.at[pl.ds(0, ZS - 1)], z_send)
    wait_bytes(xsum.at[pl.ds(0, XS - 1)], c_send)


def shards(points, cand_rows, cand_count):
    npd, width = points.shape
    npts = float(npd * lax.axis_size(("dp", "sub")))
    dma = pltpu.SemaphoreType.DMA
    operands = (cand_rows, cand_count.reshape(1, ROUNDS), points)
    return pl.pallas_call(
        lambda *refs: kernel(npts, *refs),
        out_shape=jax.ShapeDtypeStruct((ROUNDS, npd), F32),
        in_specs=[
            pl.BlockSpec(memory_space=pl.ANY),
            pl.BlockSpec(memory_space=pl.ANY),
            pl.BlockSpec(memory_space=pl.ANY),
        ],
        out_specs=pl.BlockSpec(memory_space=pltpu.VMEM),
        scratch_shapes=[
            pltpu.SMEM((ROUNDS, SLOTS), jnp.int32),
            pltpu.SMEM((1, ROUNDS), jnp.int32),
            pltpu.VMEM((npd, width), jnp.bfloat16),
            pltpu.VMEM((SUBS, RAW, width), jnp.bfloat16),
            pltpu.VMEM((XS, ZS, BLK, width), jnp.bfloat16),
            pltpu.VMEM((SUBS, width, npd), jnp.bfloat16),
            pltpu.VMEM((SUBS // 2, BLK, 2 * npd), F32),
            pltpu.VMEM((SUBS, npd), F32),
            pltpu.VMEM((SUBS, ROUNDS, SUBS, npd), F32),
            pltpu.VMEM((ROUNDS, SUBS, npd), F32),
            pltpu.VMEM((ZS, 1, npd), F32),
            pltpu.VMEM((XS, 1, npd), F32),
            dma((3,)),
            dma,
            dma,
            dma,
            dma,
            dma((17,)),
            dma((4,)),
            dma,
            dma,
            dma((3,)),
            dma((4,)),
            dma((8,)),
            dma((8,)),
            dma,
            dma,
            dma,
            dma,
            dma,
            dma,
        ],
        compiler_params=pltpu.CompilerParams(
            collective_id=0, has_side_effects=True, vmem_limit_bytes=40 * 1024 * 1024
        ),
        cost_estimate=pl.CostEstimate(
            flops=2 * 1024 * 1024 * width, bytes_accessed=npd * width * 2, transcendentals=0
        ),
    )(*(pltpu.with_memory_space_constraint(value, pltpu.HBM) for value in operands))


def solution(mesh):
    in_specs = (P(("dp", "sub"), None), P(None, ("dp", "sub")), P(None, ("dp", "sub")))
    out_specs = P(None, ("dp", "sub"))
    return jax.shard_map(shards, mesh=mesh, in_specs=in_specs, out_specs=out_specs, check_vma=False)
```

```python
import jax
import jax.numpy as jnp
from jax import lax
from jax.experimental import pallas as pl
from jax.experimental.pallas import tpu as pltpu
from jax.sharding import PartitionSpec as P

ROUNDS = 3
SLOTS = 4
XS = 4
ZS = 16
YS = 4
SUBS = 8
RAW = 16
BLK = 8
SHARE = 2
MESH = pl.DeviceIdType.MESH
F32 = jnp.float32
INF = float("inf")


def kernel(
    npts,
    rows_in,
    counts_in,
    points_ref,
    out_ref,
    rows_ref,
    cnt_ref,
    raw,
    slots,
    cand,
    pall,
    mins,
    squares,
    line,
    near,
    zsum,
    xsum,
    local_sem,
    slots_send,
    slots_recv,
    z_block_send,
    x_send,
    z_block_recv,
    x_recv,
    far_send,
    far_z_send,
    far_recv,
    far_z_recv,
    pts_send,
    pts_recv,
    line_send,
    line_recv,
    z_send,
    z_recv,
    c_send,
    c_recv,
):
    dp = lax.axis_index("dp")
    sub = lax.axis_index("sub")
    x, z = lax.div(dp, ZS), lax.rem(dp, ZS)
    y, core = lax.div(sub, 2), lax.rem(sub, 2)
    npd, width = points_ref.shape

    def at_x(d):
        return (lax.rem(x + d, XS) * ZS + z, sub)

    def at_z(d):
        return (x * ZS + lax.rem(z + d, ZS), sub)

    def at_y(d):
        return (dp, lax.rem(y + d, YS) * 2 + core)

    other_core = (dp, y * 2 + (1 - core))
    z_to = {d: at_z(d % ZS) for d in (1, -1, 2, -2, 3, -3, 4, -4)}
    x_to = {d: at_x(d) for d in (1, 2, 3)}
    y_right, y_left = at_y(1), at_y(3)

    own_points = pltpu.make_async_copy(points_ref, raw, local_sem.at[0])
    own_points.start()
    own_rows = pltpu.make_async_copy(rows_in, rows_ref, local_sem.at[1])
    own_rows.start()
    own_counts = pltpu.make_async_copy(counts_in, cnt_ref, local_sem.at[2])
    own_counts.start()
    barrier = pltpu.get_barrier_semaphore()
    far_first = ((2, 0), (2, 1), (1, 0), (3, 0), (1, 1), (3, 1), (0, 1))
    members = [(dp, lax.rem(y + d, YS) * 2 + (1 - core if other else core)) for d, other in far_first]
    partners = [*z_to.values(), *x_to.values(), *members]
    for device in partners:
        pl.semaphore_signal(barrier, inc=1, device_id=device, device_id_type=MESH)

    row = lax.broadcasted_iota(jnp.int32, (RAW, npd), 0)
    lane = lax.broadcasted_iota(jnp.int32, (RAW, npd), 1)
    here = lax.broadcasted_iota(jnp.int32, (npd, npd), 0)
    there = lax.broadcasted_iota(jnp.int32, (npd, npd), 1)
    same_round = (here & (RAW - 1)) == ROUNDS * SLOTS + ((there & (RAW - 1)) >> 2)
    before = jnp.where(same_round & ((here >> 4) < (there >> 4)), 1.0, 0.0)
    itself = jnp.where(same_round & ((here >> 4) == (there >> 4)), 1.0, 0.0)
    slot = lane & (RAW - 1)
    slot_round = jnp.where(slot < ROUNDS * SLOTS, slot >> 2, -1)
    slot_index = (slot & (SLOTS - 1)).astype(F32)
    wanted = (SHARE * sub + (row & 1)).astype(F32)
    wanted_round = slot_round == (row >> 1)
    own_rows.wait()
    own_counts.wait()
    target = jnp.full((RAW, npd), -1, jnp.int32)
    counts = jnp.zeros((RAW, npd), F32)
    for r in range(ROUNDS):
        counts = jnp.where(row == ROUNDS * SLOTS + r, cnt_ref[0, r].astype(F32), counts)
        for i in range(SLOTS):
            target = jnp.where(row == r * SLOTS + i, rows_ref[r, i], target)
    pick = jnp.where(lane == target, 1.0, 0.0).astype(jnp.bfloat16)
    own_points.wait()
    mine = raw[...]
    block = jnp.dot(pick, mine, preferred_element_type=F32)
    slots[sub, :, :npd] = (block[:, :npd] + counts).astype(jnp.bfloat16)
    slots[sub, :, npd:] = block[:, npd:].astype(jnp.bfloat16)

    pl.semaphore_wait(barrier, len(partners))

    def remote(src, dst, send, recv, device):
        return pltpu.make_async_remote_copy(
            src_ref=src, dst_ref=dst, send_sem=send, recv_sem=recv, device_id=device, device_id_type=MESH
        )

    def to_sides(place, count, group):
        for d, column in ((1, 2), (3, 3)):
            src, dst = cand.at[0, pl.ds(place, count)], cand.at[column, pl.ds(place, count)]
            remote(src, dst, x_send, x_recv.at[group], x_to[d]).start()

    def to_far(place):
        remote(cand.at[0, place], cand.at[1, place], far_send, far_recv.at[place - 12], x_to[2]).start()

    def far_along_z(src, place, count, group, d, lanes=None):
        src, dst = cand.at[1, pl.ds(src, count)], cand.at[1, pl.ds(place, count)]
        if lanes is not None:
            part = pl.ds(lanes * (width // 2), width // 2)
            src, dst = src.at[:, :, part], dst.at[:, :, part]
        remote(src, dst, far_z_send, far_z_recv.at[group], z_to[d]).start()

    def along_z(src, place, d, lanes=None):
        if lanes is None:
            src, dst = cand.at[0, src], cand.at[0, place]
        else:
            part = pl.ds(lanes * (width // 2), width // 2)
            src, dst = cand.at[0, src, :, part], cand.at[0, place, :, part]
        remote(src, dst, z_block_send, z_block_recv.at[place + (lanes or 0)], z_to[d]).start()

    def z_arrived(*places):
        for place in places:
            wait_bytes(cand.at[0, place], z_block_recv.at[place])

    def wait_bytes(ref, sem):
        pltpu.make_async_copy(ref, ref, sem).wait()

    for device in members:
        remote(slots.at[sub], slots.at[sub], slots_send, slots_recv, device).start()
    pall[sub] = mine.T
    wait_bytes(slots.at[pl.ds(0, SUBS - 1)], slots_recv)
    flat = slots[...].reshape(SUBS * RAW, width)
    known = flat[:, :npd].astype(F32)
    offset = jnp.sum(known * before, axis=0, keepdims=True)
    count = jnp.sum(known * itself, axis=0, keepdims=True)
    choice = wanted_round & (slot_index < count) & (offset + slot_index == wanted)
    share = jnp.dot(jnp.where(choice, 1.0, 0.0).astype(jnp.bfloat16), flat, preferred_element_type=F32)
    cand[0, 13] = share[:BLK].astype(jnp.bfloat16)

    along_z(13, 12, 4)
    along_z(13, 14, -4)
    to_far(13)
    for place, d in ((1, 2), (2, -2), (5, 1), (9, -1)):
        along_z(13, place, d)
    to_sides(13, 1, 3)

    slot_right, slot_left, slot_far = (lax.rem(y + d, YS) * 2 + core for d in (1, 3, 2))
    top, low = pl.ds(0, width // 2), pl.ds(width // 2, width // 2)
    mine_at = pall.at[sub]
    top_at, low_at = mine_at.at[top], mine_at.at[low]
    top_right = remote(top_at, top_at, pts_send.at[0], pts_recv.at[0], y_right)
    low_left = remote(low_at, low_at, pts_send.at[1], pts_recv.at[1], y_left)
    low_right = remote(low_at, low_at, pts_send.at[2], pts_recv.at[2], y_right)
    top_left = remote(top_at, top_at, pts_send.at[3], pts_recv.at[3], y_left)
    pts_core = remote(mine_at, mine_at, pts_send.at[4], pts_recv.at[4], other_core)
    for copy in (top_right, low_left, low_right, top_left, pts_core):
        copy.start()

    z_arrived(12)
    to_far(12)
    along_z(12, 15, 4, 0)
    for place, d in ((7, 3), (0, 2), (4, 1), (8, -1)):
        along_z(12, place, d)
    z_arrived(14)
    to_far(14)
    along_z(14, 15, -4, 1)
    for place, d in ((11, -3), (3, -2), (10, -1), (6, 1)):
        along_z(14, place, d)
    to_sides(12, 1, 3)
    to_sides(14, 1, 3)

    near_left, near_right, far = pall.at[slot_left], pall.at[slot_right], pall.at[slot_far]
    top_right.wait_recv()
    far_top = remote(near_left.at[top], near_left.at[top], pts_send.at[5], pts_recv.at[5], y_right)
    far_top.start()
    low_left.wait_recv()
    far_low = remote(near_right.at[low], near_right.at[low], pts_send.at[6], pts_recv.at[6], y_left)
    far_low.start()

    for place in (12, 13, 14):
        wait_bytes(cand.at[1, place], far_recv.at[place - 12])
    far_along_z(12, 15, 1, 3, 4, 0)
    far_along_z(14, 15, 1, 3, -4, 1)
    far_along_z(12, 7, 1, 1, 3)
    far_along_z(14, 11, 1, 2, -3)
    far_along_z(12, 0, 2, 0, 2)
    far_along_z(13, 2, 2, 0, -2)
    far_along_z(12, 4, 3, 1, 1)
    far_along_z(12, 8, 3, 2, -1)

    low_right.wait_recv()
    core_left = remote(near_left, near_left, pts_send.at[7], pts_recv.at[7], other_core)
    core_left.start()
    top_left.wait_recv()
    core_right = remote(near_right, near_right, pts_send.at[8], pts_recv.at[8], other_core)
    core_right.start()

    for group in range(3):
        z_arrived(*range(4 * group, 4 * group + 4))
        to_sides(4 * group, 4, group)
    half_block = cand.at[0, 15, :, pl.ds(0, width // 2)]
    wait_bytes(half_block, z_block_recv.at[15])
    wait_bytes(half_block, z_block_recv.at[16])
    to_sides(15, 1, 3)

    far_top.wait_recv()
    far_low.wait_recv()
    core_far = remote(far, far, pts_send.at[9], pts_recv.at[9], other_core)
    core_far.start()

    def absorb(first, count):
        for group in range(first, first + count):
            wait_bytes(cand.at[pl.ds(2, 2), pl.ds(0, 4)], x_recv.at[group])
            wait_bytes(cand.at[1, pl.ds(0, 4 if group < 3 else 1)], far_z_recv.at[group])
        blocks = XS * 4 * count
        rows = cand[:, 4 * first : 4 * (first + count)].reshape(blocks, BLK, width)
        half = jnp.zeros((blocks, BLK, npd), F32)
        for t in range(width // npd):
            piece = rows[:, :, t * npd : (t + 1) * npd].astype(F32)
            half = half + piece * piece
        half = 0.5 * jnp.sum(half, axis=2, keepdims=True)
        flat = rows.reshape(blocks * BLK, width)
        for j in range(SUBS // 2):
            group = jnp.concatenate([pall[2 * j], pall[2 * j + 1]], axis=1)
            dots = jnp.dot(flat, group, preferred_element_type=F32)
            best = jnp.min(half - dots.reshape(blocks, BLK, 2 * npd), axis=0)
            mins[j] = best if first == 0 else jnp.minimum(mins[j], best)

    pts_core.wait_recv()
    core_left.wait_recv()
    core_right.wait_recv()
    core_far.wait_recv()
    absorb(0, 3)
    for b in range(SUBS):
        wide = pall[b].astype(F32)
        squares[b : b + 1, :] = jnp.sum(wide * wide, axis=0, keepdims=True)
    absorb(3, 1)

    for j in range(SUBS // 2):
        for r in range(ROUNDS):
            low_r = jnp.min(mins[j, r * SHARE : (r + 1) * SHARE, :], axis=0, keepdims=True)
            for h in range(2):
                line[sub, r, 2 * j + h : 2 * j + h + 1, :] = low_r[:, h * npd : (h + 1) * npd]

    for device in members:
        remote(line.at[sub], line.at[sub], line_send, line_recv, device).start()
    wait_bytes(line.at[pl.ds(0, SUBS - 1)], line_recv)

    lanes = lax.broadcasted_iota(jnp.int32, (1, npd), 1)
    least = None
    total = jnp.zeros((1, npd), F32)
    for r in range(ROUNDS):
        now = jnp.min(line[:, r], axis=0)
        least = now if least is None else jnp.minimum(least, now)
        dist = jnp.maximum(squares[...] + 2.0 * least, 0.0)
        near[r] = dist
        part = jnp.sum(jnp.sum(dist, axis=0, keepdims=True), axis=1, keepdims=True)
        total = jnp.where(lanes == r, part, total)

    zsum[0] = total

    for d in (8, 7, 9, 6, 10, 5, 11, 4, 12, 3, 13, 2, 14, 1, 15):
        remote(zsum.at[0], zsum.at[ZS - d], z_send, z_recv, at_z(d)).start()
    wait_bytes(zsum.at[pl.ds(0, ZS - 1)], z_recv)
    xsum[0] = jnp.sum(zsum[...], axis=0)
    for d in (1, 3, 2):
        remote(xsum.at[0], xsum.at[XS - d], c_send, c_recv, x_to[d]).start()
    wait_bytes(xsum.at[pl.ds(0, XS - 1)], c_recv)
    cost = jnp.sum(xsum[...], axis=0)
    for r in range(ROUNDS):
        cost_r = jnp.sum(jnp.where(lanes == r, cost, 0.0), axis=1, keepdims=True)
        out_ref[r : r + 1, :] = npts * near[r, pl.ds(sub, 1), :] / cost_r

    wait_bytes(slots.at[pl.ds(0, SUBS - 1)], slots_send)
    wait_bytes(cand.at[0, pl.ds(0, 15)], z_block_send)
    wait_bytes(cand.at[pl.ds(0, 2)], x_send)
    wait_bytes(cand.at[0, pl.ds(0, 3)], far_send)
    wait_bytes(cand.at[0, pl.ds(0, 13)], far_z_send)
    for copy in (top_right, low_left, low_right, top_left, pts_core, far_top, far_low, core_left, core_right, core_far):
        copy.wait_send()
    wait_bytes(line.at[pl.ds(0, SUBS - 1)], line_send)
    wait_bytes(zsum.at[pl.ds(0, ZS - 1)], z_send)
    wait_bytes(xsum.at[pl.ds(0, XS - 1)], c_send)


def shards(points, cand_rows, cand_count):
    npd, width = points.shape
    npts = float(npd * lax.axis_size(("dp", "sub")))
    dma = pltpu.SemaphoreType.DMA
    operands = (cand_rows, cand_count.reshape(1, ROUNDS), points)
    return pl.pallas_call(
        lambda *refs: kernel(npts, *refs),
        out_shape=jax.ShapeDtypeStruct((ROUNDS, npd), F32),
        in_specs=[
            pl.BlockSpec(memory_space=pl.ANY),
            pl.BlockSpec(memory_space=pl.ANY),
            pl.BlockSpec(memory_space=pl.ANY),
        ],
        out_specs=pl.BlockSpec(memory_space=pltpu.VMEM),
        scratch_shapes=[
            pltpu.SMEM((ROUNDS, SLOTS), jnp.int32),
            pltpu.SMEM((1, ROUNDS), jnp.int32),
            pltpu.VMEM((npd, width), jnp.bfloat16),
            pltpu.VMEM((SUBS, RAW, width), jnp.bfloat16),
            pltpu.VMEM((XS, ZS, BLK, width), jnp.bfloat16),
            pltpu.VMEM((SUBS, width, npd), jnp.bfloat16),
            pltpu.VMEM((SUBS // 2, BLK, 2 * npd), F32),
            pltpu.VMEM((SUBS, npd), F32),
            pltpu.VMEM((SUBS, ROUNDS, SUBS, npd), F32),
            pltpu.VMEM((ROUNDS, SUBS, npd), F32),
            pltpu.VMEM((ZS, 1, npd), F32),
            pltpu.VMEM((XS, 1, npd), F32),
            dma((3,)),
            dma,
            dma,
            dma,
            dma,
            dma((17,)),
            dma((4,)),
            dma,
            dma,
            dma((3,)),
            dma((4,)),
            dma((10,)),
            dma((10,)),
            dma,
            dma,
            dma,
            dma,
            dma,
            dma,
        ],
        compiler_params=pltpu.CompilerParams(
            collective_id=0, has_side_effects=True, vmem_limit_bytes=40 * 1024 * 1024
        ),
        cost_estimate=pl.CostEstimate(
            flops=2 * 1024 * 1024 * width, bytes_accessed=npd * width * 2, transcendentals=0
        ),
    )(*(pltpu.with_memory_space_constraint(value, pltpu.HBM) for value in operands))


def solution(mesh):
    in_specs = (P(("dp", "sub"), None), P(None, ("dp", "sub")), P(None, ("dp", "sub")))
    out_specs = P(None, ("dp", "sub"))
    return jax.shard_map(shards, mesh=mesh, in_specs=in_specs, out_specs=out_specs, check_vma=False)
```

```python
import jax
import jax.numpy as jnp
from jax import lax
from jax.experimental import pallas as pl
from jax.experimental.pallas import tpu as pltpu
from jax.sharding import PartitionSpec as P

ROUNDS = 3
SLOTS = 4
XS = 4
ZS = 16
YS = 4
SUBS = 8
RAW = 16
BLK = 8
SHARE = 2
MESH = pl.DeviceIdType.MESH
F32 = jnp.float32
INF = float("inf")


def kernel(
    npts,
    rows_in,
    counts_in,
    points_ref,
    out_ref,
    rows_ref,
    cnt_ref,
    raw,
    slots,
    cand,
    pall,
    mins,
    squares,
    line,
    near,
    zsum,
    xsum,
    local_sem,
    slots_send,
    slots_recv,
    z_block_send,
    x_send,
    z_block_recv,
    x_recv,
    far_send,
    far_z_send,
    far_recv,
    far_z_recv,
    pts_send,
    pts_recv,
    line_send,
    line_recv,
    z_send,
    z_recv,
    c_send,
    c_recv,
):
    dp = lax.axis_index("dp")
    sub = lax.axis_index("sub")
    x, z = lax.div(dp, ZS), lax.rem(dp, ZS)
    y, core = lax.div(sub, 2), lax.rem(sub, 2)
    npd, width = points_ref.shape

    def at_x(d):
        return (lax.rem(x + d, XS) * ZS + z, sub)

    def at_z(d):
        return (x * ZS + lax.rem(z + d, ZS), sub)

    def at_y(d):
        return (dp, lax.rem(y + d, YS) * 2 + core)

    other_core = (dp, y * 2 + (1 - core))
    z_to = {d: at_z(d % ZS) for d in (1, -1, 2, -2, 3, -3, 4, -4)}
    x_to = {d: at_x(d) for d in (1, 2, 3)}
    y_right, y_left = at_y(1), at_y(3)

    own_points = pltpu.make_async_copy(points_ref, raw, local_sem.at[0])
    own_points.start()
    own_rows = pltpu.make_async_copy(rows_in, rows_ref, local_sem.at[1])
    own_rows.start()
    own_counts = pltpu.make_async_copy(counts_in, cnt_ref, local_sem.at[2])
    own_counts.start()
    barrier = pltpu.get_barrier_semaphore()
    far_first = ((2, 0), (2, 1), (1, 0), (3, 0), (1, 1), (3, 1), (0, 1))
    members = [(dp, lax.rem(y + d, YS) * 2 + (1 - core if other else core)) for d, other in far_first]
    partners = [*z_to.values(), *x_to.values(), *members]
    for device in partners:
        pl.semaphore_signal(barrier, inc=1, device_id=device, device_id_type=MESH)

    row = lax.broadcasted_iota(jnp.int32, (RAW, npd), 0)
    lane = lax.broadcasted_iota(jnp.int32, (RAW, npd), 1)
    here = lax.broadcasted_iota(jnp.int32, (npd, npd), 0)
    there = lax.broadcasted_iota(jnp.int32, (npd, npd), 1)
    same_round = (here & (RAW - 1)) == ROUNDS * SLOTS + ((there & (RAW - 1)) >> 2)
    before = jnp.where(same_round & ((here >> 4) < (there >> 4)), 1.0, 0.0)
    itself = jnp.where(same_round & ((here >> 4) == (there >> 4)), 1.0, 0.0)
    slot = lane & (RAW - 1)
    slot_round = jnp.where(slot < ROUNDS * SLOTS, slot >> 2, -1)
    slot_index = (slot & (SLOTS - 1)).astype(F32)
    wanted = (SHARE * sub + (row & 1)).astype(F32)
    wanted_round = slot_round == (row >> 1)
    own_rows.wait()
    own_counts.wait()
    target = jnp.full((RAW, npd), -1, jnp.int32)
    counts = jnp.zeros((RAW, npd), F32)
    for r in range(ROUNDS):
        counts = jnp.where(row == ROUNDS * SLOTS + r, cnt_ref[0, r].astype(F32), counts)
        for i in range(SLOTS):
            target = jnp.where(row == r * SLOTS + i, rows_ref[r, i], target)
    pick = jnp.where(lane == target, 1.0, 0.0).astype(jnp.bfloat16)
    own_points.wait()
    mine = raw[...]
    block = jnp.dot(pick, mine, preferred_element_type=F32)
    slots[sub, :, :npd] = (block[:, :npd] + counts).astype(jnp.bfloat16)
    slots[sub, :, npd:] = block[:, npd:].astype(jnp.bfloat16)

    pl.semaphore_wait(barrier, len(partners))

    def remote(src, dst, send, recv, device):
        return pltpu.make_async_remote_copy(
            src_ref=src, dst_ref=dst, send_sem=send, recv_sem=recv, device_id=device, device_id_type=MESH
        )

    def to_sides(place, count, group):
        for d, column in ((1, 2), (3, 3)):
            src, dst = cand.at[0, pl.ds(place, count)], cand.at[column, pl.ds(place, count)]
            remote(src, dst, x_send, x_recv.at[group], x_to[d]).start()

    def to_far(place):
        remote(cand.at[0, place], cand.at[1, place], far_send, far_recv.at[place - 12], x_to[2]).start()

    def far_along_z(src, place, count, group, d, lanes=None):
        src, dst = cand.at[1, pl.ds(src, count)], cand.at[1, pl.ds(place, count)]
        if lanes is not None:
            part = pl.ds(lanes * (width // 2), width // 2)
            src, dst = src.at[:, :, part], dst.at[:, :, part]
        remote(src, dst, far_z_send, far_z_recv.at[group], z_to[d]).start()

    def along_z(src, place, d, lanes=None):
        if lanes is None:
            src, dst = cand.at[0, src], cand.at[0, place]
        else:
            part = pl.ds(lanes * (width // 2), width // 2)
            src, dst = cand.at[0, src, :, part], cand.at[0, place, :, part]
        remote(src, dst, z_block_send, z_block_recv.at[place + (lanes or 0)], z_to[d]).start()

    def z_arrived(*places):
        for place in places:
            wait_bytes(cand.at[0, place], z_block_recv.at[place])

    def wait_bytes(ref, sem):
        pltpu.make_async_copy(ref, ref, sem).wait()

    for device in members:
        remote(slots.at[sub], slots.at[sub], slots_send, slots_recv, device).start()
    pall[sub] = mine.T
    mine_at = pall.at[sub]
    pts_core = remote(mine_at, mine_at, pts_send.at[2], pts_recv.at[2], other_core)
    pts_core.start()
    wait_bytes(slots.at[pl.ds(0, SUBS - 1)], slots_recv)
    flat = slots[...].reshape(SUBS * RAW, width)
    known = flat[:, :npd].astype(F32)
    offset = jnp.sum(known * before, axis=0, keepdims=True)
    count = jnp.sum(known * itself, axis=0, keepdims=True)
    choice = wanted_round & (slot_index < count) & (offset + slot_index == wanted)
    share = jnp.dot(jnp.where(choice, 1.0, 0.0).astype(jnp.bfloat16), flat, preferred_element_type=F32)
    cand[0, 13] = share[:BLK].astype(jnp.bfloat16)

    along_z(13, 12, 4)
    along_z(13, 14, -4)
    to_far(13)
    for place, d in ((1, 2), (2, -2), (5, 1), (9, -1)):
        along_z(13, place, d)
    to_sides(13, 1, 3)

    slot_right, slot_left, slot_far = (lax.rem(y + d, YS) * 2 + core for d in (1, 3, 2))
    top, low = pl.ds(0, width // 2), pl.ds(width // 2, width // 2)
    pts_right = remote(mine_at, mine_at, pts_send.at[0], pts_recv.at[0], y_right)
    pts_left = remote(mine_at, mine_at, pts_send.at[1], pts_recv.at[1], y_left)
    pts_right.start()
    pts_left.start()

    z_arrived(12)
    to_far(12)
    along_z(12, 15, 4, 0)
    for place, d in ((7, 3), (0, 2), (4, 1), (8, -1)):
        along_z(12, place, d)
    z_arrived(14)
    to_far(14)
    along_z(14, 15, -4, 1)
    for place, d in ((11, -3), (3, -2), (10, -1), (6, 1)):
        along_z(14, place, d)
    to_sides(12, 1, 3)
    to_sides(14, 1, 3)

    pts_right.wait_recv()
    near_left = pall.at[slot_left]
    far_top = remote(near_left.at[top], near_left.at[top], pts_send.at[3], pts_recv.at[3], y_right)
    core_left = remote(near_left, near_left, pts_send.at[4], pts_recv.at[4], other_core)
    far_top.start()
    core_left.start()
    pts_left.wait_recv()
    near_right = pall.at[slot_right]
    far_low = remote(near_right.at[low], near_right.at[low], pts_send.at[5], pts_recv.at[5], y_left)
    core_right = remote(near_right, near_right, pts_send.at[6], pts_recv.at[6], other_core)
    far_low.start()
    core_right.start()
    for place in (12, 13, 14):
        wait_bytes(cand.at[1, place], far_recv.at[place - 12])
    far_along_z(12, 15, 1, 3, 4, 0)
    far_along_z(14, 15, 1, 3, -4, 1)
    far_along_z(12, 7, 1, 1, 3)
    far_along_z(14, 11, 1, 2, -3)
    far_along_z(12, 0, 2, 0, 2)
    far_along_z(13, 2, 2, 0, -2)
    far_along_z(12, 4, 3, 1, 1)
    far_along_z(12, 8, 3, 2, -1)

    for group in range(3):
        z_arrived(*range(4 * group, 4 * group + 4))
        to_sides(4 * group, 4, group)
    half_block = cand.at[0, 15, :, pl.ds(0, width // 2)]
    wait_bytes(half_block, z_block_recv.at[15])
    wait_bytes(half_block, z_block_recv.at[16])
    to_sides(15, 1, 3)

    far_top.wait_recv()
    far_low.wait_recv()
    far = pall.at[slot_far]
    core_far = remote(far, far, pts_send.at[7], pts_recv.at[7], other_core)
    core_far.start()

    def absorb(first, count):
        for group in range(first, first + count):
            wait_bytes(cand.at[pl.ds(2, 2), pl.ds(0, 4)], x_recv.at[group])
            wait_bytes(cand.at[1, pl.ds(0, 4 if group < 3 else 1)], far_z_recv.at[group])
        blocks = XS * 4 * count
        rows = cand[:, 4 * first : 4 * (first + count)].reshape(blocks, BLK, width)
        half = jnp.zeros((blocks, BLK, npd), F32)
        for t in range(width // npd):
            piece = rows[:, :, t * npd : (t + 1) * npd].astype(F32)
            half = half + piece * piece
        half = 0.5 * jnp.sum(half, axis=2, keepdims=True)
        flat = rows.reshape(blocks * BLK, width)
        for j in range(SUBS // 2):
            group = jnp.concatenate([pall[2 * j], pall[2 * j + 1]], axis=1)
            dots = jnp.dot(flat, group, preferred_element_type=F32)
            best = jnp.min(half - dots.reshape(blocks, BLK, 2 * npd), axis=0)
            mins[j] = best if first == 0 else jnp.minimum(mins[j], best)

    pts_core.wait_recv()
    core_left.wait_recv()
    core_right.wait_recv()
    core_far.wait_recv()
    absorb(0, 3)
    for b in range(SUBS):
        wide = pall[b].astype(F32)
        squares[b : b + 1, :] = jnp.sum(wide * wide, axis=0, keepdims=True)
    absorb(3, 1)

    for j in range(SUBS // 2):
        for r in range(ROUNDS):
            low_r = jnp.min(mins[j, r * SHARE : (r + 1) * SHARE, :], axis=0, keepdims=True)
            for h in range(2):
                line[sub, r, 2 * j + h : 2 * j + h + 1, :] = low_r[:, h * npd : (h + 1) * npd]

    for device in members:
        remote(line.at[sub], line.at[sub], line_send, line_recv, device).start()
    wait_bytes(line.at[pl.ds(0, SUBS - 1)], line_recv)

    lanes = lax.broadcasted_iota(jnp.int32, (1, npd), 1)
    least = None
    total = jnp.zeros((1, npd), F32)
    for r in range(ROUNDS):
        now = jnp.min(line[:, r], axis=0)
        least = now if least is None else jnp.minimum(least, now)
        dist = jnp.maximum(squares[...] + 2.0 * least, 0.0)
        near[r] = dist
        part = jnp.sum(jnp.sum(dist, axis=0, keepdims=True), axis=1, keepdims=True)
        total = jnp.where(lanes == r, part, total)

    zsum[0] = total

    for d in (8, 7, 9, 6, 10, 5, 11, 4, 12, 3, 13, 2, 14, 1, 15):
        remote(zsum.at[0], zsum.at[ZS - d], z_send, z_recv, at_z(d)).start()
    wait_bytes(zsum.at[pl.ds(0, ZS - 1)], z_recv)
    xsum[0] = jnp.sum(zsum[...], axis=0)
    for d in (1, 3, 2):
        remote(xsum.at[0], xsum.at[XS - d], c_send, c_recv, x_to[d]).start()
    wait_bytes(xsum.at[pl.ds(0, XS - 1)], c_recv)
    cost = jnp.sum(xsum[...], axis=0)
    for r in range(ROUNDS):
        cost_r = jnp.sum(jnp.where(lanes == r, cost, 0.0), axis=1, keepdims=True)
        out_ref[r : r + 1, :] = npts * near[r, pl.ds(sub, 1), :] / cost_r

    wait_bytes(slots.at[pl.ds(0, SUBS - 1)], slots_send)
    wait_bytes(cand.at[0, pl.ds(0, 15)], z_block_send)
    wait_bytes(cand.at[pl.ds(0, 2)], x_send)
    wait_bytes(cand.at[0, pl.ds(0, 3)], far_send)
    wait_bytes(cand.at[0, pl.ds(0, 13)], far_z_send)
    for copy in (pts_right, pts_left, pts_core, far_top, core_left, far_low, core_right, core_far):
        copy.wait_send()
    wait_bytes(line.at[pl.ds(0, SUBS - 1)], line_send)
    wait_bytes(zsum.at[pl.ds(0, ZS - 1)], z_send)
    wait_bytes(xsum.at[pl.ds(0, XS - 1)], c_send)


def shards(points, cand_rows, cand_count):
    npd, width = points.shape
    npts = float(npd * lax.axis_size(("dp", "sub")))
    dma = pltpu.SemaphoreType.DMA
    operands = (cand_rows, cand_count.reshape(1, ROUNDS), points)
    return pl.pallas_call(
        lambda *refs: kernel(npts, *refs),
        out_shape=jax.ShapeDtypeStruct((ROUNDS, npd), F32),
        in_specs=[
            pl.BlockSpec(memory_space=pl.ANY),
            pl.BlockSpec(memory_space=pl.ANY),
            pl.BlockSpec(memory_space=pl.ANY),
        ],
        out_specs=pl.BlockSpec(memory_space=pltpu.VMEM),
        scratch_shapes=[
            pltpu.SMEM((ROUNDS, SLOTS), jnp.int32),
            pltpu.SMEM((1, ROUNDS), jnp.int32),
            pltpu.VMEM((npd, width), jnp.bfloat16),
            pltpu.VMEM((SUBS, RAW, width), jnp.bfloat16),
            pltpu.VMEM((XS, ZS, BLK, width), jnp.bfloat16),
            pltpu.VMEM((SUBS, width, npd), jnp.bfloat16),
            pltpu.VMEM((SUBS // 2, BLK, 2 * npd), F32),
            pltpu.VMEM((SUBS, npd), F32),
            pltpu.VMEM((SUBS, ROUNDS, SUBS, npd), F32),
            pltpu.VMEM((ROUNDS, SUBS, npd), F32),
            pltpu.VMEM((ZS, 1, npd), F32),
            pltpu.VMEM((XS, 1, npd), F32),
            dma((3,)),
            dma,
            dma,
            dma,
            dma,
            dma((17,)),
            dma((4,)),
            dma,
            dma,
            dma((3,)),
            dma((4,)),
            dma((8,)),
            dma((8,)),
            dma,
            dma,
            dma,
            dma,
            dma,
            dma,
        ],
        compiler_params=pltpu.CompilerParams(
            collective_id=0, has_side_effects=True, vmem_limit_bytes=40 * 1024 * 1024
        ),
        cost_estimate=pl.CostEstimate(
            flops=2 * 1024 * 1024 * width, bytes_accessed=npd * width * 2, transcendentals=0
        ),
    )(*(pltpu.with_memory_space_constraint(value, pltpu.HBM) for value in operands))


def solution(mesh):
    in_specs = (P(("dp", "sub"), None), P(None, ("dp", "sub")), P(None, ("dp", "sub")))
    out_specs = P(None, ("dp", "sub"))
    return jax.shard_map(shards, mesh=mesh, in_specs=in_specs, out_specs=out_specs, check_vma=False)
```

```python
import jax
import jax.numpy as jnp
from jax import lax
from jax.experimental import pallas as pl
from jax.experimental.pallas import tpu as pltpu
from jax.sharding import PartitionSpec as P

ROUNDS = 3
SLOTS = 4
XS = 4
ZS = 16
YS = 4
SUBS = 8
RAW = 16
BLK = 8
SHARE = 2
MESH = pl.DeviceIdType.MESH
F32 = jnp.float32
INF = float("inf")


def kernel(
    npts,
    rows_in,
    counts_in,
    points_ref,
    out_ref,
    rows_ref,
    cnt_ref,
    raw,
    slots,
    cand,
    pall,
    mins,
    squares,
    line,
    near,
    zsum,
    xsum,
    local_sem,
    slots_send,
    slots_recv,
    z_block_send,
    x_send,
    z_block_recv,
    x_recv,
    far_send,
    far_z_send,
    far_recv,
    far_z_recv,
    pts_send,
    pts_recv,
    line_send,
    line_recv,
    z_send,
    z_recv,
    c_send,
    c_recv,
):
    dp = lax.axis_index("dp")
    sub = lax.axis_index("sub")
    x, z = lax.div(dp, ZS), lax.rem(dp, ZS)
    y, core = lax.div(sub, 2), lax.rem(sub, 2)
    npd, width = points_ref.shape

    def at_x(d):
        return (lax.rem(x + d, XS) * ZS + z, sub)

    def at_z(d):
        return (x * ZS + lax.rem(z + d, ZS), sub)

    def at_y(d):
        return (dp, lax.rem(y + d, YS) * 2 + core)

    other_core = (dp, y * 2 + (1 - core))
    z_to = {d: at_z(d % ZS) for d in (1, -1, 2, -2, 3, -3, 4, -4)}
    x_to = {d: at_x(d) for d in (1, 2, 3)}
    y_right, y_left = at_y(1), at_y(3)

    own_points = pltpu.make_async_copy(points_ref, raw, local_sem.at[0])
    own_points.start()
    own_rows = pltpu.make_async_copy(rows_in, rows_ref, local_sem.at[1])
    own_rows.start()
    own_counts = pltpu.make_async_copy(counts_in, cnt_ref, local_sem.at[2])
    own_counts.start()
    barrier = pltpu.get_barrier_semaphore()
    far_first = ((2, 0), (2, 1), (1, 0), (3, 0), (1, 1), (3, 1), (0, 1))
    members = [(dp, lax.rem(y + d, YS) * 2 + (1 - core if other else core)) for d, other in far_first]
    partners = [*z_to.values(), *x_to.values(), *members]
    for device in partners:
        pl.semaphore_signal(barrier, inc=1, device_id=device, device_id_type=MESH)

    row = lax.broadcasted_iota(jnp.int32, (RAW, npd), 0)
    lane = lax.broadcasted_iota(jnp.int32, (RAW, npd), 1)
    here = lax.broadcasted_iota(jnp.int32, (npd, npd), 0)
    there = lax.broadcasted_iota(jnp.int32, (npd, npd), 1)
    same_round = (here & (RAW - 1)) == ROUNDS * SLOTS + ((there & (RAW - 1)) >> 2)
    before = jnp.where(same_round & ((here >> 4) < (there >> 4)), 1.0, 0.0)
    itself = jnp.where(same_round & ((here >> 4) == (there >> 4)), 1.0, 0.0)
    slot = lane & (RAW - 1)
    slot_round = jnp.where(slot < ROUNDS * SLOTS, slot >> 2, -1)
    slot_index = (slot & (SLOTS - 1)).astype(F32)
    wanted = (SHARE * sub + (row & 1)).astype(F32)
    wanted_round = slot_round == (row >> 1)
    own_rows.wait()
    own_counts.wait()
    target = jnp.full((RAW, npd), -1, jnp.int32)
    counts = jnp.zeros((RAW, npd), F32)
    for r in range(ROUNDS):
        counts = jnp.where(row == ROUNDS * SLOTS + r, cnt_ref[0, r].astype(F32), counts)
        for i in range(SLOTS):
            target = jnp.where(row == r * SLOTS + i, rows_ref[r, i], target)
    pick = jnp.where(lane == target, 1.0, 0.0).astype(jnp.bfloat16)
    own_points.wait()
    mine = raw[...]
    block = jnp.dot(pick, mine, preferred_element_type=F32)
    slots[sub, :, :npd] = (block[:, :npd] + counts).astype(jnp.bfloat16)
    slots[sub, :, npd:] = block[:, npd:].astype(jnp.bfloat16)

    pl.semaphore_wait(barrier, len(partners))

    def remote(src, dst, send, recv, device):
        return pltpu.make_async_remote_copy(
            src_ref=src, dst_ref=dst, send_sem=send, recv_sem=recv, device_id=device, device_id_type=MESH
        )

    def to_sides(place, count, group):
        for d, column in ((1, 2), (3, 3)):
            src, dst = cand.at[0, pl.ds(place, count)], cand.at[column, pl.ds(place, count)]
            remote(src, dst, x_send, x_recv.at[group], x_to[d]).start()

    def to_far(place):
        remote(cand.at[0, place], cand.at[1, place], far_send, far_recv.at[place - 12], x_to[2]).start()

    def far_along_z(src, place, count, group, d, lanes=None):
        src, dst = cand.at[1, pl.ds(src, count)], cand.at[1, pl.ds(place, count)]
        if lanes is not None:
            part = pl.ds(lanes * (width // 2), width // 2)
            src, dst = src.at[:, :, part], dst.at[:, :, part]
        remote(src, dst, far_z_send, far_z_recv.at[group], z_to[d]).start()

    def along_z(src, place, d, lanes=None):
        if lanes is None:
            src, dst = cand.at[0, src], cand.at[0, place]
        else:
            part = pl.ds(lanes * (width // 2), width // 2)
            src, dst = cand.at[0, src, :, part], cand.at[0, place, :, part]
        remote(src, dst, z_block_send, z_block_recv.at[place + (lanes or 0)], z_to[d]).start()

    def z_arrived(*places):
        for place in places:
            wait_bytes(cand.at[0, place], z_block_recv.at[place])

    def wait_bytes(ref, sem):
        pltpu.make_async_copy(ref, ref, sem).wait()

    for device in members:
        remote(slots.at[sub], slots.at[sub], slots_send, slots_recv, device).start()
    pall[sub] = mine.T
    wait_bytes(slots.at[pl.ds(0, SUBS - 1)], slots_recv)
    flat = slots[...].reshape(SUBS * RAW, width)
    known = flat[:, :npd].astype(F32)
    offset = jnp.sum(known * before, axis=0, keepdims=True)
    count = jnp.sum(known * itself, axis=0, keepdims=True)
    choice = wanted_round & (slot_index < count) & (offset + slot_index == wanted)
    share = jnp.dot(jnp.where(choice, 1.0, 0.0).astype(jnp.bfloat16), flat, preferred_element_type=F32)
    cand[0, 13] = share[:BLK].astype(jnp.bfloat16)

    along_z(13, 12, 4)
    along_z(13, 14, -4)
    to_far(13)
    for place, d in ((1, 2), (2, -2), (5, 1), (9, -1)):
        along_z(13, place, d)
    to_sides(13, 1, 3)

    z_arrived(12)
    to_far(12)
    along_z(12, 15, 4, 0)
    for place, d in ((7, 3), (0, 2), (4, 1), (8, -1)):
        along_z(12, place, d)
    z_arrived(14)
    to_far(14)
    along_z(14, 15, -4, 1)
    for place, d in ((11, -3), (3, -2), (10, -1), (6, 1)):
        along_z(14, place, d)
    to_sides(12, 1, 3)
    to_sides(14, 1, 3)

    slot_right, slot_left, slot_far = (lax.rem(y + d, YS) * 2 + core for d in (1, 3, 2))
    top, low = pl.ds(0, width // 2), pl.ds(width // 2, width // 2)
    mine_at = pall.at[sub]
    pts_right = remote(mine_at, mine_at, pts_send.at[0], pts_recv.at[0], y_right)
    pts_left = remote(mine_at, mine_at, pts_send.at[1], pts_recv.at[1], y_left)
    pts_core = remote(mine_at, mine_at, pts_send.at[2], pts_recv.at[2], other_core)
    pts_right.start()
    pts_left.start()
    pts_core.start()

    for place in (12, 13, 14):
        wait_bytes(cand.at[1, place], far_recv.at[place - 12])
    far_along_z(12, 15, 1, 3, 4, 0)
    far_along_z(14, 15, 1, 3, -4, 1)
    far_along_z(12, 7, 1, 1, 3)
    far_along_z(14, 11, 1, 2, -3)
    far_along_z(12, 0, 2, 0, 2)
    far_along_z(13, 2, 2, 0, -2)
    far_along_z(12, 4, 3, 1, 1)
    far_along_z(12, 8, 3, 2, -1)

    pts_right.wait_recv()
    near_left = pall.at[slot_left]
    far_top = remote(near_left.at[top], near_left.at[top], pts_send.at[3], pts_recv.at[3], y_right)
    core_left = remote(near_left, near_left, pts_send.at[4], pts_recv.at[4], other_core)
    far_top.start()
    core_left.start()
    pts_left.wait_recv()
    near_right = pall.at[slot_right]
    far_low = remote(near_right.at[low], near_right.at[low], pts_send.at[5], pts_recv.at[5], y_left)
    core_right = remote(near_right, near_right, pts_send.at[6], pts_recv.at[6], other_core)
    far_low.start()
    core_right.start()

    for group in range(3):
        z_arrived(*range(4 * group, 4 * group + 4))
        to_sides(4 * group, 4, group)
    half_block = cand.at[0, 15, :, pl.ds(0, width // 2)]
    wait_bytes(half_block, z_block_recv.at[15])
    wait_bytes(half_block, z_block_recv.at[16])
    to_sides(15, 1, 3)

    far_top.wait_recv()
    far_low.wait_recv()
    far = pall.at[slot_far]
    core_far = remote(far, far, pts_send.at[7], pts_recv.at[7], other_core)
    core_far.start()

    def absorb(first, count):
        for group in range(first, first + count):
            wait_bytes(cand.at[pl.ds(2, 2), pl.ds(0, 4)], x_recv.at[group])
            wait_bytes(cand.at[1, pl.ds(0, 4 if group < 3 else 1)], far_z_recv.at[group])
        blocks = XS * 4 * count
        rows = cand[:, 4 * first : 4 * (first + count)].reshape(blocks, BLK, width)
        half = jnp.zeros((blocks, BLK, npd), F32)
        for t in range(width // npd):
            piece = rows[:, :, t * npd : (t + 1) * npd].astype(F32)
            half = half + piece * piece
        half = 0.5 * jnp.sum(half, axis=2, keepdims=True)
        flat = rows.reshape(blocks * BLK, width)
        for j in range(SUBS // 2):
            group = jnp.concatenate([pall[2 * j], pall[2 * j + 1]], axis=1)
            dots = jnp.dot(flat, group, preferred_element_type=F32)
            best = jnp.min(half - dots.reshape(blocks, BLK, 2 * npd), axis=0)
            mins[j] = best if first == 0 else jnp.minimum(mins[j], best)

    pts_core.wait_recv()
    core_left.wait_recv()
    core_right.wait_recv()
    core_far.wait_recv()
    absorb(0, 3)
    for b in range(SUBS):
        wide = pall[b].astype(F32)
        squares[b : b + 1, :] = jnp.sum(wide * wide, axis=0, keepdims=True)
    absorb(3, 1)

    for j in range(SUBS // 2):
        for r in range(ROUNDS):
            low_r = jnp.min(mins[j, r * SHARE : (r + 1) * SHARE, :], axis=0, keepdims=True)
            for h in range(2):
                line[sub, r, 2 * j + h : 2 * j + h + 1, :] = low_r[:, h * npd : (h + 1) * npd]

    for device in members:
        remote(line.at[sub], line.at[sub], line_send, line_recv, device).start()
    wait_bytes(line.at[pl.ds(0, SUBS - 1)], line_recv)

    lanes = lax.broadcasted_iota(jnp.int32, (1, npd), 1)
    least = None
    total = jnp.zeros((1, npd), F32)
    for r in range(ROUNDS):
        now = jnp.min(line[:, r], axis=0)
        least = now if least is None else jnp.minimum(least, now)
        dist = jnp.maximum(squares[...] + 2.0 * least, 0.0)
        near[r] = dist
        part = jnp.sum(jnp.sum(dist, axis=0, keepdims=True), axis=1, keepdims=True)
        total = jnp.where(lanes == r, part, total)

    zsum[0] = total

    for d in (8, 7, 9, 6, 10, 5, 11, 4, 12, 3, 13, 2, 14, 1, 15):
        remote(zsum.at[0], zsum.at[ZS - d], z_send, z_recv, at_z(d)).start()
    wait_bytes(zsum.at[pl.ds(0, ZS - 1)], z_recv)
    xsum[0] = jnp.sum(zsum[...], axis=0)
    for d in (1, 3, 2):
        remote(xsum.at[0], xsum.at[XS - d], c_send, c_recv, x_to[d]).start()
    wait_bytes(xsum.at[pl.ds(0, XS - 1)], c_recv)
    cost = jnp.sum(xsum[...], axis=0)
    for r in range(ROUNDS):
        cost_r = jnp.sum(jnp.where(lanes == r, cost, 0.0), axis=1, keepdims=True)
        out_ref[r : r + 1, :] = npts * near[r, pl.ds(sub, 1), :] / cost_r

    wait_bytes(slots.at[pl.ds(0, SUBS - 1)], slots_send)
    wait_bytes(cand.at[0, pl.ds(0, 15)], z_block_send)
    wait_bytes(cand.at[pl.ds(0, 2)], x_send)
    wait_bytes(cand.at[0, pl.ds(0, 3)], far_send)
    wait_bytes(cand.at[0, pl.ds(0, 13)], far_z_send)
    for copy in (pts_right, pts_left, pts_core, far_top, core_left, far_low, core_right, core_far):
        copy.wait_send()
    wait_bytes(line.at[pl.ds(0, SUBS - 1)], line_send)
    wait_bytes(zsum.at[pl.ds(0, ZS - 1)], z_send)
    wait_bytes(xsum.at[pl.ds(0, XS - 1)], c_send)


def shards(points, cand_rows, cand_count):
    npd, width = points.shape
    npts = float(npd * lax.axis_size(("dp", "sub")))
    dma = pltpu.SemaphoreType.DMA
    operands = (cand_rows, cand_count.reshape(1, ROUNDS), points)
    return pl.pallas_call(
        lambda *refs: kernel(npts, *refs),
        out_shape=jax.ShapeDtypeStruct((ROUNDS, npd), F32),
        in_specs=[
            pl.BlockSpec(memory_space=pl.ANY),
            pl.BlockSpec(memory_space=pl.ANY),
            pl.BlockSpec(memory_space=pl.ANY),
        ],
        out_specs=pl.BlockSpec(memory_space=pltpu.VMEM),
        scratch_shapes=[
            pltpu.SMEM((ROUNDS, SLOTS), jnp.int32),
            pltpu.SMEM((1, ROUNDS), jnp.int32),
            pltpu.VMEM((npd, width), jnp.bfloat16),
            pltpu.VMEM((SUBS, RAW, width), jnp.bfloat16),
            pltpu.VMEM((XS, ZS, BLK, width), jnp.bfloat16),
            pltpu.VMEM((SUBS, width, npd), jnp.bfloat16),
            pltpu.VMEM((SUBS // 2, BLK, 2 * npd), F32),
            pltpu.VMEM((SUBS, npd), F32),
            pltpu.VMEM((SUBS, ROUNDS, SUBS, npd), F32),
            pltpu.VMEM((ROUNDS, SUBS, npd), F32),
            pltpu.VMEM((ZS, 1, npd), F32),
            pltpu.VMEM((XS, 1, npd), F32),
            dma((3,)),
            dma,
            dma,
            dma,
            dma,
            dma((17,)),
            dma((4,)),
            dma,
            dma,
            dma((3,)),
            dma((4,)),
            dma((8,)),
            dma((8,)),
            dma,
            dma,
            dma,
            dma,
            dma,
            dma,
        ],
        compiler_params=pltpu.CompilerParams(
            collective_id=0, has_side_effects=True, vmem_limit_bytes=40 * 1024 * 1024
        ),
        cost_estimate=pl.CostEstimate(
            flops=2 * 1024 * 1024 * width, bytes_accessed=npd * width * 2, transcendentals=0
        ),
    )(*(pltpu.with_memory_space_constraint(value, pltpu.HBM) for value in operands))


def solution(mesh):
    in_specs = (P(("dp", "sub"), None), P(None, ("dp", "sub")), P(None, ("dp", "sub")))
    out_specs = P(None, ("dp", "sub"))
    return jax.shard_map(shards, mesh=mesh, in_specs=in_specs, out_specs=out_specs, check_vma=False)
```

```python
import jax
import jax.numpy as jnp
from jax import lax
from jax.experimental import pallas as pl
from jax.experimental.pallas import tpu as pltpu
from jax.sharding import PartitionSpec as P

ROUNDS = 3
SLOTS = 4
XS = 4
ZS = 16
YS = 4
SUBS = 8
RAW = 16
BLK = 8
SHARE = 2
MESH = pl.DeviceIdType.MESH
F32 = jnp.float32
INF = float("inf")


def kernel(
    npts,
    rows_in,
    counts_in,
    points_ref,
    out_ref,
    rows_ref,
    cnt_ref,
    raw,
    slots,
    cand,
    pall,
    mins,
    squares,
    line,
    near,
    zsum,
    ysum,
    local_sem,
    slots_send,
    slots_recv,
    z_block_send,
    y_send,
    z_block_recv,
    y_recv,
    far_send,
    far_z_send,
    far_recv,
    far_z_recv,
    pts_send,
    pts_recv,
    line_send,
    line_recv,
    z_send,
    z_recv,
    c_send,
    c_recv,
):
    dp = lax.axis_index("dp")
    sub = lax.axis_index("sub")
    x, z = lax.div(dp, ZS), lax.rem(dp, ZS)
    y, core = lax.div(sub, 2), lax.rem(sub, 2)
    npd, width = points_ref.shape

    def at_x(d):
        return (lax.rem(x + d, XS) * ZS + z, sub)

    def at_z(d):
        return (x * ZS + lax.rem(z + d, ZS), sub)

    def at_y(d):
        return (dp, lax.rem(y + d, YS) * 2 + core)

    other_core = (dp, y * 2 + (1 - core))
    z_to = {d: at_z(d % ZS) for d in (1, -1, 2, -2, 3, -3, 4, -4)}
    y_to = {d: at_y(d) for d in (1, 2, 3)}
    me = x * 2 + core
    x_right, x_left = at_x(1), at_x(3)

    own_points = pltpu.make_async_copy(points_ref, raw, local_sem.at[0])
    own_points.start()
    own_rows = pltpu.make_async_copy(rows_in, rows_ref, local_sem.at[1])
    own_rows.start()
    own_counts = pltpu.make_async_copy(counts_in, cnt_ref, local_sem.at[2])
    own_counts.start()
    barrier = pltpu.get_barrier_semaphore()
    far_first = ((2, 0), (2, 1), (1, 0), (3, 0), (1, 1), (3, 1), (0, 1))
    y_line = [(dp, lax.rem(y + d, YS) * 2 + (1 - core if other else core)) for d, other in far_first]
    x_line = [(lax.rem(x + d, XS) * ZS + z, y * 2 + (1 - core if other else core)) for d, other in far_first]
    partners = [*z_to.values(), *y_line, *x_line[:-1]]
    for device in partners:
        pl.semaphore_signal(barrier, inc=1, device_id=device, device_id_type=MESH)

    row = lax.broadcasted_iota(jnp.int32, (RAW, npd), 0)
    lane = lax.broadcasted_iota(jnp.int32, (RAW, npd), 1)
    here = lax.broadcasted_iota(jnp.int32, (npd, npd), 0)
    there = lax.broadcasted_iota(jnp.int32, (npd, npd), 1)
    same_round = (here & (RAW - 1)) == ROUNDS * SLOTS + ((there & (RAW - 1)) >> 2)
    before = jnp.where(same_round & ((here >> 4) < (there >> 4)), 1.0, 0.0)
    itself = jnp.where(same_round & ((here >> 4) == (there >> 4)), 1.0, 0.0)
    slot = lane & (RAW - 1)
    slot_round = jnp.where(slot < ROUNDS * SLOTS, slot >> 2, -1)
    slot_index = (slot & (SLOTS - 1)).astype(F32)
    wanted = (SHARE * sub + (row & 1)).astype(F32)
    wanted_round = slot_round == (row >> 1)
    own_rows.wait()
    own_counts.wait()
    target = jnp.full((RAW, npd), -1, jnp.int32)
    counts = jnp.zeros((RAW, npd), F32)
    for r in range(ROUNDS):
        counts = jnp.where(row == ROUNDS * SLOTS + r, cnt_ref[0, r].astype(F32), counts)
        for i in range(SLOTS):
            target = jnp.where(row == r * SLOTS + i, rows_ref[r, i], target)
    pick = jnp.where(lane == target, 1.0, 0.0).astype(jnp.bfloat16)
    own_points.wait()
    mine = raw[...]
    block = jnp.dot(pick, mine, preferred_element_type=F32)
    slots[sub, :, :npd] = (block[:, :npd] + counts).astype(jnp.bfloat16)
    slots[sub, :, npd:] = block[:, npd:].astype(jnp.bfloat16)

    pl.semaphore_wait(barrier, len(partners))

    def remote(src, dst, send, recv, device):
        return pltpu.make_async_remote_copy(
            src_ref=src, dst_ref=dst, send_sem=send, recv_sem=recv, device_id=device, device_id_type=MESH
        )

    def to_sides(place, count, group):
        for d, column in ((1, 2), (3, 3)):
            src, dst = cand.at[0, pl.ds(place, count)], cand.at[column, pl.ds(place, count)]
            remote(src, dst, y_send, y_recv.at[group], y_to[d]).start()

    def to_far(place):
        remote(cand.at[0, place], cand.at[1, place], far_send, far_recv.at[place - 12], y_to[2]).start()

    def far_along_z(src, place, count, group, d, lanes=None):
        src, dst = cand.at[1, pl.ds(src, count)], cand.at[1, pl.ds(place, count)]
        if lanes is not None:
            part = pl.ds(lanes * (width // 2), width // 2)
            src, dst = src.at[:, :, part], dst.at[:, :, part]
        remote(src, dst, far_z_send, far_z_recv.at[group], z_to[d]).start()

    def along_z(src, place, d, lanes=None):
        if lanes is None:
            src, dst = cand.at[0, src], cand.at[0, place]
        else:
            part = pl.ds(lanes * (width // 2), width // 2)
            src, dst = cand.at[0, src, :, part], cand.at[0, place, :, part]
        remote(src, dst, z_block_send, z_block_recv.at[place + (lanes or 0)], z_to[d]).start()

    def z_arrived(*places):
        for place in places:
            wait_bytes(cand.at[0, place], z_block_recv.at[place])

    def wait_bytes(ref, sem):
        pltpu.make_async_copy(ref, ref, sem).wait()

    for device in y_line:
        remote(slots.at[sub], slots.at[sub], slots_send, slots_recv, device).start()
    pall[me] = mine.T
    slot_right, slot_left, slot_far = (lax.rem(x + d, XS) * 2 + core for d in (1, 3, 2))
    top, low = pl.ds(0, width // 2), pl.ds(width // 2, width // 2)
    mine_at = pall.at[me]
    pts_right = remote(mine_at, mine_at, pts_send.at[0], pts_recv.at[0], x_right)
    pts_left = remote(mine_at, mine_at, pts_send.at[1], pts_recv.at[1], x_left)
    pts_core = remote(mine_at, mine_at, pts_send.at[2], pts_recv.at[2], other_core)
    pts_right.start()
    pts_left.start()
    pts_core.start()

    wait_bytes(slots.at[pl.ds(0, SUBS - 1)], slots_recv)
    flat = slots[...].reshape(SUBS * RAW, width)
    known = flat[:, :npd].astype(F32)
    offset = jnp.sum(known * before, axis=0, keepdims=True)
    count = jnp.sum(known * itself, axis=0, keepdims=True)
    choice = wanted_round & (slot_index < count) & (offset + slot_index == wanted)
    share = jnp.dot(jnp.where(choice, 1.0, 0.0).astype(jnp.bfloat16), flat, preferred_element_type=F32)
    cand[0, 13] = share[:BLK].astype(jnp.bfloat16)

    along_z(13, 12, 4)
    along_z(13, 14, -4)
    to_far(13)
    for place, d in ((1, 2), (2, -2), (5, 1), (9, -1)):
        along_z(13, place, d)
    to_sides(13, 1, 3)

    z_arrived(12)
    to_far(12)
    along_z(12, 15, 4, 0)
    for place, d in ((7, 3), (0, 2), (4, 1), (8, -1)):
        along_z(12, place, d)
    z_arrived(14)
    to_far(14)
    along_z(14, 15, -4, 1)
    for place, d in ((11, -3), (3, -2), (10, -1), (6, 1)):
        along_z(14, place, d)
    to_sides(12, 1, 3)
    to_sides(14, 1, 3)

    pts_right.wait_recv()
    near_left = pall.at[slot_left]
    far_top = remote(near_left.at[top], near_left.at[top], pts_send.at[3], pts_recv.at[3], x_right)
    core_left = remote(near_left, near_left, pts_send.at[4], pts_recv.at[4], other_core)
    far_top.start()
    core_left.start()
    pts_left.wait_recv()
    near_right = pall.at[slot_right]
    far_low = remote(near_right.at[low], near_right.at[low], pts_send.at[5], pts_recv.at[5], x_left)
    core_right = remote(near_right, near_right, pts_send.at[6], pts_recv.at[6], other_core)
    far_low.start()
    core_right.start()
    for place in (12, 13, 14):
        wait_bytes(cand.at[1, place], far_recv.at[place - 12])
    far_along_z(12, 15, 1, 3, 4, 0)
    far_along_z(14, 15, 1, 3, -4, 1)
    far_along_z(12, 7, 1, 1, 3)
    far_along_z(14, 11, 1, 2, -3)
    far_along_z(12, 0, 2, 0, 2)
    far_along_z(13, 2, 2, 0, -2)
    far_along_z(12, 4, 3, 1, 1)
    far_along_z(12, 8, 3, 2, -1)

    for group in range(3):
        z_arrived(*range(4 * group, 4 * group + 4))
        to_sides(4 * group, 4, group)
    half_block = cand.at[0, 15, :, pl.ds(0, width // 2)]
    wait_bytes(half_block, z_block_recv.at[15])
    wait_bytes(half_block, z_block_recv.at[16])
    to_sides(15, 1, 3)

    far_top.wait_recv()
    far_low.wait_recv()
    far = pall.at[slot_far]
    core_far = remote(far, far, pts_send.at[7], pts_recv.at[7], other_core)
    core_far.start()

    def absorb(first, count):
        for group in range(first, first + count):
            wait_bytes(cand.at[pl.ds(2, 2), pl.ds(0, 4)], y_recv.at[group])
            wait_bytes(cand.at[1, pl.ds(0, 4 if group < 3 else 1)], far_z_recv.at[group])
        blocks = XS * 4 * count
        rows = cand[:, 4 * first : 4 * (first + count)].reshape(blocks, BLK, width)
        half = jnp.zeros((blocks, BLK, npd), F32)
        for t in range(width // npd):
            piece = rows[:, :, t * npd : (t + 1) * npd].astype(F32)
            half = half + piece * piece
        half = 0.5 * jnp.sum(half, axis=2, keepdims=True)
        flat = rows.reshape(blocks * BLK, width)
        for j in range(SUBS // 2):
            group = jnp.concatenate([pall[2 * j], pall[2 * j + 1]], axis=1)
            dots = jnp.dot(flat, group, preferred_element_type=F32)
            best = jnp.min(half - dots.reshape(blocks, BLK, 2 * npd), axis=0)
            mins[j] = best if first == 0 else jnp.minimum(mins[j], best)

    pts_core.wait_recv()
    core_left.wait_recv()
    core_right.wait_recv()
    core_far.wait_recv()
    absorb(0, 3)
    for b in range(SUBS):
        wide = pall[b].astype(F32)
        squares[b : b + 1, :] = jnp.sum(wide * wide, axis=0, keepdims=True)
    absorb(3, 1)

    for j in range(SUBS // 2):
        for r in range(ROUNDS):
            low_r = jnp.min(mins[j, r * SHARE : (r + 1) * SHARE, :], axis=0, keepdims=True)
            for h in range(2):
                line[me, r, 2 * j + h : 2 * j + h + 1, :] = low_r[:, h * npd : (h + 1) * npd]

    for device in x_line:
        remote(line.at[me], line.at[me], line_send, line_recv, device).start()
    wait_bytes(line.at[pl.ds(0, SUBS - 1)], line_recv)

    lanes = lax.broadcasted_iota(jnp.int32, (1, npd), 1)
    least = None
    total = jnp.zeros((1, npd), F32)
    for r in range(ROUNDS):
        now = jnp.min(line[:, r], axis=0)
        least = now if least is None else jnp.minimum(least, now)
        dist = jnp.maximum(squares[...] + 2.0 * least, 0.0)
        near[r] = dist
        part = jnp.sum(jnp.sum(dist, axis=0, keepdims=True), axis=1, keepdims=True)
        total = jnp.where(lanes == r, part, total)

    zsum[0] = total

    for d in (8, 7, 9, 6, 10, 5, 11, 4, 12, 3, 13, 2, 14, 1, 15):
        remote(zsum.at[0], zsum.at[ZS - d], z_send, z_recv, at_z(d)).start()
    wait_bytes(zsum.at[pl.ds(0, ZS - 1)], z_recv)
    ysum[0] = jnp.sum(zsum[...], axis=0)
    for d in (1, 3, 2):
        remote(ysum.at[0], ysum.at[XS - d], c_send, c_recv, y_to[d]).start()
    wait_bytes(ysum.at[pl.ds(0, XS - 1)], c_recv)
    cost = jnp.sum(ysum[...], axis=0)
    for r in range(ROUNDS):
        cost_r = jnp.sum(jnp.where(lanes == r, cost, 0.0), axis=1, keepdims=True)
        out_ref[r : r + 1, :] = npts * near[r, pl.ds(me, 1), :] / cost_r

    wait_bytes(slots.at[pl.ds(0, SUBS - 1)], slots_send)
    wait_bytes(cand.at[0, pl.ds(0, 15)], z_block_send)
    wait_bytes(cand.at[pl.ds(0, 2)], y_send)
    wait_bytes(cand.at[0, pl.ds(0, 3)], far_send)
    wait_bytes(cand.at[0, pl.ds(0, 13)], far_z_send)
    for copy in (pts_right, pts_left, pts_core, far_top, core_left, far_low, core_right, core_far):
        copy.wait_send()
    wait_bytes(line.at[pl.ds(0, SUBS - 1)], line_send)
    wait_bytes(zsum.at[pl.ds(0, ZS - 1)], z_send)
    wait_bytes(ysum.at[pl.ds(0, XS - 1)], c_send)


def shards(points, cand_rows, cand_count):
    npd, width = points.shape
    npts = float(npd * lax.axis_size(("dp", "sub")))
    dma = pltpu.SemaphoreType.DMA
    operands = (cand_rows, cand_count.reshape(1, ROUNDS), points)
    return pl.pallas_call(
        lambda *refs: kernel(npts, *refs),
        out_shape=jax.ShapeDtypeStruct((ROUNDS, npd), F32),
        in_specs=[
            pl.BlockSpec(memory_space=pl.ANY),
            pl.BlockSpec(memory_space=pl.ANY),
            pl.BlockSpec(memory_space=pl.ANY),
        ],
        out_specs=pl.BlockSpec(memory_space=pltpu.VMEM),
        scratch_shapes=[
            pltpu.SMEM((ROUNDS, SLOTS), jnp.int32),
            pltpu.SMEM((1, ROUNDS), jnp.int32),
            pltpu.VMEM((npd, width), jnp.bfloat16),
            pltpu.VMEM((SUBS, RAW, width), jnp.bfloat16),
            pltpu.VMEM((XS, ZS, BLK, width), jnp.bfloat16),
            pltpu.VMEM((SUBS, width, npd), jnp.bfloat16),
            pltpu.VMEM((SUBS // 2, BLK, 2 * npd), F32),
            pltpu.VMEM((SUBS, npd), F32),
            pltpu.VMEM((SUBS, ROUNDS, SUBS, npd), F32),
            pltpu.VMEM((ROUNDS, SUBS, npd), F32),
            pltpu.VMEM((ZS, 1, npd), F32),
            pltpu.VMEM((XS, 1, npd), F32),
            dma((3,)),
            dma,
            dma,
            dma,
            dma,
            dma((17,)),
            dma((4,)),
            dma,
            dma,
            dma((3,)),
            dma((4,)),
            dma((8,)),
            dma((8,)),
            dma,
            dma,
            dma,
            dma,
            dma,
            dma,
        ],
        compiler_params=pltpu.CompilerParams(
            collective_id=0, has_side_effects=True, vmem_limit_bytes=40 * 1024 * 1024
        ),
        cost_estimate=pl.CostEstimate(
            flops=2 * 1024 * 1024 * width, bytes_accessed=npd * width * 2, transcendentals=0
        ),
    )(*(pltpu.with_memory_space_constraint(value, pltpu.HBM) for value in operands))


def solution(mesh):
    in_specs = (P(("dp", "sub"), None), P(None, ("dp", "sub")), P(None, ("dp", "sub")))
    out_specs = P(None, ("dp", "sub"))
    return jax.shard_map(shards, mesh=mesh, in_specs=in_specs, out_specs=out_specs, check_vma=False)
```

```python
import jax
import jax.numpy as jnp
from jax import lax
from jax.experimental import pallas as pl
from jax.experimental.pallas import tpu as pltpu
from jax.sharding import PartitionSpec as P

ROUNDS = 3
SLOTS = 4
XS = 4
ZS = 16
YS = 4
SUBS = 8
RAW = 16
BLK = 8
SHARE = 2
MESH = pl.DeviceIdType.MESH
F32 = jnp.float32
INF = float("inf")


def kernel(
    npts,
    rows_in,
    counts_in,
    points_ref,
    out_ref,
    rows_ref,
    cnt_ref,
    raw,
    slots,
    cand,
    pall,
    mins,
    squares,
    line,
    near,
    zsum,
    ysum,
    local_sem,
    slots_send,
    slots_recv,
    z_block_send,
    y_send,
    z_block_recv,
    y_recv,
    far_send,
    far_z_send,
    far_recv,
    far_z_recv,
    pts_send,
    pts_recv,
    line_send,
    line_recv,
    z_send,
    z_recv,
    c_send,
    c_recv,
):
    dp = lax.axis_index("dp")
    sub = lax.axis_index("sub")
    x, z = lax.div(dp, ZS), lax.rem(dp, ZS)
    y, core = lax.div(sub, 2), lax.rem(sub, 2)
    npd, width = points_ref.shape

    def at_x(d):
        return (lax.rem(x + d, XS) * ZS + z, sub)

    def at_z(d):
        return (x * ZS + lax.rem(z + d, ZS), sub)

    def at_y(d):
        return (dp, lax.rem(y + d, YS) * 2 + core)

    other_core = (dp, y * 2 + (1 - core))
    z_to = {d: at_z(d % ZS) for d in (1, -1, 2, -2, 3, -3, 4, -4)}
    y_to = {d: at_y(d) for d in (1, 2, 3)}
    me = x * 2 + core
    x_right, x_left = at_x(1), at_x(3)

    own_points = pltpu.make_async_copy(points_ref, raw, local_sem.at[0])
    own_points.start()
    own_rows = pltpu.make_async_copy(rows_in, rows_ref, local_sem.at[1])
    own_rows.start()
    own_counts = pltpu.make_async_copy(counts_in, cnt_ref, local_sem.at[2])
    own_counts.start()
    barrier = pltpu.get_barrier_semaphore()
    far_first = ((2, 0), (2, 1), (1, 0), (3, 0), (1, 1), (3, 1), (0, 1))
    y_line = [(dp, lax.rem(y + d, YS) * 2 + (1 - core if other else core)) for d, other in far_first]
    x_line = [(lax.rem(x + d, XS) * ZS + z, y * 2 + (1 - core if other else core)) for d, other in far_first]
    partners = [*z_to.values(), *y_line, *x_line[:-1]]
    for device in partners:
        pl.semaphore_signal(barrier, inc=1, device_id=device, device_id_type=MESH)

    row = lax.broadcasted_iota(jnp.int32, (RAW, npd), 0)
    lane = lax.broadcasted_iota(jnp.int32, (RAW, npd), 1)
    here = lax.broadcasted_iota(jnp.int32, (npd, npd), 0)
    there = lax.broadcasted_iota(jnp.int32, (npd, npd), 1)
    same_round = (here & (RAW - 1)) == ROUNDS * SLOTS + ((there & (RAW - 1)) >> 2)
    before = jnp.where(same_round & ((here >> 4) < (there >> 4)), 1.0, 0.0)
    itself = jnp.where(same_round & ((here >> 4) == (there >> 4)), 1.0, 0.0)
    slot = lane & (RAW - 1)
    slot_round = jnp.where(slot < ROUNDS * SLOTS, slot >> 2, -1)
    slot_index = (slot & (SLOTS - 1)).astype(F32)
    wanted = (SHARE * sub + (row & 1)).astype(F32)
    wanted_round = slot_round == (row >> 1)
    own_rows.wait()
    own_counts.wait()
    target = jnp.full((RAW, npd), -1, jnp.int32)
    counts = jnp.zeros((RAW, npd), F32)
    for r in range(ROUNDS):
        counts = jnp.where(row == ROUNDS * SLOTS + r, cnt_ref[0, r].astype(F32), counts)
        for i in range(SLOTS):
            target = jnp.where(row == r * SLOTS + i, rows_ref[r, i], target)
    pick = jnp.where(lane == target, 1.0, 0.0).astype(jnp.bfloat16)
    own_points.wait()
    mine = raw[...]
    block = jnp.dot(pick, mine, preferred_element_type=F32)
    slots[sub, :, :npd] = (block[:, :npd] + counts).astype(jnp.bfloat16)
    slots[sub, :, npd:] = block[:, npd:].astype(jnp.bfloat16)

    pl.semaphore_wait(barrier, len(partners))

    def remote(src, dst, send, recv, device):
        return pltpu.make_async_remote_copy(
            src_ref=src, dst_ref=dst, send_sem=send, recv_sem=recv, device_id=device, device_id_type=MESH
        )

    def to_sides(place, count, group):
        for d, column in ((1, 2), (3, 3)):
            src, dst = cand.at[0, pl.ds(place, count)], cand.at[column, pl.ds(place, count)]
            remote(src, dst, y_send, y_recv.at[group], y_to[d]).start()

    def to_far(place):
        remote(cand.at[0, place], cand.at[1, place], far_send, far_recv.at[place - 12], y_to[2]).start()

    def far_along_z(src, place, count, group, d, lanes=None):
        src, dst = cand.at[1, pl.ds(src, count)], cand.at[1, pl.ds(place, count)]
        if lanes is not None:
            part = pl.ds(lanes * (width // 2), width // 2)
            src, dst = src.at[:, :, part], dst.at[:, :, part]
        remote(src, dst, far_z_send, far_z_recv.at[group], z_to[d]).start()

    def along_z(src, place, d, lanes=None):
        if lanes is None:
            src, dst = cand.at[0, src], cand.at[0, place]
        else:
            part = pl.ds(lanes * (width // 2), width // 2)
            src, dst = cand.at[0, src, :, part], cand.at[0, place, :, part]
        remote(src, dst, z_block_send, z_block_recv.at[place + (lanes or 0)], z_to[d]).start()

    def z_arrived(*places):
        for place in places:
            wait_bytes(cand.at[0, place], z_block_recv.at[place])

    def wait_bytes(ref, sem):
        pltpu.make_async_copy(ref, ref, sem).wait()

    for device in y_line:
        remote(slots.at[sub], slots.at[sub], slots_send, slots_recv, device).start()
    pall[me] = mine.T
    slot_right, slot_left, slot_far = (lax.rem(x + d, XS) * 2 + core for d in (1, 3, 2))
    top, low = pl.ds(0, width // 2), pl.ds(width // 2, width // 2)
    mine_at = pall.at[me]
    pts_right = remote(mine_at, mine_at, pts_send.at[0], pts_recv.at[0], x_right)
    pts_left = remote(mine_at, mine_at, pts_send.at[1], pts_recv.at[1], x_left)
    pts_core = remote(mine_at, mine_at, pts_send.at[2], pts_recv.at[2], other_core)
    pts_right.start()
    pts_left.start()
    pts_core.start()

    wait_bytes(slots.at[pl.ds(0, SUBS - 1)], slots_recv)
    flat = slots[...].reshape(SUBS * RAW, width)
    known = flat[:, :npd].astype(F32)
    offset = jnp.sum(known * before, axis=0, keepdims=True)
    count = jnp.sum(known * itself, axis=0, keepdims=True)
    choice = wanted_round & (slot_index < count) & (offset + slot_index == wanted)
    share = jnp.dot(jnp.where(choice, 1.0, 0.0).astype(jnp.bfloat16), flat, preferred_element_type=F32)
    cand[0, 13] = share[:BLK].astype(jnp.bfloat16)

    along_z(13, 12, 4)
    along_z(13, 14, -4)
    to_far(13)
    for place, d in ((1, 2), (2, -2), (5, 1), (9, -1)):
        along_z(13, place, d)
    to_sides(13, 1, 3)

    pts_right.wait_recv()
    near_left = pall.at[slot_left]
    far_top = remote(near_left.at[top], near_left.at[top], pts_send.at[3], pts_recv.at[3], x_right)
    core_left = remote(near_left, near_left, pts_send.at[4], pts_recv.at[4], other_core)
    far_top.start()
    core_left.start()
    pts_left.wait_recv()
    near_right = pall.at[slot_right]
    far_low = remote(near_right.at[low], near_right.at[low], pts_send.at[5], pts_recv.at[5], x_left)
    core_right = remote(near_right, near_right, pts_send.at[6], pts_recv.at[6], other_core)
    far_low.start()
    core_right.start()

    z_arrived(12)
    to_far(12)
    along_z(12, 15, 4, 0)
    for place, d in ((7, 3), (0, 2), (4, 1), (8, -1)):
        along_z(12, place, d)
    z_arrived(14)
    to_far(14)
    along_z(14, 15, -4, 1)
    for place, d in ((11, -3), (3, -2), (10, -1), (6, 1)):
        along_z(14, place, d)
    to_sides(12, 1, 3)
    to_sides(14, 1, 3)

    for place in (12, 13, 14):
        wait_bytes(cand.at[1, place], far_recv.at[place - 12])
    far_along_z(12, 15, 1, 3, 4, 0)
    far_along_z(14, 15, 1, 3, -4, 1)
    far_along_z(12, 7, 1, 1, 3)
    far_along_z(14, 11, 1, 2, -3)
    far_along_z(12, 0, 2, 0, 2)
    far_along_z(13, 2, 2, 0, -2)
    far_along_z(12, 4, 3, 1, 1)
    far_along_z(12, 8, 3, 2, -1)

    for group in range(3):
        z_arrived(*range(4 * group, 4 * group + 4))
        to_sides(4 * group, 4, group)
    half_block = cand.at[0, 15, :, pl.ds(0, width // 2)]
    wait_bytes(half_block, z_block_recv.at[15])
    wait_bytes(half_block, z_block_recv.at[16])
    to_sides(15, 1, 3)

    far_top.wait_recv()
    far_low.wait_recv()
    far = pall.at[slot_far]
    core_far = remote(far, far, pts_send.at[7], pts_recv.at[7], other_core)
    core_far.start()

    def absorb(first, count):
        for group in range(first, first + count):
            wait_bytes(cand.at[pl.ds(2, 2), pl.ds(0, 4)], y_recv.at[group])
            wait_bytes(cand.at[1, pl.ds(0, 4 if group < 3 else 1)], far_z_recv.at[group])
        blocks = XS * 4 * count
        rows = cand[:, 4 * first : 4 * (first + count)].reshape(blocks, BLK, width)
        half = jnp.zeros((blocks, BLK, npd), F32)
        for t in range(width // npd):
            piece = rows[:, :, t * npd : (t + 1) * npd].astype(F32)
            half = half + piece * piece
        half = 0.5 * jnp.sum(half, axis=2, keepdims=True)
        flat = rows.reshape(blocks * BLK, width)
        for j in range(SUBS // 2):
            group = jnp.concatenate([pall[2 * j], pall[2 * j + 1]], axis=1)
            dots = jnp.dot(flat, group, preferred_element_type=F32)
            best = jnp.min(half - dots.reshape(blocks, BLK, 2 * npd), axis=0)
            mins[j] = best if first == 0 else jnp.minimum(mins[j], best)

    pts_core.wait_recv()
    core_left.wait_recv()
    core_right.wait_recv()
    core_far.wait_recv()
    absorb(0, 3)
    for b in range(SUBS):
        wide = pall[b].astype(F32)
        squares[b : b + 1, :] = jnp.sum(wide * wide, axis=0, keepdims=True)
    absorb(3, 1)

    for j in range(SUBS // 2):
        for r in range(ROUNDS):
            low_r = jnp.min(mins[j, r * SHARE : (r + 1) * SHARE, :], axis=0, keepdims=True)
            for h in range(2):
                line[me, r, 2 * j + h : 2 * j + h + 1, :] = low_r[:, h * npd : (h + 1) * npd]

    for device in x_line:
        remote(line.at[me], line.at[me], line_send, line_recv, device).start()
    wait_bytes(line.at[pl.ds(0, SUBS - 1)], line_recv)

    lanes = lax.broadcasted_iota(jnp.int32, (1, npd), 1)
    least = None
    total = jnp.zeros((1, npd), F32)
    for r in range(ROUNDS):
        now = jnp.min(line[:, r], axis=0)
        least = now if least is None else jnp.minimum(least, now)
        dist = jnp.maximum(squares[...] + 2.0 * least, 0.0)
        near[r] = dist
        part = jnp.sum(jnp.sum(dist, axis=0, keepdims=True), axis=1, keepdims=True)
        total = jnp.where(lanes == r, part, total)

    zsum[0] = total

    for d in (8, 7, 9, 6, 10, 5, 11, 4, 12, 3, 13, 2, 14, 1, 15):
        remote(zsum.at[0], zsum.at[ZS - d], z_send, z_recv, at_z(d)).start()
    wait_bytes(zsum.at[pl.ds(0, ZS - 1)], z_recv)
    ysum[0] = jnp.sum(zsum[...], axis=0)
    for d in (1, 3, 2):
        remote(ysum.at[0], ysum.at[XS - d], c_send, c_recv, y_to[d]).start()
    wait_bytes(ysum.at[pl.ds(0, XS - 1)], c_recv)
    cost = jnp.sum(ysum[...], axis=0)
    for r in range(ROUNDS):
        cost_r = jnp.sum(jnp.where(lanes == r, cost, 0.0), axis=1, keepdims=True)
        out_ref[r : r + 1, :] = npts * near[r, pl.ds(me, 1), :] / cost_r

    wait_bytes(slots.at[pl.ds(0, SUBS - 1)], slots_send)
    wait_bytes(cand.at[0, pl.ds(0, 15)], z_block_send)
    wait_bytes(cand.at[pl.ds(0, 2)], y_send)
    wait_bytes(cand.at[0, pl.ds(0, 3)], far_send)
    wait_bytes(cand.at[0, pl.ds(0, 13)], far_z_send)
    for copy in (pts_right, pts_left, pts_core, far_top, core_left, far_low, core_right, core_far):
        copy.wait_send()
    wait_bytes(line.at[pl.ds(0, SUBS - 1)], line_send)
    wait_bytes(zsum.at[pl.ds(0, ZS - 1)], z_send)
    wait_bytes(ysum.at[pl.ds(0, XS - 1)], c_send)


def shards(points, cand_rows, cand_count):
    npd, width = points.shape
    npts = float(npd * lax.axis_size(("dp", "sub")))
    dma = pltpu.SemaphoreType.DMA
    operands = (cand_rows, cand_count.reshape(1, ROUNDS), points)
    return pl.pallas_call(
        lambda *refs: kernel(npts, *refs),
        out_shape=jax.ShapeDtypeStruct((ROUNDS, npd), F32),
        in_specs=[
            pl.BlockSpec(memory_space=pl.ANY),
            pl.BlockSpec(memory_space=pl.ANY),
            pl.BlockSpec(memory_space=pl.ANY),
        ],
        out_specs=pl.BlockSpec(memory_space=pltpu.VMEM),
        scratch_shapes=[
            pltpu.SMEM((ROUNDS, SLOTS), jnp.int32),
            pltpu.SMEM((1, ROUNDS), jnp.int32),
            pltpu.VMEM((npd, width), jnp.bfloat16),
            pltpu.VMEM((SUBS, RAW, width), jnp.bfloat16),
            pltpu.VMEM((XS, ZS, BLK, width), jnp.bfloat16),
            pltpu.VMEM((SUBS, width, npd), jnp.bfloat16),
            pltpu.VMEM((SUBS // 2, BLK, 2 * npd), F32),
            pltpu.VMEM((SUBS, npd), F32),
            pltpu.VMEM((SUBS, ROUNDS, SUBS, npd), F32),
            pltpu.VMEM((ROUNDS, SUBS, npd), F32),
            pltpu.VMEM((ZS, 1, npd), F32),
            pltpu.VMEM((XS, 1, npd), F32),
            dma((3,)),
            dma,
            dma,
            dma,
            dma,
            dma((17,)),
            dma((4,)),
            dma,
            dma,
            dma((3,)),
            dma((4,)),
            dma((8,)),
            dma((8,)),
            dma,
            dma,
            dma,
            dma,
            dma,
            dma,
        ],
        compiler_params=pltpu.CompilerParams(
            collective_id=0, has_side_effects=True, vmem_limit_bytes=40 * 1024 * 1024
        ),
        cost_estimate=pl.CostEstimate(
            flops=2 * 1024 * 1024 * width, bytes_accessed=npd * width * 2, transcendentals=0
        ),
    )(*(pltpu.with_memory_space_constraint(value, pltpu.HBM) for value in operands))


def solution(mesh):
    in_specs = (P(("dp", "sub"), None), P(None, ("dp", "sub")), P(None, ("dp", "sub")))
    out_specs = P(None, ("dp", "sub"))
    return jax.shard_map(shards, mesh=mesh, in_specs=in_specs, out_specs=out_specs, check_vma=False)
```

```python
import jax
import jax.numpy as jnp
from jax import lax
from jax.experimental import pallas as pl
from jax.experimental.pallas import tpu as pltpu
from jax.sharding import PartitionSpec as P

ROUNDS = 3
SLOTS = 4
XS = 4
ZS = 16
YS = 4
SUBS = 8
RAW = 16
BLK = 8
SHARE = 2
MESH = pl.DeviceIdType.MESH
F32 = jnp.float32
INF = float("inf")


def kernel(
    npts,
    rows_in,
    counts_in,
    points_ref,
    out_ref,
    rows_ref,
    cnt_ref,
    raw,
    slots,
    cand,
    pall,
    mins,
    squares,
    line,
    near,
    zsum,
    ysum,
    local_sem,
    slots_send,
    slots_recv,
    z_block_send,
    y_send,
    z_block_recv,
    y_recv,
    far_send,
    far_z_send,
    far_recv,
    far_z_recv,
    pts_send,
    pts_recv,
    line_send,
    line_recv,
    z_send,
    z_recv,
    c_send,
    c_recv,
):
    dp = lax.axis_index("dp")
    sub = lax.axis_index("sub")
    x, z = lax.div(dp, ZS), lax.rem(dp, ZS)
    y, core = lax.div(sub, 2), lax.rem(sub, 2)
    npd, width = points_ref.shape

    def at_x(d):
        return (lax.rem(x + d, XS) * ZS + z, sub)

    def at_z(d):
        return (x * ZS + lax.rem(z + d, ZS), sub)

    def at_y(d):
        return (dp, lax.rem(y + d, YS) * 2 + core)

    other_core = (dp, y * 2 + (1 - core))
    z_to = {d: at_z(d % ZS) for d in (1, -1, 2, -2, 3, -3, 4, -4)}
    y_to = {d: at_y(d) for d in (1, 2, 3)}
    me = x * 2 + core
    x_right, x_left = at_x(1), at_x(3)

    own_points = pltpu.make_async_copy(points_ref, raw, local_sem.at[0])
    own_points.start()
    own_rows = pltpu.make_async_copy(rows_in, rows_ref, local_sem.at[1])
    own_rows.start()
    own_counts = pltpu.make_async_copy(counts_in, cnt_ref, local_sem.at[2])
    own_counts.start()
    barrier = pltpu.get_barrier_semaphore()
    far_first = ((2, 0), (2, 1), (1, 0), (3, 0), (1, 1), (3, 1), (0, 1))
    y_line = [(dp, lax.rem(y + d, YS) * 2 + (1 - core if other else core)) for d, other in far_first]
    x_line = [(lax.rem(x + d, XS) * ZS + z, y * 2 + (1 - core if other else core)) for d, other in far_first]
    partners = [*z_to.values(), *y_line, *x_line[:-1]]
    for device in partners:
        pl.semaphore_signal(barrier, inc=1, device_id=device, device_id_type=MESH)

    row = lax.broadcasted_iota(jnp.int32, (RAW, npd), 0)
    lane = lax.broadcasted_iota(jnp.int32, (RAW, npd), 1)
    here = lax.broadcasted_iota(jnp.int32, (npd, npd), 0)
    there = lax.broadcasted_iota(jnp.int32, (npd, npd), 1)
    same_round = (here & (RAW - 1)) == ROUNDS * SLOTS + ((there & (RAW - 1)) >> 2)
    before = jnp.where(same_round & ((here >> 4) < (there >> 4)), 1.0, 0.0)
    itself = jnp.where(same_round & ((here >> 4) == (there >> 4)), 1.0, 0.0)
    slot = lane & (RAW - 1)
    slot_round = jnp.where(slot < ROUNDS * SLOTS, slot >> 2, -1)
    slot_index = (slot & (SLOTS - 1)).astype(F32)
    wanted = (SHARE * sub + (row & 1)).astype(F32)
    wanted_round = slot_round == (row >> 1)
    own_rows.wait()
    own_counts.wait()
    target = jnp.full((RAW, npd), -1, jnp.int32)
    counts = jnp.zeros((RAW, npd), F32)
    for r in range(ROUNDS):
        counts = jnp.where(row == ROUNDS * SLOTS + r, cnt_ref[0, r].astype(F32), counts)
        for i in range(SLOTS):
            target = jnp.where(row == r * SLOTS + i, rows_ref[r, i], target)
    pick = jnp.where(lane == target, 1.0, 0.0).astype(jnp.bfloat16)
    own_points.wait()
    mine = raw[...]
    block = jnp.dot(pick, mine, preferred_element_type=F32)
    slots[sub, :, :npd] = (block[:, :npd] + counts).astype(jnp.bfloat16)
    slots[sub, :, npd:] = block[:, npd:].astype(jnp.bfloat16)

    pl.semaphore_wait(barrier, len(partners))

    def remote(src, dst, send, recv, device):
        return pltpu.make_async_remote_copy(
            src_ref=src, dst_ref=dst, send_sem=send, recv_sem=recv, device_id=device, device_id_type=MESH
        )

    def to_sides(place, count, group):
        for d, column in ((1, 2), (3, 3)):
            src, dst = cand.at[0, pl.ds(place, count)], cand.at[column, pl.ds(place, count)]
            remote(src, dst, y_send, y_recv.at[group], y_to[d]).start()

    def to_far(place):
        remote(cand.at[0, place], cand.at[1, place], far_send, far_recv.at[place - 12], y_to[2]).start()

    def far_along_z(src, place, count, group, d, lanes=None):
        src, dst = cand.at[1, pl.ds(src, count)], cand.at[1, pl.ds(place, count)]
        if lanes is not None:
            part = pl.ds(lanes * (width // 2), width // 2)
            src, dst = src.at[:, :, part], dst.at[:, :, part]
        remote(src, dst, far_z_send, far_z_recv.at[group], z_to[d]).start()

    def along_z(src, place, d, lanes=None):
        if lanes is None:
            src, dst = cand.at[0, src], cand.at[0, place]
        else:
            part = pl.ds(lanes * (width // 2), width // 2)
            src, dst = cand.at[0, src, :, part], cand.at[0, place, :, part]
        remote(src, dst, z_block_send, z_block_recv.at[place + (lanes or 0)], z_to[d]).start()

    def z_arrived(*places):
        for place in places:
            wait_bytes(cand.at[0, place], z_block_recv.at[place])

    def wait_bytes(ref, sem):
        pltpu.make_async_copy(ref, ref, sem).wait()

    for device in y_line:
        remote(slots.at[sub], slots.at[sub], slots_send, slots_recv, device).start()
    pall[me] = mine.T
    wait_bytes(slots.at[pl.ds(0, SUBS - 1)], slots_recv)
    flat = slots[...].reshape(SUBS * RAW, width)
    known = flat[:, :npd].astype(F32)
    offset = jnp.sum(known * before, axis=0, keepdims=True)
    count = jnp.sum(known * itself, axis=0, keepdims=True)
    choice = wanted_round & (slot_index < count) & (offset + slot_index == wanted)
    share = jnp.dot(jnp.where(choice, 1.0, 0.0).astype(jnp.bfloat16), flat, preferred_element_type=F32)
    cand[0, 13] = share[:BLK].astype(jnp.bfloat16)

    along_z(13, 12, 4)
    along_z(13, 14, -4)
    to_far(13)
    for place, d in ((1, 2), (2, -2), (5, 1), (9, -1)):
        along_z(13, place, d)
    to_sides(13, 1, 3)

    slot_right, slot_left, slot_far = (lax.rem(x + d, XS) * 2 + core for d in (1, 3, 2))
    top, low = pl.ds(0, width // 2), pl.ds(width // 2, width // 2)
    mine_at = pall.at[me]
    pts_right = remote(mine_at, mine_at, pts_send.at[0], pts_recv.at[0], x_right)
    pts_left = remote(mine_at, mine_at, pts_send.at[1], pts_recv.at[1], x_left)
    pts_core = remote(mine_at, mine_at, pts_send.at[2], pts_recv.at[2], other_core)
    pts_right.start()
    pts_left.start()
    pts_core.start()

    z_arrived(12)
    to_far(12)
    along_z(12, 15, 4, 0)
    for place, d in ((7, 3), (0, 2), (4, 1), (8, -1)):
        along_z(12, place, d)
    z_arrived(14)
    to_far(14)
    along_z(14, 15, -4, 1)
    for place, d in ((11, -3), (3, -2), (10, -1), (6, 1)):
        along_z(14, place, d)
    to_sides(12, 1, 3)
    to_sides(14, 1, 3)

    pts_right.wait_recv()
    near_left = pall.at[slot_left]
    far_top = remote(near_left.at[top], near_left.at[top], pts_send.at[3], pts_recv.at[3], x_right)
    core_left = remote(near_left, near_left, pts_send.at[4], pts_recv.at[4], other_core)
    far_top.start()
    core_left.start()
    pts_left.wait_recv()
    near_right = pall.at[slot_right]
    far_low = remote(near_right.at[low], near_right.at[low], pts_send.at[5], pts_recv.at[5], x_left)
    core_right = remote(near_right, near_right, pts_send.at[6], pts_recv.at[6], other_core)
    far_low.start()
    core_right.start()

    for place in (12, 13, 14):
        wait_bytes(cand.at[1, place], far_recv.at[place - 12])
    far_along_z(12, 15, 1, 3, 4, 0)
    far_along_z(14, 15, 1, 3, -4, 1)
    far_along_z(12, 7, 1, 1, 3)
    far_along_z(14, 11, 1, 2, -3)
    far_along_z(12, 0, 2, 0, 2)
    far_along_z(13, 2, 2, 0, -2)
    far_along_z(12, 4, 3, 1, 1)
    far_along_z(12, 8, 3, 2, -1)

    for group in range(3):
        z_arrived(*range(4 * group, 4 * group + 4))
        to_sides(4 * group, 4, group)
    half_block = cand.at[0, 15, :, pl.ds(0, width // 2)]
    wait_bytes(half_block, z_block_recv.at[15])
    wait_bytes(half_block, z_block_recv.at[16])
    to_sides(15, 1, 3)

    far_top.wait_recv()
    far_low.wait_recv()
    far = pall.at[slot_far]
    core_far = remote(far, far, pts_send.at[7], pts_recv.at[7], other_core)
    core_far.start()

    pts_core.wait_recv()
    core_left.wait_recv()
    core_right.wait_recv()
    core_far.wait_recv()
    def square(b, carry):
        wide = pall[b].astype(F32)
        squares[pl.ds(b, 1), :] = jnp.sum(wide * wide, axis=0, keepdims=True)
        return carry

    lax.fori_loop(0, SUBS, square, 0)

    for group in range(4):
        wait_bytes(cand.at[pl.ds(2, 2), pl.ds(0, 4)], y_recv.at[group])
        wait_bytes(cand.at[1, pl.ds(0, 4 if group < 3 else 1)], far_z_recv.at[group])
    blocks = XS * ZS
    rows = cand[...].reshape(blocks, BLK, width)
    half = jnp.zeros((blocks, BLK, npd), F32)
    for t in range(width // npd):
        piece = rows[:, :, t * npd : (t + 1) * npd].astype(F32)
        half = half + piece * piece
    half = 0.5 * jnp.sum(half, axis=2, keepdims=True)
    flat = rows.reshape(blocks * BLK, width)

    def chip(j, carry):
        group = jnp.concatenate([pall[2 * j], pall[2 * j + 1]], axis=1)
        dots = jnp.dot(flat, group, preferred_element_type=F32)
        mins[j] = jnp.min(half - dots.reshape(blocks, BLK, 2 * npd), axis=0)
        return carry

    lax.fori_loop(0, SUBS // 2, chip, 0)

    for j in range(SUBS // 2):
        for r in range(ROUNDS):
            low_r = jnp.min(mins[j, r * SHARE : (r + 1) * SHARE, :], axis=0, keepdims=True)
            for h in range(2):
                line[me, r, 2 * j + h : 2 * j + h + 1, :] = low_r[:, h * npd : (h + 1) * npd]

    for device in x_line:
        remote(line.at[me], line.at[me], line_send, line_recv, device).start()
    wait_bytes(line.at[pl.ds(0, SUBS - 1)], line_recv)

    lanes = lax.broadcasted_iota(jnp.int32, (1, npd), 1)
    least = None
    total = jnp.zeros((1, npd), F32)
    for r in range(ROUNDS):
        now = jnp.min(line[:, r], axis=0)
        least = now if least is None else jnp.minimum(least, now)
        dist = jnp.maximum(squares[...] + 2.0 * least, 0.0)
        near[r] = dist
        part = jnp.sum(jnp.sum(dist, axis=0, keepdims=True), axis=1, keepdims=True)
        total = jnp.where(lanes == r, part, total)

    zsum[0] = total

    for d in (8, 7, 9, 6, 10, 5, 11, 4, 12, 3, 13, 2, 14, 1, 15):
        remote(zsum.at[0], zsum.at[ZS - d], z_send, z_recv, at_z(d)).start()
    wait_bytes(zsum.at[pl.ds(0, ZS - 1)], z_recv)
    ysum[0] = jnp.sum(zsum[...], axis=0)
    for d in (1, 3, 2):
        remote(ysum.at[0], ysum.at[XS - d], c_send, c_recv, y_to[d]).start()
    wait_bytes(ysum.at[pl.ds(0, XS - 1)], c_recv)
    cost = jnp.sum(ysum[...], axis=0)
    for r in range(ROUNDS):
        cost_r = jnp.sum(jnp.where(lanes == r, cost, 0.0), axis=1, keepdims=True)
        out_ref[r : r + 1, :] = npts * near[r, pl.ds(me, 1), :] / cost_r

    wait_bytes(slots.at[pl.ds(0, SUBS - 1)], slots_send)
    wait_bytes(cand.at[0, pl.ds(0, 15)], z_block_send)
    wait_bytes(cand.at[pl.ds(0, 2)], y_send)
    wait_bytes(cand.at[0, pl.ds(0, 3)], far_send)
    wait_bytes(cand.at[0, pl.ds(0, 13)], far_z_send)
    for copy in (pts_right, pts_left, pts_core, far_top, core_left, far_low, core_right, core_far):
        copy.wait_send()
    wait_bytes(line.at[pl.ds(0, SUBS - 1)], line_send)
    wait_bytes(zsum.at[pl.ds(0, ZS - 1)], z_send)
    wait_bytes(ysum.at[pl.ds(0, XS - 1)], c_send)


def shards(points, cand_rows, cand_count):
    npd, width = points.shape
    npts = float(npd * lax.axis_size(("dp", "sub")))
    dma = pltpu.SemaphoreType.DMA
    operands = (cand_rows, cand_count.reshape(1, ROUNDS), points)
    return pl.pallas_call(
        lambda *refs: kernel(npts, *refs),
        out_shape=jax.ShapeDtypeStruct((ROUNDS, npd), F32),
        in_specs=[
            pl.BlockSpec(memory_space=pl.ANY),
            pl.BlockSpec(memory_space=pl.ANY),
            pl.BlockSpec(memory_space=pl.ANY),
        ],
        out_specs=pl.BlockSpec(memory_space=pltpu.VMEM),
        scratch_shapes=[
            pltpu.SMEM((ROUNDS, SLOTS), jnp.int32),
            pltpu.SMEM((1, ROUNDS), jnp.int32),
            pltpu.VMEM((npd, width), jnp.bfloat16),
            pltpu.VMEM((SUBS, RAW, width), jnp.bfloat16),
            pltpu.VMEM((XS, ZS, BLK, width), jnp.bfloat16),
            pltpu.VMEM((SUBS, width, npd), jnp.bfloat16),
            pltpu.VMEM((SUBS // 2, BLK, 2 * npd), F32),
            pltpu.VMEM((SUBS, npd), F32),
            pltpu.VMEM((SUBS, ROUNDS, SUBS, npd), F32),
            pltpu.VMEM((ROUNDS, SUBS, npd), F32),
            pltpu.VMEM((ZS, 1, npd), F32),
            pltpu.VMEM((XS, 1, npd), F32),
            dma((3,)),
            dma,
            dma,
            dma,
            dma,
            dma((17,)),
            dma((4,)),
            dma,
            dma,
            dma((3,)),
            dma((4,)),
            dma((8,)),
            dma((8,)),
            dma,
            dma,
            dma,
            dma,
            dma,
            dma,
        ],
        compiler_params=pltpu.CompilerParams(
            collective_id=0, has_side_effects=True, vmem_limit_bytes=40 * 1024 * 1024
        ),
        cost_estimate=pl.CostEstimate(
            flops=2 * 1024 * 1024 * width, bytes_accessed=npd * width * 2, transcendentals=0
        ),
    )(*(pltpu.with_memory_space_constraint(value, pltpu.HBM) for value in operands))


def solution(mesh):
    in_specs = (P(("dp", "sub"), None), P(None, ("dp", "sub")), P(None, ("dp", "sub")))
    out_specs = P(None, ("dp", "sub"))
    return jax.shard_map(shards, mesh=mesh, in_specs=in_specs, out_specs=out_specs, check_vma=False)
```

```python
import jax
import jax.numpy as jnp
from jax import lax
from jax.experimental import pallas as pl
from jax.experimental.pallas import tpu as pltpu
from jax.sharding import PartitionSpec as P

ROUNDS = 3
SLOTS = 4
XS = 4
ZS = 16
YS = 4
SUBS = 8
RAW = 16
BLK = 8
SHARE = 2
MESH = pl.DeviceIdType.MESH
F32 = jnp.float32
INF = float("inf")


def kernel(
    npts,
    rows_in,
    counts_in,
    points_ref,
    out_ref,
    rows_ref,
    cnt_ref,
    raw,
    slots,
    cand,
    pall,
    mins,
    squares,
    line,
    near,
    zsum,
    ysum,
    local_sem,
    slots_send,
    slots_recv,
    z_block_send,
    y_send,
    z_block_recv,
    y_recv,
    far_send,
    far_z_send,
    far_recv,
    far_z_recv,
    pts_send,
    pts_recv,
    line_send,
    line_recv,
    z_send,
    z_recv,
    c_send,
    c_recv,
):
    dp = lax.axis_index("dp")
    sub = lax.axis_index("sub")
    x, z = lax.div(dp, ZS), lax.rem(dp, ZS)
    y, core = lax.div(sub, 2), lax.rem(sub, 2)
    npd, width = points_ref.shape

    def at_x(d):
        return (lax.rem(x + d, XS) * ZS + z, sub)

    def at_z(d):
        return (x * ZS + lax.rem(z + d, ZS), sub)

    def at_y(d):
        return (dp, lax.rem(y + d, YS) * 2 + core)

    other_core = (dp, y * 2 + (1 - core))
    z_to = {d: at_z(d % ZS) for d in (1, -1, 2, -2, 3, -3, 4, -4)}
    y_to = {d: at_y(d) for d in (1, 2, 3)}
    me = x * 2 + core
    x_right, x_left = at_x(1), at_x(3)

    own_points = pltpu.make_async_copy(points_ref, raw, local_sem.at[0])
    own_points.start()
    own_rows = pltpu.make_async_copy(rows_in, rows_ref, local_sem.at[1])
    own_rows.start()
    own_counts = pltpu.make_async_copy(counts_in, cnt_ref, local_sem.at[2])
    own_counts.start()
    barrier = pltpu.get_barrier_semaphore()
    far_first = ((2, 0), (2, 1), (1, 0), (3, 0), (1, 1), (3, 1), (0, 1))
    y_line = [(dp, lax.rem(y + d, YS) * 2 + (1 - core if other else core)) for d, other in far_first]
    x_line = [(lax.rem(x + d, XS) * ZS + z, y * 2 + (1 - core if other else core)) for d, other in far_first]
    partners = [*z_to.values(), *y_line, *x_line[:-1]]
    for device in partners:
        pl.semaphore_signal(barrier, inc=1, device_id=device, device_id_type=MESH)

    row = lax.broadcasted_iota(jnp.int32, (RAW, npd), 0)
    lane = lax.broadcasted_iota(jnp.int32, (RAW, npd), 1)
    here = lax.broadcasted_iota(jnp.int32, (npd, npd), 0)
    there = lax.broadcasted_iota(jnp.int32, (npd, npd), 1)
    same_round = (here & (RAW - 1)) == ROUNDS * SLOTS + ((there & (RAW - 1)) >> 2)
    before = jnp.where(same_round & ((here >> 4) < (there >> 4)), 1.0, 0.0)
    itself = jnp.where(same_round & ((here >> 4) == (there >> 4)), 1.0, 0.0)
    slot = lane & (RAW - 1)
    slot_round = jnp.where(slot < ROUNDS * SLOTS, slot >> 2, -1)
    slot_index = (slot & (SLOTS - 1)).astype(F32)
    wanted = (SHARE * sub + (row & 1)).astype(F32)
    wanted_round = slot_round == (row >> 1)
    own_rows.wait()
    own_counts.wait()
    target = jnp.full((RAW, npd), -1, jnp.int32)
    counts = jnp.zeros((RAW, npd), F32)
    for r in range(ROUNDS):
        counts = jnp.where(row == ROUNDS * SLOTS + r, cnt_ref[0, r].astype(F32), counts)
        for i in range(SLOTS):
            target = jnp.where(row == r * SLOTS + i, rows_ref[r, i], target)
    pick = jnp.where(lane == target, 1.0, 0.0).astype(jnp.bfloat16)
    own_points.wait()
    mine = raw[...]
    block = jnp.dot(pick, mine, preferred_element_type=F32)
    slots[sub, :, :npd] = (block[:, :npd] + counts).astype(jnp.bfloat16)
    slots[sub, :, npd:] = block[:, npd:].astype(jnp.bfloat16)

    pl.semaphore_wait(barrier, len(partners))

    def remote(src, dst, send, recv, device):
        return pltpu.make_async_remote_copy(
            src_ref=src, dst_ref=dst, send_sem=send, recv_sem=recv, device_id=device, device_id_type=MESH
        )

    def to_sides(place, count, group):
        for d, column in ((1, 2), (3, 3)):
            src, dst = cand.at[0, pl.ds(place, count)], cand.at[column, pl.ds(place, count)]
            remote(src, dst, y_send, y_recv.at[group], y_to[d]).start()

    def to_far(place):
        remote(cand.at[0, place], cand.at[1, place], far_send, far_recv.at[place - 12], y_to[2]).start()

    def far_along_z(src, place, count, group, d, lanes=None):
        src, dst = cand.at[1, pl.ds(src, count)], cand.at[1, pl.ds(place, count)]
        if lanes is not None:
            part = pl.ds(lanes * (width // 2), width // 2)
            src, dst = src.at[:, :, part], dst.at[:, :, part]
        remote(src, dst, far_z_send, far_z_recv.at[group], z_to[d]).start()

    def along_z(src, place, d, lanes=None):
        if lanes is None:
            src, dst = cand.at[0, src], cand.at[0, place]
        else:
            part = pl.ds(lanes * (width // 2), width // 2)
            src, dst = cand.at[0, src, :, part], cand.at[0, place, :, part]
        remote(src, dst, z_block_send, z_block_recv.at[place + (lanes or 0)], z_to[d]).start()

    def z_arrived(*places):
        for place in places:
            wait_bytes(cand.at[0, place], z_block_recv.at[place])

    def wait_bytes(ref, sem):
        pltpu.make_async_copy(ref, ref, sem).wait()

    for device in y_line:
        remote(slots.at[sub], slots.at[sub], slots_send, slots_recv, device).start()
    pall[me] = mine.T
    slot_right, slot_left, slot_far = (lax.rem(x + d, XS) * 2 + core for d in (1, 3, 2))
    top, low = pl.ds(0, width // 2), pl.ds(width // 2, width // 2)
    mine_at = pall.at[me]
    pts_right = remote(mine_at, mine_at, pts_send.at[0], pts_recv.at[0], x_right)
    pts_left = remote(mine_at, mine_at, pts_send.at[1], pts_recv.at[1], x_left)
    pts_core = remote(mine_at, mine_at, pts_send.at[2], pts_recv.at[2], other_core)
    pts_right.start()
    pts_left.start()
    pts_core.start()

    wait_bytes(slots.at[pl.ds(0, SUBS - 1)], slots_recv)
    flat = slots[...].reshape(SUBS * RAW, width)
    known = flat[:, :npd].astype(F32)
    offset = jnp.sum(known * before, axis=0, keepdims=True)
    count = jnp.sum(known * itself, axis=0, keepdims=True)
    choice = wanted_round & (slot_index < count) & (offset + slot_index == wanted)
    share = jnp.dot(jnp.where(choice, 1.0, 0.0).astype(jnp.bfloat16), flat, preferred_element_type=F32)
    cand[0, 13] = share[:BLK].astype(jnp.bfloat16)

    along_z(13, 12, 4)
    along_z(13, 14, -4)
    to_far(13)
    for place, d in ((1, 2), (2, -2), (5, 1), (9, -1)):
        along_z(13, place, d)
    to_sides(13, 1, 3)

    pts_right.wait_recv()
    near_left = pall.at[slot_left]
    far_top = remote(near_left.at[top], near_left.at[top], pts_send.at[3], pts_recv.at[3], x_right)
    core_left = remote(near_left, near_left, pts_send.at[4], pts_recv.at[4], other_core)
    far_top.start()
    core_left.start()
    pts_left.wait_recv()
    near_right = pall.at[slot_right]
    far_low = remote(near_right.at[low], near_right.at[low], pts_send.at[5], pts_recv.at[5], x_left)
    core_right = remote(near_right, near_right, pts_send.at[6], pts_recv.at[6], other_core)
    far_low.start()
    core_right.start()

    z_arrived(12)
    to_far(12)
    along_z(12, 15, 4, 0)
    for place, d in ((7, 3), (0, 2), (4, 1), (8, -1)):
        along_z(12, place, d)
    z_arrived(14)
    to_far(14)
    along_z(14, 15, -4, 1)
    for place, d in ((11, -3), (3, -2), (10, -1), (6, 1)):
        along_z(14, place, d)
    to_sides(12, 1, 3)
    to_sides(14, 1, 3)

    for place in (12, 13, 14):
        wait_bytes(cand.at[1, place], far_recv.at[place - 12])
    far_along_z(12, 15, 1, 3, 4, 0)
    far_along_z(14, 15, 1, 3, -4, 1)
    far_along_z(12, 7, 1, 1, 3)
    far_along_z(14, 11, 1, 2, -3)
    far_along_z(12, 0, 2, 0, 2)
    far_along_z(13, 2, 2, 0, -2)
    far_along_z(12, 4, 3, 1, 1)
    far_along_z(12, 8, 3, 2, -1)

    far_top.wait_recv()
    far_low.wait_recv()
    far = pall.at[slot_far]
    core_far = remote(far, far, pts_send.at[7], pts_recv.at[7], other_core)
    core_far.start()

    for group in range(3):
        z_arrived(*range(4 * group, 4 * group + 4))
        to_sides(4 * group, 4, group)
    half_block = cand.at[0, 15, :, pl.ds(0, width // 2)]
    wait_bytes(half_block, z_block_recv.at[15])
    wait_bytes(half_block, z_block_recv.at[16])
    to_sides(15, 1, 3)

    def absorb(first, count):
        for group in range(first, first + count):
            wait_bytes(cand.at[pl.ds(2, 2), pl.ds(0, 4)], y_recv.at[group])
            wait_bytes(cand.at[1, pl.ds(0, 4 if group < 3 else 1)], far_z_recv.at[group])
        blocks = XS * 4 * count
        rows = cand[:, 4 * first : 4 * (first + count)].reshape(blocks, BLK, width)
        half = jnp.zeros((blocks, BLK, npd), F32)
        for t in range(width // npd):
            piece = rows[:, :, t * npd : (t + 1) * npd].astype(F32)
            half = half + piece * piece
        half = 0.5 * jnp.sum(half, axis=2, keepdims=True)
        flat = rows.reshape(blocks * BLK, width)
        for j in range(SUBS // 2):
            group = jnp.concatenate([pall[2 * j], pall[2 * j + 1]], axis=1)
            dots = jnp.dot(flat, group, preferred_element_type=F32)
            best = jnp.min(half - dots.reshape(blocks, BLK, 2 * npd), axis=0)
            mins[j] = best if first == 0 else jnp.minimum(mins[j], best)

    pts_core.wait_recv()
    core_left.wait_recv()
    core_right.wait_recv()
    core_far.wait_recv()
    absorb(0, 3)
    for b in range(SUBS):
        wide = pall[b].astype(F32)
        squares[b : b + 1, :] = jnp.sum(wide * wide, axis=0, keepdims=True)
    absorb(3, 1)

    for j in range(SUBS // 2):
        for r in range(ROUNDS):
            low_r = jnp.min(mins[j, r * SHARE : (r + 1) * SHARE, :], axis=0, keepdims=True)
            for h in range(2):
                line[me, r, 2 * j + h : 2 * j + h + 1, :] = low_r[:, h * npd : (h + 1) * npd]

    for device in x_line:
        remote(line.at[me], line.at[me], line_send, line_recv, device).start()
    wait_bytes(line.at[pl.ds(0, SUBS - 1)], line_recv)

    lanes = lax.broadcasted_iota(jnp.int32, (1, npd), 1)
    least = None
    total = jnp.zeros((1, npd), F32)
    for r in range(ROUNDS):
        now = jnp.min(line[:, r], axis=0)
        least = now if least is None else jnp.minimum(least, now)
        dist = jnp.maximum(squares[...] + 2.0 * least, 0.0)
        near[r] = dist
        part = jnp.sum(jnp.sum(dist, axis=0, keepdims=True), axis=1, keepdims=True)
        total = jnp.where(lanes == r, part, total)

    zsum[0] = total

    for d in (8, 7, 9, 6, 10, 5, 11, 4, 12, 3, 13, 2, 14, 1, 15):
        remote(zsum.at[0], zsum.at[ZS - d], z_send, z_recv, at_z(d)).start()
    wait_bytes(slots.at[pl.ds(0, SUBS - 1)], slots_send)
    wait_bytes(cand.at[0, pl.ds(0, 15)], z_block_send)
    wait_bytes(cand.at[pl.ds(0, 2)], y_send)
    wait_bytes(cand.at[0, pl.ds(0, 3)], far_send)
    wait_bytes(cand.at[0, pl.ds(0, 13)], far_z_send)
    for copy in (pts_right, pts_left, pts_core, far_top, core_left, far_low, core_right, core_far):
        copy.wait_send()
    wait_bytes(line.at[pl.ds(0, SUBS - 1)], line_send)
    wait_bytes(zsum.at[pl.ds(0, ZS - 1)], z_recv)
    ysum[0] = jnp.sum(zsum[...], axis=0)
    for d in (1, 3, 2):
        remote(ysum.at[0], ysum.at[XS - d], c_send, c_recv, y_to[d]).start()
    wait_bytes(ysum.at[pl.ds(0, XS - 1)], c_recv)
    cost = jnp.sum(ysum[...], axis=0)
    for r in range(ROUNDS):
        cost_r = jnp.sum(jnp.where(lanes == r, cost, 0.0), axis=1, keepdims=True)
        out_ref[r : r + 1, :] = npts * near[r, pl.ds(me, 1), :] / cost_r
    wait_bytes(zsum.at[pl.ds(0, ZS - 1)], z_send)
    wait_bytes(ysum.at[pl.ds(0, XS - 1)], c_send)


def shards(points, cand_rows, cand_count):
    npd, width = points.shape
    npts = float(npd * lax.axis_size(("dp", "sub")))
    dma = pltpu.SemaphoreType.DMA
    operands = (cand_rows, cand_count.reshape(1, ROUNDS), points)
    return pl.pallas_call(
        lambda *refs: kernel(npts, *refs),
        out_shape=jax.ShapeDtypeStruct((ROUNDS, npd), F32),
        in_specs=[
            pl.BlockSpec(memory_space=pl.ANY),
            pl.BlockSpec(memory_space=pl.ANY),
            pl.BlockSpec(memory_space=pl.ANY),
        ],
        out_specs=pl.BlockSpec(memory_space=pltpu.VMEM),
        scratch_shapes=[
            pltpu.SMEM((ROUNDS, SLOTS), jnp.int32),
            pltpu.SMEM((1, ROUNDS), jnp.int32),
            pltpu.VMEM((npd, width), jnp.bfloat16),
            pltpu.VMEM((SUBS, RAW, width), jnp.bfloat16),
            pltpu.VMEM((XS, ZS, BLK, width), jnp.bfloat16),
            pltpu.VMEM((SUBS, width, npd), jnp.bfloat16),
            pltpu.VMEM((SUBS // 2, BLK, 2 * npd), F32),
            pltpu.VMEM((SUBS, npd), F32),
            pltpu.VMEM((SUBS, ROUNDS, SUBS, npd), F32),
            pltpu.VMEM((ROUNDS, SUBS, npd), F32),
            pltpu.VMEM((ZS, 1, npd), F32),
            pltpu.VMEM((XS, 1, npd), F32),
            dma((3,)),
            dma,
            dma,
            dma,
            dma,
            dma((17,)),
            dma((4,)),
            dma,
            dma,
            dma((3,)),
            dma((4,)),
            dma((8,)),
            dma((8,)),
            dma,
            dma,
            dma,
            dma,
            dma,
            dma,
        ],
        compiler_params=pltpu.CompilerParams(
            collective_id=0, has_side_effects=True, vmem_limit_bytes=40 * 1024 * 1024
        ),
        cost_estimate=pl.CostEstimate(
            flops=2 * 1024 * 1024 * width, bytes_accessed=npd * width * 2, transcendentals=0
        ),
    )(*(pltpu.with_memory_space_constraint(value, pltpu.HBM) for value in operands))


def solution(mesh):
    in_specs = (P(("dp", "sub"), None), P(None, ("dp", "sub")), P(None, ("dp", "sub")))
    out_specs = P(None, ("dp", "sub"))
    return jax.shard_map(shards, mesh=mesh, in_specs=in_specs, out_specs=out_specs, check_vma=False)
```

```python
import jax
import jax.numpy as jnp
from jax import lax
from jax.experimental import pallas as pl
from jax.experimental.pallas import tpu as pltpu
from jax.sharding import PartitionSpec as P

ROUNDS = 3
SLOTS = 4
XS = 4
ZS = 16
YS = 4
SUBS = 8
RAW = 16
BLK = 8
SHARE = 2
NEAR = 9
MESH = pl.DeviceIdType.MESH
F32 = jnp.float32
INF = float("inf")


def kernel(
    npts,
    rows_in,
    counts_in,
    points_ref,
    out_ref,
    rows_ref,
    cnt_ref,
    raw,
    slots,
    cand,
    pall,
    mins,
    squares,
    line,
    near,
    zsum,
    ysum,
    local_sem,
    slots_send,
    slots_recv,
    z_block_send,
    y_send,
    z_block_recv,
    y_recv,
    far_send,
    far_z_send,
    far_recv,
    far_z_recv,
    pts_send,
    pts_recv,
    line_send,
    line_recv,
    z_send,
    z_recv,
    c_send,
    c_recv,
):
    dp = lax.axis_index("dp")
    sub = lax.axis_index("sub")
    x, z = lax.div(dp, ZS), lax.rem(dp, ZS)
    y, core = lax.div(sub, 2), lax.rem(sub, 2)
    npd, width = points_ref.shape

    def at_x(d):
        return (lax.rem(x + d, XS) * ZS + z, sub)

    def at_z(d):
        return (x * ZS + lax.rem(z + d, ZS), sub)

    def at_y(d):
        return (dp, lax.rem(y + d, YS) * 2 + core)

    other_core = (dp, y * 2 + (1 - core))
    z_to = {d: at_z(d % ZS) for d in (1, -1, 2, -2, 3, -3, 4, -4)}
    y_to = {d: at_y(d) for d in (1, 2, 3)}
    me = x * 2 + core
    x_right, x_left = at_x(1), at_x(3)

    own_points = pltpu.make_async_copy(points_ref, raw, local_sem.at[0])
    own_points.start()
    own_rows = pltpu.make_async_copy(rows_in, rows_ref, local_sem.at[1])
    own_rows.start()
    own_counts = pltpu.make_async_copy(counts_in, cnt_ref, local_sem.at[2])
    own_counts.start()
    barrier = pltpu.get_barrier_semaphore()
    far_first = ((2, 0), (2, 1), (1, 0), (3, 0), (1, 1), (3, 1), (0, 1))
    y_line = [(dp, lax.rem(y + d, YS) * 2 + (1 - core if other else core)) for d, other in far_first]
    x_line = [(lax.rem(x + d, XS) * ZS + z, y * 2 + (1 - core if other else core)) for d, other in far_first]
    partners = [*z_to.values(), *y_line, *x_line[:-1]]
    for device in partners:
        pl.semaphore_signal(barrier, inc=1, device_id=device, device_id_type=MESH)

    row = lax.broadcasted_iota(jnp.int32, (RAW, npd), 0)
    lane = lax.broadcasted_iota(jnp.int32, (RAW, npd), 1)
    here = lax.broadcasted_iota(jnp.int32, (npd, npd), 0)
    there = lax.broadcasted_iota(jnp.int32, (npd, npd), 1)
    same_round = (here & (RAW - 1)) == ROUNDS * SLOTS + ((there & (RAW - 1)) >> 2)
    before = jnp.where(same_round & ((here >> 4) < (there >> 4)), 1.0, 0.0)
    itself = jnp.where(same_round & ((here >> 4) == (there >> 4)), 1.0, 0.0)
    slot = lane & (RAW - 1)
    slot_round = jnp.where(slot < ROUNDS * SLOTS, slot >> 2, -1)
    slot_index = (slot & (SLOTS - 1)).astype(F32)
    wanted = (SHARE * sub + (row & 1)).astype(F32)
    wanted_round = slot_round == (row >> 1)
    own_rows.wait()
    own_counts.wait()
    target = jnp.full((RAW, npd), -1, jnp.int32)
    counts = jnp.zeros((RAW, npd), F32)
    for r in range(ROUNDS):
        counts = jnp.where(row == ROUNDS * SLOTS + r, cnt_ref[0, r].astype(F32), counts)
        for i in range(SLOTS):
            target = jnp.where(row == r * SLOTS + i, rows_ref[r, i], target)
    pick = jnp.where(lane == target, 1.0, 0.0).astype(jnp.bfloat16)
    own_points.wait()
    mine = raw[...]
    block = jnp.dot(pick, mine, preferred_element_type=F32)
    slots[sub, :, :npd] = (block[:, :npd] + counts).astype(jnp.bfloat16)
    slots[sub, :, npd:] = block[:, npd:].astype(jnp.bfloat16)

    pl.semaphore_wait(barrier, len(partners))

    def remote(src, dst, send, recv, device):
        return pltpu.make_async_remote_copy(
            src_ref=src, dst_ref=dst, send_sem=send, recv_sem=recv, device_id=device, device_id_type=MESH
        )

    def to_sides(place, count, group):
        for d, column in ((1, 2), (3, 3)):
            src, dst = cand.at[0, pl.ds(place, count)], cand.at[column, pl.ds(place, count)]
            remote(src, dst, y_send, y_recv.at[group], y_to[d]).start()

    def to_far(place):
        remote(cand.at[0, place], cand.at[1, place], far_send, far_recv.at[place - 6], y_to[2]).start()

    def far_along_z(src, place, count, group, d, lanes=None):
        src, dst = cand.at[1, pl.ds(src, count)], cand.at[1, pl.ds(place, count)]
        if lanes is not None:
            part = pl.ds(lanes * (width // 2), width // 2)
            src, dst = src.at[:, :, part], dst.at[:, :, part]
        remote(src, dst, far_z_send, far_z_recv.at[group], z_to[d]).start()

    def along_z(src, place, d, lanes=None):
        if lanes is None:
            src, dst = cand.at[0, src], cand.at[0, place]
        else:
            part = pl.ds(lanes * (width // 2), width // 2)
            src, dst = cand.at[0, src, :, part], cand.at[0, place, :, part]
        remote(src, dst, z_block_send, z_block_recv.at[place + (lanes or 0)], z_to[d]).start()

    def z_arrived(*places):
        for place in places:
            wait_bytes(cand.at[0, place], z_block_recv.at[place])

    def wait_bytes(ref, sem):
        pltpu.make_async_copy(ref, ref, sem).wait()

    for device in y_line:
        remote(slots.at[sub], slots.at[sub], slots_send, slots_recv, device).start()
    pall[me] = mine.T
    slot_right, slot_left, slot_far = (lax.rem(x + d, XS) * 2 + core for d in (1, 3, 2))
    top, low = pl.ds(0, width // 2), pl.ds(width // 2, width // 2)
    mine_at = pall.at[me]
    pts_right = remote(mine_at, mine_at, pts_send.at[0], pts_recv.at[0], x_right)
    pts_left = remote(mine_at, mine_at, pts_send.at[1], pts_recv.at[1], x_left)
    pts_core = remote(mine_at, mine_at, pts_send.at[2], pts_recv.at[2], other_core)
    pts_right.start()
    pts_left.start()
    pts_core.start()

    wait_bytes(slots.at[pl.ds(0, SUBS - 1)], slots_recv)
    flat = slots[...].reshape(SUBS * RAW, width)
    known = flat[:, :npd].astype(F32)
    offset = jnp.sum(known * before, axis=0, keepdims=True)
    count = jnp.sum(known * itself, axis=0, keepdims=True)
    choice = wanted_round & (slot_index < count) & (offset + slot_index == wanted)
    share = jnp.dot(jnp.where(choice, 1.0, 0.0).astype(jnp.bfloat16), flat, preferred_element_type=F32)
    cand[0, 7] = share[:BLK].astype(jnp.bfloat16)

    along_z(7, 6, 4)
    along_z(7, 8, -4)
    to_far(7)
    for place, d in ((0, 2), (1, -2), (2, 1), (5, -1)):
        along_z(7, place, d)
    to_sides(7, 1, 0)

    pts_right.wait_recv()
    near_left = pall.at[slot_left]
    far_top = remote(near_left.at[top], near_left.at[top], pts_send.at[3], pts_recv.at[3], x_right)
    core_left = remote(near_left, near_left, pts_send.at[4], pts_recv.at[4], other_core)
    far_top.start()
    core_left.start()
    pts_left.wait_recv()
    near_right = pall.at[slot_right]
    far_low = remote(near_right.at[low], near_right.at[low], pts_send.at[5], pts_recv.at[5], x_left)
    core_right = remote(near_right, near_right, pts_send.at[6], pts_recv.at[6], other_core)
    far_low.start()
    core_right.start()

    z_arrived(6)
    to_far(6)
    along_z(6, 15, 4, 0)
    for place, d in ((13, 3), (9, 2), (11, 1), (4, -1)):
        along_z(6, place, d)
    z_arrived(8)
    to_far(8)
    along_z(8, 15, -4, 1)
    for place, d in ((14, -3), (10, -2), (12, -1), (3, 1)):
        along_z(8, place, d)
    to_sides(6, 1, 0)
    to_sides(8, 1, 0)

    for place in (6, 7, 8):
        wait_bytes(cand.at[1, place], far_recv.at[place - 6])
    far_along_z(6, 15, 1, 1, 4, 0)
    far_along_z(8, 15, 1, 1, -4, 1)
    far_along_z(6, 13, 1, 1, 3)
    far_along_z(8, 14, 1, 1, -3)
    far_along_z(6, 9, 1, 1, 2)
    far_along_z(8, 10, 1, 1, -2)
    far_along_z(6, 11, 1, 1, 1)
    far_along_z(8, 12, 1, 1, -1)
    far_along_z(7, 0, 1, 0, 2)
    far_along_z(7, 1, 1, 0, -2)
    far_along_z(7, 2, 2, 0, 1)
    far_along_z(6, 4, 2, 0, -1)

    far_top.wait_recv()
    far_low.wait_recv()
    far = pall.at[slot_far]
    core_far = remote(far, far, pts_send.at[7], pts_recv.at[7], other_core)
    core_far.start()

    z_arrived(0, 1, 2, 3, 4, 5)
    to_sides(0, 6, 0)
    z_arrived(9, 10, 11, 12, 13, 14)
    to_sides(9, 6, 1)
    half_block = cand.at[0, 15, :, pl.ds(0, width // 2)]
    wait_bytes(half_block, z_block_recv.at[15])
    wait_bytes(half_block, z_block_recv.at[16])
    to_sides(15, 1, 1)

    def absorb(first, count):
        blocks = XS * count
        rows = cand[:, first : first + count].reshape(blocks, BLK, width)
        half = jnp.zeros((blocks, BLK, npd), F32)
        for t in range(width // npd):
            piece = rows[:, :, t * npd : (t + 1) * npd].astype(F32)
            half = half + piece * piece
        half = 0.5 * jnp.sum(half, axis=2, keepdims=True)
        flat = rows.reshape(blocks * BLK, width)
        for j in range(SUBS // 2):
            group = jnp.concatenate([pall[2 * j], pall[2 * j + 1]], axis=1)
            dots = jnp.dot(flat, group, preferred_element_type=F32)
            best = jnp.min(half - dots.reshape(blocks, BLK, 2 * npd), axis=0)
            mins[j] = best if first == 0 else jnp.minimum(mins[j], best)

    pts_core.wait_recv()
    core_left.wait_recv()
    core_right.wait_recv()
    core_far.wait_recv()
    for b in range(SUBS):
        wide = pall[b].astype(F32)
        squares[b : b + 1, :] = jnp.sum(wide * wide, axis=0, keepdims=True)
    wait_bytes(cand.at[pl.ds(2, 2), pl.ds(0, NEAR)], y_recv.at[0])
    wait_bytes(cand.at[1, pl.ds(0, 6)], far_z_recv.at[0])
    absorb(0, NEAR)
    wait_bytes(cand.at[pl.ds(2, 2), pl.ds(NEAR, ZS - NEAR)], y_recv.at[1])
    wait_bytes(cand.at[1, pl.ds(NEAR, ZS - NEAR)], far_z_recv.at[1])
    absorb(NEAR, ZS - NEAR)

    for j in range(SUBS // 2):
        for r in range(ROUNDS):
            low_r = jnp.min(mins[j, r * SHARE : (r + 1) * SHARE, :], axis=0, keepdims=True)
            for h in range(2):
                line[me, r, 2 * j + h : 2 * j + h + 1, :] = low_r[:, h * npd : (h + 1) * npd]

    for device in x_line:
        remote(line.at[me], line.at[me], line_send, line_recv, device).start()
    wait_bytes(line.at[pl.ds(0, SUBS - 1)], line_recv)

    lanes = lax.broadcasted_iota(jnp.int32, (1, npd), 1)
    least = None
    total = jnp.zeros((1, npd), F32)
    for r in range(ROUNDS):
        now = jnp.min(line[:, r], axis=0)
        least = now if least is None else jnp.minimum(least, now)
        dist = jnp.maximum(squares[...] + 2.0 * least, 0.0)
        near[r] = dist
        part = jnp.sum(jnp.sum(dist, axis=0, keepdims=True), axis=1, keepdims=True)
        total = jnp.where(lanes == r, part, total)

    zsum[0] = total

    for d in (8, 7, 9, 6, 10, 5, 11, 4, 12, 3, 13, 2, 14, 1, 15):
        remote(zsum.at[0], zsum.at[ZS - d], z_send, z_recv, at_z(d)).start()
    wait_bytes(slots.at[pl.ds(0, SUBS - 1)], slots_send)
    wait_bytes(cand.at[0, pl.ds(0, 15)], z_block_send)
    wait_bytes(cand.at[pl.ds(0, 2)], y_send)
    wait_bytes(cand.at[0, pl.ds(0, 3)], far_send)
    wait_bytes(cand.at[0, pl.ds(0, 13)], far_z_send)
    for copy in (pts_right, pts_left, pts_core, far_top, core_left, far_low, core_right, core_far):
        copy.wait_send()
    wait_bytes(line.at[pl.ds(0, SUBS - 1)], line_send)
    wait_bytes(zsum.at[pl.ds(0, ZS - 1)], z_recv)
    ysum[0] = jnp.sum(zsum[...], axis=0)
    for d in (1, 3, 2):
        remote(ysum.at[0], ysum.at[XS - d], c_send, c_recv, y_to[d]).start()
    wait_bytes(ysum.at[pl.ds(0, XS - 1)], c_recv)
    cost = jnp.sum(ysum[...], axis=0)
    for r in range(ROUNDS):
        cost_r = jnp.sum(jnp.where(lanes == r, cost, 0.0), axis=1, keepdims=True)
        out_ref[r : r + 1, :] = npts * near[r, pl.ds(me, 1), :] / cost_r
    wait_bytes(zsum.at[pl.ds(0, ZS - 1)], z_send)
    wait_bytes(ysum.at[pl.ds(0, XS - 1)], c_send)


def shards(points, cand_rows, cand_count):
    npd, width = points.shape
    npts = float(npd * lax.axis_size(("dp", "sub")))
    dma = pltpu.SemaphoreType.DMA
    operands = (cand_rows, cand_count.reshape(1, ROUNDS), points)
    return pl.pallas_call(
        lambda *refs: kernel(npts, *refs),
        out_shape=jax.ShapeDtypeStruct((ROUNDS, npd), F32),
        in_specs=[
            pl.BlockSpec(memory_space=pl.ANY),
            pl.BlockSpec(memory_space=pl.ANY),
            pl.BlockSpec(memory_space=pl.ANY),
        ],
        out_specs=pl.BlockSpec(memory_space=pltpu.VMEM),
        scratch_shapes=[
            pltpu.SMEM((ROUNDS, SLOTS), jnp.int32),
            pltpu.SMEM((1, ROUNDS), jnp.int32),
            pltpu.VMEM((npd, width), jnp.bfloat16),
            pltpu.VMEM((SUBS, RAW, width), jnp.bfloat16),
            pltpu.VMEM((XS, ZS, BLK, width), jnp.bfloat16),
            pltpu.VMEM((SUBS, width, npd), jnp.bfloat16),
            pltpu.VMEM((SUBS // 2, BLK, 2 * npd), F32),
            pltpu.VMEM((SUBS, npd), F32),
            pltpu.VMEM((SUBS, ROUNDS, SUBS, npd), F32),
            pltpu.VMEM((ROUNDS, SUBS, npd), F32),
            pltpu.VMEM((ZS, 1, npd), F32),
            pltpu.VMEM((XS, 1, npd), F32),
            dma((3,)),
            dma,
            dma,
            dma,
            dma,
            dma((17,)),
            dma((2,)),
            dma,
            dma,
            dma((3,)),
            dma((2,)),
            dma((8,)),
            dma((8,)),
            dma,
            dma,
            dma,
            dma,
            dma,
            dma,
        ],
        compiler_params=pltpu.CompilerParams(
            collective_id=0, has_side_effects=True, vmem_limit_bytes=40 * 1024 * 1024
        ),
        cost_estimate=pl.CostEstimate(
            flops=2 * 1024 * 1024 * width, bytes_accessed=npd * width * 2, transcendentals=0
        ),
    )(*(pltpu.with_memory_space_constraint(value, pltpu.HBM) for value in operands))


def solution(mesh):
    in_specs = (P(("dp", "sub"), None), P(None, ("dp", "sub")), P(None, ("dp", "sub")))
    out_specs = P(None, ("dp", "sub"))
    return jax.shard_map(shards, mesh=mesh, in_specs=in_specs, out_specs=out_specs, check_vma=False)
```

```python
import jax
import jax.numpy as jnp
from jax import lax
from jax.experimental import pallas as pl
from jax.experimental.pallas import tpu as pltpu
from jax.sharding import PartitionSpec as P

ROUNDS = 3
SLOTS = 4
XS = 4
ZS = 16
YS = 4
SUBS = 8
RAW = 16
BLK = 8
SHARE = 2
NEAR = 9
PLANE = sorted(
    ((dx, dy, other) for dx in range(XS) for dy in range(YS) for other in range(2) if dx or dy or other),
    key=lambda p: -(min(p[0], XS - p[0]) + min(p[1], YS - p[1]) + 0.5 * p[2]),
)
MESH = pl.DeviceIdType.MESH
F32 = jnp.float32
INF = float("inf")


def kernel(
    npts,
    rows_in,
    counts_in,
    points_ref,
    out_ref,
    rows_ref,
    cnt_ref,
    raw,
    slots,
    cand,
    pall,
    mins,
    squares,
    found,
    line,
    zsum,
    psum,
    local_sem,
    slots_send,
    slots_recv,
    z_block_send,
    y_send,
    z_block_recv,
    y_recv,
    far_send,
    far_z_send,
    far_recv,
    far_z_recv,
    pts_send,
    pts_recv,
    line_send,
    line_recv,
    z_send,
    z_recv,
    p_send,
    p_recv,
):
    dp = lax.axis_index("dp")
    sub = lax.axis_index("sub")
    x, z = lax.div(dp, ZS), lax.rem(dp, ZS)
    y, core = lax.div(sub, 2), lax.rem(sub, 2)
    npd, width = points_ref.shape

    def at_x(d):
        return (lax.rem(x + d, XS) * ZS + z, sub)

    def at_z(d):
        return (x * ZS + lax.rem(z + d, ZS), sub)

    def at_y(d):
        return (dp, lax.rem(y + d, YS) * 2 + core)

    other_core = (dp, y * 2 + (1 - core))
    z_to = {d: at_z(d % ZS) for d in (1, -1, 2, -2, 3, -3, 4, -4)}
    y_to = {d: at_y(d) for d in (1, 2, 3)}
    me = x * 2 + core
    x_right, x_left = at_x(1), at_x(3)

    own_points = pltpu.make_async_copy(points_ref, raw, local_sem.at[0])
    own_points.start()
    own_rows = pltpu.make_async_copy(rows_in, rows_ref, local_sem.at[1])
    own_rows.start()
    own_counts = pltpu.make_async_copy(counts_in, cnt_ref, local_sem.at[2])
    own_counts.start()
    barrier = pltpu.get_barrier_semaphore()
    far_first = ((2, 0), (2, 1), (1, 0), (3, 0), (1, 1), (3, 1), (0, 1))
    y_line = [(dp, lax.rem(y + d, YS) * 2 + (1 - core if other else core)) for d, other in far_first]
    x_line = [(lax.rem(x + d, XS) * ZS + z, y * 2 + (1 - core if other else core)) for d, other in far_first]
    x_places = [lax.rem(x + d, XS) * 2 + (1 - core if other else core) for d, other in far_first]
    partners = [*z_to.values(), *y_line, *x_line[:-1]]
    for device in partners:
        pl.semaphore_signal(barrier, inc=1, device_id=device, device_id_type=MESH)

    row = lax.broadcasted_iota(jnp.int32, (RAW, npd), 0)
    lane = lax.broadcasted_iota(jnp.int32, (RAW, npd), 1)
    here = lax.broadcasted_iota(jnp.int32, (npd, npd), 0)
    there = lax.broadcasted_iota(jnp.int32, (npd, npd), 1)
    same_round = (here & (RAW - 1)) == ROUNDS * SLOTS + ((there & (RAW - 1)) >> 2)
    before = jnp.where(same_round & ((here >> 4) < (there >> 4)), 1.0, 0.0)
    itself = jnp.where(same_round & ((here >> 4) == (there >> 4)), 1.0, 0.0)
    slot = lane & (RAW - 1)
    slot_round = jnp.where(slot < ROUNDS * SLOTS, slot >> 2, -1)
    slot_index = (slot & (SLOTS - 1)).astype(F32)
    wanted = (SHARE * sub + (row & 1)).astype(F32)
    wanted_round = slot_round == (row >> 1)
    own_rows.wait()
    own_counts.wait()
    target = jnp.full((RAW, npd), -1, jnp.int32)
    counts = jnp.zeros((RAW, npd), F32)
    for r in range(ROUNDS):
        counts = jnp.where(row == ROUNDS * SLOTS + r, cnt_ref[0, r].astype(F32), counts)
        for i in range(SLOTS):
            target = jnp.where(row == r * SLOTS + i, rows_ref[r, i], target)
    pick = jnp.where(lane == target, 1.0, 0.0).astype(jnp.bfloat16)
    own_points.wait()
    mine = raw[...]
    block = jnp.dot(pick, mine, preferred_element_type=F32)
    slots[sub, :, :npd] = (block[:, :npd] + counts).astype(jnp.bfloat16)
    slots[sub, :, npd:] = block[:, npd:].astype(jnp.bfloat16)

    pl.semaphore_wait(barrier, len(partners))

    def remote(src, dst, send, recv, device):
        return pltpu.make_async_remote_copy(
            src_ref=src, dst_ref=dst, send_sem=send, recv_sem=recv, device_id=device, device_id_type=MESH
        )

    def to_sides(place, count, group):
        for d, column in ((1, 2), (3, 3)):
            src, dst = cand.at[0, pl.ds(place, count)], cand.at[column, pl.ds(place, count)]
            remote(src, dst, y_send, y_recv.at[group], y_to[d]).start()

    def to_far(place):
        remote(cand.at[0, place], cand.at[1, place], far_send, far_recv.at[place - 6], y_to[2]).start()

    def far_along_z(src, place, count, group, d, lanes=None):
        src, dst = cand.at[1, pl.ds(src, count)], cand.at[1, pl.ds(place, count)]
        if lanes is not None:
            part = pl.ds(lanes * (width // 2), width // 2)
            src, dst = src.at[:, :, part], dst.at[:, :, part]
        remote(src, dst, far_z_send, far_z_recv.at[group], z_to[d]).start()

    def along_z(src, place, d, lanes=None):
        if lanes is None:
            src, dst = cand.at[0, src], cand.at[0, place]
        else:
            part = pl.ds(lanes * (width // 2), width // 2)
            src, dst = cand.at[0, src, :, part], cand.at[0, place, :, part]
        remote(src, dst, z_block_send, z_block_recv.at[place + (lanes or 0)], z_to[d]).start()

    def z_arrived(*places):
        for place in places:
            wait_bytes(cand.at[0, place], z_block_recv.at[place])

    def wait_bytes(ref, sem):
        pltpu.make_async_copy(ref, ref, sem).wait()

    for device in y_line:
        remote(slots.at[sub], slots.at[sub], slots_send, slots_recv, device).start()
    pall[me] = mine.T
    slot_right, slot_left, slot_far = (lax.rem(x + d, XS) * 2 + core for d in (1, 3, 2))
    top, low = pl.ds(0, width // 2), pl.ds(width // 2, width // 2)
    mine_at = pall.at[me]
    pts_right = remote(mine_at, mine_at, pts_send.at[0], pts_recv.at[0], x_right)
    pts_left = remote(mine_at, mine_at, pts_send.at[1], pts_recv.at[1], x_left)
    pts_core = remote(mine_at, mine_at, pts_send.at[2], pts_recv.at[2], other_core)
    pts_right.start()
    pts_left.start()
    pts_core.start()

    wait_bytes(slots.at[pl.ds(0, SUBS - 1)], slots_recv)
    flat = slots[...].reshape(SUBS * RAW, width)
    known = flat[:, :npd].astype(F32)
    offset = jnp.sum(known * before, axis=0, keepdims=True)
    count = jnp.sum(known * itself, axis=0, keepdims=True)
    choice = wanted_round & (slot_index < count) & (offset + slot_index == wanted)
    share = jnp.dot(jnp.where(choice, 1.0, 0.0).astype(jnp.bfloat16), flat, preferred_element_type=F32)
    cand[0, 7] = share[:BLK].astype(jnp.bfloat16)

    along_z(7, 6, 4)
    along_z(7, 8, -4)
    to_far(7)
    for place, d in ((0, 2), (1, -2), (2, 1), (5, -1)):
        along_z(7, place, d)
    to_sides(7, 1, 0)

    pts_right.wait_recv()
    near_left = pall.at[slot_left]
    far_top = remote(near_left.at[top], near_left.at[top], pts_send.at[3], pts_recv.at[3], x_right)
    core_left = remote(near_left, near_left, pts_send.at[4], pts_recv.at[4], other_core)
    far_top.start()
    core_left.start()
    pts_left.wait_recv()
    near_right = pall.at[slot_right]
    far_low = remote(near_right.at[low], near_right.at[low], pts_send.at[5], pts_recv.at[5], x_left)
    core_right = remote(near_right, near_right, pts_send.at[6], pts_recv.at[6], other_core)
    far_low.start()
    core_right.start()

    z_arrived(6)
    to_far(6)
    along_z(6, 15, 4, 0)
    for place, d in ((13, 3), (9, 2), (11, 1), (4, -1)):
        along_z(6, place, d)
    z_arrived(8)
    to_far(8)
    along_z(8, 15, -4, 1)
    for place, d in ((14, -3), (10, -2), (12, -1), (3, 1)):
        along_z(8, place, d)
    to_sides(6, 1, 0)
    to_sides(8, 1, 0)

    for place in (6, 7, 8):
        wait_bytes(cand.at[1, place], far_recv.at[place - 6])
    far_along_z(6, 15, 1, 1, 4, 0)
    far_along_z(8, 15, 1, 1, -4, 1)
    far_along_z(6, 13, 1, 1, 3)
    far_along_z(8, 14, 1, 1, -3)
    far_along_z(6, 9, 1, 1, 2)
    far_along_z(8, 10, 1, 1, -2)
    far_along_z(6, 11, 1, 1, 1)
    far_along_z(8, 12, 1, 1, -1)
    far_along_z(7, 0, 1, 0, 2)
    far_along_z(7, 1, 1, 0, -2)
    far_along_z(7, 2, 2, 0, 1)
    far_along_z(6, 4, 2, 0, -1)

    far_top.wait_recv()
    far_low.wait_recv()
    far = pall.at[slot_far]
    core_far = remote(far, far, pts_send.at[7], pts_recv.at[7], other_core)
    core_far.start()

    z_arrived(0, 1, 2, 3, 4, 5)
    to_sides(0, 6, 0)
    z_arrived(9, 10, 11, 12, 13, 14)
    to_sides(9, 6, 1)
    half_block = cand.at[0, 15, :, pl.ds(0, width // 2)]
    wait_bytes(half_block, z_block_recv.at[15])
    wait_bytes(half_block, z_block_recv.at[16])
    to_sides(15, 1, 1)

    def absorb(first, count):
        blocks = XS * count
        rows = cand[:, first : first + count].reshape(blocks, BLK, width)
        half = jnp.zeros((blocks, BLK, npd), F32)
        for t in range(width // npd):
            piece = rows[:, :, t * npd : (t + 1) * npd].astype(F32)
            half = half + piece * piece
        half = 0.5 * jnp.sum(half, axis=2, keepdims=True)
        flat = rows.reshape(blocks * BLK, width)
        for j in range(SUBS // 2):
            group = jnp.concatenate([pall[2 * j], pall[2 * j + 1]], axis=1)
            dots = jnp.dot(flat, group, preferred_element_type=F32)
            best = jnp.min(half - dots.reshape(blocks, BLK, 2 * npd), axis=0)
            mins[j] = best if first == 0 else jnp.minimum(mins[j], best)

    pts_core.wait_recv()
    core_left.wait_recv()
    core_right.wait_recv()
    core_far.wait_recv()
    wide = pall[me].astype(F32)
    squares[...] = jnp.sum(wide * wide, axis=0, keepdims=True)
    found[...] = jnp.zeros(found.shape, F32)
    wait_bytes(cand.at[pl.ds(2, 2), pl.ds(0, NEAR)], y_recv.at[0])
    wait_bytes(cand.at[1, pl.ds(0, 6)], far_z_recv.at[0])
    absorb(0, NEAR)
    wait_bytes(cand.at[pl.ds(2, 2), pl.ds(NEAR, ZS - NEAR)], y_recv.at[1])
    wait_bytes(cand.at[1, pl.ds(NEAR, ZS - NEAR)], far_z_recv.at[1])
    absorb(NEAR, ZS - NEAR)

    for j in range(SUBS // 2):
        for r in range(ROUNDS):
            low_r = jnp.min(mins[j, r * SHARE : (r + 1) * SHARE, :], axis=0, keepdims=True)
            for h in range(2):
                found[2 * j + h, r : r + 1, :] = low_r[:, h * npd : (h + 1) * npd]

    for device, place in zip(x_line, x_places):
        remote(found.at[place], line.at[me], line_send, line_recv, device).start()
    line[me] = found[me]
    wait_bytes(line.at[pl.ds(0, SUBS - 1)], line_recv)

    lanes = lax.broadcasted_iota(jnp.int32, (1, npd), 1)
    best = jnp.min(line[...], axis=0)
    least = None
    total = jnp.zeros((1, npd), F32)
    near = []
    for r in range(ROUNDS):
        now = best[r : r + 1, :]
        least = now if least is None else jnp.minimum(least, now)
        dist = jnp.maximum(squares[...] + 2.0 * least, 0.0)
        near.append(dist)
        total = jnp.where(lanes == r, jnp.sum(dist, axis=1, keepdims=True), total)

    zsum[0] = total
    for d in (8, 7, 9, 6, 10, 5, 11, 4, 12, 3, 13, 2, 14, 1, 15):
        remote(zsum.at[0], zsum.at[ZS - d], z_send, z_recv, at_z(d)).start()
    wait_bytes(slots.at[pl.ds(0, SUBS - 1)], slots_send)
    wait_bytes(cand.at[0, pl.ds(0, 15)], z_block_send)
    wait_bytes(cand.at[pl.ds(0, 2)], y_send)
    wait_bytes(cand.at[0, pl.ds(0, 3)], far_send)
    wait_bytes(cand.at[0, pl.ds(0, 13)], far_z_send)
    for copy in (pts_right, pts_left, pts_core, far_top, core_left, far_low, core_right, core_far):
        copy.wait_send()
    wait_bytes(line.at[pl.ds(0, SUBS - 1)], line_send)
    wait_bytes(zsum.at[pl.ds(0, ZS - 1)], z_recv)
    psum[0] = jnp.sum(zsum[...], axis=0)
    for dx, dy, other in PLANE:
        device = (lax.rem(x + dx, XS) * ZS + z, lax.rem(y + dy, YS) * 2 + (1 - core if other else core))
        there = (-dx % XS * YS + -dy % YS) * 2 + other
        remote(psum.at[0], psum.at[there], p_send, p_recv, device).start()
    wait_bytes(psum.at[pl.ds(0, len(PLANE))], p_recv)
    cost = jnp.sum(psum[...], axis=0)
    for r in range(ROUNDS):
        cost_r = jnp.sum(jnp.where(lanes == r, cost, 0.0), axis=1, keepdims=True)
        out_ref[r : r + 1, :] = npts * near[r] / cost_r
    wait_bytes(zsum.at[pl.ds(0, ZS - 1)], z_send)
    wait_bytes(psum.at[pl.ds(0, len(PLANE))], p_send)


def shards(points, cand_rows, cand_count):
    npd, width = points.shape
    npts = float(npd * lax.axis_size(("dp", "sub")))
    dma = pltpu.SemaphoreType.DMA
    operands = (cand_rows, cand_count.reshape(1, ROUNDS), points)
    return pl.pallas_call(
        lambda *refs: kernel(npts, *refs),
        out_shape=jax.ShapeDtypeStruct((ROUNDS, npd), F32),
        in_specs=[
            pl.BlockSpec(memory_space=pl.ANY),
            pl.BlockSpec(memory_space=pl.ANY),
            pl.BlockSpec(memory_space=pl.ANY),
        ],
        out_specs=pl.BlockSpec(memory_space=pltpu.VMEM),
        scratch_shapes=[
            pltpu.SMEM((ROUNDS, SLOTS), jnp.int32),
            pltpu.SMEM((1, ROUNDS), jnp.int32),
            pltpu.VMEM((npd, width), jnp.bfloat16),
            pltpu.VMEM((SUBS, RAW, width), jnp.bfloat16),
            pltpu.VMEM((XS, ZS, BLK, width), jnp.bfloat16),
            pltpu.VMEM((SUBS, width, npd), jnp.bfloat16),
            pltpu.VMEM((SUBS // 2, BLK, 2 * npd), F32),
            pltpu.VMEM((1, npd), F32),
            pltpu.VMEM((SUBS, 4, npd), F32),
            pltpu.VMEM((SUBS, 4, npd), F32),
            pltpu.VMEM((ZS, 1, npd), F32),
            pltpu.VMEM((len(PLANE) + 1, 1, npd), F32),
            dma((3,)),
            dma,
            dma,
            dma,
            dma,
            dma((17,)),
            dma((2,)),
            dma,
            dma,
            dma((3,)),
            dma((2,)),
            dma((8,)),
            dma((8,)),
            dma,
            dma,
            dma,
            dma,
            dma,
            dma,
        ],
        compiler_params=pltpu.CompilerParams(
            collective_id=0, has_side_effects=True, vmem_limit_bytes=40 * 1024 * 1024
        ),
        cost_estimate=pl.CostEstimate(
            flops=2 * 1024 * 1024 * width, bytes_accessed=npd * width * 2, transcendentals=0
        ),
    )(*(pltpu.with_memory_space_constraint(value, pltpu.HBM) for value in operands))


def solution(mesh):
    in_specs = (P(("dp", "sub"), None), P(None, ("dp", "sub")), P(None, ("dp", "sub")))
    out_specs = P(None, ("dp", "sub"))
    return jax.shard_map(shards, mesh=mesh, in_specs=in_specs, out_specs=out_specs, check_vma=False)
```

```python
import jax
import jax.numpy as jnp
from jax import lax
from jax.experimental import pallas as pl
from jax.experimental.pallas import tpu as pltpu
from jax.sharding import PartitionSpec as P

ROUNDS = 3
SLOTS = 4
XS = 4
ZS = 16
YS = 4
SUBS = 8
RAW = 16
BLK = 8
SHARE = 2
NEAR = 9
MESH = pl.DeviceIdType.MESH
F32 = jnp.float32
INF = float("inf")


def kernel(
    npts,
    rows_in,
    counts_in,
    points_ref,
    out_ref,
    rows_ref,
    cnt_ref,
    raw,
    slots,
    cand,
    pall,
    mins,
    squares,
    line,
    near,
    zsum,
    ysum,
    local_sem,
    slots_send,
    slots_recv,
    z_block_send,
    y_send,
    z_block_recv,
    y_recv,
    pts_send,
    pts_recv,
    line_send,
    line_recv,
    z_send,
    z_recv,
    c_send,
    c_recv,
):
    dp = lax.axis_index("dp")
    sub = lax.axis_index("sub")
    x, z = lax.div(dp, ZS), lax.rem(dp, ZS)
    y, core = lax.div(sub, 2), lax.rem(sub, 2)
    npd, width = points_ref.shape

    def at_x(d):
        return (lax.rem(x + d, XS) * ZS + z, sub)

    def at_z(d):
        return (x * ZS + lax.rem(z + d, ZS), sub)

    def at_y(d):
        return (dp, lax.rem(y + d, YS) * 2 + core)

    other_core = (dp, y * 2 + (1 - core))
    z_to = {d: at_z(d % ZS) for d in (1, -1, 2, -2, 3, -3, 4, -4)}
    y_to = {d: at_y(d) for d in (1, 2, 3)}
    me = x * 2 + core
    x_right, x_left = at_x(1), at_x(3)

    own_points = pltpu.make_async_copy(points_ref, raw, local_sem.at[0])
    own_points.start()
    own_rows = pltpu.make_async_copy(rows_in, rows_ref, local_sem.at[1])
    own_rows.start()
    own_counts = pltpu.make_async_copy(counts_in, cnt_ref, local_sem.at[2])
    own_counts.start()
    barrier = pltpu.get_barrier_semaphore()
    far_first = ((2, 0), (2, 1), (1, 0), (3, 0), (1, 1), (3, 1), (0, 1))
    y_line = [(dp, lax.rem(y + d, YS) * 2 + (1 - core if other else core)) for d, other in far_first]
    x_line = [(lax.rem(x + d, XS) * ZS + z, y * 2 + (1 - core if other else core)) for d, other in far_first]
    partners = [*z_to.values(), *y_line, *x_line[:-1]]
    for device in partners:
        pl.semaphore_signal(barrier, inc=1, device_id=device, device_id_type=MESH)

    row = lax.broadcasted_iota(jnp.int32, (RAW, npd), 0)
    lane = lax.broadcasted_iota(jnp.int32, (RAW, npd), 1)
    here = lax.broadcasted_iota(jnp.int32, (npd, npd), 0)
    there = lax.broadcasted_iota(jnp.int32, (npd, npd), 1)
    same_round = (here & (RAW - 1)) == ROUNDS * SLOTS + ((there & (RAW - 1)) >> 2)
    before = jnp.where(same_round & ((here >> 4) < (there >> 4)), 1.0, 0.0)
    itself = jnp.where(same_round & ((here >> 4) == (there >> 4)), 1.0, 0.0)
    slot = lane & (RAW - 1)
    slot_round = jnp.where(slot < ROUNDS * SLOTS, slot >> 2, -1)
    slot_index = (slot & (SLOTS - 1)).astype(F32)
    wanted = (SHARE * sub + (row & 1)).astype(F32)
    wanted_round = slot_round == (row >> 1)
    own_rows.wait()
    own_counts.wait()
    target = jnp.full((RAW, npd), -1, jnp.int32)
    counts = jnp.zeros((RAW, npd), F32)
    for r in range(ROUNDS):
        counts = jnp.where(row == ROUNDS * SLOTS + r, cnt_ref[0, r].astype(F32), counts)
        for i in range(SLOTS):
            target = jnp.where(row == r * SLOTS + i, rows_ref[r, i], target)
    pick = jnp.where(lane == target, 1.0, 0.0).astype(jnp.bfloat16)
    own_points.wait()
    mine = raw[...]
    block = jnp.dot(pick, mine, preferred_element_type=F32)
    slots[sub, :, :npd] = (block[:, :npd] + counts).astype(jnp.bfloat16)
    slots[sub, :, npd:] = block[:, npd:].astype(jnp.bfloat16)

    pl.semaphore_wait(barrier, len(partners))

    def remote(src, dst, send, recv, device):
        return pltpu.make_async_remote_copy(
            src_ref=src, dst_ref=dst, send_sem=send, recv_sem=recv, device_id=device, device_id_type=MESH
        )

    def to_columns(place, count, group):
        for d in (2, 1, 3):
            src, dst = cand.at[0, pl.ds(place, count)], cand.at[d, pl.ds(place, count)]
            remote(src, dst, y_send, y_recv.at[group], y_to[d]).start()

    def along_z(src, place, d, lanes=None):
        if lanes is None:
            src, dst = cand.at[0, src], cand.at[0, place]
        else:
            part = pl.ds(lanes * (width // 2), width // 2)
            src, dst = cand.at[0, src, :, part], cand.at[0, place, :, part]
        remote(src, dst, z_block_send, z_block_recv.at[place + (lanes or 0)], z_to[d]).start()

    def z_arrived(*places):
        for place in places:
            wait_bytes(cand.at[0, place], z_block_recv.at[place])

    def wait_bytes(ref, sem):
        pltpu.make_async_copy(ref, ref, sem).wait()

    for device in y_line:
        remote(slots.at[sub], slots.at[sub], slots_send, slots_recv, device).start()
    pall[me] = mine.T
    slot_right, slot_left, slot_far = (lax.rem(x + d, XS) * 2 + core for d in (1, 3, 2))
    top, low = pl.ds(0, width // 2), pl.ds(width // 2, width // 2)
    mine_at = pall.at[me]
    pts_right = remote(mine_at, mine_at, pts_send.at[0], pts_recv.at[0], x_right)
    pts_left = remote(mine_at, mine_at, pts_send.at[1], pts_recv.at[1], x_left)
    pts_core = remote(mine_at, mine_at, pts_send.at[2], pts_recv.at[2], other_core)
    pts_right.start()
    pts_left.start()
    pts_core.start()

    wait_bytes(slots.at[pl.ds(0, SUBS - 1)], slots_recv)
    flat = slots[...].reshape(SUBS * RAW, width)
    known = flat[:, :npd].astype(F32)
    offset = jnp.sum(known * before, axis=0, keepdims=True)
    count = jnp.sum(known * itself, axis=0, keepdims=True)
    choice = wanted_round & (slot_index < count) & (offset + slot_index == wanted)
    share = jnp.dot(jnp.where(choice, 1.0, 0.0).astype(jnp.bfloat16), flat, preferred_element_type=F32)
    cand[0, 0] = share[:BLK].astype(jnp.bfloat16)

    for place, d in ((7, 4), (8, -4), (1, 2), (2, -2), (3, 1), (6, -1)):
        along_z(0, place, d)
    to_columns(0, 1, 0)

    pts_right.wait_recv()
    near_left = pall.at[slot_left]
    far_top = remote(near_left.at[top], near_left.at[top], pts_send.at[3], pts_recv.at[3], x_right)
    core_left = remote(near_left, near_left, pts_send.at[4], pts_recv.at[4], other_core)
    far_top.start()
    core_left.start()
    pts_left.wait_recv()
    near_right = pall.at[slot_right]
    far_low = remote(near_right.at[low], near_right.at[low], pts_send.at[5], pts_recv.at[5], x_left)
    core_right = remote(near_right, near_right, pts_send.at[6], pts_recv.at[6], other_core)
    far_low.start()
    core_right.start()

    z_arrived(7)
    along_z(7, 15, 4, 0)
    for place, d in ((13, 3), (9, 2), (11, 1), (5, -1)):
        along_z(7, place, d)
    z_arrived(8)
    along_z(8, 15, -4, 1)
    for place, d in ((14, -3), (10, -2), (12, -1), (4, 1)):
        along_z(8, place, d)

    far_top.wait_recv()
    far_low.wait_recv()
    far = pall.at[slot_far]
    core_far = remote(far, far, pts_send.at[7], pts_recv.at[7], other_core)
    core_far.start()

    z_arrived(1, 2, 3, 4, 5, 6)
    to_columns(1, NEAR - 1, 0)
    z_arrived(9, 10, 11, 12, 13, 14)
    to_columns(NEAR, 6, 1)
    half_block = cand.at[0, 15, :, pl.ds(0, width // 2)]
    wait_bytes(half_block, z_block_recv.at[15])
    wait_bytes(half_block, z_block_recv.at[16])
    to_columns(15, 1, 1)

    def absorb(first, count):
        blocks = XS * count
        rows = cand[:, first : first + count].reshape(blocks, BLK, width)
        half = jnp.zeros((blocks, BLK, npd), F32)
        for t in range(width // npd):
            piece = rows[:, :, t * npd : (t + 1) * npd].astype(F32)
            half = half + piece * piece
        half = 0.5 * jnp.sum(half, axis=2, keepdims=True)
        flat = rows.reshape(blocks * BLK, width)
        for j in range(SUBS // 2):
            group = jnp.concatenate([pall[2 * j], pall[2 * j + 1]], axis=1)
            dots = jnp.dot(flat, group, preferred_element_type=F32)
            best = jnp.min(half - dots.reshape(blocks, BLK, 2 * npd), axis=0)
            mins[j] = best if first == 0 else jnp.minimum(mins[j], best)

    pts_core.wait_recv()
    core_left.wait_recv()
    core_right.wait_recv()
    core_far.wait_recv()
    for b in range(SUBS):
        wide = pall[b].astype(F32)
        squares[b : b + 1, :] = jnp.sum(wide * wide, axis=0, keepdims=True)
    wait_bytes(cand.at[pl.ds(1, 3), pl.ds(0, NEAR)], y_recv.at[0])
    absorb(0, NEAR)
    wait_bytes(cand.at[pl.ds(1, 3), pl.ds(NEAR, ZS - NEAR)], y_recv.at[1])
    absorb(NEAR, ZS - NEAR)

    for j in range(SUBS // 2):
        for r in range(ROUNDS):
            low_r = jnp.min(mins[j, r * SHARE : (r + 1) * SHARE, :], axis=0, keepdims=True)
            for h in range(2):
                line[me, r, 2 * j + h : 2 * j + h + 1, :] = low_r[:, h * npd : (h + 1) * npd]

    for device in x_line:
        remote(line.at[me], line.at[me], line_send, line_recv, device).start()
    wait_bytes(line.at[pl.ds(0, SUBS - 1)], line_recv)

    lanes = lax.broadcasted_iota(jnp.int32, (1, npd), 1)
    least = None
    total = jnp.zeros((1, npd), F32)
    for r in range(ROUNDS):
        now = jnp.min(line[:, r], axis=0)
        least = now if least is None else jnp.minimum(least, now)
        dist = jnp.maximum(squares[...] + 2.0 * least, 0.0)
        near[r] = dist
        part = jnp.sum(jnp.sum(dist, axis=0, keepdims=True), axis=1, keepdims=True)
        total = jnp.where(lanes == r, part, total)

    zsum[0] = total

    for d in (8, 7, 9, 6, 10, 5, 11, 4, 12, 3, 13, 2, 14, 1, 15):
        remote(zsum.at[0], zsum.at[ZS - d], z_send, z_recv, at_z(d)).start()
    wait_bytes(slots.at[pl.ds(0, SUBS - 1)], slots_send)
    wait_bytes(cand.at[0, pl.ds(0, 15)], z_block_send)
    wait_bytes(cand.at[pl.ds(0, 3)], y_send)
    for copy in (pts_right, pts_left, pts_core, far_top, core_left, far_low, core_right, core_far):
        copy.wait_send()
    wait_bytes(line.at[pl.ds(0, SUBS - 1)], line_send)
    wait_bytes(zsum.at[pl.ds(0, ZS - 1)], z_recv)
    ysum[0] = jnp.sum(zsum[...], axis=0)
    for d in (1, 3, 2):
        remote(ysum.at[0], ysum.at[XS - d], c_send, c_recv, y_to[d]).start()
    wait_bytes(ysum.at[pl.ds(0, XS - 1)], c_recv)
    cost = jnp.sum(ysum[...], axis=0)
    for r in range(ROUNDS):
        cost_r = jnp.sum(jnp.where(lanes == r, cost, 0.0), axis=1, keepdims=True)
        out_ref[r : r + 1, :] = npts * near[r, pl.ds(me, 1), :] / cost_r
    wait_bytes(zsum.at[pl.ds(0, ZS - 1)], z_send)
    wait_bytes(ysum.at[pl.ds(0, XS - 1)], c_send)


def shards(points, cand_rows, cand_count):
    npd, width = points.shape
    npts = float(npd * lax.axis_size(("dp", "sub")))
    dma = pltpu.SemaphoreType.DMA
    operands = (cand_rows, cand_count.reshape(1, ROUNDS), points)
    return pl.pallas_call(
        lambda *refs: kernel(npts, *refs),
        out_shape=jax.ShapeDtypeStruct((ROUNDS, npd), F32),
        in_specs=[
            pl.BlockSpec(memory_space=pl.ANY),
            pl.BlockSpec(memory_space=pl.ANY),
            pl.BlockSpec(memory_space=pl.ANY),
        ],
        out_specs=pl.BlockSpec(memory_space=pltpu.VMEM),
        scratch_shapes=[
            pltpu.SMEM((ROUNDS, SLOTS), jnp.int32),
            pltpu.SMEM((1, ROUNDS), jnp.int32),
            pltpu.VMEM((npd, width), jnp.bfloat16),
            pltpu.VMEM((SUBS, RAW, width), jnp.bfloat16),
            pltpu.VMEM((XS, ZS, BLK, width), jnp.bfloat16),
            pltpu.VMEM((SUBS, width, npd), jnp.bfloat16),
            pltpu.VMEM((SUBS // 2, BLK, 2 * npd), F32),
            pltpu.VMEM((SUBS, npd), F32),
            pltpu.VMEM((SUBS, ROUNDS, SUBS, npd), F32),
            pltpu.VMEM((ROUNDS, SUBS, npd), F32),
            pltpu.VMEM((ZS, 1, npd), F32),
            pltpu.VMEM((XS, 1, npd), F32),
            dma((3,)),
            dma,
            dma,
            dma,
            dma,
            dma((17,)),
            dma((2,)),
            dma((8,)),
            dma((8,)),
            dma,
            dma,
            dma,
            dma,
            dma,
            dma,
        ],
        compiler_params=pltpu.CompilerParams(
            collective_id=0, has_side_effects=True, vmem_limit_bytes=40 * 1024 * 1024
        ),
        cost_estimate=pl.CostEstimate(
            flops=2 * 1024 * 1024 * width, bytes_accessed=npd * width * 2, transcendentals=0
        ),
    )(*(pltpu.with_memory_space_constraint(value, pltpu.HBM) for value in operands))


def solution(mesh):
    in_specs = (P(("dp", "sub"), None), P(None, ("dp", "sub")), P(None, ("dp", "sub")))
    out_specs = P(None, ("dp", "sub"))
    return jax.shard_map(shards, mesh=mesh, in_specs=in_specs, out_specs=out_specs, check_vma=False)
```

```python
import jax
import jax.numpy as jnp
from jax import lax
from jax.experimental import pallas as pl
from jax.experimental.pallas import tpu as pltpu
from jax.sharding import PartitionSpec as P

ROUNDS = 3
SLOTS = 4
XS = 4
ZS = 16
YS = 4
SUBS = 8
RAW = 16
BLK = 8
SHARE = 2
USED_ROWS = pl.ds(0, ROUNDS * SHARE)
NEAR = 9
MESH = pl.DeviceIdType.MESH
F32 = jnp.float32
INF = float("inf")


def kernel(
    npts,
    rows_in,
    counts_in,
    points_ref,
    out_ref,
    rows_ref,
    cnt_ref,
    raw,
    slots,
    cand,
    pall,
    mins,
    squares,
    line,
    near,
    zsum,
    ysum,
    local_sem,
    slots_send,
    slots_recv,
    z_block_send,
    y_send,
    z_block_recv,
    y_recv,
    far_send,
    far_z_send,
    far_recv,
    far_z_recv,
    pts_send,
    pts_recv,
    line_send,
    line_recv,
    z_send,
    z_recv,
    c_send,
    c_recv,
):
    dp = lax.axis_index("dp")
    sub = lax.axis_index("sub")
    x, z = lax.div(dp, ZS), lax.rem(dp, ZS)
    y, core = lax.div(sub, 2), lax.rem(sub, 2)
    npd, width = points_ref.shape

    def at_x(d):
        return (lax.rem(x + d, XS) * ZS + z, sub)

    def at_z(d):
        return (x * ZS + lax.rem(z + d, ZS), sub)

    def at_y(d):
        return (dp, lax.rem(y + d, YS) * 2 + core)

    other_core = (dp, y * 2 + (1 - core))
    z_to = {d: at_z(d % ZS) for d in (1, -1, 2, -2, 3, -3, 4, -4)}
    y_to = {d: at_y(d) for d in (1, 2, 3)}
    me = x * 2 + core
    x_right, x_left = at_x(1), at_x(3)

    own_points = pltpu.make_async_copy(points_ref, raw, local_sem.at[0])
    own_points.start()
    own_rows = pltpu.make_async_copy(rows_in, rows_ref, local_sem.at[1])
    own_rows.start()
    own_counts = pltpu.make_async_copy(counts_in, cnt_ref, local_sem.at[2])
    own_counts.start()
    barrier = pltpu.get_barrier_semaphore()
    far_first = ((2, 0), (2, 1), (1, 0), (3, 0), (1, 1), (3, 1), (0, 1))
    y_line = [(dp, lax.rem(y + d, YS) * 2 + (1 - core if other else core)) for d, other in far_first]
    x_line = [(lax.rem(x + d, XS) * ZS + z, y * 2 + (1 - core if other else core)) for d, other in far_first]
    partners = [*z_to.values(), *y_line, *x_line[:-1]]
    for device in partners:
        pl.semaphore_signal(barrier, inc=1, device_id=device, device_id_type=MESH)

    row = lax.broadcasted_iota(jnp.int32, (RAW, npd), 0)
    lane = lax.broadcasted_iota(jnp.int32, (RAW, npd), 1)
    here = lax.broadcasted_iota(jnp.int32, (npd, npd), 0)
    there = lax.broadcasted_iota(jnp.int32, (npd, npd), 1)
    same_round = (here & (RAW - 1)) == ROUNDS * SLOTS + ((there & (RAW - 1)) >> 2)
    before = jnp.where(same_round & ((here >> 4) < (there >> 4)), 1.0, 0.0)
    itself = jnp.where(same_round & ((here >> 4) == (there >> 4)), 1.0, 0.0)
    slot = lane & (RAW - 1)
    slot_round = jnp.where(slot < ROUNDS * SLOTS, slot >> 2, -1)
    slot_index = (slot & (SLOTS - 1)).astype(F32)
    wanted = (SHARE * sub + (row & 1)).astype(F32)
    wanted_round = slot_round == (row >> 1)
    own_rows.wait()
    own_counts.wait()
    target = jnp.full((RAW, npd), -1, jnp.int32)
    counts = jnp.zeros((RAW, npd), F32)
    for r in range(ROUNDS):
        counts = jnp.where(row == ROUNDS * SLOTS + r, cnt_ref[0, r].astype(F32), counts)
        for i in range(SLOTS):
            target = jnp.where(row == r * SLOTS + i, rows_ref[r, i], target)
    pick = jnp.where(lane == target, 1.0, 0.0).astype(jnp.bfloat16)
    own_points.wait()
    mine = raw[...]
    block = jnp.dot(pick, mine, preferred_element_type=F32)
    slots[sub, :, :npd] = (block[:, :npd] + counts).astype(jnp.bfloat16)
    slots[sub, :, npd:] = block[:, npd:].astype(jnp.bfloat16)

    pl.semaphore_wait(barrier, len(partners))

    def remote(src, dst, send, recv, device):
        return pltpu.make_async_remote_copy(
            src_ref=src, dst_ref=dst, send_sem=send, recv_sem=recv, device_id=device, device_id_type=MESH
        )

    def to_sides(place, count, group):
        for d, column in ((1, 2), (3, 3)):
            src, dst = cand.at[0, pl.ds(place, count), USED_ROWS], cand.at[column, pl.ds(place, count), USED_ROWS]
            remote(src, dst, y_send, y_recv.at[group], y_to[d]).start()

    def to_far(place):
        remote(cand.at[0, place, USED_ROWS], cand.at[1, place, USED_ROWS], far_send, far_recv.at[place - 6], y_to[2]).start()

    def far_along_z(src, place, count, group, d, lanes=None):
        src, dst = cand.at[1, pl.ds(src, count), USED_ROWS], cand.at[1, pl.ds(place, count), USED_ROWS]
        if lanes is not None:
            part = pl.ds(lanes * (width // 2), width // 2)
            src, dst = src.at[:, :, part], dst.at[:, :, part]
        remote(src, dst, far_z_send, far_z_recv.at[group], z_to[d]).start()

    def along_z(src, place, d, lanes=None):
        if lanes is None:
            src, dst = cand.at[0, src, USED_ROWS], cand.at[0, place, USED_ROWS]
        else:
            part = pl.ds(lanes * (width // 2), width // 2)
            src, dst = cand.at[0, src, USED_ROWS, part], cand.at[0, place, USED_ROWS, part]
        remote(src, dst, z_block_send, z_block_recv.at[place + (lanes or 0)], z_to[d]).start()

    def z_arrived(*places):
        for place in places:
            wait_bytes(cand.at[0, place, USED_ROWS], z_block_recv.at[place])

    def wait_bytes(ref, sem):
        pltpu.make_async_copy(ref, ref, sem).wait()

    for device in y_line:
        remote(slots.at[sub], slots.at[sub], slots_send, slots_recv, device).start()
    pall[me] = mine.T
    slot_right, slot_left, slot_far = (lax.rem(x + d, XS) * 2 + core for d in (1, 3, 2))
    top, low = pl.ds(0, width // 2), pl.ds(width // 2, width // 2)
    mine_at = pall.at[me]
    pts_right = remote(mine_at, mine_at, pts_send.at[0], pts_recv.at[0], x_right)
    pts_left = remote(mine_at, mine_at, pts_send.at[1], pts_recv.at[1], x_left)
    pts_core = remote(mine_at, mine_at, pts_send.at[2], pts_recv.at[2], other_core)
    pts_right.start()
    pts_left.start()
    pts_core.start()

    wait_bytes(slots.at[pl.ds(0, SUBS - 1)], slots_recv)
    flat = slots[...].reshape(SUBS * RAW, width)
    known = flat[:, :npd].astype(F32)
    offset = jnp.sum(known * before, axis=0, keepdims=True)
    count = jnp.sum(known * itself, axis=0, keepdims=True)
    choice = wanted_round & (slot_index < count) & (offset + slot_index == wanted)
    share = jnp.dot(jnp.where(choice, 1.0, 0.0).astype(jnp.bfloat16), flat, preferred_element_type=F32)
    cand[0, 7] = share[:BLK].astype(jnp.bfloat16)

    along_z(7, 6, 4)
    along_z(7, 8, -4)
    to_far(7)
    for place, d in ((0, 2), (1, -2), (2, 1), (5, -1)):
        along_z(7, place, d)
    to_sides(7, 1, 0)

    pts_right.wait_recv()
    near_left = pall.at[slot_left]
    far_top = remote(near_left.at[top], near_left.at[top], pts_send.at[3], pts_recv.at[3], x_right)
    core_left = remote(near_left, near_left, pts_send.at[4], pts_recv.at[4], other_core)
    far_top.start()
    core_left.start()
    pts_left.wait_recv()
    near_right = pall.at[slot_right]
    far_low = remote(near_right.at[low], near_right.at[low], pts_send.at[5], pts_recv.at[5], x_left)
    core_right = remote(near_right, near_right, pts_send.at[6], pts_recv.at[6], other_core)
    far_low.start()
    core_right.start()

    z_arrived(6)
    to_far(6)
    along_z(6, 15, 4, 0)
    for place, d in ((13, 3), (9, 2), (11, 1), (4, -1)):
        along_z(6, place, d)
    z_arrived(8)
    to_far(8)
    along_z(8, 15, -4, 1)
    for place, d in ((14, -3), (10, -2), (12, -1), (3, 1)):
        along_z(8, place, d)
    to_sides(6, 1, 0)
    to_sides(8, 1, 0)

    for place in (6, 7, 8):
        wait_bytes(cand.at[1, place, USED_ROWS], far_recv.at[place - 6])
    far_along_z(6, 15, 1, 1, 4, 0)
    far_along_z(8, 15, 1, 1, -4, 1)
    far_along_z(6, 13, 1, 1, 3)
    far_along_z(8, 14, 1, 1, -3)
    far_along_z(6, 9, 1, 1, 2)
    far_along_z(8, 10, 1, 1, -2)
    far_along_z(6, 11, 1, 1, 1)
    far_along_z(8, 12, 1, 1, -1)
    far_along_z(7, 0, 1, 0, 2)
    far_along_z(7, 1, 1, 0, -2)
    far_along_z(7, 2, 2, 0, 1)
    far_along_z(6, 4, 2, 0, -1)

    far_top.wait_recv()
    far_low.wait_recv()
    far = pall.at[slot_far]
    core_far = remote(far, far, pts_send.at[7], pts_recv.at[7], other_core)
    core_far.start()

    z_arrived(0, 1, 2, 3, 4, 5)
    to_sides(0, 6, 0)
    z_arrived(9, 10, 11, 12, 13, 14)
    to_sides(9, 6, 1)
    half_block = cand.at[0, 15, USED_ROWS, pl.ds(0, width // 2)]
    wait_bytes(half_block, z_block_recv.at[15])
    wait_bytes(half_block, z_block_recv.at[16])
    to_sides(15, 1, 1)

    def absorb(first, count):
        blocks = XS * count
        rows = cand[:, first : first + count].reshape(blocks, BLK, width)
        half = jnp.zeros((blocks, BLK, npd), F32)
        for t in range(width // npd):
            piece = rows[:, :, t * npd : (t + 1) * npd].astype(F32)
            half = half + piece * piece
        half = 0.5 * jnp.sum(half, axis=2, keepdims=True)
        flat = rows.reshape(blocks * BLK, width)
        for j in range(SUBS // 2):
            group = jnp.concatenate([pall[2 * j], pall[2 * j + 1]], axis=1)
            dots = jnp.dot(flat, group, preferred_element_type=F32)
            best = jnp.min(half - dots.reshape(blocks, BLK, 2 * npd), axis=0)
            mins[j] = best if first == 0 else jnp.minimum(mins[j], best)

    pts_core.wait_recv()
    core_left.wait_recv()
    core_right.wait_recv()
    core_far.wait_recv()
    for b in range(SUBS):
        wide = pall[b].astype(F32)
        squares[b : b + 1, :] = jnp.sum(wide * wide, axis=0, keepdims=True)
    wait_bytes(cand.at[pl.ds(2, 2), pl.ds(0, NEAR), USED_ROWS], y_recv.at[0])
    wait_bytes(cand.at[1, pl.ds(0, 6), USED_ROWS], far_z_recv.at[0])
    absorb(0, NEAR)
    wait_bytes(cand.at[pl.ds(2, 2), pl.ds(NEAR, ZS - NEAR), USED_ROWS], y_recv.at[1])
    wait_bytes(cand.at[1, pl.ds(NEAR, ZS - NEAR), USED_ROWS], far_z_recv.at[1])
    absorb(NEAR, ZS - NEAR)

    for j in range(SUBS // 2):
        for r in range(ROUNDS):
            low_r = jnp.min(mins[j, r * SHARE : (r + 1) * SHARE, :], axis=0, keepdims=True)
            for h in range(2):
                line[me, r, 2 * j + h : 2 * j + h + 1, :] = low_r[:, h * npd : (h + 1) * npd]

    for device in x_line:
        remote(line.at[me], line.at[me], line_send, line_recv, device).start()
    wait_bytes(line.at[pl.ds(0, SUBS - 1)], line_recv)

    lanes = lax.broadcasted_iota(jnp.int32, (1, npd), 1)
    least = None
    total = jnp.zeros((1, npd), F32)
    for r in range(ROUNDS):
        now = jnp.min(line[:, r], axis=0)
        least = now if least is None else jnp.minimum(least, now)
        dist = jnp.maximum(squares[...] + 2.0 * least, 0.0)
        near[r] = dist
        part = jnp.sum(jnp.sum(dist, axis=0, keepdims=True), axis=1, keepdims=True)
        total = jnp.where(lanes == r, part, total)

    zsum[0] = total

    for d in (8, 7, 9, 6, 10, 5, 11, 4, 12, 3, 13, 2, 14, 1, 15):
        remote(zsum.at[0], zsum.at[ZS - d], z_send, z_recv, at_z(d)).start()
    wait_bytes(slots.at[pl.ds(0, SUBS - 1)], slots_send)
    wait_bytes(cand.at[0, pl.ds(0, 15), USED_ROWS], z_block_send)
    wait_bytes(cand.at[pl.ds(0, 2), :, USED_ROWS], y_send)
    wait_bytes(cand.at[0, pl.ds(0, 3), USED_ROWS], far_send)
    wait_bytes(cand.at[0, pl.ds(0, 13), USED_ROWS], far_z_send)
    for copy in (pts_right, pts_left, pts_core, far_top, core_left, far_low, core_right, core_far):
        copy.wait_send()
    wait_bytes(line.at[pl.ds(0, SUBS - 1)], line_send)
    wait_bytes(zsum.at[pl.ds(0, ZS - 1)], z_recv)
    ysum[0] = jnp.sum(zsum[...], axis=0)
    for d in (1, 3, 2):
        remote(ysum.at[0], ysum.at[XS - d], c_send, c_recv, y_to[d]).start()
    wait_bytes(ysum.at[pl.ds(0, XS - 1)], c_recv)
    cost = jnp.sum(ysum[...], axis=0)
    for r in range(ROUNDS):
        cost_r = jnp.sum(jnp.where(lanes == r, cost, 0.0), axis=1, keepdims=True)
        out_ref[r : r + 1, :] = npts * near[r, pl.ds(me, 1), :] / cost_r
    wait_bytes(zsum.at[pl.ds(0, ZS - 1)], z_send)
    wait_bytes(ysum.at[pl.ds(0, XS - 1)], c_send)


def shards(points, cand_rows, cand_count):
    npd, width = points.shape
    npts = float(npd * lax.axis_size(("dp", "sub")))
    dma = pltpu.SemaphoreType.DMA
    operands = (cand_rows, cand_count.reshape(1, ROUNDS), points)
    return pl.pallas_call(
        lambda *refs: kernel(npts, *refs),
        out_shape=jax.ShapeDtypeStruct((ROUNDS, npd), F32),
        in_specs=[
            pl.BlockSpec(memory_space=pl.ANY),
            pl.BlockSpec(memory_space=pl.ANY),
            pl.BlockSpec(memory_space=pl.ANY),
        ],
        out_specs=pl.BlockSpec(memory_space=pltpu.VMEM),
        scratch_shapes=[
            pltpu.SMEM((ROUNDS, SLOTS), jnp.int32),
            pltpu.SMEM((1, ROUNDS), jnp.int32),
            pltpu.VMEM((npd, width), jnp.bfloat16),
            pltpu.VMEM((SUBS, RAW, width), jnp.bfloat16),
            pltpu.VMEM((XS, ZS, BLK, width), jnp.bfloat16),
            pltpu.VMEM((SUBS, width, npd), jnp.bfloat16),
            pltpu.VMEM((SUBS // 2, BLK, 2 * npd), F32),
            pltpu.VMEM((SUBS, npd), F32),
            pltpu.VMEM((SUBS, ROUNDS, SUBS, npd), F32),
            pltpu.VMEM((ROUNDS, SUBS, npd), F32),
            pltpu.VMEM((ZS, 1, npd), F32),
            pltpu.VMEM((XS, 1, npd), F32),
            dma((3,)),
            dma,
            dma,
            dma,
            dma,
            dma((17,)),
            dma((2,)),
            dma,
            dma,
            dma((3,)),
            dma((2,)),
            dma((8,)),
            dma((8,)),
            dma,
            dma,
            dma,
            dma,
            dma,
            dma,
        ],
        compiler_params=pltpu.CompilerParams(
            collective_id=0, has_side_effects=True, vmem_limit_bytes=40 * 1024 * 1024
        ),
        cost_estimate=pl.CostEstimate(
            flops=2 * 1024 * 1024 * width, bytes_accessed=npd * width * 2, transcendentals=0
        ),
    )(*(pltpu.with_memory_space_constraint(value, pltpu.HBM) for value in operands))


def solution(mesh):
    in_specs = (P(("dp", "sub"), None), P(None, ("dp", "sub")), P(None, ("dp", "sub")))
    out_specs = P(None, ("dp", "sub"))
    return jax.shard_map(shards, mesh=mesh, in_specs=in_specs, out_specs=out_specs, check_vma=False)
```

```python
import jax
import jax.numpy as jnp
from jax import lax
from jax.experimental import pallas as pl
from jax.experimental.pallas import tpu as pltpu
from jax.sharding import PartitionSpec as P

ROUNDS = 3
SLOTS = 4
XS = 4
ZS = 16
YS = 4
SUBS = 8
RAW = 16
BLK = 8
SHARE = 2
USED_ROWS = pl.ds(0, ROUNDS * SHARE)
NEAR = 9
MESH = pl.DeviceIdType.MESH
F32 = jnp.float32
INF = float("inf")


def kernel(
    npts,
    rows_in,
    counts_in,
    points_ref,
    out_ref,
    rows_ref,
    cnt_ref,
    raw,
    slots,
    cand,
    pall,
    mins,
    squares,
    line,
    near,
    zsum,
    ysum,
    local_sem,
    slots_send,
    slots_recv,
    z_block_send,
    y_send,
    z_block_recv,
    y_recv,
    far_send,
    far_z_send,
    far_recv,
    far_z_recv,
    pts_send,
    pts_recv,
    line_send,
    line_recv,
    z_send,
    z_recv,
    c_send,
    c_recv,
):
    dp = lax.axis_index("dp")
    sub = lax.axis_index("sub")
    x, z = lax.div(dp, ZS), lax.rem(dp, ZS)
    y, core = lax.div(sub, 2), lax.rem(sub, 2)
    npd, width = points_ref.shape

    def at_x(d):
        return (lax.rem(x + d, XS) * ZS + z, sub)

    def at_z(d):
        return (x * ZS + lax.rem(z + d, ZS), sub)

    def at_y(d):
        return (dp, lax.rem(y + d, YS) * 2 + core)

    other_core = (dp, y * 2 + (1 - core))
    z_to = {d: at_z(d % ZS) for d in (1, -1, 2, -2, 3, -3, 4, -4)}
    y_to = {d: at_y(d) for d in (1, 2, 3)}
    me = x * 2 + core
    x_right, x_left = at_x(1), at_x(3)

    own_points = pltpu.make_async_copy(points_ref, raw, local_sem.at[0])
    own_points.start()
    own_rows = pltpu.make_async_copy(rows_in, rows_ref, local_sem.at[1])
    own_rows.start()
    own_counts = pltpu.make_async_copy(counts_in, cnt_ref, local_sem.at[2])
    own_counts.start()
    barrier = pltpu.get_barrier_semaphore()
    far_first = ((2, 0), (2, 1), (1, 0), (3, 0), (1, 1), (3, 1), (0, 1))
    y_line = [(dp, lax.rem(y + d, YS) * 2 + (1 - core if other else core)) for d, other in far_first]
    x_line = [(lax.rem(x + d, XS) * ZS + z, y * 2 + (1 - core if other else core)) for d, other in far_first]
    partners = [*(z_to[d] for d in (4, -4, 2, -2, 1, -1)), *y_line, x_right, x_left]
    for device in partners:
        pl.semaphore_signal(barrier, inc=1, device_id=device, device_id_type=MESH)

    row = lax.broadcasted_iota(jnp.int32, (RAW, npd), 0)
    lane = lax.broadcasted_iota(jnp.int32, (RAW, npd), 1)
    here = lax.broadcasted_iota(jnp.int32, (npd, npd), 0)
    there = lax.broadcasted_iota(jnp.int32, (npd, npd), 1)
    same_round = (here & (RAW - 1)) == ROUNDS * SLOTS + ((there & (RAW - 1)) >> 2)
    before = jnp.where(same_round & ((here >> 4) < (there >> 4)), 1.0, 0.0)
    itself = jnp.where(same_round & ((here >> 4) == (there >> 4)), 1.0, 0.0)
    slot = lane & (RAW - 1)
    slot_round = jnp.where(slot < ROUNDS * SLOTS, slot >> 2, -1)
    slot_index = (slot & (SLOTS - 1)).astype(F32)
    wanted = (SHARE * sub + (row & 1)).astype(F32)
    wanted_round = slot_round == (row >> 1)
    own_rows.wait()
    own_counts.wait()
    target = jnp.full((RAW, npd), -1, jnp.int32)
    counts = jnp.zeros((RAW, npd), F32)
    for r in range(ROUNDS):
        counts = jnp.where(row == ROUNDS * SLOTS + r, cnt_ref[0, r].astype(F32), counts)
        for i in range(SLOTS):
            target = jnp.where(row == r * SLOTS + i, rows_ref[r, i], target)
    pick = jnp.where(lane == target, 1.0, 0.0).astype(jnp.bfloat16)
    own_points.wait()
    mine = raw[...]
    block = jnp.dot(pick, mine, preferred_element_type=F32)
    slots[sub, :, :npd] = (block[:, :npd] + counts).astype(jnp.bfloat16)
    slots[sub, :, npd:] = block[:, npd:].astype(jnp.bfloat16)

    pl.semaphore_wait(barrier, len(partners))

    def remote(src, dst, send, recv, device):
        return pltpu.make_async_remote_copy(
            src_ref=src, dst_ref=dst, send_sem=send, recv_sem=recv, device_id=device, device_id_type=MESH
        )

    def to_sides(place, count, group):
        for d, column in ((1, 2), (3, 3)):
            src, dst = cand.at[0, pl.ds(place, count), USED_ROWS], cand.at[column, pl.ds(place, count), USED_ROWS]
            remote(src, dst, y_send, y_recv.at[group], y_to[d]).start()

    def to_far(place):
        remote(cand.at[0, place, USED_ROWS], cand.at[1, place, USED_ROWS], far_send, far_recv.at[place - 6], y_to[2]).start()

    def far_along_z(src, place, count, group, d, lanes=None):
        src, dst = cand.at[1, pl.ds(src, count), USED_ROWS], cand.at[1, pl.ds(place, count), USED_ROWS]
        if lanes is not None:
            part = pl.ds(lanes * (width // 2), width // 2)
            src, dst = src.at[:, :, part], dst.at[:, :, part]
        remote(src, dst, far_z_send, far_z_recv.at[group], z_to[d]).start()

    def along_z(src, place, d, lanes=None):
        if lanes is None:
            src, dst = cand.at[0, src, USED_ROWS], cand.at[0, place, USED_ROWS]
        else:
            part = pl.ds(lanes * (width // 2), width // 2)
            src, dst = cand.at[0, src, USED_ROWS, part], cand.at[0, place, USED_ROWS, part]
        remote(src, dst, z_block_send, z_block_recv.at[place + (lanes or 0)], z_to[d]).start()

    def z_arrived(*places):
        for place in places:
            wait_bytes(cand.at[0, place, USED_ROWS], z_block_recv.at[place])

    def wait_bytes(ref, sem):
        pltpu.make_async_copy(ref, ref, sem).wait()

    for device in y_line:
        remote(slots.at[sub], slots.at[sub], slots_send, slots_recv, device).start()
    pall[me] = mine.T
    slot_right, slot_left, slot_far = (lax.rem(x + d, XS) * 2 + core for d in (1, 3, 2))
    top, low = pl.ds(0, width // 2), pl.ds(width // 2, width // 2)
    mine_at = pall.at[me]
    pts_right = remote(mine_at, mine_at, pts_send.at[0], pts_recv.at[0], x_right)
    pts_left = remote(mine_at, mine_at, pts_send.at[1], pts_recv.at[1], x_left)
    pts_core = remote(mine_at, mine_at, pts_send.at[2], pts_recv.at[2], other_core)
    pts_right.start()
    pts_left.start()
    pts_core.start()

    wait_bytes(slots.at[pl.ds(0, SUBS - 1)], slots_recv)
    flat = slots[...].reshape(SUBS * RAW, width)
    known = flat[:, :npd].astype(F32)
    offset = jnp.sum(known * before, axis=0, keepdims=True)
    count = jnp.sum(known * itself, axis=0, keepdims=True)
    choice = wanted_round & (slot_index < count) & (offset + slot_index == wanted)
    share = jnp.dot(jnp.where(choice, 1.0, 0.0).astype(jnp.bfloat16), flat, preferred_element_type=F32)
    cand[0, 7] = share[:BLK].astype(jnp.bfloat16)

    along_z(7, 6, 4)
    along_z(7, 8, -4)
    to_far(7)
    for place, d in ((0, 2), (1, -2), (2, 1), (5, -1)):
        along_z(7, place, d)
    to_sides(7, 1, 0)

    pts_right.wait_recv()
    near_left = pall.at[slot_left]
    far_top = remote(near_left.at[top], near_left.at[top], pts_send.at[3], pts_recv.at[3], x_right)
    core_left = remote(near_left, near_left, pts_send.at[4], pts_recv.at[4], other_core)
    far_top.start()
    core_left.start()
    pts_left.wait_recv()
    near_right = pall.at[slot_right]
    far_low = remote(near_right.at[low], near_right.at[low], pts_send.at[5], pts_recv.at[5], x_left)
    core_right = remote(near_right, near_right, pts_send.at[6], pts_recv.at[6], other_core)
    far_low.start()
    core_right.start()

    z_arrived(6)
    to_far(6)
    along_z(6, 15, 4, 0)
    for place, d in ((9, 2), (11, 1), (4, -1)):
        along_z(6, place, d)
    z_arrived(8)
    to_far(8)
    along_z(8, 15, -4, 1)
    along_z(8, 14, -3)
    along_z(6, 13, 3)
    for place, d in ((10, -2), (12, -1), (3, 1)):
        along_z(8, place, d)
    to_sides(6, 1, 0)
    to_sides(8, 1, 0)

    for place in (6, 7, 8):
        wait_bytes(cand.at[1, place, USED_ROWS], far_recv.at[place - 6])
    far_along_z(6, 15, 1, 1, 4, 0)
    far_along_z(8, 15, 1, 1, -4, 1)
    far_along_z(6, 13, 1, 1, 3)
    far_along_z(8, 14, 1, 1, -3)
    far_along_z(6, 9, 1, 1, 2)
    far_along_z(8, 10, 1, 1, -2)
    far_along_z(6, 11, 1, 1, 1)
    far_along_z(8, 12, 1, 1, -1)
    far_along_z(7, 0, 1, 0, 2)
    far_along_z(7, 1, 1, 0, -2)
    far_along_z(7, 2, 2, 0, 1)
    far_along_z(6, 4, 2, 0, -1)

    far_top.wait_recv()
    far_low.wait_recv()
    far = pall.at[slot_far]
    core_far = remote(far, far, pts_send.at[7], pts_recv.at[7], other_core)
    core_far.start()

    z_arrived(0, 1, 2, 3, 4, 5)
    to_sides(0, 6, 0)
    z_arrived(9, 10, 11, 12, 13, 14)
    to_sides(9, 6, 1)
    half_block = cand.at[0, 15, USED_ROWS, pl.ds(0, width // 2)]
    wait_bytes(half_block, z_block_recv.at[15])
    wait_bytes(half_block, z_block_recv.at[16])
    to_sides(15, 1, 1)

    def absorb(first, count):
        blocks = XS * count
        rows = cand[:, first : first + count].reshape(blocks, BLK, width)
        half = jnp.zeros((blocks, BLK, npd), F32)
        for t in range(width // npd):
            piece = rows[:, :, t * npd : (t + 1) * npd].astype(F32)
            half = half + piece * piece
        half = 0.5 * jnp.sum(half, axis=2, keepdims=True)
        flat = rows.reshape(blocks * BLK, width)
        for j in range(SUBS // 2):
            group = jnp.concatenate([pall[2 * j], pall[2 * j + 1]], axis=1)
            dots = jnp.dot(flat, group, preferred_element_type=F32)
            best = jnp.min(half - dots.reshape(blocks, BLK, 2 * npd), axis=0)
            mins[j] = best if first == 0 else jnp.minimum(mins[j], best)

    pts_core.wait_recv()
    core_left.wait_recv()
    core_right.wait_recv()
    core_far.wait_recv()
    for b in range(SUBS):
        wide = pall[b].astype(F32)
        squares[b : b + 1, :] = jnp.sum(wide * wide, axis=0, keepdims=True)
    wait_bytes(cand.at[pl.ds(2, 2), pl.ds(0, NEAR), USED_ROWS], y_recv.at[0])
    wait_bytes(cand.at[1, pl.ds(0, 6), USED_ROWS], far_z_recv.at[0])
    absorb(0, NEAR)
    wait_bytes(cand.at[pl.ds(2, 2), pl.ds(NEAR, ZS - NEAR), USED_ROWS], y_recv.at[1])
    wait_bytes(cand.at[1, pl.ds(NEAR, ZS - NEAR), USED_ROWS], far_z_recv.at[1])
    absorb(NEAR, ZS - NEAR)

    for j in range(SUBS // 2):
        for r in range(ROUNDS):
            low_r = jnp.min(mins[j, r * SHARE : (r + 1) * SHARE, :], axis=0, keepdims=True)
            for h in range(2):
                line[me, r, 2 * j + h : 2 * j + h + 1, :] = low_r[:, h * npd : (h + 1) * npd]

    for device in x_line:
        remote(line.at[me], line.at[me], line_send, line_recv, device).start()
    wait_bytes(line.at[pl.ds(0, SUBS - 1)], line_recv)

    lanes = lax.broadcasted_iota(jnp.int32, (1, npd), 1)
    least = None
    total = jnp.zeros((1, npd), F32)
    for r in range(ROUNDS):
        now = jnp.min(line[:, r], axis=0)
        least = now if least is None else jnp.minimum(least, now)
        dist = jnp.maximum(squares[...] + 2.0 * least, 0.0)
        near[r] = dist
        part = jnp.sum(jnp.sum(dist, axis=0, keepdims=True), axis=1, keepdims=True)
        total = jnp.where(lanes == r, part, total)

    zsum[0] = total

    for d in (8, 7, 9, 6, 10, 5, 11, 4, 12, 3, 13, 2, 14, 1, 15):
        remote(zsum.at[0], zsum.at[ZS - d], z_send, z_recv, at_z(d)).start()
    wait_bytes(slots.at[pl.ds(0, SUBS - 1)], slots_send)
    wait_bytes(cand.at[0, pl.ds(0, 15), USED_ROWS], z_block_send)
    wait_bytes(cand.at[pl.ds(0, 2), :, USED_ROWS], y_send)
    wait_bytes(cand.at[0, pl.ds(0, 3), USED_ROWS], far_send)
    wait_bytes(cand.at[0, pl.ds(0, 13), USED_ROWS], far_z_send)
    for copy in (pts_right, pts_left, pts_core, far_top, core_left, far_low, core_right, core_far):
        copy.wait_send()
    wait_bytes(line.at[pl.ds(0, SUBS - 1)], line_send)
    wait_bytes(zsum.at[pl.ds(0, ZS - 1)], z_recv)
    ysum[0] = jnp.sum(zsum[...], axis=0)
    for d in (1, 3, 2):
        remote(ysum.at[0], ysum.at[XS - d], c_send, c_recv, y_to[d]).start()
    wait_bytes(ysum.at[pl.ds(0, XS - 1)], c_recv)
    cost = jnp.sum(ysum[...], axis=0)
    for r in range(ROUNDS):
        cost_r = jnp.sum(jnp.where(lanes == r, cost, 0.0), axis=1, keepdims=True)
        out_ref[r : r + 1, :] = npts * near[r, pl.ds(me, 1), :] / cost_r
    wait_bytes(zsum.at[pl.ds(0, ZS - 1)], z_send)
    wait_bytes(ysum.at[pl.ds(0, XS - 1)], c_send)


def shards(points, cand_rows, cand_count):
    npd, width = points.shape
    npts = float(npd * lax.axis_size(("dp", "sub")))
    dma = pltpu.SemaphoreType.DMA
    operands = (cand_rows, cand_count.reshape(1, ROUNDS), points)
    return pl.pallas_call(
        lambda *refs: kernel(npts, *refs),
        out_shape=jax.ShapeDtypeStruct((ROUNDS, npd), F32),
        in_specs=[
            pl.BlockSpec(memory_space=pl.ANY),
            pl.BlockSpec(memory_space=pl.ANY),
            pl.BlockSpec(memory_space=pl.ANY),
        ],
        out_specs=pl.BlockSpec(memory_space=pltpu.VMEM),
        scratch_shapes=[
            pltpu.SMEM((ROUNDS, SLOTS), jnp.int32),
            pltpu.SMEM((1, ROUNDS), jnp.int32),
            pltpu.VMEM((npd, width), jnp.bfloat16),
            pltpu.VMEM((SUBS, RAW, width), jnp.bfloat16),
            pltpu.VMEM((XS, ZS, BLK, width), jnp.bfloat16),
            pltpu.VMEM((SUBS, width, npd), jnp.bfloat16),
            pltpu.VMEM((SUBS // 2, BLK, 2 * npd), F32),
            pltpu.VMEM((SUBS, npd), F32),
            pltpu.VMEM((SUBS, ROUNDS, SUBS, npd), F32),
            pltpu.VMEM((ROUNDS, SUBS, npd), F32),
            pltpu.VMEM((ZS, 1, npd), F32),
            pltpu.VMEM((XS, 1, npd), F32),
            dma((3,)),
            dma,
            dma,
            dma,
            dma,
            dma((17,)),
            dma((2,)),
            dma,
            dma,
            dma((3,)),
            dma((2,)),
            dma((8,)),
            dma((8,)),
            dma,
            dma,
            dma,
            dma,
            dma,
            dma,
        ],
        compiler_params=pltpu.CompilerParams(
            collective_id=0, has_side_effects=True, vmem_limit_bytes=40 * 1024 * 1024
        ),
        cost_estimate=pl.CostEstimate(
            flops=2 * 1024 * 1024 * width, bytes_accessed=npd * width * 2, transcendentals=0
        ),
    )(*(pltpu.with_memory_space_constraint(value, pltpu.HBM) for value in operands))


def solution(mesh):
    in_specs = (P(("dp", "sub"), None), P(None, ("dp", "sub")), P(None, ("dp", "sub")))
    out_specs = P(None, ("dp", "sub"))
    return jax.shard_map(shards, mesh=mesh, in_specs=in_specs, out_specs=out_specs, check_vma=False)
```

```python
import jax
import jax.numpy as jnp
from jax import lax
from jax.experimental import pallas as pl
from jax.experimental.pallas import tpu as pltpu
from jax.sharding import PartitionSpec as P

ROUNDS = 3
SLOTS = 4
XS = 4
ZS = 16
YS = 4
SUBS = 8
RAW = 16
BLK = 8
SHARE = 2
USED_ROWS = pl.ds(0, ROUNDS * SHARE)
NEAR = 9
HALF = ZS // 2
MESH = pl.DeviceIdType.MESH
F32 = jnp.float32
INF = float("inf")


def kernel(
    npts,
    rows_in,
    counts_in,
    points_ref,
    out_ref,
    rows_ref,
    cnt_ref,
    raw,
    slots,
    cand,
    pall,
    mins,
    squares,
    line,
    near,
    line_sum,
    zsum,
    ysum,
    local_sem,
    slots_send,
    slots_recv,
    z_block_send,
    y_send,
    z_block_recv,
    y_recv,
    far_send,
    far_z_send,
    far_recv,
    far_z_recv,
    pts_send,
    pts_recv,
    line_send,
    line_recv,
    z_send,
    z_recv,
    c_send,
    c_recv,
):
    dp = lax.axis_index("dp")
    sub = lax.axis_index("sub")
    x, z = lax.div(dp, ZS), lax.rem(dp, ZS)
    y, core = lax.div(sub, 2), lax.rem(sub, 2)
    npd, width = points_ref.shape

    def at_x(d):
        return (lax.rem(x + d, XS) * ZS + z, sub)

    def at_z(d):
        return (x * ZS + lax.rem(z + d, ZS), sub)

    def at_y(d):
        return (dp, lax.rem(y + d, YS) * 2 + core)

    other_core = (dp, y * 2 + (1 - core))
    z_to = {d: at_z(d % ZS) for d in (1, -1, 2, -2, 3, -3, 4, -4)}
    y_to = {d: at_y(d) for d in (1, 2, 3)}
    me = x * 2 + core
    x_right, x_left = at_x(1), at_x(3)

    own_points = pltpu.make_async_copy(points_ref, raw, local_sem.at[0])
    own_points.start()
    own_rows = pltpu.make_async_copy(rows_in, rows_ref, local_sem.at[1])
    own_rows.start()
    own_counts = pltpu.make_async_copy(counts_in, cnt_ref, local_sem.at[2])
    own_counts.start()
    barrier = pltpu.get_barrier_semaphore()
    far_first = ((2, 0), (2, 1), (1, 0), (3, 0), (1, 1), (3, 1), (0, 1))
    y_line = [(dp, lax.rem(y + d, YS) * 2 + (1 - core if other else core)) for d, other in far_first]
    x_line = [(lax.rem(x + d, XS) * ZS + z, y * 2 + (1 - core if other else core)) for d, other in far_first]
    partners = [*z_to.values(), *y_line, *x_line[:-1]]
    for device in partners:
        pl.semaphore_signal(barrier, inc=1, device_id=device, device_id_type=MESH)

    row = lax.broadcasted_iota(jnp.int32, (RAW, npd), 0)
    lane = lax.broadcasted_iota(jnp.int32, (RAW, npd), 1)
    here = lax.broadcasted_iota(jnp.int32, (npd, npd), 0)
    there = lax.broadcasted_iota(jnp.int32, (npd, npd), 1)
    same_round = (here & (RAW - 1)) == ROUNDS * SLOTS + ((there & (RAW - 1)) >> 2)
    before = jnp.where(same_round & ((here >> 4) < (there >> 4)), 1.0, 0.0)
    itself = jnp.where(same_round & ((here >> 4) == (there >> 4)), 1.0, 0.0)
    slot = lane & (RAW - 1)
    slot_round = jnp.where(slot < ROUNDS * SLOTS, slot >> 2, -1)
    slot_index = (slot & (SLOTS - 1)).astype(F32)
    wanted = (SHARE * sub + (row & 1)).astype(F32)
    wanted_round = slot_round == (row >> 1)
    own_rows.wait()
    own_counts.wait()
    target = jnp.full((RAW, npd), -1, jnp.int32)
    counts = jnp.zeros((RAW, npd), F32)
    for r in range(ROUNDS):
        counts = jnp.where(row == ROUNDS * SLOTS + r, cnt_ref[0, r].astype(F32), counts)
        for i in range(SLOTS):
            target = jnp.where(row == r * SLOTS + i, rows_ref[r, i], target)
    pick = jnp.where(lane == target, 1.0, 0.0).astype(jnp.bfloat16)
    own_points.wait()
    mine = raw[...]
    block = jnp.dot(pick, mine, preferred_element_type=F32)
    slots[sub, :, :npd] = (block[:, :npd] + counts).astype(jnp.bfloat16)
    slots[sub, :, npd:] = block[:, npd:].astype(jnp.bfloat16)

    pl.semaphore_wait(barrier, len(partners))

    def remote(src, dst, send, recv, device):
        return pltpu.make_async_remote_copy(
            src_ref=src, dst_ref=dst, send_sem=send, recv_sem=recv, device_id=device, device_id_type=MESH
        )

    def to_sides(place, count, group):
        for d, column in ((1, 2), (3, 3)):
            src, dst = cand.at[0, pl.ds(place, count), USED_ROWS], cand.at[column, pl.ds(place, count), USED_ROWS]
            remote(src, dst, y_send, y_recv.at[group], y_to[d]).start()

    def to_far(place):
        remote(cand.at[0, place, USED_ROWS], cand.at[1, place, USED_ROWS], far_send, far_recv.at[place - 6], y_to[2]).start()

    def far_along_z(src, place, count, group, d, lanes=None):
        src, dst = cand.at[1, pl.ds(src, count), USED_ROWS], cand.at[1, pl.ds(place, count), USED_ROWS]
        if lanes is not None:
            part = pl.ds(lanes * (width // 2), width // 2)
            src, dst = src.at[:, :, part], dst.at[:, :, part]
        remote(src, dst, far_z_send, far_z_recv.at[group], z_to[d]).start()

    def along_z(src, place, d, lanes=None):
        if lanes is None:
            src, dst = cand.at[0, src, USED_ROWS], cand.at[0, place, USED_ROWS]
        else:
            part = pl.ds(lanes * (width // 2), width // 2)
            src, dst = cand.at[0, src, USED_ROWS, part], cand.at[0, place, USED_ROWS, part]
        remote(src, dst, z_block_send, z_block_recv.at[place + (lanes or 0)], z_to[d]).start()

    def z_arrived(*places):
        for place in places:
            wait_bytes(cand.at[0, place, USED_ROWS], z_block_recv.at[place])

    def wait_bytes(ref, sem):
        pltpu.make_async_copy(ref, ref, sem).wait()

    for device in y_line:
        remote(slots.at[sub], slots.at[sub], slots_send, slots_recv, device).start()
    pall[me] = mine.T
    slot_right, slot_left, slot_far = (lax.rem(x + d, XS) * 2 + core for d in (1, 3, 2))
    top, low = pl.ds(0, width // 2), pl.ds(width // 2, width // 2)
    mine_at = pall.at[me]
    pts_right = remote(mine_at, mine_at, pts_send.at[0], pts_recv.at[0], x_right)
    pts_left = remote(mine_at, mine_at, pts_send.at[1], pts_recv.at[1], x_left)
    pts_core = remote(mine_at, mine_at, pts_send.at[2], pts_recv.at[2], other_core)
    pts_right.start()
    pts_left.start()
    pts_core.start()

    wait_bytes(slots.at[pl.ds(0, SUBS - 1)], slots_recv)
    flat = slots[...].reshape(SUBS * RAW, width)
    known = flat[:, :npd].astype(F32)
    offset = jnp.sum(known * before, axis=0, keepdims=True)
    count = jnp.sum(known * itself, axis=0, keepdims=True)
    choice = wanted_round & (slot_index < count) & (offset + slot_index == wanted)
    share = jnp.dot(jnp.where(choice, 1.0, 0.0).astype(jnp.bfloat16), flat, preferred_element_type=F32)
    cand[0, 7] = share[:BLK].astype(jnp.bfloat16)

    along_z(7, 6, 4)
    along_z(7, 8, -4)
    to_far(7)
    for place, d in ((0, 2), (1, -2), (2, 1), (5, -1)):
        along_z(7, place, d)
    to_sides(7, 1, 0)

    pts_right.wait_recv()
    near_left = pall.at[slot_left]
    far_top = remote(near_left.at[top], near_left.at[top], pts_send.at[3], pts_recv.at[3], x_right)
    core_left = remote(near_left, near_left, pts_send.at[4], pts_recv.at[4], other_core)
    far_top.start()
    core_left.start()
    pts_left.wait_recv()
    near_right = pall.at[slot_right]
    far_low = remote(near_right.at[low], near_right.at[low], pts_send.at[5], pts_recv.at[5], x_left)
    core_right = remote(near_right, near_right, pts_send.at[6], pts_recv.at[6], other_core)
    far_low.start()
    core_right.start()

    z_arrived(6)
    to_far(6)
    along_z(6, 15, 4, 0)
    for place, d in ((13, 3), (9, 2), (11, 1), (4, -1)):
        along_z(6, place, d)
    z_arrived(8)
    to_far(8)
    along_z(8, 15, -4, 1)
    for place, d in ((14, -3), (10, -2), (12, -1), (3, 1)):
        along_z(8, place, d)
    to_sides(6, 1, 0)
    to_sides(8, 1, 0)

    for place in (6, 7, 8):
        wait_bytes(cand.at[1, place, USED_ROWS], far_recv.at[place - 6])
    far_along_z(6, 15, 1, 1, 4, 0)
    far_along_z(8, 15, 1, 1, -4, 1)
    far_along_z(6, 13, 1, 1, 3)
    far_along_z(8, 14, 1, 1, -3)
    far_along_z(6, 9, 1, 1, 2)
    far_along_z(8, 10, 1, 1, -2)
    far_along_z(6, 11, 1, 1, 1)
    far_along_z(8, 12, 1, 1, -1)
    far_along_z(7, 0, 1, 0, 2)
    far_along_z(7, 1, 1, 0, -2)
    far_along_z(7, 2, 2, 0, 1)
    far_along_z(6, 4, 2, 0, -1)

    far_top.wait_recv()
    far_low.wait_recv()
    far = pall.at[slot_far]
    core_far = remote(far, far, pts_send.at[7], pts_recv.at[7], other_core)
    core_far.start()

    z_arrived(0, 1, 2, 3, 4, 5)
    to_sides(0, 6, 0)
    z_arrived(9, 10, 11, 12, 13, 14)
    to_sides(9, 6, 1)
    half_block = cand.at[0, 15, USED_ROWS, pl.ds(0, width // 2)]
    wait_bytes(half_block, z_block_recv.at[15])
    wait_bytes(half_block, z_block_recv.at[16])
    to_sides(15, 1, 1)

    def absorb(first, count):
        blocks = XS * count
        rows = cand[:, first : first + count].reshape(blocks, BLK, width)
        half = jnp.zeros((blocks, BLK, npd), F32)
        for t in range(width // npd):
            piece = rows[:, :, t * npd : (t + 1) * npd].astype(F32)
            half = half + piece * piece
        half = 0.5 * jnp.sum(half, axis=2, keepdims=True)
        flat = rows.reshape(blocks * BLK, width)
        for j in range(SUBS // 2):
            group = jnp.concatenate([pall[2 * j], pall[2 * j + 1]], axis=1)
            dots = jnp.dot(flat, group, preferred_element_type=F32)
            best = jnp.min(half - dots.reshape(blocks, BLK, 2 * npd), axis=0)
            mins[j] = best if first == 0 else jnp.minimum(mins[j], best)

    pts_core.wait_recv()
    core_left.wait_recv()
    core_right.wait_recv()
    core_far.wait_recv()
    for b in range(SUBS):
        wide = pall[b].astype(F32)
        squares[b : b + 1, :] = jnp.sum(wide * wide, axis=0, keepdims=True)
    wait_bytes(cand.at[pl.ds(2, 2), pl.ds(0, NEAR), USED_ROWS], y_recv.at[0])
    wait_bytes(cand.at[1, pl.ds(0, 6), USED_ROWS], far_z_recv.at[0])
    absorb(0, NEAR)
    wait_bytes(cand.at[pl.ds(2, 2), pl.ds(NEAR, ZS - NEAR), USED_ROWS], y_recv.at[1])
    wait_bytes(cand.at[1, pl.ds(NEAR, ZS - NEAR), USED_ROWS], far_z_recv.at[1])
    absorb(NEAR, ZS - NEAR)

    for j in range(SUBS // 2):
        for r in range(ROUNDS):
            low_r = jnp.min(mins[j, r * SHARE : (r + 1) * SHARE, :], axis=0, keepdims=True)
            for h in range(2):
                line[me, r, 2 * j + h : 2 * j + h + 1, :] = low_r[:, h * npd : (h + 1) * npd]

    for device in x_line:
        remote(line.at[me], line.at[me], line_send, line_recv, device).start()
    wait_bytes(line.at[pl.ds(0, SUBS - 1)], line_recv)

    lanes = lax.broadcasted_iota(jnp.int32, (1, npd), 1)
    least = None
    total = jnp.zeros((1, npd), F32)
    for r in range(ROUNDS):
        now = jnp.min(line[:, r], axis=0)
        least = now if least is None else jnp.minimum(least, now)
        dist = jnp.maximum(squares[...] + 2.0 * least, 0.0)
        near[r] = dist
        part = jnp.sum(jnp.sum(dist, axis=0, keepdims=True), axis=1, keepdims=True)
        total = jnp.where(lanes == r, part, total)

    line_sum[...] = total

    @pl.when(core == 0)
    def _():
        zsum[0] = total

    @pl.when(core == 1)
    def _():
        remote(line_sum, zsum.at[0], z_send, z_recv, at_z(HALF)).start()

    for k in range(HALF - 1):
        place = HALF - 1 - k + core * (2 * k + 2 - HALF)
        remote(line_sum, zsum.at[place], z_send, z_recv, at_z(HALF * core + place)).start()

    def wait_z(sem):
        @pl.when(core == 0)
        def _():
            wait_bytes(zsum.at[pl.ds(0, HALF - 1)], sem)

        @pl.when(core == 1)
        def _():
            wait_bytes(zsum, sem)

    wait_bytes(slots.at[pl.ds(0, SUBS - 1)], slots_send)
    wait_bytes(cand.at[0, pl.ds(0, 15), USED_ROWS], z_block_send)
    wait_bytes(cand.at[pl.ds(0, 2), :, USED_ROWS], y_send)
    wait_bytes(cand.at[0, pl.ds(0, 3), USED_ROWS], far_send)
    wait_bytes(cand.at[0, pl.ds(0, 13), USED_ROWS], far_z_send)
    for copy in (pts_right, pts_left, pts_core, far_top, core_left, far_low, core_right, core_far):
        copy.wait_send()
    wait_bytes(line.at[pl.ds(0, SUBS - 1)], line_send)
    wait_z(z_recv)
    ysum[0] = jnp.sum(zsum[...], axis=0)
    for (d, other), device in zip(far_first, y_line):
        remote(ysum.at[0], ysum.at[(YS - d) % YS * 2 + other], c_send, c_recv, device).start()
    wait_bytes(ysum.at[pl.ds(0, SUBS - 1)], c_recv)
    cost = jnp.sum(ysum[...], axis=0)
    for r in range(ROUNDS):
        cost_r = jnp.sum(jnp.where(lanes == r, cost, 0.0), axis=1, keepdims=True)
        out_ref[r : r + 1, :] = npts * near[r, pl.ds(me, 1), :] / cost_r
    wait_z(z_send)
    wait_bytes(ysum.at[pl.ds(0, SUBS - 1)], c_send)


def shards(points, cand_rows, cand_count):
    npd, width = points.shape
    npts = float(npd * lax.axis_size(("dp", "sub")))
    dma = pltpu.SemaphoreType.DMA
    operands = (cand_rows, cand_count.reshape(1, ROUNDS), points)
    return pl.pallas_call(
        lambda *refs: kernel(npts, *refs),
        out_shape=jax.ShapeDtypeStruct((ROUNDS, npd), F32),
        in_specs=[
            pl.BlockSpec(memory_space=pl.ANY),
            pl.BlockSpec(memory_space=pl.ANY),
            pl.BlockSpec(memory_space=pl.ANY),
        ],
        out_specs=pl.BlockSpec(memory_space=pltpu.VMEM),
        scratch_shapes=[
            pltpu.SMEM((ROUNDS, SLOTS), jnp.int32),
            pltpu.SMEM((1, ROUNDS), jnp.int32),
            pltpu.VMEM((npd, width), jnp.bfloat16),
            pltpu.VMEM((SUBS, RAW, width), jnp.bfloat16),
            pltpu.VMEM((XS, ZS, BLK, width), jnp.bfloat16),
            pltpu.VMEM((SUBS, width, npd), jnp.bfloat16),
            pltpu.VMEM((SUBS // 2, BLK, 2 * npd), F32),
            pltpu.VMEM((SUBS, npd), F32),
            pltpu.VMEM((SUBS, ROUNDS, SUBS, npd), F32),
            pltpu.VMEM((ROUNDS, SUBS, npd), F32),
            pltpu.VMEM((1, npd), F32),
            pltpu.VMEM((HALF, 1, npd), F32),
            pltpu.VMEM((SUBS, 1, npd), F32),
            dma((3,)),
            dma,
            dma,
            dma,
            dma,
            dma((17,)),
            dma((2,)),
            dma,
            dma,
            dma((3,)),
            dma((2,)),
            dma((8,)),
            dma((8,)),
            dma,
            dma,
            dma,
            dma,
            dma,
            dma,
        ],
        compiler_params=pltpu.CompilerParams(
            collective_id=0, has_side_effects=True, vmem_limit_bytes=40 * 1024 * 1024
        ),
        cost_estimate=pl.CostEstimate(
            flops=2 * 1024 * 1024 * width, bytes_accessed=npd * width * 2, transcendentals=0
        ),
    )(*(pltpu.with_memory_space_constraint(value, pltpu.HBM) for value in operands))


def solution(mesh):
    in_specs = (P(("dp", "sub"), None), P(None, ("dp", "sub")), P(None, ("dp", "sub")))
    out_specs = P(None, ("dp", "sub"))
    return jax.shard_map(shards, mesh=mesh, in_specs=in_specs, out_specs=out_specs, check_vma=False)
```

```python
import jax
import jax.numpy as jnp
from jax import lax
from jax.experimental import pallas as pl
from jax.experimental.pallas import tpu as pltpu
from jax.sharding import PartitionSpec as P

ROUNDS = 3
SLOTS = 4
XS = 4
ZS = 16
YS = 4
SUBS = 8
RAW = 16
BLK = 8
SHARE = 2
USED_ROWS = pl.ds(0, ROUNDS * SHARE)
NEAR = 9
MESH = pl.DeviceIdType.MESH
F32 = jnp.float32
INF = float("inf")


def kernel(
    npts,
    rows_in,
    counts_in,
    points_ref,
    out_ref,
    rows_ref,
    cnt_ref,
    raw,
    slots,
    cand,
    pall,
    mins,
    squares,
    line,
    near,
    zsum,
    ysum,
    local_sem,
    slots_send,
    slots_recv,
    z_block_send,
    y_send,
    z_block_recv,
    y_recv,
    far_send,
    far_z_send,
    far_recv,
    far_z_recv,
    pts_send,
    pts_recv,
    line_send,
    line_recv,
    z_send,
    z_recv,
    c_send,
    c_recv,
):
    dp = lax.axis_index("dp")
    sub = lax.axis_index("sub")
    x, z = lax.div(dp, ZS), lax.rem(dp, ZS)
    y, core = lax.div(sub, 2), lax.rem(sub, 2)
    npd, width = points_ref.shape

    def at_x(d):
        return (lax.rem(x + d, XS) * ZS + z, sub)

    def at_z(d):
        return (x * ZS + lax.rem(z + d, ZS), sub)

    def at_y(d):
        return (dp, lax.rem(y + d, YS) * 2 + core)

    other_core = (dp, y * 2 + (1 - core))
    z_to = {d: at_z(d % ZS) for d in (1, -1, 2, -2, 3, -3, 4, -4)}
    y_to = {d: at_y(d) for d in (1, 2, 3)}
    me = x * 2 + core
    x_right, x_left = at_x(1), at_x(3)

    own_points = pltpu.make_async_copy(points_ref, raw, local_sem.at[0])
    own_points.start()
    own_rows = pltpu.make_async_copy(rows_in, rows_ref, local_sem.at[1])
    own_rows.start()
    own_counts = pltpu.make_async_copy(counts_in, cnt_ref, local_sem.at[2])
    own_counts.start()
    barrier = pltpu.get_barrier_semaphore()
    far_first = ((2, 0), (2, 1), (1, 0), (3, 0), (1, 1), (3, 1), (0, 1))
    y_line = [(dp, lax.rem(y + d, YS) * 2 + (1 - core if other else core)) for d, other in far_first]
    x_line = [(lax.rem(x + d, XS) * ZS + z, y * 2 + (1 - core if other else core)) for d, other in far_first]
    partners = [*z_to.values(), *y_line, *x_line[:-1]]
    for device in partners:
        pl.semaphore_signal(barrier, inc=1, device_id=device, device_id_type=MESH)

    row = lax.broadcasted_iota(jnp.int32, (RAW, npd), 0)
    lane = lax.broadcasted_iota(jnp.int32, (RAW, npd), 1)
    here = lax.broadcasted_iota(jnp.int32, (npd, npd), 0)
    there = lax.broadcasted_iota(jnp.int32, (npd, npd), 1)
    same_round = (here & (RAW - 1)) == ROUNDS * SLOTS + ((there & (RAW - 1)) >> 2)
    before = jnp.where(same_round & ((here >> 4) < (there >> 4)), 1.0, 0.0)
    itself = jnp.where(same_round & ((here >> 4) == (there >> 4)), 1.0, 0.0)
    slot = lane & (RAW - 1)
    slot_round = jnp.where(slot < ROUNDS * SLOTS, slot >> 2, -1)
    slot_index = (slot & (SLOTS - 1)).astype(F32)
    wanted = (SHARE * sub + (row & 1)).astype(F32)
    wanted_round = slot_round == (row >> 1)
    own_rows.wait()
    own_counts.wait()
    target = jnp.full((RAW, npd), -1, jnp.int32)
    counts = jnp.zeros((RAW, npd), F32)
    for r in range(ROUNDS):
        counts = jnp.where(row == ROUNDS * SLOTS + r, cnt_ref[0, r].astype(F32), counts)
        for i in range(SLOTS):
            target = jnp.where(row == r * SLOTS + i, rows_ref[r, i], target)
    pick = jnp.where(lane == target, 1.0, 0.0).astype(jnp.bfloat16)
    own_points.wait()
    mine = raw[...]
    block = jnp.dot(pick, mine, preferred_element_type=F32)
    slots[sub, :, :npd] = (block[:, :npd] + counts).astype(jnp.bfloat16)
    slots[sub, :, npd:] = block[:, npd:].astype(jnp.bfloat16)

    pl.semaphore_wait(barrier, len(partners))

    def remote(src, dst, send, recv, device):
        return pltpu.make_async_remote_copy(
            src_ref=src, dst_ref=dst, send_sem=send, recv_sem=recv, device_id=device, device_id_type=MESH
        )

    def to_sides(place, count, group):
        for d, column in ((1, 2), (3, 3)):
            src, dst = cand.at[0, pl.ds(place, count), USED_ROWS], cand.at[column, pl.ds(place, count), USED_ROWS]
            remote(src, dst, y_send, y_recv.at[group], y_to[d]).start()

    def to_far(place):
        remote(cand.at[0, place, USED_ROWS], cand.at[1, place, USED_ROWS], far_send, far_recv.at[place - 6], y_to[2]).start()

    def far_along_z(src, place, count, group, d, lanes=None):
        src, dst = cand.at[1, pl.ds(src, count), USED_ROWS], cand.at[1, pl.ds(place, count), USED_ROWS]
        if lanes is not None:
            part = pl.ds(lanes * (width // 2), width // 2)
            src, dst = src.at[:, :, part], dst.at[:, :, part]
        remote(src, dst, far_z_send, far_z_recv.at[group], z_to[d]).start()

    def along_z(src, place, d, lanes=None):
        if lanes is None:
            src, dst = cand.at[0, src, USED_ROWS], cand.at[0, place, USED_ROWS]
        else:
            part = pl.ds(lanes * (width // 2), width // 2)
            src, dst = cand.at[0, src, USED_ROWS, part], cand.at[0, place, USED_ROWS, part]
        remote(src, dst, z_block_send, z_block_recv.at[place + (lanes or 0)], z_to[d]).start()

    def z_arrived(*places):
        for place in places:
            wait_bytes(cand.at[0, place, USED_ROWS], z_block_recv.at[place])

    def wait_bytes(ref, sem):
        pltpu.make_async_copy(ref, ref, sem).wait()

    for device in y_line:
        remote(slots.at[sub], slots.at[sub], slots_send, slots_recv, device).start()
    pall[me] = mine.T
    slot_right, slot_left, slot_far = (lax.rem(x + d, XS) * 2 + core for d in (1, 3, 2))
    top, low = pl.ds(0, width // 2), pl.ds(width // 2, width // 2)
    mine_at = pall.at[me]
    pts_right = remote(mine_at, mine_at, pts_send.at[0], pts_recv.at[0], x_right)
    pts_left = remote(mine_at, mine_at, pts_send.at[1], pts_recv.at[1], x_left)
    pts_core = remote(mine_at, mine_at, pts_send.at[2], pts_recv.at[2], other_core)
    pts_right.start()
    pts_left.start()
    pts_core.start()

    wait_bytes(slots.at[pl.ds(0, SUBS - 1)], slots_recv)
    flat = slots[...].reshape(SUBS * RAW, width)
    known = flat[:, :npd].astype(F32)
    offset = jnp.sum(known * before, axis=0, keepdims=True)
    count = jnp.sum(known * itself, axis=0, keepdims=True)
    choice = wanted_round & (slot_index < count) & (offset + slot_index == wanted)
    share = jnp.dot(jnp.where(choice, 1.0, 0.0).astype(jnp.bfloat16), flat, preferred_element_type=F32)
    cand[0, 7] = share[:BLK].astype(jnp.bfloat16)

    along_z(7, 6, 4)
    along_z(7, 8, -4)
    to_far(7)
    for place, d in ((0, 2), (1, -2), (2, 1), (5, -1)):
        along_z(7, place, d)
    to_sides(7, 1, 0)

    pts_right.wait_recv()
    near_left = pall.at[slot_left]
    far_top = remote(near_left.at[top], near_left.at[top], pts_send.at[3], pts_recv.at[3], x_right)
    core_left = remote(near_left, near_left, pts_send.at[4], pts_recv.at[4], other_core)
    far_top.start()
    core_left.start()
    pts_left.wait_recv()
    near_right = pall.at[slot_right]
    far_low = remote(near_right.at[low], near_right.at[low], pts_send.at[5], pts_recv.at[5], x_left)
    core_right = remote(near_right, near_right, pts_send.at[6], pts_recv.at[6], other_core)
    far_low.start()
    core_right.start()

    z_arrived(6)
    to_far(6)
    along_z(6, 15, 4, 0)
    for place, d in ((13, 3), (9, 2), (11, 1), (4, -1)):
        along_z(6, place, d)
    z_arrived(8)
    to_far(8)
    along_z(8, 15, -4, 1)
    for place, d in ((14, -3), (10, -2), (12, -1), (3, 1)):
        along_z(8, place, d)
    to_sides(6, 1, 0)
    to_sides(8, 1, 0)

    for place in (6, 7, 8):
        wait_bytes(cand.at[1, place, USED_ROWS], far_recv.at[place - 6])
    far_along_z(6, 15, 1, 1, 4, 0)
    far_along_z(8, 15, 1, 1, -4, 1)
    far_along_z(6, 13, 1, 1, 3)
    far_along_z(8, 14, 1, 1, -3)
    far_along_z(6, 9, 1, 1, 2)
    far_along_z(8, 10, 1, 1, -2)
    far_along_z(6, 11, 1, 1, 1)
    far_along_z(8, 12, 1, 1, -1)
    far_along_z(7, 0, 1, 0, 2)
    far_along_z(7, 1, 1, 0, -2)
    far_along_z(7, 2, 2, 0, 1)
    far_along_z(6, 4, 2, 0, -1)

    far_top.wait_recv()
    far_low.wait_recv()
    far = pall.at[slot_far]
    core_far = remote(far, far, pts_send.at[7], pts_recv.at[7], other_core)
    core_far.start()

    z_arrived(0, 1, 2, 3, 4, 5)
    to_sides(0, 6, 0)
    for place in (11, 9, 13):
        z_arrived(place, place + 1)
        to_sides(place, 2, 1)
    half_block = cand.at[0, 15, USED_ROWS, pl.ds(0, width // 2)]
    wait_bytes(half_block, z_block_recv.at[15])
    wait_bytes(half_block, z_block_recv.at[16])
    to_sides(15, 1, 1)

    def absorb(first, count):
        blocks = XS * count
        rows = cand[:, first : first + count].reshape(blocks, BLK, width)
        half = jnp.zeros((blocks, BLK, npd), F32)
        for t in range(width // npd):
            piece = rows[:, :, t * npd : (t + 1) * npd].astype(F32)
            half = half + piece * piece
        half = 0.5 * jnp.sum(half, axis=2, keepdims=True)
        flat = rows.reshape(blocks * BLK, width)
        for j in range(SUBS // 2):
            group = jnp.concatenate([pall[2 * j], pall[2 * j + 1]], axis=1)
            dots = jnp.dot(flat, group, preferred_element_type=F32)
            best = jnp.min(half - dots.reshape(blocks, BLK, 2 * npd), axis=0)
            mins[j] = best if first == 0 else jnp.minimum(mins[j], best)

    pts_core.wait_recv()
    core_left.wait_recv()
    core_right.wait_recv()
    core_far.wait_recv()
    for b in range(SUBS):
        wide = pall[b].astype(F32)
        squares[b : b + 1, :] = jnp.sum(wide * wide, axis=0, keepdims=True)
    wait_bytes(cand.at[pl.ds(2, 2), pl.ds(0, NEAR), USED_ROWS], y_recv.at[0])
    wait_bytes(cand.at[1, pl.ds(0, 6), USED_ROWS], far_z_recv.at[0])
    absorb(0, NEAR)
    wait_bytes(cand.at[pl.ds(2, 2), pl.ds(NEAR, ZS - NEAR), USED_ROWS], y_recv.at[1])
    wait_bytes(cand.at[1, pl.ds(NEAR, ZS - NEAR), USED_ROWS], far_z_recv.at[1])
    absorb(NEAR, ZS - NEAR)

    for j in range(SUBS // 2):
        for r in range(ROUNDS):
            low_r = jnp.min(mins[j, r * SHARE : (r + 1) * SHARE, :], axis=0, keepdims=True)
            for h in range(2):
                line[me, r, 2 * j + h : 2 * j + h + 1, :] = low_r[:, h * npd : (h + 1) * npd]

    for device in x_line:
        remote(line.at[me], line.at[me], line_send, line_recv, device).start()
    wait_bytes(line.at[pl.ds(0, SUBS - 1)], line_recv)

    lanes = lax.broadcasted_iota(jnp.int32, (1, npd), 1)
    least = None
    total = jnp.zeros((1, npd), F32)
    for r in range(ROUNDS):
        now = jnp.min(line[:, r], axis=0)
        least = now if least is None else jnp.minimum(least, now)
        dist = jnp.maximum(squares[...] + 2.0 * least, 0.0)
        near[r] = dist
        part = jnp.sum(jnp.sum(dist, axis=0, keepdims=True), axis=1, keepdims=True)
        total = jnp.where(lanes == r, part, total)

    zsum[0] = total

    for d in (8, 7, 9, 6, 10, 5, 11, 4, 12, 3, 13, 2, 14, 1, 15):
        remote(zsum.at[0], zsum.at[ZS - d], z_send, z_recv, at_z(d)).start()
    wait_bytes(slots.at[pl.ds(0, SUBS - 1)], slots_send)
    wait_bytes(cand.at[0, pl.ds(0, 15), USED_ROWS], z_block_send)
    wait_bytes(cand.at[pl.ds(0, 2), :, USED_ROWS], y_send)
    wait_bytes(cand.at[0, pl.ds(0, 3), USED_ROWS], far_send)
    wait_bytes(cand.at[0, pl.ds(0, 13), USED_ROWS], far_z_send)
    for copy in (pts_right, pts_left, pts_core, far_top, core_left, far_low, core_right, core_far):
        copy.wait_send()
    wait_bytes(line.at[pl.ds(0, SUBS - 1)], line_send)
    wait_bytes(zsum.at[pl.ds(0, ZS - 1)], z_recv)
    ysum[0] = jnp.sum(zsum[...], axis=0)
    for d in (1, 3, 2):
        remote(ysum.at[0], ysum.at[XS - d], c_send, c_recv, y_to[d]).start()
    wait_bytes(ysum.at[pl.ds(0, XS - 1)], c_recv)
    cost = jnp.sum(ysum[...], axis=0)
    for r in range(ROUNDS):
        cost_r = jnp.sum(jnp.where(lanes == r, cost, 0.0), axis=1, keepdims=True)
        out_ref[r : r + 1, :] = npts * near[r, pl.ds(me, 1), :] / cost_r
    wait_bytes(zsum.at[pl.ds(0, ZS - 1)], z_send)
    wait_bytes(ysum.at[pl.ds(0, XS - 1)], c_send)


def shards(points, cand_rows, cand_count):
    npd, width = points.shape
    npts = float(npd * lax.axis_size(("dp", "sub")))
    dma = pltpu.SemaphoreType.DMA
    operands = (cand_rows, cand_count.reshape(1, ROUNDS), points)
    return pl.pallas_call(
        lambda *refs: kernel(npts, *refs),
        out_shape=jax.ShapeDtypeStruct((ROUNDS, npd), F32),
        in_specs=[
            pl.BlockSpec(memory_space=pl.ANY),
            pl.BlockSpec(memory_space=pl.ANY),
            pl.BlockSpec(memory_space=pl.ANY),
        ],
        out_specs=pl.BlockSpec(memory_space=pltpu.VMEM),
        scratch_shapes=[
            pltpu.SMEM((ROUNDS, SLOTS), jnp.int32),
            pltpu.SMEM((1, ROUNDS), jnp.int32),
            pltpu.VMEM((npd, width), jnp.bfloat16),
            pltpu.VMEM((SUBS, RAW, width), jnp.bfloat16),
            pltpu.VMEM((XS, ZS, BLK, width), jnp.bfloat16),
            pltpu.VMEM((SUBS, width, npd), jnp.bfloat16),
            pltpu.VMEM((SUBS // 2, BLK, 2 * npd), F32),
            pltpu.VMEM((SUBS, npd), F32),
            pltpu.VMEM((SUBS, ROUNDS, SUBS, npd), F32),
            pltpu.VMEM((ROUNDS, SUBS, npd), F32),
            pltpu.VMEM((ZS, 1, npd), F32),
            pltpu.VMEM((XS, 1, npd), F32),
            dma((3,)),
            dma,
            dma,
            dma,
            dma,
            dma((17,)),
            dma((2,)),
            dma,
            dma,
            dma((3,)),
            dma((2,)),
            dma((8,)),
            dma((8,)),
            dma,
            dma,
            dma,
            dma,
            dma,
            dma,
        ],
        compiler_params=pltpu.CompilerParams(
            collective_id=0, has_side_effects=True, vmem_limit_bytes=40 * 1024 * 1024
        ),
        cost_estimate=pl.CostEstimate(
            flops=2 * 1024 * 1024 * width, bytes_accessed=npd * width * 2, transcendentals=0
        ),
    )(*(pltpu.with_memory_space_constraint(value, pltpu.HBM) for value in operands))


def solution(mesh):
    in_specs = (P(("dp", "sub"), None), P(None, ("dp", "sub")), P(None, ("dp", "sub")))
    out_specs = P(None, ("dp", "sub"))
    return jax.shard_map(shards, mesh=mesh, in_specs=in_specs, out_specs=out_specs, check_vma=False)
```

```python
import jax
import jax.numpy as jnp
from jax import lax
from jax.experimental import pallas as pl
from jax.experimental.pallas import tpu as pltpu
from jax.sharding import PartitionSpec as P

ROUNDS = 3
SLOTS = 4
XS = 4
ZS = 16
YS = 4
SUBS = 8
RAW = 16
BLK = 8
SHARE = 2
USED_ROWS = pl.ds(0, ROUNDS * SHARE)
NEAR = 9
MESH = pl.DeviceIdType.MESH
F32 = jnp.float32
INF = float("inf")


def kernel(
    npts,
    rows_in,
    counts_in,
    points_ref,
    out_ref,
    rows_ref,
    cnt_ref,
    raw,
    slots,
    cand,
    pall,
    mins,
    squares,
    pair,
    line,
    near,
    zsum,
    ysum,
    local_sem,
    slots_send,
    slots_recv,
    z_block_send,
    y_send,
    z_block_recv,
    y_recv,
    far_send,
    far_z_send,
    far_recv,
    far_z_recv,
    pts_send,
    pts_recv,
    pair_send,
    pair_recv,
    line_send,
    line_recv,
    z_send,
    z_recv,
    c_send,
    c_recv,
):
    dp = lax.axis_index("dp")
    sub = lax.axis_index("sub")
    x, z = lax.div(dp, ZS), lax.rem(dp, ZS)
    y, core = lax.div(sub, 2), lax.rem(sub, 2)
    npd, width = points_ref.shape

    def at_x(d):
        return (lax.rem(x + d, XS) * ZS + z, sub)

    def at_z(d):
        return (x * ZS + lax.rem(z + d, ZS), sub)

    def at_y(d):
        return (dp, lax.rem(y + d, YS) * 2 + core)

    other_core = (dp, y * 2 + (1 - core))
    z_to = {d: at_z(d % ZS) for d in (1, -1, 2, -2, 3, -3, 4, -4)}
    y_to = {d: at_y(d) for d in (1, 2, 3)}
    me = x * 2 + core
    x_right, x_left = at_x(1), at_x(3)

    own_points = pltpu.make_async_copy(points_ref, raw, local_sem.at[0])
    own_points.start()
    own_rows = pltpu.make_async_copy(rows_in, rows_ref, local_sem.at[1])
    own_rows.start()
    own_counts = pltpu.make_async_copy(counts_in, cnt_ref, local_sem.at[2])
    own_counts.start()
    barrier = pltpu.get_barrier_semaphore()
    far_first = ((2, 0), (2, 1), (1, 0), (3, 0), (1, 1), (3, 1), (0, 1))
    y_line = [(dp, lax.rem(y + d, YS) * 2 + (1 - core if other else core)) for d, other in far_first]
    x_line = [(lax.rem(x + d, XS) * ZS + z, y * 2 + (1 - core if other else core)) for d, other in far_first]
    partners = [*z_to.values(), *y_line, *x_line[:-1]]
    for device in partners:
        pl.semaphore_signal(barrier, inc=1, device_id=device, device_id_type=MESH)

    row = lax.broadcasted_iota(jnp.int32, (RAW, npd), 0)
    lane = lax.broadcasted_iota(jnp.int32, (RAW, npd), 1)
    here = lax.broadcasted_iota(jnp.int32, (npd, npd), 0)
    there = lax.broadcasted_iota(jnp.int32, (npd, npd), 1)
    same_round = (here & (RAW - 1)) == ROUNDS * SLOTS + ((there & (RAW - 1)) >> 2)
    before = jnp.where(same_round & ((here >> 4) < (there >> 4)), 1.0, 0.0)
    itself = jnp.where(same_round & ((here >> 4) == (there >> 4)), 1.0, 0.0)
    slot = lane & (RAW - 1)
    slot_round = jnp.where(slot < ROUNDS * SLOTS, slot >> 2, -1)
    slot_index = (slot & (SLOTS - 1)).astype(F32)
    wanted = (SHARE * sub + (row & 1)).astype(F32)
    wanted_round = slot_round == (row >> 1)
    own_rows.wait()
    own_counts.wait()
    target = jnp.full((RAW, npd), -1, jnp.int32)
    counts = jnp.zeros((RAW, npd), F32)
    for r in range(ROUNDS):
        counts = jnp.where(row == ROUNDS * SLOTS + r, cnt_ref[0, r].astype(F32), counts)
        for i in range(SLOTS):
            target = jnp.where(row == r * SLOTS + i, rows_ref[r, i], target)
    pick = jnp.where(lane == target, 1.0, 0.0).astype(jnp.bfloat16)
    own_points.wait()
    mine = raw[...]
    block = jnp.dot(pick, mine, preferred_element_type=F32)
    slots[sub, :, :npd] = (block[:, :npd] + counts).astype(jnp.bfloat16)
    slots[sub, :, npd:] = block[:, npd:].astype(jnp.bfloat16)

    pl.semaphore_wait(barrier, len(partners))

    def remote(src, dst, send, recv, device):
        return pltpu.make_async_remote_copy(
            src_ref=src, dst_ref=dst, send_sem=send, recv_sem=recv, device_id=device, device_id_type=MESH
        )

    def to_sides(place, count, group):
        for d, column in ((1, 2), (3, 3)):
            src, dst = cand.at[0, pl.ds(place, count), USED_ROWS], cand.at[column, pl.ds(place, count), USED_ROWS]
            remote(src, dst, y_send, y_recv.at[group], y_to[d]).start()

    def to_far(place):
        remote(cand.at[0, place, USED_ROWS], cand.at[1, place, USED_ROWS], far_send, far_recv.at[place - 6], y_to[2]).start()

    def far_along_z(src, place, count, group, d, lanes=None):
        src, dst = cand.at[1, pl.ds(src, count), USED_ROWS], cand.at[1, pl.ds(place, count), USED_ROWS]
        if lanes is not None:
            part = pl.ds(lanes * (width // 2), width // 2)
            src, dst = src.at[:, :, part], dst.at[:, :, part]
        remote(src, dst, far_z_send, far_z_recv.at[group], z_to[d]).start()

    def along_z(src, place, d, lanes=None):
        if lanes is None:
            src, dst = cand.at[0, src, USED_ROWS], cand.at[0, place, USED_ROWS]
        else:
            part = pl.ds(lanes * (width // 2), width // 2)
            src, dst = cand.at[0, src, USED_ROWS, part], cand.at[0, place, USED_ROWS, part]
        remote(src, dst, z_block_send, z_block_recv.at[place + (lanes or 0)], z_to[d]).start()

    def z_arrived(*places):
        for place in places:
            wait_bytes(cand.at[0, place, USED_ROWS], z_block_recv.at[place])

    def wait_bytes(ref, sem):
        pltpu.make_async_copy(ref, ref, sem).wait()

    for device in y_line:
        remote(slots.at[sub], slots.at[sub], slots_send, slots_recv, device).start()
    pall[me] = mine.T
    slot_right, slot_left, slot_far = (lax.rem(x + d, XS) * 2 + core for d in (1, 3, 2))
    top, low = pl.ds(0, width // 2), pl.ds(width // 2, width // 2)
    mine_at = pall.at[me]
    pts_right = remote(mine_at, mine_at, pts_send.at[0], pts_recv.at[0], x_right)
    pts_left = remote(mine_at, mine_at, pts_send.at[1], pts_recv.at[1], x_left)
    pts_core = remote(mine_at, mine_at, pts_send.at[2], pts_recv.at[2], other_core)
    pts_right.start()
    pts_left.start()
    pts_core.start()

    wait_bytes(slots.at[pl.ds(0, SUBS - 1)], slots_recv)
    flat = slots[...].reshape(SUBS * RAW, width)
    known = flat[:, :npd].astype(F32)
    offset = jnp.sum(known * before, axis=0, keepdims=True)
    count = jnp.sum(known * itself, axis=0, keepdims=True)
    choice = wanted_round & (slot_index < count) & (offset + slot_index == wanted)
    share = jnp.dot(jnp.where(choice, 1.0, 0.0).astype(jnp.bfloat16), flat, preferred_element_type=F32)
    cand[0, 7] = share[:BLK].astype(jnp.bfloat16)

    along_z(7, 6, 4)
    along_z(7, 8, -4)
    to_far(7)
    for place, d in ((0, 2), (1, -2), (2, 1), (5, -1)):
        along_z(7, place, d)
    to_sides(7, 1, 0)

    pts_right.wait_recv()
    near_left = pall.at[slot_left]
    far_top = remote(near_left.at[top], near_left.at[top], pts_send.at[3], pts_recv.at[3], x_right)
    core_left = remote(near_left, near_left, pts_send.at[4], pts_recv.at[4], other_core)
    far_top.start()
    core_left.start()
    pts_left.wait_recv()
    near_right = pall.at[slot_right]
    far_low = remote(near_right.at[low], near_right.at[low], pts_send.at[5], pts_recv.at[5], x_left)
    core_right = remote(near_right, near_right, pts_send.at[6], pts_recv.at[6], other_core)
    far_low.start()
    core_right.start()

    z_arrived(6)
    to_far(6)
    along_z(6, 15, 4, 0)
    for place, d in ((13, 3), (9, 2), (11, 1), (4, -1)):
        along_z(6, place, d)
    z_arrived(8)
    to_far(8)
    along_z(8, 15, -4, 1)
    for place, d in ((14, -3), (10, -2), (12, -1), (3, 1)):
        along_z(8, place, d)
    to_sides(6, 1, 0)
    to_sides(8, 1, 0)

    for place in (6, 7, 8):
        wait_bytes(cand.at[1, place, USED_ROWS], far_recv.at[place - 6])
    far_along_z(6, 15, 1, 1, 4, 0)
    far_along_z(8, 15, 1, 1, -4, 1)
    far_along_z(6, 13, 1, 1, 3)
    far_along_z(8, 14, 1, 1, -3)
    far_along_z(6, 9, 1, 1, 2)
    far_along_z(8, 10, 1, 1, -2)
    far_along_z(6, 11, 1, 1, 1)
    far_along_z(8, 12, 1, 1, -1)
    far_along_z(7, 0, 1, 0, 2)
    far_along_z(7, 1, 1, 0, -2)
    far_along_z(7, 2, 2, 0, 1)
    far_along_z(6, 4, 2, 0, -1)

    far_top.wait_recv()
    far_low.wait_recv()
    far = pall.at[slot_far]
    core_far = remote(far, far, pts_send.at[7], pts_recv.at[7], other_core)
    core_far.start()

    z_arrived(0, 1, 2, 3, 4, 5)
    to_sides(0, 6, 0)
    z_arrived(9, 10, 11, 12, 13, 14)
    to_sides(9, 6, 1)
    half_block = cand.at[0, 15, USED_ROWS, pl.ds(0, width // 2)]
    wait_bytes(half_block, z_block_recv.at[15])
    wait_bytes(half_block, z_block_recv.at[16])
    to_sides(15, 1, 1)

    def absorb(first, count):
        blocks = XS * count
        rows = cand[:, first : first + count].reshape(blocks, BLK, width)
        half = jnp.zeros((blocks, BLK, npd), F32)
        for t in range(width // npd):
            piece = rows[:, :, t * npd : (t + 1) * npd].astype(F32)
            half = half + piece * piece
        half = 0.5 * jnp.sum(half, axis=2, keepdims=True)
        flat = rows.reshape(blocks * BLK, width)
        for j in range(SUBS // 2):
            group = jnp.concatenate([pall[2 * j], pall[2 * j + 1]], axis=1)
            dots = jnp.dot(flat, group, preferred_element_type=F32)
            best = jnp.min(half - dots.reshape(blocks, BLK, 2 * npd), axis=0)
            mins[j] = best if first == 0 else jnp.minimum(mins[j], best)

    pts_core.wait_recv()
    core_left.wait_recv()
    core_right.wait_recv()
    core_far.wait_recv()
    for b in range(SUBS):
        wide = pall[b].astype(F32)
        squares[b : b + 1, :] = jnp.sum(wide * wide, axis=0, keepdims=True)
    wait_bytes(cand.at[pl.ds(2, 2), pl.ds(0, NEAR), USED_ROWS], y_recv.at[0])
    wait_bytes(cand.at[1, pl.ds(0, 6), USED_ROWS], far_z_recv.at[0])
    absorb(0, NEAR)
    wait_bytes(cand.at[pl.ds(2, 2), pl.ds(NEAR, ZS - NEAR), USED_ROWS], y_recv.at[1])
    wait_bytes(cand.at[1, pl.ds(NEAR, ZS - NEAR), USED_ROWS], far_z_recv.at[1])
    absorb(NEAR, ZS - NEAR)

    for j in range(SUBS // 2):
        for r in range(ROUNDS):
            low_r = jnp.min(mins[j, r * SHARE : (r + 1) * SHARE, :], axis=0, keepdims=True)
            for h in range(2):
                pair[0, r, 2 * j + h : 2 * j + h + 1, :] = low_r[:, h * npd : (h + 1) * npd]

    swap = remote(pair.at[0], pair.at[1], pair_send, pair_recv, other_core)
    swap.start()
    swap.wait_recv()
    line[0] = jnp.minimum(pair[0], pair[1])
    for d in (2, 1, 3):
        remote(line.at[0], line.at[XS - d], line_send, line_recv, at_x(d)).start()
    wait_bytes(line.at[pl.ds(0, XS - 1)], line_recv)

    lanes = lax.broadcasted_iota(jnp.int32, (1, npd), 1)
    least = None
    total = jnp.zeros((1, npd), F32)
    for r in range(ROUNDS):
        now = jnp.min(line[:, r], axis=0)
        least = now if least is None else jnp.minimum(least, now)
        dist = jnp.maximum(squares[...] + 2.0 * least, 0.0)
        near[r] = dist
        part = jnp.sum(jnp.sum(dist, axis=0, keepdims=True), axis=1, keepdims=True)
        total = jnp.where(lanes == r, part, total)

    zsum[0] = total

    for d in (8, 7, 9, 6, 10, 5, 11, 4, 12, 3, 13, 2, 14, 1, 15):
        remote(zsum.at[0], zsum.at[ZS - d], z_send, z_recv, at_z(d)).start()
    wait_bytes(slots.at[pl.ds(0, SUBS - 1)], slots_send)
    wait_bytes(cand.at[0, pl.ds(0, 15), USED_ROWS], z_block_send)
    wait_bytes(cand.at[pl.ds(0, 2), :, USED_ROWS], y_send)
    wait_bytes(cand.at[0, pl.ds(0, 3), USED_ROWS], far_send)
    wait_bytes(cand.at[0, pl.ds(0, 13), USED_ROWS], far_z_send)
    for copy in (pts_right, pts_left, pts_core, far_top, core_left, far_low, core_right, core_far):
        copy.wait_send()
    swap.wait_send()
    wait_bytes(line.at[pl.ds(0, XS - 1)], line_send)
    wait_bytes(zsum.at[pl.ds(0, ZS - 1)], z_recv)
    ysum[0] = jnp.sum(zsum[...], axis=0)
    for d in (1, 3, 2):
        remote(ysum.at[0], ysum.at[XS - d], c_send, c_recv, y_to[d]).start()
    wait_bytes(ysum.at[pl.ds(0, XS - 1)], c_recv)
    cost = jnp.sum(ysum[...], axis=0)
    for r in range(ROUNDS):
        cost_r = jnp.sum(jnp.where(lanes == r, cost, 0.0), axis=1, keepdims=True)
        out_ref[r : r + 1, :] = npts * near[r, pl.ds(me, 1), :] / cost_r
    wait_bytes(zsum.at[pl.ds(0, ZS - 1)], z_send)
    wait_bytes(ysum.at[pl.ds(0, XS - 1)], c_send)


def shards(points, cand_rows, cand_count):
    npd, width = points.shape
    npts = float(npd * lax.axis_size(("dp", "sub")))
    dma = pltpu.SemaphoreType.DMA
    operands = (cand_rows, cand_count.reshape(1, ROUNDS), points)
    return pl.pallas_call(
        lambda *refs: kernel(npts, *refs),
        out_shape=jax.ShapeDtypeStruct((ROUNDS, npd), F32),
        in_specs=[
            pl.BlockSpec(memory_space=pl.ANY),
            pl.BlockSpec(memory_space=pl.ANY),
            pl.BlockSpec(memory_space=pl.ANY),
        ],
        out_specs=pl.BlockSpec(memory_space=pltpu.VMEM),
        scratch_shapes=[
            pltpu.SMEM((ROUNDS, SLOTS), jnp.int32),
            pltpu.SMEM((1, ROUNDS), jnp.int32),
            pltpu.VMEM((npd, width), jnp.bfloat16),
            pltpu.VMEM((SUBS, RAW, width), jnp.bfloat16),
            pltpu.VMEM((XS, ZS, BLK, width), jnp.bfloat16),
            pltpu.VMEM((SUBS, width, npd), jnp.bfloat16),
            pltpu.VMEM((SUBS // 2, BLK, 2 * npd), F32),
            pltpu.VMEM((SUBS, npd), F32),
            pltpu.VMEM((2, ROUNDS, SUBS, npd), F32),
            pltpu.VMEM((XS, ROUNDS, SUBS, npd), F32),
            pltpu.VMEM((ROUNDS, SUBS, npd), F32),
            pltpu.VMEM((ZS, 1, npd), F32),
            pltpu.VMEM((XS, 1, npd), F32),
            dma((3,)),
            dma,
            dma,
            dma,
            dma,
            dma((17,)),
            dma((2,)),
            dma,
            dma,
            dma((3,)),
            dma((2,)),
            dma((8,)),
            dma((8,)),
            dma,
            dma,
            dma,
            dma,
            dma,
            dma,
            dma,
            dma,
        ],
        compiler_params=pltpu.CompilerParams(
            collective_id=0, has_side_effects=True, vmem_limit_bytes=40 * 1024 * 1024
        ),
        cost_estimate=pl.CostEstimate(
            flops=2 * 1024 * 1024 * width, bytes_accessed=npd * width * 2, transcendentals=0
        ),
    )(*(pltpu.with_memory_space_constraint(value, pltpu.HBM) for value in operands))


def solution(mesh):
    in_specs = (P(("dp", "sub"), None), P(None, ("dp", "sub")), P(None, ("dp", "sub")))
    out_specs = P(None, ("dp", "sub"))
    return jax.shard_map(shards, mesh=mesh, in_specs=in_specs, out_specs=out_specs, check_vma=False)
```

```python
import jax
import jax.numpy as jnp
from jax import lax
from jax.experimental import pallas as pl
from jax.experimental.pallas import tpu as pltpu
from jax.sharding import PartitionSpec as P

ROUNDS = 3
SLOTS = 4
XS = 4
ZS = 16
YS = 4
SUBS = 8
RAW = 16
BLK = 8
SHARE = 2
USED_ROWS = pl.ds(0, ROUNDS * SHARE)
NEAR = 9
MESH = pl.DeviceIdType.MESH
F32 = jnp.float32
INF = float("inf")


def kernel(
    npts,
    rows_in,
    counts_in,
    points_ref,
    out_ref,
    rows_ref,
    cnt_ref,
    raw,
    slots,
    live,
    cand,
    pall,
    mins,
    squares,
    line,
    near,
    zsum,
    ysum,
    local_sem,
    slots_send,
    slots_recv,
    live_send,
    live_recv,
    z_block_send,
    y_send,
    z_block_recv,
    y_recv,
    far_send,
    far_z_send,
    far_recv,
    far_z_recv,
    pts_send,
    pts_recv,
    line_send,
    line_recv,
    z_send,
    z_recv,
    c_send,
    c_recv,
):
    dp = lax.axis_index("dp")
    sub = lax.axis_index("sub")
    x, z = lax.div(dp, ZS), lax.rem(dp, ZS)
    y, core = lax.div(sub, 2), lax.rem(sub, 2)
    npd, width = points_ref.shape

    def at_x(d):
        return (lax.rem(x + d, XS) * ZS + z, sub)

    def at_z(d):
        return (x * ZS + lax.rem(z + d, ZS), sub)

    def at_y(d):
        return (dp, lax.rem(y + d, YS) * 2 + core)

    other_core = (dp, y * 2 + (1 - core))
    z_to = {d: at_z(d % ZS) for d in (1, -1, 2, -2, 3, -3, 4, -4)}
    y_to = {d: at_y(d) for d in (1, 2, 3)}
    me = x * 2 + core
    x_right, x_left = at_x(1), at_x(3)

    own_points = pltpu.make_async_copy(points_ref, raw, local_sem.at[0])
    own_points.start()
    own_rows = pltpu.make_async_copy(rows_in, rows_ref, local_sem.at[1])
    own_rows.start()
    own_counts = pltpu.make_async_copy(counts_in, cnt_ref, local_sem.at[2])
    own_counts.start()
    slots[...] = jnp.zeros(slots.shape, jnp.bfloat16)
    barrier = pltpu.get_barrier_semaphore()
    far_first = ((2, 0), (2, 1), (1, 0), (3, 0), (1, 1), (3, 1), (0, 1))
    y_line = [(dp, lax.rem(y + d, YS) * 2 + (1 - core if other else core)) for d, other in far_first]
    x_line = [(lax.rem(x + d, XS) * ZS + z, y * 2 + (1 - core if other else core)) for d, other in far_first]
    partners = [*z_to.values(), *y_line, *x_line[:-1]]
    for device in partners:
        pl.semaphore_signal(barrier, inc=1, device_id=device, device_id_type=MESH)

    row = lax.broadcasted_iota(jnp.int32, (RAW, npd), 0)
    lane = lax.broadcasted_iota(jnp.int32, (RAW, npd), 1)
    within = lane & (RAW // 2 - 1)
    slot = within + ((lane & (RAW // 2)) >> 3) * 6
    slot_round = jnp.where(within < 6, slot >> 2, -1)
    slot_index = (slot & (SLOTS - 1)).astype(F32)
    wanted = (SHARE * sub + (row & 1)).astype(F32)
    wanted_round = slot_round == (row >> 1)
    sender = lax.broadcasted_iota(jnp.int32, (SUBS, 1, npd), 0)
    owner = lax.broadcasted_iota(jnp.int32, (SUBS, 1, npd), 2) >> 4
    own_rows.wait()
    own_counts.wait()
    target = jnp.full((RAW, npd), -1, jnp.int32)
    counts = jnp.zeros((1, npd), F32)
    for r in range(ROUNDS):
        counts = jnp.where(slot_round[:1] == r, cnt_ref[0, r].astype(F32), counts)
        for i in range(SLOTS):
            j = r * SLOTS + i
            target = jnp.where(row == j // 6 * 8 + j % 6, rows_ref[r, i], target)
    live[sub] = counts
    pick = jnp.where(lane == target, 1.0, 0.0).astype(jnp.bfloat16)
    own_points.wait()
    mine = raw[...]
    block = jnp.dot(pick, mine, preferred_element_type=F32)
    slots[sub] = block.reshape(2, RAW // 2, width).astype(jnp.bfloat16)

    pl.semaphore_wait(barrier, len(partners))

    def remote(src, dst, send, recv, device):
        return pltpu.make_async_remote_copy(
            src_ref=src, dst_ref=dst, send_sem=send, recv_sem=recv, device_id=device, device_id_type=MESH
        )

    def to_sides(place, count, group):
        for d, column in ((1, 2), (3, 3)):
            src, dst = cand.at[0, pl.ds(place, count), USED_ROWS], cand.at[column, pl.ds(place, count), USED_ROWS]
            remote(src, dst, y_send, y_recv.at[group], y_to[d]).start()

    def to_far(place):
        remote(cand.at[0, place, USED_ROWS], cand.at[1, place, USED_ROWS], far_send, far_recv.at[place - 6], y_to[2]).start()

    def far_along_z(src, place, count, group, d, lanes=None):
        src, dst = cand.at[1, pl.ds(src, count), USED_ROWS], cand.at[1, pl.ds(place, count), USED_ROWS]
        if lanes is not None:
            part = pl.ds(lanes * (width // 2), width // 2)
            src, dst = src.at[:, :, part], dst.at[:, :, part]
        remote(src, dst, far_z_send, far_z_recv.at[group], z_to[d]).start()

    def along_z(src, place, d, lanes=None):
        if lanes is None:
            src, dst = cand.at[0, src, USED_ROWS], cand.at[0, place, USED_ROWS]
        else:
            part = pl.ds(lanes * (width // 2), width // 2)
            src, dst = cand.at[0, src, USED_ROWS, part], cand.at[0, place, USED_ROWS, part]
        remote(src, dst, z_block_send, z_block_recv.at[place + (lanes or 0)], z_to[d]).start()

    def z_arrived(*places):
        for place in places:
            wait_bytes(cand.at[0, place, USED_ROWS], z_block_recv.at[place])

    def wait_bytes(ref, sem):
        pltpu.make_async_copy(ref, ref, sem).wait()

    for device in y_line:
        half_rows = slots.at[sub, :, USED_ROWS]
        remote(half_rows, half_rows, slots_send, slots_recv, device).start()
    for device in y_line:
        remote(live.at[sub], live.at[sub], live_send, live_recv, device).start()
    pall[me] = mine.T
    slot_right, slot_left, slot_far = (lax.rem(x + d, XS) * 2 + core for d in (1, 3, 2))
    top, low = pl.ds(0, width // 2), pl.ds(width // 2, width // 2)
    mine_at = pall.at[me]
    pts_right = remote(mine_at, mine_at, pts_send.at[0], pts_recv.at[0], x_right)
    pts_left = remote(mine_at, mine_at, pts_send.at[1], pts_recv.at[1], x_left)
    pts_core = remote(mine_at, mine_at, pts_send.at[2], pts_recv.at[2], other_core)
    pts_right.start()
    pts_left.start()
    pts_core.start()

    wait_bytes(live.at[pl.ds(0, SUBS - 1)], live_recv)
    offset = jnp.sum(jnp.where(sender < owner, live[...], 0.0), axis=0)
    count = jnp.sum(jnp.where(sender == owner, live[...], 0.0), axis=0)
    choice = wanted_round & (slot_index < count) & (offset + slot_index == wanted)
    choice = jnp.where(choice, 1.0, 0.0).astype(jnp.bfloat16)
    wait_bytes(slots.at[pl.ds(0, SUBS - 1), :, USED_ROWS], slots_recv)
    flat = slots[...].reshape(SUBS * RAW, width)
    share = jnp.dot(choice, flat, preferred_element_type=F32)
    cand[0, 7] = share[:BLK].astype(jnp.bfloat16)

    along_z(7, 6, 4)
    along_z(7, 8, -4)
    to_far(7)
    for place, d in ((0, 2), (1, -2), (2, 1), (5, -1)):
        along_z(7, place, d)
    to_sides(7, 1, 0)

    pts_right.wait_recv()
    near_left = pall.at[slot_left]
    far_top = remote(near_left.at[top], near_left.at[top], pts_send.at[3], pts_recv.at[3], x_right)
    core_left = remote(near_left, near_left, pts_send.at[4], pts_recv.at[4], other_core)
    far_top.start()
    core_left.start()
    pts_left.wait_recv()
    near_right = pall.at[slot_right]
    far_low = remote(near_right.at[low], near_right.at[low], pts_send.at[5], pts_recv.at[5], x_left)
    core_right = remote(near_right, near_right, pts_send.at[6], pts_recv.at[6], other_core)
    far_low.start()
    core_right.start()

    z_arrived(6)
    to_far(6)
    along_z(6, 15, 4, 0)
    for place, d in ((13, 3), (9, 2), (11, 1), (4, -1)):
        along_z(6, place, d)
    z_arrived(8)
    to_far(8)
    along_z(8, 15, -4, 1)
    for place, d in ((14, -3), (10, -2), (12, -1), (3, 1)):
        along_z(8, place, d)
    to_sides(6, 1, 0)
    to_sides(8, 1, 0)

    for place in (6, 7, 8):
        wait_bytes(cand.at[1, place, USED_ROWS], far_recv.at[place - 6])
    far_along_z(6, 15, 1, 1, 4, 0)
    far_along_z(8, 15, 1, 1, -4, 1)
    far_along_z(6, 13, 1, 1, 3)
    far_along_z(8, 14, 1, 1, -3)
    far_along_z(6, 9, 1, 1, 2)
    far_along_z(8, 10, 1, 1, -2)
    far_along_z(6, 11, 1, 1, 1)
    far_along_z(8, 12, 1, 1, -1)
    far_along_z(7, 0, 1, 0, 2)
    far_along_z(7, 1, 1, 0, -2)
    far_along_z(7, 2, 2, 0, 1)
    far_along_z(6, 4, 2, 0, -1)

    far_top.wait_recv()
    far_low.wait_recv()
    far = pall.at[slot_far]
    core_far = remote(far, far, pts_send.at[7], pts_recv.at[7], other_core)
    core_far.start()

    z_arrived(0, 1, 2, 3, 4, 5)
    to_sides(0, 6, 0)
    z_arrived(9, 10, 11, 12, 13, 14)
    to_sides(9, 6, 1)
    half_block = cand.at[0, 15, USED_ROWS, pl.ds(0, width // 2)]
    wait_bytes(half_block, z_block_recv.at[15])
    wait_bytes(half_block, z_block_recv.at[16])
    to_sides(15, 1, 1)

    def absorb(first, count):
        blocks = XS * count
        rows = cand[:, first : first + count].reshape(blocks, BLK, width)
        half = jnp.zeros((blocks, BLK, npd), F32)
        for t in range(width // npd):
            piece = rows[:, :, t * npd : (t + 1) * npd].astype(F32)
            half = half + piece * piece
        half = 0.5 * jnp.sum(half, axis=2, keepdims=True)
        flat = rows.reshape(blocks * BLK, width)
        for j in range(SUBS // 2):
            group = jnp.concatenate([pall[2 * j], pall[2 * j + 1]], axis=1)
            dots = jnp.dot(flat, group, preferred_element_type=F32)
            best = jnp.min(half - dots.reshape(blocks, BLK, 2 * npd), axis=0)
            mins[j] = best if first == 0 else jnp.minimum(mins[j], best)

    pts_core.wait_recv()
    core_left.wait_recv()
    core_right.wait_recv()
    core_far.wait_recv()
    for b in range(SUBS):
        wide = pall[b].astype(F32)
        squares[b : b + 1, :] = jnp.sum(wide * wide, axis=0, keepdims=True)
    wait_bytes(cand.at[pl.ds(2, 2), pl.ds(0, NEAR), USED_ROWS], y_recv.at[0])
    wait_bytes(cand.at[1, pl.ds(0, 6), USED_ROWS], far_z_recv.at[0])
    absorb(0, NEAR)
    wait_bytes(cand.at[pl.ds(2, 2), pl.ds(NEAR, ZS - NEAR), USED_ROWS], y_recv.at[1])
    wait_bytes(cand.at[1, pl.ds(NEAR, ZS - NEAR), USED_ROWS], far_z_recv.at[1])
    absorb(NEAR, ZS - NEAR)

    for j in range(SUBS // 2):
        for r in range(ROUNDS):
            low_r = jnp.min(mins[j, r * SHARE : (r + 1) * SHARE, :], axis=0, keepdims=True)
            for h in range(2):
                line[me, r, 2 * j + h : 2 * j + h + 1, :] = low_r[:, h * npd : (h + 1) * npd]

    for device in x_line:
        remote(line.at[me], line.at[me], line_send, line_recv, device).start()
    wait_bytes(line.at[pl.ds(0, SUBS - 1)], line_recv)

    lanes = lax.broadcasted_iota(jnp.int32, (1, npd), 1)
    least = None
    total = jnp.zeros((1, npd), F32)
    for r in range(ROUNDS):
        now = jnp.min(line[:, r], axis=0)
        least = now if least is None else jnp.minimum(least, now)
        dist = jnp.maximum(squares[...] + 2.0 * least, 0.0)
        near[r] = dist
        part = jnp.sum(jnp.sum(dist, axis=0, keepdims=True), axis=1, keepdims=True)
        total = jnp.where(lanes == r, part, total)

    zsum[0] = total

    for d in (8, 7, 9, 6, 10, 5, 11, 4, 12, 3, 13, 2, 14, 1, 15):
        remote(zsum.at[0], zsum.at[ZS - d], z_send, z_recv, at_z(d)).start()
    wait_bytes(slots.at[pl.ds(0, SUBS - 1), :, USED_ROWS], slots_send)
    wait_bytes(live.at[pl.ds(0, SUBS - 1)], live_send)
    wait_bytes(cand.at[0, pl.ds(0, 15), USED_ROWS], z_block_send)
    wait_bytes(cand.at[pl.ds(0, 2), :, USED_ROWS], y_send)
    wait_bytes(cand.at[0, pl.ds(0, 3), USED_ROWS], far_send)
    wait_bytes(cand.at[0, pl.ds(0, 13), USED_ROWS], far_z_send)
    for copy in (pts_right, pts_left, pts_core, far_top, core_left, far_low, core_right, core_far):
        copy.wait_send()
    wait_bytes(line.at[pl.ds(0, SUBS - 1)], line_send)
    wait_bytes(zsum.at[pl.ds(0, ZS - 1)], z_recv)
    ysum[0] = jnp.sum(zsum[...], axis=0)
    for d in (1, 3, 2):
        remote(ysum.at[0], ysum.at[XS - d], c_send, c_recv, y_to[d]).start()
    wait_bytes(ysum.at[pl.ds(0, XS - 1)], c_recv)
    cost = jnp.sum(ysum[...], axis=0)
    for r in range(ROUNDS):
        cost_r = jnp.sum(jnp.where(lanes == r, cost, 0.0), axis=1, keepdims=True)
        out_ref[r : r + 1, :] = npts * near[r, pl.ds(me, 1), :] / cost_r
    wait_bytes(zsum.at[pl.ds(0, ZS - 1)], z_send)
    wait_bytes(ysum.at[pl.ds(0, XS - 1)], c_send)


def shards(points, cand_rows, cand_count):
    npd, width = points.shape
    npts = float(npd * lax.axis_size(("dp", "sub")))
    dma = pltpu.SemaphoreType.DMA
    operands = (cand_rows, cand_count.reshape(1, ROUNDS), points)
    return pl.pallas_call(
        lambda *refs: kernel(npts, *refs),
        out_shape=jax.ShapeDtypeStruct((ROUNDS, npd), F32),
        in_specs=[
            pl.BlockSpec(memory_space=pl.ANY),
            pl.BlockSpec(memory_space=pl.ANY),
            pl.BlockSpec(memory_space=pl.ANY),
        ],
        out_specs=pl.BlockSpec(memory_space=pltpu.VMEM),
        scratch_shapes=[
            pltpu.SMEM((ROUNDS, SLOTS), jnp.int32),
            pltpu.SMEM((1, ROUNDS), jnp.int32),
            pltpu.VMEM((npd, width), jnp.bfloat16),
            pltpu.VMEM((SUBS, 2, RAW // 2, width), jnp.bfloat16),
            pltpu.VMEM((SUBS, 1, npd), F32),
            pltpu.VMEM((XS, ZS, BLK, width), jnp.bfloat16),
            pltpu.VMEM((SUBS, width, npd), jnp.bfloat16),
            pltpu.VMEM((SUBS // 2, BLK, 2 * npd), F32),
            pltpu.VMEM((SUBS, npd), F32),
            pltpu.VMEM((SUBS, ROUNDS, SUBS, npd), F32),
            pltpu.VMEM((ROUNDS, SUBS, npd), F32),
            pltpu.VMEM((ZS, 1, npd), F32),
            pltpu.VMEM((XS, 1, npd), F32),
            dma((3,)),
            dma,
            dma,
            dma,
            dma,
            dma,
            dma,
            dma((17,)),
            dma((2,)),
            dma,
            dma,
            dma((3,)),
            dma((2,)),
            dma((8,)),
            dma((8,)),
            dma,
            dma,
            dma,
            dma,
            dma,
            dma,
        ],
        compiler_params=pltpu.CompilerParams(
            collective_id=0, has_side_effects=True, vmem_limit_bytes=40 * 1024 * 1024
        ),
        cost_estimate=pl.CostEstimate(
            flops=2 * 1024 * 1024 * width, bytes_accessed=npd * width * 2, transcendentals=0
        ),
    )(*(pltpu.with_memory_space_constraint(value, pltpu.HBM) for value in operands))


def solution(mesh):
    in_specs = (P(("dp", "sub"), None), P(None, ("dp", "sub")), P(None, ("dp", "sub")))
    out_specs = P(None, ("dp", "sub"))
    return jax.shard_map(shards, mesh=mesh, in_specs=in_specs, out_specs=out_specs, check_vma=False)
```

```python
import jax
import jax.numpy as jnp
from jax import lax
from jax.experimental import pallas as pl
from jax.experimental.pallas import tpu as pltpu
from jax.sharding import PartitionSpec as P

ROUNDS = 3
SLOTS = 4
XS = 4
ZS = 16
YS = 4
SUBS = 8
RAW = 16
BLK = 8
SHARE = 2
USED_ROWS = pl.ds(0, ROUNDS * SHARE)
NEAR = 9
MESH = pl.DeviceIdType.MESH
F32 = jnp.float32
INF = float("inf")


def kernel(
    npts,
    rows_in,
    counts_in,
    points_ref,
    out_ref,
    rows_ref,
    cnt_ref,
    raw,
    slots,
    cand,
    pall,
    mins,
    squares,
    line,
    near,
    zsum,
    ysum,
    local_sem,
    slots_send,
    slots_recv,
    z_block_send,
    y_send,
    z_block_recv,
    y_recv,
    pts_send,
    pts_recv,
    line_send,
    line_recv,
    z_send,
    z_recv,
    c_send,
    c_recv,
):
    dp = lax.axis_index("dp")
    sub = lax.axis_index("sub")
    x, z = lax.div(dp, ZS), lax.rem(dp, ZS)
    y, core = lax.div(sub, 2), lax.rem(sub, 2)
    npd, width = points_ref.shape

    def at_x(d):
        return (lax.rem(x + d, XS) * ZS + z, sub)

    def at_z(d):
        return (x * ZS + lax.rem(z + d, ZS), sub)

    def at_y(d):
        return (dp, lax.rem(y + d, YS) * 2 + core)

    other_core = (dp, y * 2 + (1 - core))
    z_to = {d: at_z(d % ZS) for d in (1, -1, 2, -2, 3, -3, 4, -4)}
    y_to = {d: at_y(d) for d in (1, 2, 3)}
    me = x * 2 + core
    x_right, x_left = at_x(1), at_x(3)

    own_points = pltpu.make_async_copy(points_ref, raw, local_sem.at[0])
    own_points.start()
    own_rows = pltpu.make_async_copy(rows_in, rows_ref, local_sem.at[1])
    own_rows.start()
    own_counts = pltpu.make_async_copy(counts_in, cnt_ref, local_sem.at[2])
    own_counts.start()
    barrier = pltpu.get_barrier_semaphore()
    far_first = ((2, 0), (2, 1), (1, 0), (3, 0), (1, 1), (3, 1), (0, 1))
    y_line = [(dp, lax.rem(y + d, YS) * 2 + (1 - core if other else core)) for d, other in far_first]
    x_line = [(lax.rem(x + d, XS) * ZS + z, y * 2 + (1 - core if other else core)) for d, other in far_first]
    partners = [*z_to.values(), *y_line, *x_line[:-1]]
    for device in partners:
        pl.semaphore_signal(barrier, inc=1, device_id=device, device_id_type=MESH)

    row = lax.broadcasted_iota(jnp.int32, (RAW, npd), 0)
    lane = lax.broadcasted_iota(jnp.int32, (RAW, npd), 1)
    here = lax.broadcasted_iota(jnp.int32, (npd, npd), 0)
    there = lax.broadcasted_iota(jnp.int32, (npd, npd), 1)
    same_round = (here & (RAW - 1)) == ROUNDS * SLOTS + ((there & (RAW - 1)) >> 2)
    before = jnp.where(same_round & ((here >> 4) < (there >> 4)), 1.0, 0.0)
    itself = jnp.where(same_round & ((here >> 4) == (there >> 4)), 1.0, 0.0)
    slot = lane & (RAW - 1)
    slot_round = jnp.where(slot < ROUNDS * SLOTS, slot >> 2, -1)
    slot_index = (slot & (SLOTS - 1)).astype(F32)
    want = lax.broadcasted_iota(jnp.int32, (XS * BLK, npd), 0)
    column = want >> 3
    ahead = jnp.where(column == 1, 2, jnp.where(column == 2, 3, jnp.where(column == 3, 1, 0)))
    holder = ((y + ahead) & (YS - 1)) * 2 + core
    wanted = (SHARE * holder + (want & 1)).astype(F32)
    wanted_round = slot_round[:1] == ((want & (BLK - 1)) >> 1)
    slot_index = slot_index[:1]
    own_rows.wait()
    own_counts.wait()
    target = jnp.full((RAW, npd), -1, jnp.int32)
    counts = jnp.zeros((RAW, npd), F32)
    for r in range(ROUNDS):
        counts = jnp.where(row == ROUNDS * SLOTS + r, cnt_ref[0, r].astype(F32), counts)
        for i in range(SLOTS):
            target = jnp.where(row == r * SLOTS + i, rows_ref[r, i], target)
    pick = jnp.where(lane == target, 1.0, 0.0).astype(jnp.bfloat16)
    own_points.wait()
    mine = raw[...]
    block = jnp.dot(pick, mine, preferred_element_type=F32)
    slots[sub, :, :npd] = (block[:, :npd] + counts).astype(jnp.bfloat16)
    slots[sub, :, npd:] = block[:, npd:].astype(jnp.bfloat16)

    pl.semaphore_wait(barrier, len(partners))

    def remote(src, dst, send, recv, device):
        return pltpu.make_async_remote_copy(
            src_ref=src, dst_ref=dst, send_sem=send, recv_sem=recv, device_id=device, device_id_type=MESH
        )

    def to_sides(place, count, group):
        for d, column in ((1, 2), (3, 3)):
            src, dst = cand.at[0, pl.ds(place, count), USED_ROWS], cand.at[column, pl.ds(place, count), USED_ROWS]
            remote(src, dst, y_send, y_recv.at[group], y_to[d]).start()

    def along_z(src, place, d, lanes=None):
        both = pl.ds(0, 2)
        if lanes is None:
            src, dst = cand.at[both, src, USED_ROWS], cand.at[both, place, USED_ROWS]
        else:
            part = pl.ds(lanes * (width // 2), width // 2)
            src, dst = cand.at[both, src, USED_ROWS, part], cand.at[both, place, USED_ROWS, part]
        remote(src, dst, z_block_send, z_block_recv.at[place + (lanes or 0)], z_to[d]).start()

    def z_arrived(*places):
        both = pl.ds(0, 2)
        for place in places:
            wait_bytes(cand.at[both, place, USED_ROWS], z_block_recv.at[place])

    def wait_bytes(ref, sem):
        pltpu.make_async_copy(ref, ref, sem).wait()

    for device in y_line:
        remote(slots.at[sub], slots.at[sub], slots_send, slots_recv, device).start()
    pall[me] = mine.T
    slot_right, slot_left, slot_far = (lax.rem(x + d, XS) * 2 + core for d in (1, 3, 2))
    top, low = pl.ds(0, width // 2), pl.ds(width // 2, width // 2)
    mine_at = pall.at[me]
    pts_right = remote(mine_at, mine_at, pts_send.at[0], pts_recv.at[0], x_right)
    pts_left = remote(mine_at, mine_at, pts_send.at[1], pts_recv.at[1], x_left)
    pts_core = remote(mine_at, mine_at, pts_send.at[2], pts_recv.at[2], other_core)
    pts_right.start()
    pts_left.start()
    pts_core.start()

    wait_bytes(slots.at[pl.ds(0, SUBS - 1)], slots_recv)
    flat = slots[...].reshape(SUBS * RAW, width)
    known = flat[:, :npd].astype(F32)
    offset = jnp.sum(known * before, axis=0, keepdims=True)
    count = jnp.sum(known * itself, axis=0, keepdims=True)
    choice = wanted_round & (slot_index < count) & (offset + slot_index == wanted)
    share = jnp.dot(jnp.where(choice, 1.0, 0.0).astype(jnp.bfloat16), flat, preferred_element_type=F32)
    cand[:, 7] = share.reshape(XS, BLK, width).astype(jnp.bfloat16)

    along_z(7, 6, 4)
    along_z(7, 8, -4)
    for place, d in ((0, 2), (1, -2), (2, 1), (5, -1)):
        along_z(7, place, d)

    pts_right.wait_recv()
    near_left = pall.at[slot_left]
    far_top = remote(near_left.at[top], near_left.at[top], pts_send.at[3], pts_recv.at[3], x_right)
    core_left = remote(near_left, near_left, pts_send.at[4], pts_recv.at[4], other_core)
    far_top.start()
    core_left.start()
    pts_left.wait_recv()
    near_right = pall.at[slot_right]
    far_low = remote(near_right.at[low], near_right.at[low], pts_send.at[5], pts_recv.at[5], x_left)
    core_right = remote(near_right, near_right, pts_send.at[6], pts_recv.at[6], other_core)
    far_low.start()
    core_right.start()

    z_arrived(6)
    along_z(6, 15, 4, 0)
    for place, d in ((13, 3), (9, 2), (11, 1), (4, -1)):
        along_z(6, place, d)
    z_arrived(8)
    along_z(8, 15, -4, 1)
    for place, d in ((14, -3), (10, -2), (12, -1), (3, 1)):
        along_z(8, place, d)
    to_sides(6, 1, 0)
    to_sides(8, 1, 0)

    far_top.wait_recv()
    far_low.wait_recv()
    far = pall.at[slot_far]
    core_far = remote(far, far, pts_send.at[7], pts_recv.at[7], other_core)
    core_far.start()

    z_arrived(0, 1, 2, 3, 4, 5)
    to_sides(0, 6, 0)
    z_arrived(9, 10, 11, 12, 13, 14)
    to_sides(9, 6, 1)
    half_block = cand.at[pl.ds(0, 2), 15, USED_ROWS, pl.ds(0, width // 2)]
    wait_bytes(half_block, z_block_recv.at[15])
    wait_bytes(half_block, z_block_recv.at[16])
    to_sides(15, 1, 1)

    def absorb(first, count):
        blocks = XS * count
        rows = cand[:, first : first + count].reshape(blocks, BLK, width)
        half = jnp.zeros((blocks, BLK, npd), F32)
        for t in range(width // npd):
            piece = rows[:, :, t * npd : (t + 1) * npd].astype(F32)
            half = half + piece * piece
        half = 0.5 * jnp.sum(half, axis=2, keepdims=True)
        flat = rows.reshape(blocks * BLK, width)
        for j in range(SUBS // 2):
            group = jnp.concatenate([pall[2 * j], pall[2 * j + 1]], axis=1)
            dots = jnp.dot(flat, group, preferred_element_type=F32)
            best = jnp.min(half - dots.reshape(blocks, BLK, 2 * npd), axis=0)
            mins[j] = best if first == 0 else jnp.minimum(mins[j], best)

    pts_core.wait_recv()
    core_left.wait_recv()
    core_right.wait_recv()
    core_far.wait_recv()
    for b in range(SUBS):
        wide = pall[b].astype(F32)
        squares[b : b + 1, :] = jnp.sum(wide * wide, axis=0, keepdims=True)
    wait_bytes(cand.at[pl.ds(2, 2), pl.ds(0, NEAR - 1), USED_ROWS], y_recv.at[0])
    absorb(0, NEAR)
    wait_bytes(cand.at[pl.ds(2, 2), pl.ds(NEAR, ZS - NEAR), USED_ROWS], y_recv.at[1])
    absorb(NEAR, ZS - NEAR)

    for j in range(SUBS // 2):
        for r in range(ROUNDS):
            low_r = jnp.min(mins[j, r * SHARE : (r + 1) * SHARE, :], axis=0, keepdims=True)
            for h in range(2):
                line[me, r, 2 * j + h : 2 * j + h + 1, :] = low_r[:, h * npd : (h + 1) * npd]

    for device in x_line:
        remote(line.at[me], line.at[me], line_send, line_recv, device).start()
    wait_bytes(line.at[pl.ds(0, SUBS - 1)], line_recv)

    lanes = lax.broadcasted_iota(jnp.int32, (1, npd), 1)
    least = None
    total = jnp.zeros((1, npd), F32)
    for r in range(ROUNDS):
        now = jnp.min(line[:, r], axis=0)
        least = now if least is None else jnp.minimum(least, now)
        dist = jnp.maximum(squares[...] + 2.0 * least, 0.0)
        near[r] = dist
        part = jnp.sum(jnp.sum(dist, axis=0, keepdims=True), axis=1, keepdims=True)
        total = jnp.where(lanes == r, part, total)

    zsum[0] = total

    for d in (8, 7, 9, 6, 10, 5, 11, 4, 12, 3, 13, 2, 14, 1, 15):
        remote(zsum.at[0], zsum.at[ZS - d], z_send, z_recv, at_z(d)).start()
    wait_bytes(slots.at[pl.ds(0, SUBS - 1)], slots_send)
    wait_bytes(cand.at[pl.ds(0, 2), pl.ds(0, 15), USED_ROWS], z_block_send)
    wait_bytes(cand.at[pl.ds(0, 2), pl.ds(0, 15), USED_ROWS], y_send)
    for copy in (pts_right, pts_left, pts_core, far_top, core_left, far_low, core_right, core_far):
        copy.wait_send()
    wait_bytes(line.at[pl.ds(0, SUBS - 1)], line_send)
    wait_bytes(zsum.at[pl.ds(0, ZS - 1)], z_recv)
    ysum[0] = jnp.sum(zsum[...], axis=0)
    for d in (1, 3, 2):
        remote(ysum.at[0], ysum.at[XS - d], c_send, c_recv, y_to[d]).start()
    wait_bytes(ysum.at[pl.ds(0, XS - 1)], c_recv)
    cost = jnp.sum(ysum[...], axis=0)
    for r in range(ROUNDS):
        cost_r = jnp.sum(jnp.where(lanes == r, cost, 0.0), axis=1, keepdims=True)
        out_ref[r : r + 1, :] = npts * near[r, pl.ds(me, 1), :] / cost_r
    wait_bytes(zsum.at[pl.ds(0, ZS - 1)], z_send)
    wait_bytes(ysum.at[pl.ds(0, XS - 1)], c_send)


def shards(points, cand_rows, cand_count):
    npd, width = points.shape
    npts = float(npd * lax.axis_size(("dp", "sub")))
    dma = pltpu.SemaphoreType.DMA
    operands = (cand_rows, cand_count.reshape(1, ROUNDS), points)
    return pl.pallas_call(
        lambda *refs: kernel(npts, *refs),
        out_shape=jax.ShapeDtypeStruct((ROUNDS, npd), F32),
        in_specs=[
            pl.BlockSpec(memory_space=pl.ANY),
            pl.BlockSpec(memory_space=pl.ANY),
            pl.BlockSpec(memory_space=pl.ANY),
        ],
        out_specs=pl.BlockSpec(memory_space=pltpu.VMEM),
        scratch_shapes=[
            pltpu.SMEM((ROUNDS, SLOTS), jnp.int32),
            pltpu.SMEM((1, ROUNDS), jnp.int32),
            pltpu.VMEM((npd, width), jnp.bfloat16),
            pltpu.VMEM((SUBS, RAW, width), jnp.bfloat16),
            pltpu.VMEM((XS, ZS, BLK, width), jnp.bfloat16),
            pltpu.VMEM((SUBS, width, npd), jnp.bfloat16),
            pltpu.VMEM((SUBS // 2, BLK, 2 * npd), F32),
            pltpu.VMEM((SUBS, npd), F32),
            pltpu.VMEM((SUBS, ROUNDS, SUBS, npd), F32),
            pltpu.VMEM((ROUNDS, SUBS, npd), F32),
            pltpu.VMEM((ZS, 1, npd), F32),
            pltpu.VMEM((XS, 1, npd), F32),
            dma((3,)),
            dma,
            dma,
            dma,
            dma,
            dma((17,)),
            dma((2,)),
            dma((8,)),
            dma((8,)),
            dma,
            dma,
            dma,
            dma,
            dma,
            dma,
        ],
        compiler_params=pltpu.CompilerParams(
            collective_id=0, has_side_effects=True, vmem_limit_bytes=40 * 1024 * 1024
        ),
        cost_estimate=pl.CostEstimate(
            flops=2 * 1024 * 1024 * width, bytes_accessed=npd * width * 2, transcendentals=0
        ),
    )(*(pltpu.with_memory_space_constraint(value, pltpu.HBM) for value in operands))


def solution(mesh):
    in_specs = (P(("dp", "sub"), None), P(None, ("dp", "sub")), P(None, ("dp", "sub")))
    out_specs = P(None, ("dp", "sub"))
    return jax.shard_map(shards, mesh=mesh, in_specs=in_specs, out_specs=out_specs, check_vma=False)
```

```python
import jax
import jax.numpy as jnp
from jax import lax
from jax.experimental import pallas as pl
from jax.experimental.pallas import tpu as pltpu
from jax.sharding import PartitionSpec as P

ROUNDS = 3
SLOTS = 4
XS = 4
ZS = 16
YS = 4
SUBS = 8
RAW = 16
BLK = 8
SHARE = 2
USED_ROWS = pl.ds(0, ROUNDS * SHARE)
NEAR = 9
MESH = pl.DeviceIdType.MESH
F32 = jnp.float32
INF = float("inf")


def kernel(
    npts,
    rows_in,
    counts_in,
    points_ref,
    out_ref,
    rows_ref,
    cnt_ref,
    raw,
    slots,
    cand,
    pall,
    mins,
    squares,
    line,
    near,
    zsum,
    ysum,
    local_sem,
    slots_send,
    slots_recv,
    z_block_send,
    y_send,
    z_block_recv,
    y_recv,
    far_z_send,
    far_recv,
    far_z_recv,
    pts_send,
    pts_recv,
    line_send,
    line_recv,
    z_send,
    z_recv,
    c_send,
    c_recv,
):
    dp = lax.axis_index("dp")
    sub = lax.axis_index("sub")
    x, z = lax.div(dp, ZS), lax.rem(dp, ZS)
    y, core = lax.div(sub, 2), lax.rem(sub, 2)
    npd, width = points_ref.shape

    def at_x(d):
        return (lax.rem(x + d, XS) * ZS + z, sub)

    def at_z(d):
        return (x * ZS + lax.rem(z + d, ZS), sub)

    def at_y(d):
        return (dp, lax.rem(y + d, YS) * 2 + core)

    other_core = (dp, y * 2 + (1 - core))
    z_to = {d: at_z(d % ZS) for d in (1, -1, 2, -2, 3, -3, 4, -4)}
    y_to = {d: at_y(d) for d in (1, 2, 3)}
    me = x * 2 + core
    x_right, x_left = at_x(1), at_x(3)

    own_points = pltpu.make_async_copy(points_ref, raw, local_sem.at[0])
    own_points.start()
    own_rows = pltpu.make_async_copy(rows_in, rows_ref, local_sem.at[1])
    own_rows.start()
    own_counts = pltpu.make_async_copy(counts_in, cnt_ref, local_sem.at[2])
    own_counts.start()
    barrier = pltpu.get_barrier_semaphore()
    far_first = ((2, 0), (2, 1), (1, 0), (3, 0), (1, 1), (3, 1), (0, 1))
    y_line = [(dp, lax.rem(y + d, YS) * 2 + (1 - core if other else core)) for d, other in far_first]
    x_line = [(lax.rem(x + d, XS) * ZS + z, y * 2 + (1 - core if other else core)) for d, other in far_first]
    partners = [*z_to.values(), *y_line, *x_line[:-1]]
    for device in partners:
        pl.semaphore_signal(barrier, inc=1, device_id=device, device_id_type=MESH)

    row = lax.broadcasted_iota(jnp.int32, (RAW, npd), 0)
    lane = lax.broadcasted_iota(jnp.int32, (RAW, npd), 1)
    here = lax.broadcasted_iota(jnp.int32, (npd, npd), 0)
    there = lax.broadcasted_iota(jnp.int32, (npd, npd), 1)
    same_round = (here & (RAW - 1)) == ROUNDS * SLOTS + ((there & (RAW - 1)) >> 2)
    before = jnp.where(same_round & ((here >> 4) < (there >> 4)), 1.0, 0.0)
    itself = jnp.where(same_round & ((here >> 4) == (there >> 4)), 1.0, 0.0)
    slot = lane & (RAW - 1)
    slot_round = jnp.where(slot < ROUNDS * SLOTS, slot >> 2, -1)
    slot_index = (slot & (SLOTS - 1)).astype(F32)
    want = lax.broadcasted_iota(jnp.int32, (XS * BLK, npd), 0)
    column = want >> 3
    ahead = jnp.where(column == 1, 2, jnp.where(column == 2, 3, jnp.where(column == 3, 1, 0)))
    holder = ((y + ahead) & (YS - 1)) * 2 + core
    wanted = (SHARE * holder + (want & 1)).astype(F32)
    wanted_round = slot_round[:1] == ((want & (BLK - 1)) >> 1)
    slot_index = slot_index[:1]
    own_rows.wait()
    own_counts.wait()
    target = jnp.full((RAW, npd), -1, jnp.int32)
    counts = jnp.zeros((RAW, npd), F32)
    for r in range(ROUNDS):
        counts = jnp.where(row == ROUNDS * SLOTS + r, cnt_ref[0, r].astype(F32), counts)
        for i in range(SLOTS):
            target = jnp.where(row == r * SLOTS + i, rows_ref[r, i], target)
    pick = jnp.where(lane == target, 1.0, 0.0).astype(jnp.bfloat16)
    own_points.wait()
    mine = raw[...]
    block = jnp.dot(pick, mine, preferred_element_type=F32)
    slots[sub, :, :npd] = (block[:, :npd] + counts).astype(jnp.bfloat16)
    slots[sub, :, npd:] = block[:, npd:].astype(jnp.bfloat16)

    pl.semaphore_wait(barrier, len(partners))

    def remote(src, dst, send, recv, device):
        return pltpu.make_async_remote_copy(
            src_ref=src, dst_ref=dst, send_sem=send, recv_sem=recv, device_id=device, device_id_type=MESH
        )

    def to_sides(place, count, group):
        for d, column in ((1, 2), (3, 3)):
            src, dst = cand.at[0, pl.ds(place, count), USED_ROWS], cand.at[column, pl.ds(place, count), USED_ROWS]
            remote(src, dst, y_send, y_recv.at[group], y_to[d]).start()

    def along_z(src, place, d, lanes=None, column=0):
        if lanes is None:
            src, dst = cand.at[column, src, USED_ROWS], cand.at[column, place, USED_ROWS]
        else:
            part = pl.ds(lanes * (width // 2), width // 2)
            src, dst = cand.at[column, src, USED_ROWS, part], cand.at[column, place, USED_ROWS, part]
        if column == 0:
            recv = z_block_recv.at[place + (lanes or 0)]
        elif place in (6, 8):
            recv = far_recv.at[place // 2 - 3]
        else:
            recv = far_z_recv.at[0 if place < NEAR else 1]
        remote(src, dst, (z_block_send, far_z_send)[column], recv, z_to[d]).start()

    def z_arrived(*places):
        for place in places:
            wait_bytes(cand.at[0, place, USED_ROWS], z_block_recv.at[place])

    def wait_bytes(ref, sem):
        pltpu.make_async_copy(ref, ref, sem).wait()

    for device in y_line:
        remote(slots.at[sub], slots.at[sub], slots_send, slots_recv, device).start()
    pall[me] = mine.T
    slot_right, slot_left, slot_far = (lax.rem(x + d, XS) * 2 + core for d in (1, 3, 2))
    top, low = pl.ds(0, width // 2), pl.ds(width // 2, width // 2)
    mine_at = pall.at[me]
    pts_right = remote(mine_at, mine_at, pts_send.at[0], pts_recv.at[0], x_right)
    pts_left = remote(mine_at, mine_at, pts_send.at[1], pts_recv.at[1], x_left)
    pts_core = remote(mine_at, mine_at, pts_send.at[2], pts_recv.at[2], other_core)
    pts_right.start()
    pts_left.start()
    pts_core.start()

    wait_bytes(slots.at[pl.ds(0, SUBS - 1)], slots_recv)
    flat = slots[...].reshape(SUBS * RAW, width)
    known = flat[:, :npd].astype(F32)
    offset = jnp.sum(known * before, axis=0, keepdims=True)
    count = jnp.sum(known * itself, axis=0, keepdims=True)
    choice = wanted_round & (slot_index < count) & (offset + slot_index == wanted)
    share = jnp.dot(jnp.where(choice, 1.0, 0.0).astype(jnp.bfloat16), flat, preferred_element_type=F32)
    cand[:, 7] = share.reshape(XS, BLK, width).astype(jnp.bfloat16)

    for column in range(2):
        along_z(7, 6, 4, None, column)
        along_z(7, 8, -4, None, column)
    for column in range(2):
        for place, d in ((0, 2), (1, -2), (2, 1), (5, -1)):
            along_z(7, place, d, None, column)

    pts_right.wait_recv()
    near_left = pall.at[slot_left]
    far_top = remote(near_left.at[top], near_left.at[top], pts_send.at[3], pts_recv.at[3], x_right)
    core_left = remote(near_left, near_left, pts_send.at[4], pts_recv.at[4], other_core)
    far_top.start()
    core_left.start()
    pts_left.wait_recv()
    near_right = pall.at[slot_right]
    far_low = remote(near_right.at[low], near_right.at[low], pts_send.at[5], pts_recv.at[5], x_left)
    core_right = remote(near_right, near_right, pts_send.at[6], pts_recv.at[6], other_core)
    far_low.start()
    core_right.start()

    z_arrived(6)
    along_z(6, 15, 4, 0)
    for place, d in ((13, 3), (9, 2), (11, 1), (4, -1)):
        along_z(6, place, d)
    z_arrived(8)
    along_z(8, 15, -4, 1)
    for place, d in ((14, -3), (10, -2), (12, -1), (3, 1)):
        along_z(8, place, d)
    to_sides(6, 1, 0)
    to_sides(8, 1, 0)

    wait_bytes(cand.at[1, 6, USED_ROWS], far_recv.at[0])
    along_z(6, 15, 4, 0, 1)
    for place, d in ((13, 3), (9, 2), (11, 1), (4, -1)):
        along_z(6, place, d, None, 1)
    wait_bytes(cand.at[1, 8, USED_ROWS], far_recv.at[1])
    along_z(8, 15, -4, 1, 1)
    for place, d in ((14, -3), (10, -2), (12, -1), (3, 1)):
        along_z(8, place, d, None, 1)

    far_top.wait_recv()
    far_low.wait_recv()
    far = pall.at[slot_far]
    core_far = remote(far, far, pts_send.at[7], pts_recv.at[7], other_core)
    core_far.start()

    z_arrived(0, 1, 2, 3, 4, 5)
    to_sides(0, 6, 0)
    z_arrived(9, 10, 11, 12, 13, 14)
    to_sides(9, 6, 1)
    half_block = cand.at[0, 15, USED_ROWS, pl.ds(0, width // 2)]
    wait_bytes(half_block, z_block_recv.at[15])
    wait_bytes(half_block, z_block_recv.at[16])
    to_sides(15, 1, 1)

    def absorb(first, count):
        blocks = XS * count
        rows = cand[:, first : first + count].reshape(blocks, BLK, width)
        half = jnp.zeros((blocks, BLK, npd), F32)
        for t in range(width // npd):
            piece = rows[:, :, t * npd : (t + 1) * npd].astype(F32)
            half = half + piece * piece
        half = 0.5 * jnp.sum(half, axis=2, keepdims=True)
        flat = rows.reshape(blocks * BLK, width)
        for j in range(SUBS // 2):
            group = jnp.concatenate([pall[2 * j], pall[2 * j + 1]], axis=1)
            dots = jnp.dot(flat, group, preferred_element_type=F32)
            best = jnp.min(half - dots.reshape(blocks, BLK, 2 * npd), axis=0)
            mins[j] = best if first == 0 else jnp.minimum(mins[j], best)

    pts_core.wait_recv()
    core_left.wait_recv()
    core_right.wait_recv()
    core_far.wait_recv()
    for b in range(SUBS):
        wide = pall[b].astype(F32)
        squares[b : b + 1, :] = jnp.sum(wide * wide, axis=0, keepdims=True)
    wait_bytes(cand.at[pl.ds(2, 2), pl.ds(0, NEAR - 1), USED_ROWS], y_recv.at[0])
    wait_bytes(cand.at[1, pl.ds(0, 6), USED_ROWS], far_z_recv.at[0])
    absorb(0, NEAR)
    wait_bytes(cand.at[pl.ds(2, 2), pl.ds(NEAR, ZS - NEAR), USED_ROWS], y_recv.at[1])
    wait_bytes(cand.at[1, pl.ds(NEAR, ZS - NEAR), USED_ROWS], far_z_recv.at[1])
    absorb(NEAR, ZS - NEAR)

    for j in range(SUBS // 2):
        for r in range(ROUNDS):
            low_r = jnp.min(mins[j, r * SHARE : (r + 1) * SHARE, :], axis=0, keepdims=True)
            for h in range(2):
                line[me, r, 2 * j + h : 2 * j + h + 1, :] = low_r[:, h * npd : (h + 1) * npd]

    for device in x_line:
        remote(line.at[me], line.at[me], line_send, line_recv, device).start()
    wait_bytes(line.at[pl.ds(0, SUBS - 1)], line_recv)

    lanes = lax.broadcasted_iota(jnp.int32, (1, npd), 1)
    least = None
    total = jnp.zeros((1, npd), F32)
    for r in range(ROUNDS):
        now = jnp.min(line[:, r], axis=0)
        least = now if least is None else jnp.minimum(least, now)
        dist = jnp.maximum(squares[...] + 2.0 * least, 0.0)
        near[r] = dist
        part = jnp.sum(jnp.sum(dist, axis=0, keepdims=True), axis=1, keepdims=True)
        total = jnp.where(lanes == r, part, total)

    zsum[0] = total

    for d in (8, 7, 9, 6, 10, 5, 11, 4, 12, 3, 13, 2, 14, 1, 15):
        remote(zsum.at[0], zsum.at[ZS - d], z_send, z_recv, at_z(d)).start()
    wait_bytes(slots.at[pl.ds(0, SUBS - 1)], slots_send)
    wait_bytes(cand.at[0, pl.ds(0, 15), USED_ROWS], z_block_send)
    wait_bytes(cand.at[0, pl.ds(0, 15), USED_ROWS], far_z_send)
    wait_bytes(cand.at[pl.ds(0, 2), pl.ds(0, 15), USED_ROWS], y_send)
    for copy in (pts_right, pts_left, pts_core, far_top, core_left, far_low, core_right, core_far):
        copy.wait_send()
    wait_bytes(line.at[pl.ds(0, SUBS - 1)], line_send)
    wait_bytes(zsum.at[pl.ds(0, ZS - 1)], z_recv)
    ysum[0] = jnp.sum(zsum[...], axis=0)
    for d in (1, 3, 2):
        remote(ysum.at[0], ysum.at[XS - d], c_send, c_recv, y_to[d]).start()
    wait_bytes(ysum.at[pl.ds(0, XS - 1)], c_recv)
    cost = jnp.sum(ysum[...], axis=0)
    for r in range(ROUNDS):
        cost_r = jnp.sum(jnp.where(lanes == r, cost, 0.0), axis=1, keepdims=True)
        out_ref[r : r + 1, :] = npts * near[r, pl.ds(me, 1), :] / cost_r
    wait_bytes(zsum.at[pl.ds(0, ZS - 1)], z_send)
    wait_bytes(ysum.at[pl.ds(0, XS - 1)], c_send)


def shards(points, cand_rows, cand_count):
    npd, width = points.shape
    npts = float(npd * lax.axis_size(("dp", "sub")))
    dma = pltpu.SemaphoreType.DMA
    operands = (cand_rows, cand_count.reshape(1, ROUNDS), points)
    return pl.pallas_call(
        lambda *refs: kernel(npts, *refs),
        out_shape=jax.ShapeDtypeStruct((ROUNDS, npd), F32),
        in_specs=[
            pl.BlockSpec(memory_space=pl.ANY),
            pl.BlockSpec(memory_space=pl.ANY),
            pl.BlockSpec(memory_space=pl.ANY),
        ],
        out_specs=pl.BlockSpec(memory_space=pltpu.VMEM),
        scratch_shapes=[
            pltpu.SMEM((ROUNDS, SLOTS), jnp.int32),
            pltpu.SMEM((1, ROUNDS), jnp.int32),
            pltpu.VMEM((npd, width), jnp.bfloat16),
            pltpu.VMEM((SUBS, RAW, width), jnp.bfloat16),
            pltpu.VMEM((XS, ZS, BLK, width), jnp.bfloat16),
            pltpu.VMEM((SUBS, width, npd), jnp.bfloat16),
            pltpu.VMEM((SUBS // 2, BLK, 2 * npd), F32),
            pltpu.VMEM((SUBS, npd), F32),
            pltpu.VMEM((SUBS, ROUNDS, SUBS, npd), F32),
            pltpu.VMEM((ROUNDS, SUBS, npd), F32),
            pltpu.VMEM((ZS, 1, npd), F32),
            pltpu.VMEM((XS, 1, npd), F32),
            dma((3,)),
            dma,
            dma,
            dma,
            dma,
            dma((17,)),
            dma((2,)),
            dma,
            dma((2,)),
            dma((2,)),
            dma((8,)),
            dma((8,)),
            dma,
            dma,
            dma,
            dma,
            dma,
            dma,
        ],
        compiler_params=pltpu.CompilerParams(
            collective_id=0, has_side_effects=True, vmem_limit_bytes=40 * 1024 * 1024
        ),
        cost_estimate=pl.CostEstimate(
            flops=2 * 1024 * 1024 * width, bytes_accessed=npd * width * 2, transcendentals=0
        ),
    )(*(pltpu.with_memory_space_constraint(value, pltpu.HBM) for value in operands))


def solution(mesh):
    in_specs = (P(("dp", "sub"), None), P(None, ("dp", "sub")), P(None, ("dp", "sub")))
    out_specs = P(None, ("dp", "sub"))
    return jax.shard_map(shards, mesh=mesh, in_specs=in_specs, out_specs=out_specs, check_vma=False)
```

```python
import jax
import jax.numpy as jnp
from jax import lax
from jax.experimental import pallas as pl
from jax.experimental.pallas import tpu as pltpu
from jax.sharding import PartitionSpec as P

ROUNDS = 3
SLOTS = 4
XS = 4
ZS = 16
YS = 4
SUBS = 8
RAW = 16
BLK = 8
SHARE = 2
USED_ROWS = pl.ds(0, ROUNDS * SHARE)
NEAR = 9
MESH = pl.DeviceIdType.MESH
F32 = jnp.float32
INF = float("inf")


def kernel(
    npts,
    rows_in,
    counts_in,
    points_ref,
    out_ref,
    rows_ref,
    cnt_ref,
    raw,
    slots,
    cand,
    pall,
    mins,
    squares,
    line,
    near,
    zsum,
    ysum,
    local_sem,
    slots_send,
    slots_recv,
    z_block_send,
    y_send,
    z_block_recv,
    y_recv,
    far_z_send,
    far_recv,
    far_z_recv,
    pts_send,
    pts_recv,
    line_send,
    line_recv,
    z_send,
    z_recv,
    c_send,
    c_recv,
):
    dp = lax.axis_index("dp")
    sub = lax.axis_index("sub")
    x, z = lax.div(dp, ZS), lax.rem(dp, ZS)
    y, core = lax.div(sub, 2), lax.rem(sub, 2)
    npd, width = points_ref.shape

    def at_x(d):
        return (lax.rem(x + d, XS) * ZS + z, sub)

    def at_z(d):
        return (x * ZS + lax.rem(z + d, ZS), sub)

    def at_y(d):
        return (dp, lax.rem(y + d, YS) * 2 + core)

    other_core = (dp, y * 2 + (1 - core))
    z_to = {d: at_z(d % ZS) for d in (1, -1, 2, -2, 3, -3, 4, -4)}
    y_to = {d: at_y(d) for d in (1, 2, 3)}
    me = x * 2 + core
    x_right, x_left = at_x(1), at_x(3)

    own_points = pltpu.make_async_copy(points_ref, raw, local_sem.at[0])
    own_points.start()
    own_rows = pltpu.make_async_copy(rows_in, rows_ref, local_sem.at[1])
    own_rows.start()
    own_counts = pltpu.make_async_copy(counts_in, cnt_ref, local_sem.at[2])
    own_counts.start()
    barrier = pltpu.get_barrier_semaphore()
    far_first = ((2, 0), (2, 1), (1, 0), (3, 0), (1, 1), (3, 1), (0, 1))
    y_line = [(dp, lax.rem(y + d, YS) * 2 + (1 - core if other else core)) for d, other in far_first]
    x_line = [(lax.rem(x + d, XS) * ZS + z, y * 2 + (1 - core if other else core)) for d, other in far_first]
    partners = [*z_to.values(), *y_line, *x_line[:-1]]
    for device in partners:
        pl.semaphore_signal(barrier, inc=1, device_id=device, device_id_type=MESH)

    row = lax.broadcasted_iota(jnp.int32, (RAW, npd), 0)
    lane = lax.broadcasted_iota(jnp.int32, (RAW, npd), 1)
    here = lax.broadcasted_iota(jnp.int32, (npd, npd), 0)
    there = lax.broadcasted_iota(jnp.int32, (npd, npd), 1)
    same_round = (here & (RAW - 1)) == ROUNDS * SLOTS + ((there & (RAW - 1)) >> 2)
    before = jnp.where(same_round & ((here >> 4) < (there >> 4)), 1.0, 0.0)
    itself = jnp.where(same_round & ((here >> 4) == (there >> 4)), 1.0, 0.0)
    slot = lane & (RAW - 1)
    slot_round = jnp.where(slot < ROUNDS * SLOTS, slot >> 2, -1)
    slot_index = (slot & (SLOTS - 1)).astype(F32)
    want = lax.broadcasted_iota(jnp.int32, (XS * BLK, npd), 0)
    column = want >> 3
    ahead = jnp.where(column == 1, 2, jnp.where(column == 2, 3, jnp.where(column == 3, 1, 0)))
    holder = ((y + ahead) & (YS - 1)) * 2 + core
    wanted = (SHARE * holder + (want & 1)).astype(F32)
    wanted_round = slot_round[:1] == ((want & (BLK - 1)) >> 1)
    slot_index = slot_index[:1]
    own_rows.wait()
    own_counts.wait()
    target = jnp.full((RAW, npd), -1, jnp.int32)
    counts = jnp.zeros((RAW, npd), F32)
    for r in range(ROUNDS):
        counts = jnp.where(row == ROUNDS * SLOTS + r, cnt_ref[0, r].astype(F32), counts)
        for i in range(SLOTS):
            target = jnp.where(row == r * SLOTS + i, rows_ref[r, i], target)
    pick = jnp.where(lane == target, 1.0, 0.0).astype(jnp.bfloat16)
    own_points.wait()
    mine = raw[...]
    block = jnp.dot(pick, mine, preferred_element_type=F32)
    slots[sub, :, :npd] = (block[:, :npd] + counts).astype(jnp.bfloat16)
    slots[sub, :, npd:] = block[:, npd:].astype(jnp.bfloat16)

    pl.semaphore_wait(barrier, len(partners))

    def remote(src, dst, send, recv, device):
        return pltpu.make_async_remote_copy(
            src_ref=src, dst_ref=dst, send_sem=send, recv_sem=recv, device_id=device, device_id_type=MESH
        )

    def to_sides(place, count, group):
        for d, column in ((1, 2), (3, 3)):
            src, dst = cand.at[0, pl.ds(place, count), USED_ROWS], cand.at[column, pl.ds(place, count), USED_ROWS]
            remote(src, dst, y_send, y_recv.at[group], y_to[d]).start()

    def along_z(src, place, d, lanes=None, column=0):
        if lanes is None:
            src, dst = cand.at[column, src, USED_ROWS], cand.at[column, place, USED_ROWS]
        else:
            part = pl.ds(lanes * (width // 2), width // 2)
            src, dst = cand.at[column, src, USED_ROWS, part], cand.at[column, place, USED_ROWS, part]
        if column == 0:
            recv = z_block_recv.at[place + (lanes or 0)]
        elif place in (6, 8):
            recv = far_recv.at[place // 2 - 3]
        else:
            recv = far_z_recv.at[0 if place < NEAR else 1]
        remote(src, dst, (z_block_send, far_z_send)[column], recv, z_to[d]).start()

    def z_arrived(*places):
        for place in places:
            wait_bytes(cand.at[0, place, USED_ROWS], z_block_recv.at[place])

    def wait_bytes(ref, sem):
        pltpu.make_async_copy(ref, ref, sem).wait()

    for device in y_line:
        remote(slots.at[sub], slots.at[sub], slots_send, slots_recv, device).start()
    pall[me] = mine.T
    slot_right, slot_left, slot_far = (lax.rem(x + d, XS) * 2 + core for d in (1, 3, 2))
    top, low = pl.ds(0, width // 2), pl.ds(width // 2, width // 2)
    mine_at = pall.at[me]
    pts_right = remote(mine_at, mine_at, pts_send.at[0], pts_recv.at[0], x_right)
    pts_left = remote(mine_at, mine_at, pts_send.at[1], pts_recv.at[1], x_left)
    pts_core = remote(mine_at, mine_at, pts_send.at[2], pts_recv.at[2], other_core)
    pts_right.start()
    pts_left.start()
    pts_core.start()

    wait_bytes(slots.at[pl.ds(0, SUBS - 1)], slots_recv)
    flat = slots[...].reshape(SUBS * RAW, width)
    known = flat[:, :npd].astype(F32)
    offset = jnp.sum(known * before, axis=0, keepdims=True)
    count = jnp.sum(known * itself, axis=0, keepdims=True)
    choice = wanted_round & (slot_index < count) & (offset + slot_index == wanted)
    share = jnp.dot(jnp.where(choice, 1.0, 0.0).astype(jnp.bfloat16), flat, preferred_element_type=F32)
    cand[:, 7] = share.reshape(XS, BLK, width).astype(jnp.bfloat16)

    for column in range(2):
        along_z(7, 6, 4, None, column)
        along_z(7, 8, -4, None, column)
    for place, d in ((0, 2), (1, -2), (2, 1), (5, -1)):
        along_z(7, place, d)

    pts_right.wait_recv()
    near_left = pall.at[slot_left]
    far_top = remote(near_left.at[top], near_left.at[top], pts_send.at[3], pts_recv.at[3], x_right)
    core_left = remote(near_left, near_left, pts_send.at[4], pts_recv.at[4], other_core)
    far_top.start()
    core_left.start()
    pts_left.wait_recv()
    near_right = pall.at[slot_right]
    far_low = remote(near_right.at[low], near_right.at[low], pts_send.at[5], pts_recv.at[5], x_left)
    core_right = remote(near_right, near_right, pts_send.at[6], pts_recv.at[6], other_core)
    far_low.start()
    core_right.start()

    z_arrived(6)
    along_z(6, 15, 4, 0)
    for place, d in ((13, 3), (9, 2), (11, 1), (4, -1)):
        along_z(6, place, d)
    z_arrived(8)
    along_z(8, 15, -4, 1)
    for place, d in ((14, -3), (10, -2), (12, -1), (3, 1)):
        along_z(8, place, d)
    to_sides(6, 1, 0)
    to_sides(8, 1, 0)

    for place, d in ((0, 2), (1, -2), (2, 1), (5, -1)):
        along_z(7, place, d, None, 1)
    wait_bytes(cand.at[1, 6, USED_ROWS], far_recv.at[0])
    along_z(6, 15, 4, 0, 1)
    for place, d in ((13, 3), (9, 2), (11, 1), (4, -1)):
        along_z(6, place, d, None, 1)
    wait_bytes(cand.at[1, 8, USED_ROWS], far_recv.at[1])
    along_z(8, 15, -4, 1, 1)
    for place, d in ((14, -3), (10, -2), (12, -1), (3, 1)):
        along_z(8, place, d, None, 1)

    far_top.wait_recv()
    far_low.wait_recv()
    far = pall.at[slot_far]
    core_far = remote(far, far, pts_send.at[7], pts_recv.at[7], other_core)
    core_far.start()

    z_arrived(0, 1, 2, 3, 4, 5)
    to_sides(0, 6, 0)
    z_arrived(9, 10, 11, 12, 13, 14)
    to_sides(9, 6, 1)
    half_block = cand.at[0, 15, USED_ROWS, pl.ds(0, width // 2)]
    wait_bytes(half_block, z_block_recv.at[15])
    wait_bytes(half_block, z_block_recv.at[16])
    to_sides(15, 1, 1)

    def absorb(first, count):
        blocks = XS * count
        rows = cand[:, first : first + count].reshape(blocks, BLK, width)
        half = jnp.zeros((blocks, BLK, npd), F32)
        for t in range(width // npd):
            piece = rows[:, :, t * npd : (t + 1) * npd].astype(F32)
            half = half + piece * piece
        half = 0.5 * jnp.sum(half, axis=2, keepdims=True)
        flat = rows.reshape(blocks * BLK, width)
        for j in range(SUBS // 2):
            group = jnp.concatenate([pall[2 * j], pall[2 * j + 1]], axis=1)
            dots = jnp.dot(flat, group, preferred_element_type=F32)
            best = jnp.min(half - dots.reshape(blocks, BLK, 2 * npd), axis=0)
            mins[j] = best if first == 0 else jnp.minimum(mins[j], best)

    pts_core.wait_recv()
    core_left.wait_recv()
    core_right.wait_recv()
    core_far.wait_recv()
    for b in range(SUBS):
        wide = pall[b].astype(F32)
        squares[b : b + 1, :] = jnp.sum(wide * wide, axis=0, keepdims=True)
    wait_bytes(cand.at[pl.ds(2, 2), pl.ds(0, NEAR - 1), USED_ROWS], y_recv.at[0])
    wait_bytes(cand.at[1, pl.ds(0, 6), USED_ROWS], far_z_recv.at[0])
    absorb(0, NEAR)
    wait_bytes(cand.at[pl.ds(2, 2), pl.ds(NEAR, ZS - NEAR), USED_ROWS], y_recv.at[1])
    wait_bytes(cand.at[1, pl.ds(NEAR, ZS - NEAR), USED_ROWS], far_z_recv.at[1])
    absorb(NEAR, ZS - NEAR)

    for j in range(SUBS // 2):
        for r in range(ROUNDS):
            low_r = jnp.min(mins[j, r * SHARE : (r + 1) * SHARE, :], axis=0, keepdims=True)
            for h in range(2):
                line[me, r, 2 * j + h : 2 * j + h + 1, :] = low_r[:, h * npd : (h + 1) * npd]

    for device in x_line:
        remote(line.at[me], line.at[me], line_send, line_recv, device).start()
    wait_bytes(line.at[pl.ds(0, SUBS - 1)], line_recv)

    lanes = lax.broadcasted_iota(jnp.int32, (1, npd), 1)
    least = None
    total = jnp.zeros((1, npd), F32)
    for r in range(ROUNDS):
        now = jnp.min(line[:, r], axis=0)
        least = now if least is None else jnp.minimum(least, now)
        dist = jnp.maximum(squares[...] + 2.0 * least, 0.0)
        near[r] = dist
        part = jnp.sum(jnp.sum(dist, axis=0, keepdims=True), axis=1, keepdims=True)
        total = jnp.where(lanes == r, part, total)

    zsum[0] = total

    for d in (8, 7, 9, 6, 10, 5, 11, 4, 12, 3, 13, 2, 14, 1, 15):
        remote(zsum.at[0], zsum.at[ZS - d], z_send, z_recv, at_z(d)).start()
    wait_bytes(slots.at[pl.ds(0, SUBS - 1)], slots_send)
    wait_bytes(cand.at[0, pl.ds(0, 15), USED_ROWS], z_block_send)
    wait_bytes(cand.at[0, pl.ds(0, 15), USED_ROWS], far_z_send)
    wait_bytes(cand.at[pl.ds(0, 2), pl.ds(0, 15), USED_ROWS], y_send)
    for copy in (pts_right, pts_left, pts_core, far_top, core_left, far_low, core_right, core_far):
        copy.wait_send()
    wait_bytes(line.at[pl.ds(0, SUBS - 1)], line_send)
    wait_bytes(zsum.at[pl.ds(0, ZS - 1)], z_recv)
    ysum[0] = jnp.sum(zsum[...], axis=0)
    for d in (1, 3, 2):
        remote(ysum.at[0], ysum.at[XS - d], c_send, c_recv, y_to[d]).start()
    wait_bytes(ysum.at[pl.ds(0, XS - 1)], c_recv)
    cost = jnp.sum(ysum[...], axis=0)
    for r in range(ROUNDS):
        cost_r = jnp.sum(jnp.where(lanes == r, cost, 0.0), axis=1, keepdims=True)
        out_ref[r : r + 1, :] = npts * near[r, pl.ds(me, 1), :] / cost_r
    wait_bytes(zsum.at[pl.ds(0, ZS - 1)], z_send)
    wait_bytes(ysum.at[pl.ds(0, XS - 1)], c_send)


def shards(points, cand_rows, cand_count):
    npd, width = points.shape
    npts = float(npd * lax.axis_size(("dp", "sub")))
    dma = pltpu.SemaphoreType.DMA
    operands = (cand_rows, cand_count.reshape(1, ROUNDS), points)
    return pl.pallas_call(
        lambda *refs: kernel(npts, *refs),
        out_shape=jax.ShapeDtypeStruct((ROUNDS, npd), F32),
        in_specs=[
            pl.BlockSpec(memory_space=pl.ANY),
            pl.BlockSpec(memory_space=pl.ANY),
            pl.BlockSpec(memory_space=pl.ANY),
        ],
        out_specs=pl.BlockSpec(memory_space=pltpu.VMEM),
        scratch_shapes=[
            pltpu.SMEM((ROUNDS, SLOTS), jnp.int32),
            pltpu.SMEM((1, ROUNDS), jnp.int32),
            pltpu.VMEM((npd, width), jnp.bfloat16),
            pltpu.VMEM((SUBS, RAW, width), jnp.bfloat16),
            pltpu.VMEM((XS, ZS, BLK, width), jnp.bfloat16),
            pltpu.VMEM((SUBS, width, npd), jnp.bfloat16),
            pltpu.VMEM((SUBS // 2, BLK, 2 * npd), F32),
            pltpu.VMEM((SUBS, npd), F32),
            pltpu.VMEM((SUBS, ROUNDS, SUBS, npd), F32),
            pltpu.VMEM((ROUNDS, SUBS, npd), F32),
            pltpu.VMEM((ZS, 1, npd), F32),
            pltpu.VMEM((XS, 1, npd), F32),
            dma((3,)),
            dma,
            dma,
            dma,
            dma,
            dma((17,)),
            dma((2,)),
            dma,
            dma((2,)),
            dma((2,)),
            dma((8,)),
            dma((8,)),
            dma,
            dma,
            dma,
            dma,
            dma,
            dma,
        ],
        compiler_params=pltpu.CompilerParams(
            collective_id=0, has_side_effects=True, vmem_limit_bytes=40 * 1024 * 1024
        ),
        cost_estimate=pl.CostEstimate(
            flops=2 * 1024 * 1024 * width, bytes_accessed=npd * width * 2, transcendentals=0
        ),
    )(*(pltpu.with_memory_space_constraint(value, pltpu.HBM) for value in operands))


def solution(mesh):
    in_specs = (P(("dp", "sub"), None), P(None, ("dp", "sub")), P(None, ("dp", "sub")))
    out_specs = P(None, ("dp", "sub"))
    return jax.shard_map(shards, mesh=mesh, in_specs=in_specs, out_specs=out_specs, check_vma=False)
```

```python
import jax
import jax.numpy as jnp
from jax import lax
from jax.experimental import pallas as pl
from jax.experimental.pallas import tpu as pltpu
from jax.sharding import PartitionSpec as P

ROUNDS = 3
SLOTS = 4
XS = 4
ZS = 16
YS = 4
SUBS = 8
RAW = 16
BLK = 8
SHARE = 2
USED_ROWS = pl.ds(0, ROUNDS * SHARE)
NEAR = 9
MESH = pl.DeviceIdType.MESH
F32 = jnp.float32
INF = float("inf")


def kernel(
    npts,
    rows_in,
    counts_in,
    points_ref,
    out_ref,
    rows_ref,
    cnt_ref,
    raw,
    slots,
    cand,
    pall,
    mins,
    squares,
    line,
    near,
    zsum,
    ysum,
    local_sem,
    slots_send,
    slots_recv,
    z_block_send,
    y_send,
    z_block_recv,
    y_recv,
    far_send,
    far_z_send,
    far_recv,
    far_z_recv,
    pts_send,
    pts_recv,
    line_send,
    line_recv,
    z_send,
    z_recv,
    c_send,
    c_recv,
):
    dp = lax.axis_index("dp")
    sub = lax.axis_index("sub")
    x, z = lax.div(dp, ZS), lax.rem(dp, ZS)
    y, core = lax.div(sub, 2), lax.rem(sub, 2)
    npd, width = points_ref.shape

    def at_x(d):
        return (lax.rem(x + d, XS) * ZS + z, sub)

    def at_z(d):
        return (x * ZS + lax.rem(z + d, ZS), sub)

    def at_y(d):
        return (dp, lax.rem(y + d, YS) * 2 + core)

    other_core = (dp, y * 2 + (1 - core))
    z_to = {d: at_z(d % ZS) for d in (1, -1, 2, -2, 3, -3, 4, -4)}
    y_to = {d: at_y(d) for d in (1, 2, 3)}
    me = x * 2 + core
    x_right, x_left = at_x(1), at_x(3)

    own_points = pltpu.make_async_copy(points_ref, raw, local_sem.at[0])
    own_points.start()
    own_rows = pltpu.make_async_copy(rows_in, rows_ref, local_sem.at[1])
    own_rows.start()
    own_counts = pltpu.make_async_copy(counts_in, cnt_ref, local_sem.at[2])
    own_counts.start()
    barrier = pltpu.get_barrier_semaphore()
    far_first = ((2, 0), (2, 1), (1, 0), (3, 0), (1, 1), (3, 1), (0, 1))
    y_line = [(dp, lax.rem(y + d, YS) * 2 + (1 - core if other else core)) for d, other in far_first]
    x_line = [(lax.rem(x + d, XS) * ZS + z, y * 2 + (1 - core if other else core)) for d, other in far_first]
    partners = [*z_to.values(), *y_line, *x_line[:-1]]
    for device in partners:
        pl.semaphore_signal(barrier, inc=1, device_id=device, device_id_type=MESH)

    row = lax.broadcasted_iota(jnp.int32, (RAW, npd), 0)
    lane = lax.broadcasted_iota(jnp.int32, (RAW, npd), 1)
    here = lax.broadcasted_iota(jnp.int32, (npd, npd), 0)
    there = lax.broadcasted_iota(jnp.int32, (npd, npd), 1)
    same_round = (here & (RAW - 1)) == ROUNDS * SLOTS + ((there & (RAW - 1)) >> 2)
    before = jnp.where(same_round & ((here >> 4) < (there >> 4)), 1.0, 0.0)
    itself = jnp.where(same_round & ((here >> 4) == (there >> 4)), 1.0, 0.0)
    slot = lane & (RAW - 1)
    slot_round = jnp.where(slot < ROUNDS * SLOTS, slot >> 2, -1)
    slot_index = (slot & (SLOTS - 1)).astype(F32)
    want = lax.broadcasted_iota(jnp.int32, (XS * BLK, npd), 0)
    column = want >> 3
    ahead = jnp.where(column == 1, 2, jnp.where(column == 2, 3, jnp.where(column == 3, 1, 0)))
    holder = ((y + ahead) & (YS - 1)) * 2 + core
    wanted = (SHARE * holder + (want & 1)).astype(F32)
    wanted_round = slot_round[:1] == ((want & (BLK - 1)) >> 1)
    slot_index = slot_index[:1]
    own_rows.wait()
    own_counts.wait()
    target = jnp.full((RAW, npd), -1, jnp.int32)
    counts = jnp.zeros((RAW, npd), F32)
    for r in range(ROUNDS):
        counts = jnp.where(row == ROUNDS * SLOTS + r, cnt_ref[0, r].astype(F32), counts)
        for i in range(SLOTS):
            target = jnp.where(row == r * SLOTS + i, rows_ref[r, i], target)
    pick = jnp.where(lane == target, 1.0, 0.0).astype(jnp.bfloat16)
    own_points.wait()
    mine = raw[...]
    block = jnp.dot(pick, mine, preferred_element_type=F32)
    slots[sub, :, :npd] = (block[:, :npd] + counts).astype(jnp.bfloat16)
    slots[sub, :, npd:] = block[:, npd:].astype(jnp.bfloat16)

    pl.semaphore_wait(barrier, len(partners))

    def remote(src, dst, send, recv, device):
        return pltpu.make_async_remote_copy(
            src_ref=src, dst_ref=dst, send_sem=send, recv_sem=recv, device_id=device, device_id_type=MESH
        )

    def to_sides(place, count, group):
        for d, column in ((1, 2), (3, 3)):
            src, dst = cand.at[0, pl.ds(place, count), USED_ROWS], cand.at[column, pl.ds(place, count), USED_ROWS]
            remote(src, dst, y_send, y_recv.at[group], y_to[d]).start()

    def to_far(place):
        remote(cand.at[0, place, USED_ROWS], cand.at[1, place, USED_ROWS], far_send, far_recv.at[place - 6], y_to[2]).start()

    def far_along_z(src, place, count, group, d, lanes=None):
        src, dst = cand.at[1, pl.ds(src, count), USED_ROWS], cand.at[1, pl.ds(place, count), USED_ROWS]
        if lanes is not None:
            part = pl.ds(lanes * (width // 2), width // 2)
            src, dst = src.at[:, :, part], dst.at[:, :, part]
        remote(src, dst, far_z_send, far_z_recv.at[group], z_to[d]).start()

    def along_z(src, place, d, lanes=None):
        if lanes is None:
            src, dst = cand.at[0, src, USED_ROWS], cand.at[0, place, USED_ROWS]
        else:
            part = pl.ds(lanes * (width // 2), width // 2)
            src, dst = cand.at[0, src, USED_ROWS, part], cand.at[0, place, USED_ROWS, part]
        remote(src, dst, z_block_send, z_block_recv.at[place + (lanes or 0)], z_to[d]).start()

    def z_arrived(*places):
        for place in places:
            wait_bytes(cand.at[0, place, USED_ROWS], z_block_recv.at[place])

    def wait_bytes(ref, sem):
        pltpu.make_async_copy(ref, ref, sem).wait()

    for device in y_line:
        remote(slots.at[sub], slots.at[sub], slots_send, slots_recv, device).start()
    pall[me] = mine.T
    slot_right, slot_left, slot_far = (lax.rem(x + d, XS) * 2 + core for d in (1, 3, 2))
    top, low = pl.ds(0, width // 2), pl.ds(width // 2, width // 2)
    mine_at = pall.at[me]
    pts_right = remote(mine_at, mine_at, pts_send.at[0], pts_recv.at[0], x_right)
    pts_left = remote(mine_at, mine_at, pts_send.at[1], pts_recv.at[1], x_left)
    pts_core = remote(mine_at, mine_at, pts_send.at[2], pts_recv.at[2], other_core)
    pts_right.start()
    pts_left.start()
    pts_core.start()

    wait_bytes(slots.at[pl.ds(0, SUBS - 1)], slots_recv)
    flat = slots[...].reshape(SUBS * RAW, width)
    known = flat[:, :npd].astype(F32)
    offset = jnp.sum(known * before, axis=0, keepdims=True)
    count = jnp.sum(known * itself, axis=0, keepdims=True)
    choice = wanted_round & (slot_index < count) & (offset + slot_index == wanted)
    share = jnp.dot(jnp.where(choice, 1.0, 0.0).astype(jnp.bfloat16), flat, preferred_element_type=F32)
    cand[:, 7] = share.reshape(XS, BLK, width).astype(jnp.bfloat16)

    along_z(7, 6, 4)
    along_z(7, 8, -4)
    for place, d in ((0, 2), (1, -2), (2, 1), (5, -1)):
        along_z(7, place, d)

    pts_right.wait_recv()
    near_left = pall.at[slot_left]
    far_top = remote(near_left.at[top], near_left.at[top], pts_send.at[3], pts_recv.at[3], x_right)
    core_left = remote(near_left, near_left, pts_send.at[4], pts_recv.at[4], other_core)
    far_top.start()
    core_left.start()
    pts_left.wait_recv()
    near_right = pall.at[slot_right]
    far_low = remote(near_right.at[low], near_right.at[low], pts_send.at[5], pts_recv.at[5], x_left)
    core_right = remote(near_right, near_right, pts_send.at[6], pts_recv.at[6], other_core)
    far_low.start()
    core_right.start()

    z_arrived(6)
    to_far(6)
    along_z(6, 15, 4, 0)
    for place, d in ((13, 3), (9, 2), (11, 1), (4, -1)):
        along_z(6, place, d)
    z_arrived(8)
    to_far(8)
    along_z(8, 15, -4, 1)
    for place, d in ((14, -3), (10, -2), (12, -1), (3, 1)):
        along_z(8, place, d)
    to_sides(6, 1, 0)
    to_sides(8, 1, 0)

    for place in (6, 8):
        wait_bytes(cand.at[1, place, USED_ROWS], far_recv.at[place - 6])
    far_along_z(6, 15, 1, 1, 4, 0)
    far_along_z(8, 15, 1, 1, -4, 1)
    far_along_z(6, 13, 1, 1, 3)
    far_along_z(8, 14, 1, 1, -3)
    far_along_z(6, 9, 1, 1, 2)
    far_along_z(8, 10, 1, 1, -2)
    far_along_z(6, 11, 1, 1, 1)
    far_along_z(8, 12, 1, 1, -1)
    far_along_z(7, 0, 1, 0, 2)
    far_along_z(7, 1, 1, 0, -2)
    far_along_z(7, 2, 2, 0, 1)
    far_along_z(6, 4, 2, 0, -1)

    far_top.wait_recv()
    far_low.wait_recv()
    far = pall.at[slot_far]
    core_far = remote(far, far, pts_send.at[7], pts_recv.at[7], other_core)
    core_far.start()

    z_arrived(0, 1, 2, 3, 4, 5)
    to_sides(0, 6, 0)
    z_arrived(9, 10, 11, 12, 13, 14)
    to_sides(9, 6, 1)
    half_block = cand.at[0, 15, USED_ROWS, pl.ds(0, width // 2)]
    wait_bytes(half_block, z_block_recv.at[15])
    wait_bytes(half_block, z_block_recv.at[16])
    to_sides(15, 1, 1)

    def absorb(first, count):
        blocks = XS * count
        rows = cand[:, first : first + count].reshape(blocks, BLK, width)
        half = jnp.zeros((blocks, BLK, npd), F32)
        for t in range(width // npd):
            piece = rows[:, :, t * npd : (t + 1) * npd].astype(F32)
            half = half + piece * piece
        half = 0.5 * jnp.sum(half, axis=2, keepdims=True)
        flat = rows.reshape(blocks * BLK, width)
        for j in range(SUBS // 2):
            group = jnp.concatenate([pall[2 * j], pall[2 * j + 1]], axis=1)
            dots = jnp.dot(flat, group, preferred_element_type=F32)
            best = jnp.min(half - dots.reshape(blocks, BLK, 2 * npd), axis=0)
            mins[j] = best if first == 0 else jnp.minimum(mins[j], best)

    pts_core.wait_recv()
    core_left.wait_recv()
    core_right.wait_recv()
    core_far.wait_recv()
    for b in range(SUBS):
        wide = pall[b].astype(F32)
        squares[b : b + 1, :] = jnp.sum(wide * wide, axis=0, keepdims=True)
    wait_bytes(cand.at[pl.ds(2, 2), pl.ds(0, NEAR - 1), USED_ROWS], y_recv.at[0])
    wait_bytes(cand.at[1, pl.ds(0, 6), USED_ROWS], far_z_recv.at[0])
    absorb(0, NEAR)
    wait_bytes(cand.at[pl.ds(2, 2), pl.ds(NEAR, ZS - NEAR), USED_ROWS], y_recv.at[1])
    wait_bytes(cand.at[1, pl.ds(NEAR, ZS - NEAR), USED_ROWS], far_z_recv.at[1])
    absorb(NEAR, ZS - NEAR)

    for j in range(SUBS // 2):
        for r in range(ROUNDS):
            low_r = jnp.min(mins[j, r * SHARE : (r + 1) * SHARE, :], axis=0, keepdims=True)
            for h in range(2):
                line[me, r, 2 * j + h : 2 * j + h + 1, :] = low_r[:, h * npd : (h + 1) * npd]

    for device in x_line:
        remote(line.at[me], line.at[me], line_send, line_recv, device).start()
    wait_bytes(line.at[pl.ds(0, SUBS - 1)], line_recv)

    lanes = lax.broadcasted_iota(jnp.int32, (1, npd), 1)
    least = None
    total = jnp.zeros((1, npd), F32)
    for r in range(ROUNDS):
        now = jnp.min(line[:, r], axis=0)
        least = now if least is None else jnp.minimum(least, now)
        dist = jnp.maximum(squares[...] + 2.0 * least, 0.0)
        near[r] = dist
        part = jnp.sum(jnp.sum(dist, axis=0, keepdims=True), axis=1, keepdims=True)
        total = jnp.where(lanes == r, part, total)

    zsum[0] = total

    for d in (8, 7, 9, 6, 10, 5, 11, 4, 12, 3, 13, 2, 14, 1, 15):
        remote(zsum.at[0], zsum.at[ZS - d], z_send, z_recv, at_z(d)).start()
    wait_bytes(slots.at[pl.ds(0, SUBS - 1)], slots_send)
    wait_bytes(cand.at[0, pl.ds(0, 15), USED_ROWS], z_block_send)
    wait_bytes(cand.at[pl.ds(0, 2), pl.ds(0, 15), USED_ROWS], y_send)
    wait_bytes(cand.at[0, pl.ds(0, 2), USED_ROWS], far_send)
    wait_bytes(cand.at[0, pl.ds(0, 13), USED_ROWS], far_z_send)
    for copy in (pts_right, pts_left, pts_core, far_top, core_left, far_low, core_right, core_far):
        copy.wait_send()
    wait_bytes(line.at[pl.ds(0, SUBS - 1)], line_send)
    wait_bytes(zsum.at[pl.ds(0, ZS - 1)], z_recv)
    ysum[0] = jnp.sum(zsum[...], axis=0)
    for d in (1, 3, 2):
        remote(ysum.at[0], ysum.at[XS - d], c_send, c_recv, y_to[d]).start()
    wait_bytes(ysum.at[pl.ds(0, XS - 1)], c_recv)
    cost = jnp.sum(ysum[...], axis=0)
    for r in range(ROUNDS):
        cost_r = jnp.sum(jnp.where(lanes == r, cost, 0.0), axis=1, keepdims=True)
        out_ref[r : r + 1, :] = npts * near[r, pl.ds(me, 1), :] / cost_r
    wait_bytes(zsum.at[pl.ds(0, ZS - 1)], z_send)
    wait_bytes(ysum.at[pl.ds(0, XS - 1)], c_send)


def shards(points, cand_rows, cand_count):
    npd, width = points.shape
    npts = float(npd * lax.axis_size(("dp", "sub")))
    dma = pltpu.SemaphoreType.DMA
    operands = (cand_rows, cand_count.reshape(1, ROUNDS), points)
    return pl.pallas_call(
        lambda *refs: kernel(npts, *refs),
        out_shape=jax.ShapeDtypeStruct((ROUNDS, npd), F32),
        in_specs=[
            pl.BlockSpec(memory_space=pl.ANY),
            pl.BlockSpec(memory_space=pl.ANY),
            pl.BlockSpec(memory_space=pl.ANY),
        ],
        out_specs=pl.BlockSpec(memory_space=pltpu.VMEM),
        scratch_shapes=[
            pltpu.SMEM((ROUNDS, SLOTS), jnp.int32),
            pltpu.SMEM((1, ROUNDS), jnp.int32),
            pltpu.VMEM((npd, width), jnp.bfloat16),
            pltpu.VMEM((SUBS, RAW, width), jnp.bfloat16),
            pltpu.VMEM((XS, ZS, BLK, width), jnp.bfloat16),
            pltpu.VMEM((SUBS, width, npd), jnp.bfloat16),
            pltpu.VMEM((SUBS // 2, BLK, 2 * npd), F32),
            pltpu.VMEM((SUBS, npd), F32),
            pltpu.VMEM((SUBS, ROUNDS, SUBS, npd), F32),
            pltpu.VMEM((ROUNDS, SUBS, npd), F32),
            pltpu.VMEM((ZS, 1, npd), F32),
            pltpu.VMEM((XS, 1, npd), F32),
            dma((3,)),
            dma,
            dma,
            dma,
            dma,
            dma((17,)),
            dma((2,)),
            dma,
            dma,
            dma((3,)),
            dma((2,)),
            dma((8,)),
            dma((8,)),
            dma,
            dma,
            dma,
            dma,
            dma,
            dma,
        ],
        compiler_params=pltpu.CompilerParams(
            collective_id=0, has_side_effects=True, vmem_limit_bytes=40 * 1024 * 1024
        ),
        cost_estimate=pl.CostEstimate(
            flops=2 * 1024 * 1024 * width, bytes_accessed=npd * width * 2, transcendentals=0
        ),
    )(*(pltpu.with_memory_space_constraint(value, pltpu.HBM) for value in operands))


def solution(mesh):
    in_specs = (P(("dp", "sub"), None), P(None, ("dp", "sub")), P(None, ("dp", "sub")))
    out_specs = P(None, ("dp", "sub"))
    return jax.shard_map(shards, mesh=mesh, in_specs=in_specs, out_specs=out_specs, check_vma=False)
```

```python
import jax
import jax.numpy as jnp
from jax import lax
from jax.experimental import pallas as pl
from jax.experimental.pallas import tpu as pltpu
from jax.sharding import PartitionSpec as P

ROUNDS = 3
SLOTS = 4
XS = 4
ZS = 16
YS = 4
SUBS = 8
RAW = 16
BLK = 8
SHARE = 2
USED_ROWS = pl.ds(0, ROUNDS * SHARE)
NEAR = 9
MESH = pl.DeviceIdType.MESH
F32 = jnp.float32
INF = float("inf")


def kernel(
    npts,
    rows_in,
    counts_in,
    points_ref,
    out_ref,
    rows_ref,
    cnt_ref,
    raw,
    slots,
    cand,
    pall,
    mins,
    squares,
    line,
    near,
    zsum,
    ysum,
    local_sem,
    slots_send,
    slots_recv,
    z_block_send,
    y_send,
    z_block_recv,
    y_recv,
    far_send,
    far_z_send,
    far_recv,
    far_z_recv,
    pts_send,
    pts_recv,
    line_send,
    line_recv,
    z_send,
    z_recv,
    c_send,
    c_recv,
):
    dp = lax.axis_index("dp")
    sub = lax.axis_index("sub")
    x, z = lax.div(dp, ZS), lax.rem(dp, ZS)
    y, core = lax.div(sub, 2), lax.rem(sub, 2)
    npd, width = points_ref.shape

    def at_x(d):
        return (lax.rem(x + d, XS) * ZS + z, sub)

    def at_z(d):
        return (x * ZS + lax.rem(z + d, ZS), sub)

    def at_y(d):
        return (dp, lax.rem(y + d, YS) * 2 + core)

    other_core = (dp, y * 2 + (1 - core))
    z_to = {d: at_z(d % ZS) for d in (1, -1, 2, -2, 3, -3, 4, -4)}
    y_to = {d: at_y(d) for d in (1, 2, 3)}
    me = x * 2 + core
    x_right, x_left = at_x(1), at_x(3)

    own_points = pltpu.make_async_copy(points_ref, raw, local_sem.at[0])
    own_points.start()
    own_rows = pltpu.make_async_copy(rows_in, rows_ref, local_sem.at[1])
    own_rows.start()
    own_counts = pltpu.make_async_copy(counts_in, cnt_ref, local_sem.at[2])
    own_counts.start()
    barrier = pltpu.get_barrier_semaphore()
    far_first = ((2, 0), (2, 1), (1, 0), (3, 0), (1, 1), (3, 1), (0, 1))
    y_line = [(dp, lax.rem(y + d, YS) * 2 + (1 - core if other else core)) for d, other in far_first]
    x_line = [(lax.rem(x + d, XS) * ZS + z, y * 2 + (1 - core if other else core)) for d, other in far_first]
    partners = [*z_to.values(), *y_line, *x_line[:-1]]
    for device in partners:
        pl.semaphore_signal(barrier, inc=1, device_id=device, device_id_type=MESH)

    row = lax.broadcasted_iota(jnp.int32, (RAW, npd), 0)
    lane = lax.broadcasted_iota(jnp.int32, (RAW, npd), 1)
    here = lax.broadcasted_iota(jnp.int32, (npd, npd), 0)
    there = lax.broadcasted_iota(jnp.int32, (npd, npd), 1)
    same_round = (here & (RAW - 1)) == ROUNDS * SLOTS + ((there & (RAW - 1)) >> 2)
    before = jnp.where(same_round & ((here >> 4) < (there >> 4)), 1.0, 0.0)
    itself = jnp.where(same_round & ((here >> 4) == (there >> 4)), 1.0, 0.0)
    slot = lane & (RAW - 1)
    slot_round = jnp.where(slot < ROUNDS * SLOTS, slot >> 2, -1)
    slot_index = (slot & (SLOTS - 1)).astype(F32)
    want = lax.broadcasted_iota(jnp.int32, (XS * BLK, npd), 0)
    column = want >> 3
    ahead = jnp.where(column == 1, 2, jnp.where(column == 2, 3, jnp.where(column == 3, 1, 0)))
    holder = ((y + ahead) & (YS - 1)) * 2 + core
    wanted = (SHARE * holder + (want & 1)).astype(F32)
    wanted_round = slot_round[:1] == ((want & (BLK - 1)) >> 1)
    slot_index = slot_index[:1]
    own_rows.wait()
    own_counts.wait()
    target = jnp.full((RAW, npd), -1, jnp.int32)
    counts = jnp.zeros((RAW, npd), F32)
    for r in range(ROUNDS):
        counts = jnp.where(row == ROUNDS * SLOTS + r, cnt_ref[0, r].astype(F32), counts)
        for i in range(SLOTS):
            target = jnp.where(row == r * SLOTS + i, rows_ref[r, i], target)
    pick = jnp.where(lane == target, 1.0, 0.0).astype(jnp.bfloat16)
    own_points.wait()
    mine = raw[...]
    block = jnp.dot(pick, mine, preferred_element_type=F32)
    slots[sub, :, :npd] = (block[:, :npd] + counts).astype(jnp.bfloat16)
    slots[sub, :, npd:] = block[:, npd:].astype(jnp.bfloat16)

    pl.semaphore_wait(barrier, len(partners))

    def remote(src, dst, send, recv, device):
        return pltpu.make_async_remote_copy(
            src_ref=src, dst_ref=dst, send_sem=send, recv_sem=recv, device_id=device, device_id_type=MESH
        )

    def to_sides(place, count, group):
        for d, column in ((1, 2), (3, 3)):
            src, dst = cand.at[0, pl.ds(place, count), USED_ROWS], cand.at[column, pl.ds(place, count), USED_ROWS]
            remote(src, dst, y_send, y_recv.at[group], y_to[d]).start()

    def to_far(place):
        remote(cand.at[0, place, USED_ROWS], cand.at[1, place, USED_ROWS], far_send, far_recv.at[place - 6], y_to[2]).start()

    def far_along_z(src, place, count, group, d, lanes=None):
        src, dst = cand.at[1, pl.ds(src, count), USED_ROWS], cand.at[1, pl.ds(place, count), USED_ROWS]
        if lanes is not None:
            part = pl.ds(lanes * (width // 2), width // 2)
            src, dst = src.at[:, :, part], dst.at[:, :, part]
        remote(src, dst, far_z_send, far_z_recv.at[group], z_to[d]).start()

    def along_z(src, place, d, lanes=None):
        if lanes is None:
            src, dst = cand.at[0, src, USED_ROWS], cand.at[0, place, USED_ROWS]
        else:
            part = pl.ds(lanes * (width // 2), width // 2)
            src, dst = cand.at[0, src, USED_ROWS, part], cand.at[0, place, USED_ROWS, part]
        remote(src, dst, z_block_send, z_block_recv.at[place + (lanes or 0)], z_to[d]).start()

    def z_arrived(*places):
        for place in places:
            wait_bytes(cand.at[0, place, USED_ROWS], z_block_recv.at[place])

    def wait_bytes(ref, sem):
        pltpu.make_async_copy(ref, ref, sem).wait()

    for device in y_line:
        remote(slots.at[sub], slots.at[sub], slots_send, slots_recv, device).start()
    pall[me] = mine.T
    slot_right, slot_left, slot_far = (lax.rem(x + d, XS) * 2 + core for d in (1, 3, 2))
    top, low = pl.ds(0, width // 2), pl.ds(width // 2, width // 2)
    mine_at = pall.at[me]
    pts_right = remote(mine_at, mine_at, pts_send.at[0], pts_recv.at[0], x_right)
    pts_left = remote(mine_at, mine_at, pts_send.at[1], pts_recv.at[1], x_left)
    pts_core = remote(mine_at, mine_at, pts_send.at[2], pts_recv.at[2], other_core)
    pts_right.start()
    pts_left.start()
    pts_core.start()

    wait_bytes(slots.at[pl.ds(0, SUBS - 1)], slots_recv)
    flat = slots[...].reshape(SUBS * RAW, width)
    known = flat[:, :npd].astype(F32)
    offset = jnp.sum(known * before, axis=0, keepdims=True)
    count = jnp.sum(known * itself, axis=0, keepdims=True)
    choice = wanted_round & (slot_index < count) & (offset + slot_index == wanted)
    share = jnp.dot(jnp.where(choice, 1.0, 0.0).astype(jnp.bfloat16), flat, preferred_element_type=F32)
    cand[:, 7] = share.reshape(XS, BLK, width).astype(jnp.bfloat16)

    along_z(7, 6, 4)
    along_z(7, 8, -4)
    for place, d in ((0, 2), (1, -2), (2, 1), (5, -1)):
        along_z(7, place, d)

    pts_right.wait_recv()
    near_left = pall.at[slot_left]
    far_top = remote(near_left.at[top], near_left.at[top], pts_send.at[3], pts_recv.at[3], x_right)
    core_left = remote(near_left, near_left, pts_send.at[4], pts_recv.at[4], other_core)
    far_top.start()
    core_left.start()
    pts_left.wait_recv()
    near_right = pall.at[slot_right]
    far_low = remote(near_right.at[low], near_right.at[low], pts_send.at[5], pts_recv.at[5], x_left)
    core_right = remote(near_right, near_right, pts_send.at[6], pts_recv.at[6], other_core)
    far_low.start()
    core_right.start()

    z_arrived(6)
    to_far(6)
    along_z(6, 15, 4, 0)
    for place, d in ((13, 3), (9, 2), (11, 1), (4, -1)):
        along_z(6, place, d)
    z_arrived(8)
    to_far(8)
    along_z(8, 15, -4, 1)
    for place, d in ((14, -3), (10, -2), (12, -1), (3, 1)):
        along_z(8, place, d)

    for place in (6, 8):
        wait_bytes(cand.at[1, place, USED_ROWS], far_recv.at[place - 6])
    far_along_z(6, 15, 1, 1, 4, 0)
    far_along_z(8, 15, 1, 1, -4, 1)
    far_along_z(6, 13, 1, 1, 3)
    far_along_z(8, 14, 1, 1, -3)
    far_along_z(6, 9, 1, 1, 2)
    far_along_z(8, 10, 1, 1, -2)
    far_along_z(6, 11, 1, 1, 1)
    far_along_z(8, 12, 1, 1, -1)
    far_along_z(7, 0, 1, 0, 2)
    far_along_z(7, 1, 1, 0, -2)
    far_along_z(7, 2, 2, 0, 1)
    far_along_z(6, 4, 2, 0, -1)

    far_top.wait_recv()
    far_low.wait_recv()
    far = pall.at[slot_far]
    core_far = remote(far, far, pts_send.at[7], pts_recv.at[7], other_core)
    core_far.start()

    z_arrived(0, 1, 2, 3, 4, 5)
    to_sides(0, 7, 0)
    z_arrived(9, 10, 11, 12, 13, 14)
    half_block = cand.at[0, 15, USED_ROWS, pl.ds(0, width // 2)]
    wait_bytes(half_block, z_block_recv.at[15])
    wait_bytes(half_block, z_block_recv.at[16])
    to_sides(8, 8, 1)

    def absorb(first, count):
        blocks = XS * count
        rows = cand[:, first : first + count].reshape(blocks, BLK, width)
        half = jnp.zeros((blocks, BLK, npd), F32)
        for t in range(width // npd):
            piece = rows[:, :, t * npd : (t + 1) * npd].astype(F32)
            half = half + piece * piece
        half = 0.5 * jnp.sum(half, axis=2, keepdims=True)
        flat = rows.reshape(blocks * BLK, width)
        for j in range(SUBS // 2):
            group = jnp.concatenate([pall[2 * j], pall[2 * j + 1]], axis=1)
            dots = jnp.dot(flat, group, preferred_element_type=F32)
            best = jnp.min(half - dots.reshape(blocks, BLK, 2 * npd), axis=0)
            mins[j] = best if first == 0 else jnp.minimum(mins[j], best)

    pts_core.wait_recv()
    core_left.wait_recv()
    core_right.wait_recv()
    core_far.wait_recv()
    for b in range(SUBS):
        wide = pall[b].astype(F32)
        squares[b : b + 1, :] = jnp.sum(wide * wide, axis=0, keepdims=True)
    wait_bytes(cand.at[pl.ds(2, 2), pl.ds(0, 7), USED_ROWS], y_recv.at[0])
    wait_bytes(cand.at[1, pl.ds(0, 6), USED_ROWS], far_z_recv.at[0])
    absorb(0, 8)
    wait_bytes(cand.at[pl.ds(2, 2), pl.ds(8, 8), USED_ROWS], y_recv.at[1])
    wait_bytes(cand.at[1, pl.ds(NEAR, ZS - NEAR), USED_ROWS], far_z_recv.at[1])
    absorb(8, 8)

    for j in range(SUBS // 2):
        for r in range(ROUNDS):
            low_r = jnp.min(mins[j, r * SHARE : (r + 1) * SHARE, :], axis=0, keepdims=True)
            for h in range(2):
                line[me, r, 2 * j + h : 2 * j + h + 1, :] = low_r[:, h * npd : (h + 1) * npd]

    for device in x_line:
        remote(line.at[me], line.at[me], line_send, line_recv, device).start()
    wait_bytes(line.at[pl.ds(0, SUBS - 1)], line_recv)

    lanes = lax.broadcasted_iota(jnp.int32, (1, npd), 1)
    least = None
    total = jnp.zeros((1, npd), F32)
    for r in range(ROUNDS):
        now = jnp.min(line[:, r], axis=0)
        least = now if least is None else jnp.minimum(least, now)
        dist = jnp.maximum(squares[...] + 2.0 * least, 0.0)
        near[r] = dist
        part = jnp.sum(jnp.sum(dist, axis=0, keepdims=True), axis=1, keepdims=True)
        total = jnp.where(lanes == r, part, total)

    zsum[0] = total

    for d in (8, 7, 9, 6, 10, 5, 11, 4, 12, 3, 13, 2, 14, 1, 15):
        remote(zsum.at[0], zsum.at[ZS - d], z_send, z_recv, at_z(d)).start()
    wait_bytes(slots.at[pl.ds(0, SUBS - 1)], slots_send)
    wait_bytes(cand.at[0, pl.ds(0, 15), USED_ROWS], z_block_send)
    wait_bytes(cand.at[pl.ds(0, 2), pl.ds(0, 15), USED_ROWS], y_send)
    wait_bytes(cand.at[0, pl.ds(0, 2), USED_ROWS], far_send)
    wait_bytes(cand.at[0, pl.ds(0, 13), USED_ROWS], far_z_send)
    for copy in (pts_right, pts_left, pts_core, far_top, core_left, far_low, core_right, core_far):
        copy.wait_send()
    wait_bytes(line.at[pl.ds(0, SUBS - 1)], line_send)
    wait_bytes(zsum.at[pl.ds(0, ZS - 1)], z_recv)
    ysum[0] = jnp.sum(zsum[...], axis=0)
    for d in (1, 3, 2):
        remote(ysum.at[0], ysum.at[XS - d], c_send, c_recv, y_to[d]).start()
    wait_bytes(ysum.at[pl.ds(0, XS - 1)], c_recv)
    cost = jnp.sum(ysum[...], axis=0)
    for r in range(ROUNDS):
        cost_r = jnp.sum(jnp.where(lanes == r, cost, 0.0), axis=1, keepdims=True)
        out_ref[r : r + 1, :] = npts * near[r, pl.ds(me, 1), :] / cost_r
    wait_bytes(zsum.at[pl.ds(0, ZS - 1)], z_send)
    wait_bytes(ysum.at[pl.ds(0, XS - 1)], c_send)


def shards(points, cand_rows, cand_count):
    npd, width = points.shape
    npts = float(npd * lax.axis_size(("dp", "sub")))
    dma = pltpu.SemaphoreType.DMA
    operands = (cand_rows, cand_count.reshape(1, ROUNDS), points)
    return pl.pallas_call(
        lambda *refs: kernel(npts, *refs),
        out_shape=jax.ShapeDtypeStruct((ROUNDS, npd), F32),
        in_specs=[
            pl.BlockSpec(memory_space=pl.ANY),
            pl.BlockSpec(memory_space=pl.ANY),
            pl.BlockSpec(memory_space=pl.ANY),
        ],
        out_specs=pl.BlockSpec(memory_space=pltpu.VMEM),
        scratch_shapes=[
            pltpu.SMEM((ROUNDS, SLOTS), jnp.int32),
            pltpu.SMEM((1, ROUNDS), jnp.int32),
            pltpu.VMEM((npd, width), jnp.bfloat16),
            pltpu.VMEM((SUBS, RAW, width), jnp.bfloat16),
            pltpu.VMEM((XS, ZS, BLK, width), jnp.bfloat16),
            pltpu.VMEM((SUBS, width, npd), jnp.bfloat16),
            pltpu.VMEM((SUBS // 2, BLK, 2 * npd), F32),
            pltpu.VMEM((SUBS, npd), F32),
            pltpu.VMEM((SUBS, ROUNDS, SUBS, npd), F32),
            pltpu.VMEM((ROUNDS, SUBS, npd), F32),
            pltpu.VMEM((ZS, 1, npd), F32),
            pltpu.VMEM((XS, 1, npd), F32),
            dma((3,)),
            dma,
            dma,
            dma,
            dma,
            dma((17,)),
            dma((2,)),
            dma,
            dma,
            dma((3,)),
            dma((2,)),
            dma((8,)),
            dma((8,)),
            dma,
            dma,
            dma,
            dma,
            dma,
            dma,
        ],
        compiler_params=pltpu.CompilerParams(
            collective_id=0, has_side_effects=True, vmem_limit_bytes=40 * 1024 * 1024
        ),
        cost_estimate=pl.CostEstimate(
            flops=2 * 1024 * 1024 * width, bytes_accessed=npd * width * 2, transcendentals=0
        ),
    )(*(pltpu.with_memory_space_constraint(value, pltpu.HBM) for value in operands))


def solution(mesh):
    in_specs = (P(("dp", "sub"), None), P(None, ("dp", "sub")), P(None, ("dp", "sub")))
    out_specs = P(None, ("dp", "sub"))
    return jax.shard_map(shards, mesh=mesh, in_specs=in_specs, out_specs=out_specs, check_vma=False)
```

```python
import jax
import jax.numpy as jnp
from jax import lax
from jax.experimental import pallas as pl
from jax.experimental.pallas import tpu as pltpu
from jax.sharding import PartitionSpec as P

ROUNDS = 3
SLOTS = 4
XS = 4
ZS = 16
YS = 4
SUBS = 8
RAW = 16
BLK = 8
SHARE = 2
USED_ROWS = pl.ds(0, ROUNDS * SHARE)
NEAR = 11
MESH = pl.DeviceIdType.MESH
F32 = jnp.float32
INF = float("inf")


def kernel(
    npts,
    rows_in,
    counts_in,
    points_ref,
    out_ref,
    rows_ref,
    cnt_ref,
    raw,
    slots,
    cand,
    pall,
    mins,
    squares,
    line,
    near,
    zsum,
    ysum,
    local_sem,
    slots_send,
    slots_recv,
    z_block_send,
    y_send,
    z_block_recv,
    y_recv,
    far_send,
    far_z_send,
    far_recv,
    far_z_recv,
    pts_send,
    pts_recv,
    line_send,
    line_recv,
    z_send,
    z_recv,
    c_send,
    c_recv,
):
    dp = lax.axis_index("dp")
    sub = lax.axis_index("sub")
    x, z = lax.div(dp, ZS), lax.rem(dp, ZS)
    y, core = lax.div(sub, 2), lax.rem(sub, 2)
    npd, width = points_ref.shape

    def at_x(d):
        return (lax.rem(x + d, XS) * ZS + z, sub)

    def at_z(d):
        return (x * ZS + lax.rem(z + d, ZS), sub)

    def at_y(d):
        return (dp, lax.rem(y + d, YS) * 2 + core)

    other_core = (dp, y * 2 + (1 - core))
    z_to = {d: at_z(d % ZS) for d in (1, -1, 2, -2, 3, -3, 4, -4)}
    y_to = {d: at_y(d) for d in (1, 2, 3)}
    me = x * 2 + core
    x_right, x_left = at_x(1), at_x(3)

    own_points = pltpu.make_async_copy(points_ref, raw, local_sem.at[0])
    own_points.start()
    own_rows = pltpu.make_async_copy(rows_in, rows_ref, local_sem.at[1])
    own_rows.start()
    own_counts = pltpu.make_async_copy(counts_in, cnt_ref, local_sem.at[2])
    own_counts.start()
    barrier = pltpu.get_barrier_semaphore()
    far_first = ((2, 0), (2, 1), (1, 0), (3, 0), (1, 1), (3, 1), (0, 1))
    y_line = [(dp, lax.rem(y + d, YS) * 2 + (1 - core if other else core)) for d, other in far_first]
    x_line = [(lax.rem(x + d, XS) * ZS + z, y * 2 + (1 - core if other else core)) for d, other in far_first]
    partners = [*z_to.values(), *y_line, *x_line[:-1]]
    for device in partners:
        pl.semaphore_signal(barrier, inc=1, device_id=device, device_id_type=MESH)

    row = lax.broadcasted_iota(jnp.int32, (RAW, npd), 0)
    lane = lax.broadcasted_iota(jnp.int32, (RAW, npd), 1)
    here = lax.broadcasted_iota(jnp.int32, (npd, npd), 0)
    there = lax.broadcasted_iota(jnp.int32, (npd, npd), 1)
    same_round = (here & (RAW - 1)) == ROUNDS * SLOTS + ((there & (RAW - 1)) >> 2)
    before = jnp.where(same_round & ((here >> 4) < (there >> 4)), 1.0, 0.0)
    itself = jnp.where(same_round & ((here >> 4) == (there >> 4)), 1.0, 0.0)
    slot = lane & (RAW - 1)
    slot_round = jnp.where(slot < ROUNDS * SLOTS, slot >> 2, -1)
    slot_index = (slot & (SLOTS - 1)).astype(F32)
    want = lax.broadcasted_iota(jnp.int32, (XS * BLK, npd), 0)
    column = want >> 3
    ahead = jnp.where(column == 1, 2, jnp.where(column == 2, 3, jnp.where(column == 3, 1, 0)))
    holder = ((y + ahead) & (YS - 1)) * 2 + core
    wanted = (SHARE * holder + (want & 1)).astype(F32)
    wanted_round = slot_round[:1] == ((want & (BLK - 1)) >> 1)
    slot_index = slot_index[:1]
    own_rows.wait()
    own_counts.wait()
    target = jnp.full((RAW, npd), -1, jnp.int32)
    counts = jnp.zeros((RAW, npd), F32)
    for r in range(ROUNDS):
        counts = jnp.where(row == ROUNDS * SLOTS + r, cnt_ref[0, r].astype(F32), counts)
        for i in range(SLOTS):
            target = jnp.where(row == r * SLOTS + i, rows_ref[r, i], target)
    pick = jnp.where(lane == target, 1.0, 0.0).astype(jnp.bfloat16)
    own_points.wait()
    mine = raw[...]
    block = jnp.dot(pick, mine, preferred_element_type=F32)
    slots[sub, :, :npd] = (block[:, :npd] + counts).astype(jnp.bfloat16)
    slots[sub, :, npd:] = block[:, npd:].astype(jnp.bfloat16)

    pl.semaphore_wait(barrier, len(partners))

    def remote(src, dst, send, recv, device):
        return pltpu.make_async_remote_copy(
            src_ref=src, dst_ref=dst, send_sem=send, recv_sem=recv, device_id=device, device_id_type=MESH
        )

    def to_sides(place, count, group):
        for d, column in ((1, 2), (3, 3)):
            src, dst = cand.at[0, pl.ds(place, count), USED_ROWS], cand.at[column, pl.ds(place, count), USED_ROWS]
            remote(src, dst, y_send, y_recv.at[group], y_to[d]).start()

    def to_far(place):
        remote(cand.at[0, place, USED_ROWS], cand.at[1, place, USED_ROWS], far_send, far_recv.at[place - 6], y_to[2]).start()

    def far_along_z(src, place, count, group, d, lanes=None):
        src, dst = cand.at[1, pl.ds(src, count), USED_ROWS], cand.at[1, pl.ds(place, count), USED_ROWS]
        if lanes is not None:
            part = pl.ds(lanes * (width // 2), width // 2)
            src, dst = src.at[:, :, part], dst.at[:, :, part]
        remote(src, dst, far_z_send, far_z_recv.at[group], z_to[d]).start()

    def along_z(src, place, d, lanes=None):
        if lanes is None:
            src, dst = cand.at[0, src, USED_ROWS], cand.at[0, place, USED_ROWS]
        else:
            part = pl.ds(lanes * (width // 2), width // 2)
            src, dst = cand.at[0, src, USED_ROWS, part], cand.at[0, place, USED_ROWS, part]
        remote(src, dst, z_block_send, z_block_recv.at[place + (lanes or 0)], z_to[d]).start()

    def z_arrived(*places):
        for place in places:
            wait_bytes(cand.at[0, place, USED_ROWS], z_block_recv.at[place])

    def wait_bytes(ref, sem):
        pltpu.make_async_copy(ref, ref, sem).wait()

    for device in y_line:
        remote(slots.at[sub], slots.at[sub], slots_send, slots_recv, device).start()
    pall[me] = mine.T
    slot_right, slot_left, slot_far = (lax.rem(x + d, XS) * 2 + core for d in (1, 3, 2))
    top, low = pl.ds(0, width // 2), pl.ds(width // 2, width // 2)
    mine_at = pall.at[me]
    pts_right = remote(mine_at, mine_at, pts_send.at[0], pts_recv.at[0], x_right)
    pts_left = remote(mine_at, mine_at, pts_send.at[1], pts_recv.at[1], x_left)
    pts_core = remote(mine_at, mine_at, pts_send.at[2], pts_recv.at[2], other_core)
    pts_right.start()
    pts_left.start()
    pts_core.start()

    wait_bytes(slots.at[pl.ds(0, SUBS - 1)], slots_recv)
    flat = slots[...].reshape(SUBS * RAW, width)
    known = flat[:, :npd].astype(F32)
    offset = jnp.sum(known * before, axis=0, keepdims=True)
    count = jnp.sum(known * itself, axis=0, keepdims=True)
    choice = wanted_round & (slot_index < count) & (offset + slot_index == wanted)
    share = jnp.dot(jnp.where(choice, 1.0, 0.0).astype(jnp.bfloat16), flat, preferred_element_type=F32)
    cand[:, 7] = share.reshape(XS, BLK, width).astype(jnp.bfloat16)

    along_z(7, 6, 4)
    along_z(7, 8, -4)
    for place, d in ((0, 2), (1, -2), (2, 1), (5, -1)):
        along_z(7, place, d)

    pts_right.wait_recv()
    near_left = pall.at[slot_left]
    far_top = remote(near_left.at[top], near_left.at[top], pts_send.at[3], pts_recv.at[3], x_right)
    core_left = remote(near_left, near_left, pts_send.at[4], pts_recv.at[4], other_core)
    far_top.start()
    core_left.start()
    pts_left.wait_recv()
    near_right = pall.at[slot_right]
    far_low = remote(near_right.at[low], near_right.at[low], pts_send.at[5], pts_recv.at[5], x_left)
    core_right = remote(near_right, near_right, pts_send.at[6], pts_recv.at[6], other_core)
    far_low.start()
    core_right.start()

    z_arrived(6)
    to_far(6)
    along_z(6, 15, 4, 0)
    for place, d in ((13, 3), (11, 2), (9, 1), (4, -1)):
        along_z(6, place, d)
    z_arrived(8)
    to_far(8)
    along_z(8, 15, -4, 1)
    for place, d in ((14, -3), (12, -2), (10, -1), (3, 1)):
        along_z(8, place, d)
    to_sides(6, 1, 0)
    to_sides(8, 1, 0)

    for place in (6, 8):
        wait_bytes(cand.at[1, place, USED_ROWS], far_recv.at[place - 6])
    far_along_z(6, 15, 1, 1, 4, 0)
    far_along_z(8, 15, 1, 1, -4, 1)
    far_along_z(6, 13, 1, 1, 3)
    far_along_z(8, 14, 1, 1, -3)
    far_along_z(6, 11, 1, 1, 2)
    far_along_z(8, 12, 1, 1, -2)
    far_along_z(6, 9, 1, 0, 1)
    far_along_z(8, 10, 1, 0, -1)
    far_along_z(7, 0, 1, 0, 2)
    far_along_z(7, 1, 1, 0, -2)
    far_along_z(7, 2, 2, 0, 1)
    far_along_z(6, 4, 2, 0, -1)

    far_top.wait_recv()
    far_low.wait_recv()
    far = pall.at[slot_far]
    core_far = remote(far, far, pts_send.at[7], pts_recv.at[7], other_core)
    core_far.start()

    z_arrived(0, 1, 2, 3, 4, 5)
    to_sides(0, 6, 0)
    z_arrived(9, 10)
    to_sides(9, 2, 0)
    z_arrived(11, 12, 13, 14)
    to_sides(11, 4, 1)
    half_block = cand.at[0, 15, USED_ROWS, pl.ds(0, width // 2)]
    wait_bytes(half_block, z_block_recv.at[15])
    wait_bytes(half_block, z_block_recv.at[16])
    to_sides(15, 1, 1)

    def absorb(first, count):
        blocks = XS * count
        rows = cand[:, first : first + count].reshape(blocks, BLK, width)
        half = jnp.zeros((blocks, BLK, npd), F32)
        for t in range(width // npd):
            piece = rows[:, :, t * npd : (t + 1) * npd].astype(F32)
            half = half + piece * piece
        half = 0.5 * jnp.sum(half, axis=2, keepdims=True)
        flat = rows.reshape(blocks * BLK, width)
        for j in range(SUBS // 2):
            group = jnp.concatenate([pall[2 * j], pall[2 * j + 1]], axis=1)
            dots = jnp.dot(flat, group, preferred_element_type=F32)
            best = jnp.min(half - dots.reshape(blocks, BLK, 2 * npd), axis=0)
            mins[j] = best if first == 0 else jnp.minimum(mins[j], best)

    pts_core.wait_recv()
    core_left.wait_recv()
    core_right.wait_recv()
    core_far.wait_recv()
    for b in range(SUBS):
        wide = pall[b].astype(F32)
        squares[b : b + 1, :] = jnp.sum(wide * wide, axis=0, keepdims=True)
    wait_bytes(cand.at[pl.ds(2, 2), pl.ds(0, NEAR - 1), USED_ROWS], y_recv.at[0])
    wait_bytes(cand.at[1, pl.ds(0, 8), USED_ROWS], far_z_recv.at[0])
    absorb(0, NEAR)
    wait_bytes(cand.at[pl.ds(2, 2), pl.ds(NEAR, ZS - NEAR), USED_ROWS], y_recv.at[1])
    wait_bytes(cand.at[1, pl.ds(NEAR, ZS - NEAR), USED_ROWS], far_z_recv.at[1])
    absorb(NEAR, ZS - NEAR)

    for j in range(SUBS // 2):
        for r in range(ROUNDS):
            low_r = jnp.min(mins[j, r * SHARE : (r + 1) * SHARE, :], axis=0, keepdims=True)
            for h in range(2):
                line[me, r, 2 * j + h : 2 * j + h + 1, :] = low_r[:, h * npd : (h + 1) * npd]

    for device in x_line:
        remote(line.at[me], line.at[me], line_send, line_recv, device).start()
    wait_bytes(line.at[pl.ds(0, SUBS - 1)], line_recv)

    lanes = lax.broadcasted_iota(jnp.int32, (1, npd), 1)
    least = None
    total = jnp.zeros((1, npd), F32)
    for r in range(ROUNDS):
        now = jnp.min(line[:, r], axis=0)
        least = now if least is None else jnp.minimum(least, now)
        dist = jnp.maximum(squares[...] + 2.0 * least, 0.0)
        near[r] = dist
        part = jnp.sum(jnp.sum(dist, axis=0, keepdims=True), axis=1, keepdims=True)
        total = jnp.where(lanes == r, part, total)

    zsum[0] = total

    for d in (8, 7, 9, 6, 10, 5, 11, 4, 12, 3, 13, 2, 14, 1, 15):
        remote(zsum.at[0], zsum.at[ZS - d], z_send, z_recv, at_z(d)).start()
    wait_bytes(slots.at[pl.ds(0, SUBS - 1)], slots_send)
    wait_bytes(cand.at[0, pl.ds(0, 15), USED_ROWS], z_block_send)
    wait_bytes(cand.at[pl.ds(0, 2), pl.ds(0, 15), USED_ROWS], y_send)
    wait_bytes(cand.at[0, pl.ds(0, 2), USED_ROWS], far_send)
    wait_bytes(cand.at[0, pl.ds(0, 13), USED_ROWS], far_z_send)
    for copy in (pts_right, pts_left, pts_core, far_top, core_left, far_low, core_right, core_far):
        copy.wait_send()
    wait_bytes(line.at[pl.ds(0, SUBS - 1)], line_send)
    wait_bytes(zsum.at[pl.ds(0, ZS - 1)], z_recv)
    ysum[0] = jnp.sum(zsum[...], axis=0)
    for d in (1, 3, 2):
        remote(ysum.at[0], ysum.at[XS - d], c_send, c_recv, y_to[d]).start()
    wait_bytes(ysum.at[pl.ds(0, XS - 1)], c_recv)
    cost = jnp.sum(ysum[...], axis=0)
    for r in range(ROUNDS):
        cost_r = jnp.sum(jnp.where(lanes == r, cost, 0.0), axis=1, keepdims=True)
        out_ref[r : r + 1, :] = npts * near[r, pl.ds(me, 1), :] / cost_r
    wait_bytes(zsum.at[pl.ds(0, ZS - 1)], z_send)
    wait_bytes(ysum.at[pl.ds(0, XS - 1)], c_send)


def shards(points, cand_rows, cand_count):
    npd, width = points.shape
    npts = float(npd * lax.axis_size(("dp", "sub")))
    dma = pltpu.SemaphoreType.DMA
    operands = (cand_rows, cand_count.reshape(1, ROUNDS), points)
    return pl.pallas_call(
        lambda *refs: kernel(npts, *refs),
        out_shape=jax.ShapeDtypeStruct((ROUNDS, npd), F32),
        in_specs=[
            pl.BlockSpec(memory_space=pl.ANY),
            pl.BlockSpec(memory_space=pl.ANY),
            pl.BlockSpec(memory_space=pl.ANY),
        ],
        out_specs=pl.BlockSpec(memory_space=pltpu.VMEM),
        scratch_shapes=[
            pltpu.SMEM((ROUNDS, SLOTS), jnp.int32),
            pltpu.SMEM((1, ROUNDS), jnp.int32),
            pltpu.VMEM((npd, width), jnp.bfloat16),
            pltpu.VMEM((SUBS, RAW, width), jnp.bfloat16),
            pltpu.VMEM((XS, ZS, BLK, width), jnp.bfloat16),
            pltpu.VMEM((SUBS, width, npd), jnp.bfloat16),
            pltpu.VMEM((SUBS // 2, BLK, 2 * npd), F32),
            pltpu.VMEM((SUBS, npd), F32),
            pltpu.VMEM((SUBS, ROUNDS, SUBS, npd), F32),
            pltpu.VMEM((ROUNDS, SUBS, npd), F32),
            pltpu.VMEM((ZS, 1, npd), F32),
            pltpu.VMEM((XS, 1, npd), F32),
            dma((3,)),
            dma,
            dma,
            dma,
            dma,
            dma((17,)),
            dma((2,)),
            dma,
            dma,
            dma((3,)),
            dma((2,)),
            dma((8,)),
            dma((8,)),
            dma,
            dma,
            dma,
            dma,
            dma,
            dma,
        ],
        compiler_params=pltpu.CompilerParams(
            collective_id=0, has_side_effects=True, vmem_limit_bytes=40 * 1024 * 1024
        ),
        cost_estimate=pl.CostEstimate(
            flops=2 * 1024 * 1024 * width, bytes_accessed=npd * width * 2, transcendentals=0
        ),
    )(*(pltpu.with_memory_space_constraint(value, pltpu.HBM) for value in operands))


def solution(mesh):
    in_specs = (P(("dp", "sub"), None), P(None, ("dp", "sub")), P(None, ("dp", "sub")))
    out_specs = P(None, ("dp", "sub"))
    return jax.shard_map(shards, mesh=mesh, in_specs=in_specs, out_specs=out_specs, check_vma=False)
```
